32 devices in a mesh: sec: 4 (over x, core), px: 2 (over y), py: 4 (over z).
Axes of the slice: x: 2, y: 2, z: 4, core: 2. Of those that a mesh axis runs over, the one named last changes fastest.
Arguments:
- background: bfloat16 [2, 4, 512, 8192], P(None, 'sec', 'px', 'py'), may hold values from -6 to 6
- src_pos: int32 [16], replicated, may hold values from 0 to 1048575
- coupling: bfloat16 [4, 512, 512], P('sec', 'px'), may hold values from 0.3984375 to 1
- x_factor: bfloat16 [4, 2, 512, 512], P('sec', None, ('px', 'py')), may hold values from -1.25 to 1.25, as said below
- y_factor: bfloat16 [4, 2, 512, 512], P('sec', None, ('px', 'py')), may hold values from -1.25 to 1.25, as said below
Outputs:
- sweep_out: bfloat16 [2, 4, 512, 8192], P(None, 'sec', 'px', 'py')
The draws below stay inside these ranges and needn't reach their ends.
Inputs may be any that keep to these rules, and one draw needn't show every extreme that they name: `x_factor`: factor entries; each is a dense complex matrix. `y_factor`: factor entries; each is a dense complex matrix.
All inputs are finite; a program needn't handle non-finite values.
Results may differ from the reference program's by a relative error of at most 0.02.
Values may be sent and summed in bfloat16 or wider, within the bound.
No kernel may reach another device: no remote copies, remote signals or barrier semaphores. Data moves between devices by JAX's collectives and lax.ppermute only.
A program may use at most 64 MiB of HBM per device.

```python
import math
import jax
import jax.numpy as jnp

NX = 512
NY = 512
NSRC = 16
LAYERS = 4


def front_factor(key, layer_count, matrix_order):
    phase_key = jax.random.fold_in(key, 11)
    spread_key = jax.random.fold_in(key, 12)
    phases = jax.random.uniform(phase_key, (layer_count, matrix_order), jnp.float32, -math.pi, math.pi)
    spread = jnp.clip(jax.random.normal(spread_key, (layer_count, 2, matrix_order, matrix_order), jnp.float32), -4.0, 4.0)
    spread = spread * (0.5 / math.sqrt(matrix_order))
    identity = jnp.eye(matrix_order, dtype=jnp.float32)
    diagonal = jnp.stack([jnp.cos(phases), jnp.sin(phases)], axis=1)[:, :, :, None] * identity
    return (spread + diagonal).astype(jnp.bfloat16)


def draw_x_factor(key, part):
    return front_factor(key, LAYERS, NX)


def draw_y_factor(key, part):
    return front_factor(jax.random.fold_in(key, 5), LAYERS, NY)


def place_ends(entries, stream_key, low, high):
    shape = entries.shape
    spot = [jax.random.randint(jax.random.fold_in(stream_key, axis), (), 0, shape[axis]) for axis in range(len(shape))]
    entries = entries.at[tuple(spot)].set(low)
    longest = shape.index(max(shape))
    spot[longest] = (spot[longest] + 1) % shape[longest]
    return entries.at[tuple(spot)].set(high)


def shard_levels(stream_key, dims, shards, least, top_value):
    def one(axis_at, blocks):
        draws = jax.random.uniform(jax.random.fold_in(jax.random.fold_in(stream_key, 6), axis_at), (blocks,), jnp.float32, least / len(shards), top_value / len(shards))
        return jnp.repeat(jnp.exp(draws), dims[axis_at] // blocks).reshape((-1,) + (1,) * (len(dims) - axis_at - 1))

    factor_of = one(*shards[0])
    for cut in shards[1:]:
        factor_of = factor_of * one(*cut)
    return factor_of


def bell_draw(stream_key, extent, scale, limit, pieces=(), kind=jnp.bfloat16):
    factor_of = shard_levels(stream_key, extent, pieces, -0.22, 0.18) if pieces else 1.0
    entries = jax.random.normal(stream_key, extent, jnp.float32) * scale * factor_of
    return jnp.minimum(jnp.maximum(entries, -limit), limit).astype(kind)


def setup_inputs(seed: int = 0) -> dict:
    streams_of = jax.random.split(jax.random.key(seed), 6)
    return {
        "background": bell_draw(streams_of[0], (2, LAYERS, NX, NSRC * NY), 1.0, 6.0, ((1, 4), (2, 2), (3, 4))),
        "src_pos": place_ends(jax.random.randint(streams_of[1], (NSRC,), 0, LAYERS * NX * NY), jax.random.fold_in(streams_of[1], 1), 0, (LAYERS * NX * NY) - 1).astype(jnp.int32),
        "coupling": jnp.clip(0.3984375 + 0.6015625 * jax.random.uniform(streams_of[2], (LAYERS, NX, NY), jnp.float32) ** shard_levels(streams_of[2], (LAYERS, NX, NY), ((0, 4), (1, 2)), -0.2, 0.2), 0.3984375, 1.0).astype(jnp.bfloat16),
        "x_factor": draw_x_factor(jax.random.fold_in(streams_of[5], 71), 0),
        "y_factor": draw_y_factor(jax.random.fold_in(streams_of[5], 71), 0),
    }


source_amplitude = 8.0


def transform(factor, field_in, pattern):
    factor32 = factor.astype(jnp.float32)
    field32 = field_in.astype(jnp.float32)
    real_part = jnp.einsum(pattern, factor32[0], field32[0]) - jnp.einsum(pattern, factor32[1], field32[1])
    imag_part = jnp.einsum(pattern, factor32[0], field32[1]) + jnp.einsum(pattern, factor32[1], field32[0])
    return jnp.stack([real_part, imag_part]).astype(jnp.bfloat16)


def apply_front(x_layer, y_layer, field_in):
    inner_field = transform(y_layer, field_in, "yk,xsk->xsy")
    return transform(x_layer, inner_field, "xk,ksy->xsy")


def reference(background, src_pos, coupling, x_factor, y_factor):
    rhs_field = background.astype(jnp.float32).reshape(2, LAYERS, NX, NSRC, NY)
    layer_of = src_pos // (NX * NY)
    remainder = src_pos % (NX * NY)
    row_of = remainder // NY
    column_of = remainder % NY
    sources = jnp.arange(NSRC, dtype=jnp.int32)
    rhs_field = rhs_field.at[0, layer_of, row_of, sources, column_of].add(source_amplitude)
    weights = coupling.astype(jnp.float32)[:, None, :, None, :]
    forward = []
    previous = jnp.zeros((2, NX, NSRC, NY), jnp.bfloat16)
    for layer_index in range(LAYERS):
        reduced = (rhs_field[:, layer_index] - weights[layer_index] * previous.astype(jnp.float32)).astype(jnp.bfloat16)
        previous = apply_front(x_factor[layer_index], y_factor[layer_index], reduced)
        forward.append(previous)
    result = [forward[LAYERS - 1] for layer_index in range(LAYERS)]
    later_field = forward[LAYERS - 1]
    for layer_index in range(LAYERS - 2, -1, -1):
        sent_field = (weights[layer_index + 1] * later_field.astype(jnp.float32)).astype(jnp.bfloat16)
        solved = apply_front(x_factor[layer_index], y_factor[layer_index], sent_field)
        later_field = (forward[layer_index].astype(jnp.float32) - solved.astype(jnp.float32)).astype(jnp.bfloat16)
        result[layer_index] = later_field
    return jnp.stack(result, axis=1).reshape(2, LAYERS, NX, NSRC * NY)
```

```python
import functools

import jax
import jax.numpy as jnp
from jax import lax
from jax.experimental import pallas as pl
from jax.experimental.pallas import tpu as pltpu
from jax.sharding import PartitionSpec as P

source_amplitude = 8.0
vmem_bytes = 40 * 1024 * 1024
bf16 = jnp.bfloat16
f32 = jnp.float32
anywhere = pl.BlockSpec(memory_space=pl.ANY)
in_smem = pl.BlockSpec(memory_space=pltpu.SMEM)
in_vmem = pl.BlockSpec(memory_space=pltpu.VMEM)


def shifted(x, axis, by):
    peers = lax.axis_size(axis)
    pairs = [(i, i + by) for i in range(peers) if 0 <= i + by < peers]
    return lax.ppermute(x, axis, pairs)


def complex_block(factor):
    upper = jnp.concatenate([factor[0], -factor[1]], axis=1)
    lower = jnp.concatenate([factor[1], factor[0]], axis=1)
    return jnp.concatenate([upper, lower], axis=0)


def y_transform(real_turned, imag_turned, field_in):
    real_part = jnp.dot(field_in[0], real_turned, preferred_element_type=jnp.float32) - jnp.dot(
        field_in[1], imag_turned, preferred_element_type=jnp.float32
    )
    imag_part = jnp.dot(field_in[0], imag_turned, preferred_element_type=jnp.float32) + jnp.dot(
        field_in[1], real_turned, preferred_element_type=jnp.float32
    )
    return jnp.stack([real_part, imag_part]).astype(jnp.bfloat16)


def x_transform(x_block, field_in):
    planes, rows_all, width = field_in.shape
    output = jnp.dot(
        x_block, field_in.reshape(planes * rows_all, width), preferred_element_type=jnp.float32
    )
    return output.astype(jnp.bfloat16).reshape(planes, rows_all, width)


def scale_rows(field_in, weights, width):
    planes, rows_here, merged = field_in.shape
    spread = field_in.astype(jnp.float32).reshape(planes, rows_here, merged // width, width)
    return (spread * weights.astype(jnp.float32)[None, :, None, :]).reshape(
        planes, rows_here, merged
    )


def pick_batch(field, batch_count, batch_index):
    planes, rows_here, merged = field.shape
    split_field = field.reshape(planes, rows_here, batch_count, merged // batch_count)
    return lax.dynamic_index_in_dim(split_field, batch_index, 2, keepdims=False)


def place_batch(field, piece, batch_count, batch_index):
    planes, rows_here, merged = field.shape
    split_field = field.reshape(planes, rows_here, batch_count, merged // batch_count)
    shaped = piece.reshape(planes, rows_here, 1, merged // batch_count)
    updated = lax.dynamic_update_slice_in_dim(split_field, shaped, batch_index, 2)
    return updated.reshape(planes, rows_here, merged)


def on_device_by_layer(background, src_pos, coupling, x_factor, y_factor):
    source_count = src_pos.shape[0]
    sec_count = lax.axis_size("sec")
    sec_index = lax.axis_index("sec")
    grid_y = lax.axis_size("py")
    own_x = lax.axis_index("px")
    own_y = lax.axis_index("py")
    local_sources = source_count // grid_y
    x_pieces, y_pieces = (
        lax.all_gather(x_factor[0], ("px", "py"), axis=1, tiled=True),
        lax.all_gather(y_factor[0], ("px", "py"), axis=1, tiled=True),
    )
    x_block = complex_block(x_pieces)
    real_turned = y_pieces[0].T
    imag_turned = y_pieces[1].T
    local_field = background[:, 0]
    local_weights = coupling[0]
    rows_here = local_field.shape[1]
    full_cols = y_factor.shape[3]
    plane_cells = x_factor.shape[3] * full_cols
    own_sources = lax.dynamic_slice_in_dim(src_pos, own_y * local_sources, local_sources)
    layer_of = own_sources // plane_cells
    remainder = own_sources % plane_cells
    row_of = remainder // full_cols
    column_of = remainder % full_cols
    row_start = own_x * rows_here
    row_hit = row_of[None, :] == row_start + jnp.arange(rows_here, dtype=jnp.int32)[:, None]
    col_hit = column_of[:, None] == jnp.arange(full_cols, dtype=jnp.int32)[None, :]
    layer_hit = layer_of == sec_index
    delta = (row_hit[:, :, None] & col_hit[None, :, :] & layer_hit[None, :, None]).astype(
        jnp.float32
    )
    delta = (delta * source_amplitude).reshape(rows_here, local_sources * full_cols)
    real_rhs = local_field[0].astype(jnp.float32) + delta
    rhs_field = jnp.stack([real_rhs, local_field[1].astype(jnp.float32)])

    def apply_front(field_in):
        turned = y_transform(real_turned, imag_turned, field_in)
        line_field = lax.all_to_all(turned, "px", split_axis=2, concat_axis=1, tiled=True)
        finished = x_transform(x_block, line_field)
        return lax.all_to_all(finished, "px", split_axis=1, concat_axis=2, tiled=True)

    forward_field = jnp.zeros(local_field.shape, jnp.bfloat16)
    outgoing = pick_batch(forward_field, sec_count, 0)
    for step in range(2 * sec_count - 1):
        incoming = shifted(outgoing, "sec", 1)
        batch_index = step - sec_index
        active = (batch_index >= 0) & (batch_index < sec_count)
        clamped = jnp.clip(batch_index, 0, sec_count - 1)
        rhs_batch = pick_batch(rhs_field, sec_count, clamped)
        reduced = (rhs_batch - scale_rows(incoming, local_weights, full_cols)).astype(jnp.bfloat16)
        candidate = apply_front(reduced)
        previous = pick_batch(forward_field, sec_count, clamped)
        kept = jnp.where(active, candidate, previous)
        forward_field = place_batch(forward_field, kept, sec_count, clamped)
        outgoing = candidate
    sweep_field = forward_field
    for step in range(2 * sec_count - 2):
        send_index = jnp.clip(step - (sec_count - 1 - sec_index), 0, sec_count - 1)
        own_batch = pick_batch(sweep_field, sec_count, send_index)
        sent_field = scale_rows(own_batch, local_weights, full_cols).astype(jnp.bfloat16)
        incoming = shifted(sent_field, "sec", -1)
        batch_index = step - (sec_count - 2 - sec_index)
        active = (batch_index >= 0) & (batch_index < sec_count) & (sec_index <= sec_count - 2)
        clamped = jnp.clip(batch_index, 0, sec_count - 1)
        solved = apply_front(incoming)
        forward_batch = pick_batch(forward_field, sec_count, clamped)
        candidate = (forward_batch.astype(jnp.float32) - solved.astype(jnp.float32)).astype(
            jnp.bfloat16
        )
        previous = pick_batch(sweep_field, sec_count, clamped)
        kept = jnp.where(active, candidate, previous)
        sweep_field = place_batch(sweep_field, kept, sec_count, clamped)
    return sweep_field[:, None]


def start_all(copies):
    for copy in copies:
        copy.start()


def wait_all(copies):
    for copy in copies:
        copy.wait()


def row_chunks(order, step):
    step = min(step, order)
    return [slice(first, first + step) for first in range(0, order, step)]


def pack_kernel(place, field, *rest):
    pieces, sems = rest[:-1], rest[-1]
    copies = []
    for index, piece in enumerate(pieces):
        width = piece.shape[2]
        offset = pl.multiple_of(place[index] * width, width)
        copies.append(
            pltpu.make_async_copy(field.at[:, :, pl.ds(offset, width)], piece, sems.at[index])
        )
    start_all(copies)
    wait_all(copies)


def unpack_kernel(place, *rest):
    pieces, field, sems = rest[:-2], rest[-2], rest[-1]
    copies = []
    for index, piece in enumerate(pieces):
        width = piece.shape[2]
        offset = pl.multiple_of(place[index] * width, width)
        copies.append(
            pltpu.make_async_copy(piece, field.at[:, :, pl.ds(offset, width)], sems.at[index])
        )
    start_all(copies)
    wait_all(copies)


class Factors:
    def __init__(self, gathered, slot_from, slot, plain, crossed, sems):
        order = gathered.shape[-1]
        left, right = pl.ds(0, order), pl.ds(order, order)
        self.order, self.slot = order, slot
        self.plain, self.crossed = plain, crossed
        self.copies = []
        for which in range(2):
            real = gathered.at[:, slot_from, 2 * which]
            imag = gathered.at[:, slot_from, 2 * which + 1]
            ends = (
                (real, plain, left),
                (imag, plain, right),
                (imag, crossed, left),
                (real, crossed, right),
            )
            self.copies.append(
                [
                    pltpu.make_async_copy(
                        source, target.at[slot, which, :, :, half], sems.at[slot, which, index]
                    )
                    for index, (source, target, half) in enumerate(ends)
                ]
            )

    def start(self):
        start_all(self.copies[1])
        start_all(self.copies[0])

    def ready(self, which):
        wait_all(self.copies[which])
        right = slice(self.order, 2 * self.order)
        self.plain[self.slot, which, :, :, right] = -self.plain[self.slot, which, :, :, right]

    def apply(self, beside, below, store, fresh):
        order = self.order
        turned = (((1,), (1,)), ((), ()))
        if fresh:
            self.ready(1)
        for plane, ref in enumerate((self.plain, self.crossed)):
            blocks, height = ref.shape[2:4]
            for columns in row_chunks(order, 256):
                rows = ref[self.slot, 1, columns.start // height : columns.stop // height]
                rows = rows.reshape(columns.stop - columns.start, 2 * order)
                part = lax.dot_general(beside[...], rows, turned, preferred_element_type=f32)
                below[plane * order : (plane + 1) * order, columns] = part.astype(bf16)
        if fresh:
            self.ready(0)
        for plane, ref in enumerate((self.plain, self.crossed)):
            matrix = ref[self.slot, 0].reshape(order, 2 * order)
            for columns in row_chunks(order, 256):
                store(
                    plane,
                    columns,
                    jnp.dot(matrix, below[:, columns], preferred_element_type=f32),
                )


def rows_of(blocked, slot, rows):
    height = blocked.shape[2]
    part = blocked[slot, rows.start // height : rows.stop // height]
    return part.reshape(rows.stop - rows.start, part.shape[-1])


def reduce_into(beside, rhs, info, slot, weights, incoming):
    order = beside.shape[0]
    for plane in range(2):
        for rows in row_chunks(order, 128):
            values = rhs[slot, plane, rows].astype(f32)
            if plane == 0:
                row = lax.broadcasted_iota(jnp.int32, values.shape, 0) + rows.start
                column = lax.broadcasted_iota(jnp.int32, values.shape, 1)
                hit = (row == info[1]) & (column == info[2]) & (info[0] == slot)
                values = values + jnp.where(hit, f32(source_amplitude), f32(0.0))
            scaled = rows_of(weights, slot, rows).astype(f32) * incoming(plane, rows)
            beside[rows, plane * order : (plane + 1) * order] = (values - scaled).astype(bf16)


def sent_into(beside, weights, slot, field):
    order = beside.shape[0]
    for plane in range(2):
        for rows in row_chunks(order, 128):
            scaled = rows_of(weights, slot, rows).astype(f32) * field(plane, rows)
            beside[rows, plane * order : (plane + 1) * order] = scaled.astype(bf16)


def subtract_into(target, forward):
    def store(plane, columns, values):
        solved = values.astype(bf16).astype(f32)
        target[plane, :, columns] = (forward(plane, columns).astype(f32) - solved).astype(bf16)

    return store


def round_into(target):
    def store(plane, columns, values):
        target[plane, :, columns] = values.astype(bf16)

    return store


def rhs_copies(info, pieces, rhs, sems):
    copies = []
    for index, piece in enumerate(pieces):
        height = piece.shape[1]
        rows = pl.ds(pl.multiple_of(info[5 + 2 * index] * height, height), height)
        copies.append(
            pltpu.make_async_copy(piece, rhs.at[info[4 + 2 * index], :, rows, :], sems.at[index])
        )
    return copies


def weight_copies(info, gathered, weights, sems):
    return [
        pltpu.make_async_copy(gathered.at[:, info[12 + slot], 4], weights.at[slot], sems.at[slot])
        for slot in range(2)
    ]


def layer_factors(info, gathered, plain, crossed, sems):
    return [Factors(gathered, info[12 + slot], slot, plain, crossed, sems) for slot in range(2)]


def first_kernel(info, gathered, p0, p1, p2, p3, w_low, w_high, plain, crossed, weights, rhs,
                 beside, below, sems, fsems):
    @pl.when(info[3] == 0)
    def _():
        low, high = layer_factors(info, gathered, plain, crossed, fsems)
        early = rhs_copies(info, (p0, p1, p2, p3), rhs, sems)
        early += weight_copies(info, gathered, weights, sems.at[pl.ds(4, 2)])
        start_all(early)
        low.start()
        high.start()
        wait_all(early)
        reduce_into(beside, rhs, info, 0, weights, lambda plane, rows: f32(0.0))
        low.apply(beside, below, round_into(w_low), True)
        reduce_into(
            beside, rhs, info, 1, weights, lambda plane, rows: w_low[plane, rows].astype(f32)
        )
        high.apply(beside, below, round_into(w_high), True)


def last_kernel(info, gathered, p0, p1, p2, p3, incoming, field, sent, plain, crossed, weights, rhs,
                arrived, kept, beside, below, sems, fsems, osems):
    @pl.when(info[3] == 1)
    def _():
        low, high = layer_factors(info, gathered, plain, crossed, fsems)
        early = rhs_copies(info, (p0, p1, p2, p3), rhs, sems)
        early += weight_copies(info, gathered, weights, sems.at[pl.ds(4, 2)])
        early.append(pltpu.make_async_copy(incoming, arrived, sems.at[6]))
        start_all(early)
        low.start()
        high.start()
        wait_all(early)
        order = beside.shape[0]
        reduce_into(
            beside, rhs, info, 0, weights, lambda plane, rows: arrived[plane, rows].astype(f32)
        )
        w_low, w_high = kept.at[0], kept.at[1]
        low.apply(beside, below, round_into(w_low), True)
        reduce_into(
            beside, rhs, info, 1, weights, lambda plane, rows: w_low[plane, rows].astype(f32)
        )
        high.apply(beside, below, round_into(w_high), True)
        out_high = pltpu.make_async_copy(w_high, field.at[1], osems.at[1])
        out_high.start()
        sent_into(beside, weights, 1, lambda plane, rows: w_high[plane, rows].astype(f32))
        low.apply(
            beside,
            below,
            subtract_into(w_low, lambda plane, columns: w_low[plane, :, columns]),
            False,
        )
        out_low = pltpu.make_async_copy(w_low, field.at[0], osems.at[0])
        out_low.start()
        sent_into(beside, weights, 0, lambda plane, rows: w_low[plane, rows].astype(f32))
        for plane in range(2):
            sent[plane] = beside[:, plane * order : (plane + 1) * order]
        out_high.wait()
        out_low.wait()


def back_kernel(info, gathered, w_low, w_high, incoming, field, p0, p1, p2, p3, plain, crossed,
                weights, kept, beside, below, sems, fsems, osems):
    pieces = (p0, p1, p2, p3)

    def piece_copies(source):
        copies = []
        for index, piece in enumerate(pieces):
            height = piece.shape[1]
            rows = pl.ds(pl.multiple_of(info[5 + 2 * index] * height, height), height)
            copies.append(
                pltpu.make_async_copy(
                    source.at[info[4 + 2 * index], :, rows, :], piece, osems.at[index]
                )
            )
        return copies

    @pl.when(info[3] == 0)
    def _():
        low, high = layer_factors(info, gathered, plain, crossed, fsems)
        order = beside.shape[0]
        columns = [pl.ds(plane * order, order) for plane in range(2)]
        early = [
            pltpu.make_async_copy(incoming.at[plane], beside.at[:, columns[plane]], sems.at[plane])
            for plane in range(2)
        ]
        start_all(early)
        high.start()
        later = weight_copies(info, gathered, weights, sems.at[pl.ds(2, 2)])
        later.append(pltpu.make_async_copy(w_low, kept.at[0], sems.at[4]))
        later.append(pltpu.make_async_copy(w_high, kept.at[1], sems.at[5]))
        start_all(later)
        low.start()
        wait_all(early)
        wait_all(later)
        u_low, u_high = kept.at[0], kept.at[1]
        high.apply(
            beside,
            below,
            subtract_into(u_high, lambda plane, columns: u_high[plane, :, columns]),
            True,
        )
        sent_into(beside, weights, 1, lambda plane, rows: u_high[plane, rows].astype(f32))
        low.apply(
            beside,
            below,
            subtract_into(u_low, lambda plane, columns: u_low[plane, :, columns]),
            True,
        )
        copies = piece_copies(kept)
        start_all(copies)
        wait_all(copies)

    @pl.when(info[3] != 0)
    def _():
        copies = piece_copies(field)
        start_all(copies)
        wait_all(copies)


def on_device(background, src_pos, coupling, x_factor, y_factor):
    px_count = lax.axis_size("px")
    sec_index, own_x, own_y = (lax.axis_index(axis) for axis in ("sec", "px", "py"))
    group, member = sec_index // 2, sec_index % 2
    groups = lax.axis_size("sec") // 2
    order = y_factor.shape[3]
    field = background[:, 0]
    rows_here = field.shape[1]
    height = x_factor.shape[2]
    params = pltpu.CompilerParams(vmem_limit_bytes=vmem_bytes)
    rounds = [(a, b) for a in range(groups) for b in range(px_count)]

    def pairs(a, b):
        return [
            ((2 * x + c) * px_count + y, (2 * ((c + a) % 2) + x) * px_count + (y + b) % px_count)
            for x in range(groups)
            for c in range(2)
            for y in range(px_count)
        ]

    def back_pairs(a, b):
        return [(target, source) for source, target in pairs(a, b)]

    shard_weights = lax.dynamic_slice_in_dim(coupling[0], own_y * height, height)
    shard = jnp.concatenate([x_factor[0], y_factor[0], shard_weights[None]], axis=0)
    shards = [lax.ppermute(shard, ("sec", "px"), pairs(a, 0)) for a in range(2)]
    gathered = lax.all_gather(jnp.stack(shards), ("px", "py"), axis=0, tiled=False)

    sends_to = jnp.stack(
        [((member + a) % 2) * px_count + (own_x + b) % px_count for a, b in rounds]
    ).astype(jnp.int32)
    piece_shape = jax.ShapeDtypeStruct((2, rows_here, order), bf16)
    pieces = pl.pallas_call(
        pack_kernel,
        out_shape=[piece_shape] * len(rounds),
        in_specs=[in_smem, anywhere],
        out_specs=[anywhere] * len(rounds),
        scratch_shapes=[pltpu.SemaphoreType.DMA((len(rounds),))],
        compiler_params=params,
    )(sends_to, field)
    pieces = [
        lax.ppermute(piece, ("sec", "px"), pairs(a, b)) for piece, (a, b) in zip(pieces, rounds)
    ]

    own_source = src_pos[own_y * groups * px_count + group * px_count + own_x]
    plane_cells = x_factor.shape[3] * order
    layer = own_source // plane_cells
    remainder = own_source % plane_cells
    entries = [
        jnp.where(layer // 2 == member, layer % 2, -1),
        remainder // order,
        remainder % order,
        member,
    ]
    for a, b in rounds:
        entries += [(group + a) % 2, (own_x - b) % px_count]
    entries += [group, (group + 1) % 2]
    info = jnp.stack([jnp.asarray(entry, jnp.int32) for entry in entries])

    full_shape = jax.ShapeDtypeStruct((2, order, order), bf16)
    blocks = gathered.shape[0]
    factor_scratch = pltpu.VMEM((2, 2, blocks, height, 2 * order), bf16)
    weight_scratch = pltpu.VMEM((2, blocks, height, order), bf16)
    field_scratch = pltpu.VMEM((2, 2, order, order), bf16)
    beside_scratch = pltpu.VMEM((order, 2 * order), bf16)
    below_scratch = pltpu.VMEM((2 * order, order), bf16)
    factor_sems = pltpu.SemaphoreType.DMA((2, 2, 4))
    solve_flops = 16 * order**3
    w_low, w_high = pl.pallas_call(
        first_kernel,
        out_shape=[full_shape] * 2,
        in_specs=[in_smem] + [anywhere] * 5,
        out_specs=[in_vmem] * 2,
        scratch_shapes=[
            factor_scratch,
            factor_scratch,
            weight_scratch,
            field_scratch,
            beside_scratch,
            below_scratch,
            pltpu.SemaphoreType.DMA((6,)),
            factor_sems,
        ],
        compiler_params=params,
        cost_estimate=pl.CostEstimate(
            flops=2 * solve_flops, bytes_accessed=16 * order * order * 2, transcendentals=0
        ),
    )(info, gathered, *pieces)

    up = [(2 * x, 2 * x + 1) for x in range(groups)]
    incoming = lax.ppermute(w_high, "sec", up)
    solved, sent = pl.pallas_call(
        last_kernel,
        out_shape=[jax.ShapeDtypeStruct((2, 2, order, order), bf16), full_shape],
        in_specs=[in_smem] + [anywhere] * 6,
        out_specs=[anywhere, in_vmem],
        scratch_shapes=[
            factor_scratch,
            factor_scratch,
            weight_scratch,
            field_scratch,
            pltpu.VMEM((2, order, order), bf16),
            field_scratch,
            beside_scratch,
            below_scratch,
            pltpu.SemaphoreType.DMA((7,)),
            factor_sems,
            pltpu.SemaphoreType.DMA((2,)),
        ],
        compiler_params=params,
        cost_estimate=pl.CostEstimate(
            flops=3 * solve_flops, bytes_accessed=16 * order * order * 2, transcendentals=0
        ),
    )(info, gathered, *pieces, incoming)

    down = [(target, source) for source, target in up]
    incoming = lax.ppermute(sent, "sec", down)
    results = pl.pallas_call(
        back_kernel,
        out_shape=[piece_shape] * len(rounds),
        in_specs=[in_smem] + [anywhere] * 5,
        out_specs=[anywhere] * len(rounds),
        scratch_shapes=[
            factor_scratch,
            factor_scratch,
            weight_scratch,
            field_scratch,
            beside_scratch,
            below_scratch,
            pltpu.SemaphoreType.DMA((6,)),
            factor_sems,
            pltpu.SemaphoreType.DMA((len(rounds),)),
        ],
        compiler_params=params,
        cost_estimate=pl.CostEstimate(
            flops=2 * solve_flops, bytes_accessed=16 * order * order * 2, transcendentals=0
        ),
    )(info, gathered, w_low, w_high, incoming, solved)
    results = [
        lax.ppermute(piece, ("sec", "px"), back_pairs(a, b)) for piece, (a, b) in zip(results, rounds)
    ]
    output = pl.pallas_call(
        unpack_kernel,
        out_shape=jax.ShapeDtypeStruct(field.shape, bf16),
        in_specs=[in_smem] + [anywhere] * len(rounds),
        out_specs=anywhere,
        scratch_shapes=[pltpu.SemaphoreType.DMA((len(rounds),))],
        compiler_params=params,
    )(sends_to, *results)
    return output[:, None]


def chip_plan_fits(mesh):
    return mesh.shape["sec"] == 4 and mesh.shape["px"] == 2


def solution(mesh):
    placed = (
        P(None, "sec", "px", "py"),
        P(),
        P("sec", "px", None),
        P("sec", None, ("px", "py"), None),
        P("sec", None, ("px", "py"), None),
    )
    return jax.shard_map(
        on_device if chip_plan_fits(mesh) else on_device_by_layer,
        mesh=mesh,
        in_specs=placed,
        out_specs=P(None, "sec", "px", "py"),
        check_vma=False,
    )
```

```python
import functools

import jax
import jax.numpy as jnp
from jax import lax
from jax.experimental import pallas as pl
from jax.experimental.pallas import tpu as pltpu
from jax.sharding import PartitionSpec as P

source_amplitude = 8.0
vmem_bytes = 60 * 1024 * 1024
bf16 = jnp.bfloat16
f32 = jnp.float32
anywhere = pl.BlockSpec(memory_space=pl.ANY)
in_smem = pl.BlockSpec(memory_space=pltpu.SMEM)
in_vmem = pl.BlockSpec(memory_space=pltpu.VMEM)

info_member, info_piece, info_slot, info_half, info_block = 3, 4, 12, 14, 16


def shifted(x, axis, by):
    peers = lax.axis_size(axis)
    pairs = [(i, i + by) for i in range(peers) if 0 <= i + by < peers]
    return lax.ppermute(x, axis, pairs)


def complex_block(factor):
    upper = jnp.concatenate([factor[0], -factor[1]], axis=1)
    lower = jnp.concatenate([factor[1], factor[0]], axis=1)
    return jnp.concatenate([upper, lower], axis=0)


def y_transform(real_turned, imag_turned, field_in):
    real_part = jnp.dot(field_in[0], real_turned, preferred_element_type=jnp.float32) - jnp.dot(
        field_in[1], imag_turned, preferred_element_type=jnp.float32
    )
    imag_part = jnp.dot(field_in[0], imag_turned, preferred_element_type=jnp.float32) + jnp.dot(
        field_in[1], real_turned, preferred_element_type=jnp.float32
    )
    return jnp.stack([real_part, imag_part]).astype(jnp.bfloat16)


def x_transform(x_block, field_in):
    planes, rows_all, width = field_in.shape
    output = jnp.dot(
        x_block, field_in.reshape(planes * rows_all, width), preferred_element_type=jnp.float32
    )
    return output.astype(jnp.bfloat16).reshape(planes, rows_all, width)


def scale_rows(field_in, weights, width):
    planes, rows_here, merged = field_in.shape
    spread = field_in.astype(jnp.float32).reshape(planes, rows_here, merged // width, width)
    return (spread * weights.astype(jnp.float32)[None, :, None, :]).reshape(
        planes, rows_here, merged
    )


def pick_batch(field, batch_count, batch_index):
    planes, rows_here, merged = field.shape
    split_field = field.reshape(planes, rows_here, batch_count, merged // batch_count)
    return lax.dynamic_index_in_dim(split_field, batch_index, 2, keepdims=False)


def place_batch(field, piece, batch_count, batch_index):
    planes, rows_here, merged = field.shape
    split_field = field.reshape(planes, rows_here, batch_count, merged // batch_count)
    shaped = piece.reshape(planes, rows_here, 1, merged // batch_count)
    updated = lax.dynamic_update_slice_in_dim(split_field, shaped, batch_index, 2)
    return updated.reshape(planes, rows_here, merged)


def on_device_by_layer(background, src_pos, coupling, x_factor, y_factor):
    source_count = src_pos.shape[0]
    sec_count = lax.axis_size("sec")
    sec_index = lax.axis_index("sec")
    grid_y = lax.axis_size("py")
    own_x = lax.axis_index("px")
    own_y = lax.axis_index("py")
    local_sources = source_count // grid_y
    x_pieces, y_pieces = (
        lax.all_gather(x_factor[0], ("px", "py"), axis=1, tiled=True),
        lax.all_gather(y_factor[0], ("px", "py"), axis=1, tiled=True),
    )
    x_block = complex_block(x_pieces)
    real_turned = y_pieces[0].T
    imag_turned = y_pieces[1].T
    local_field = background[:, 0]
    local_weights = coupling[0]
    rows_here = local_field.shape[1]
    full_cols = y_factor.shape[3]
    plane_cells = x_factor.shape[3] * full_cols
    own_sources = lax.dynamic_slice_in_dim(src_pos, own_y * local_sources, local_sources)
    layer_of = own_sources // plane_cells
    remainder = own_sources % plane_cells
    row_of = remainder // full_cols
    column_of = remainder % full_cols
    row_start = own_x * rows_here
    row_hit = row_of[None, :] == row_start + jnp.arange(rows_here, dtype=jnp.int32)[:, None]
    col_hit = column_of[:, None] == jnp.arange(full_cols, dtype=jnp.int32)[None, :]
    layer_hit = layer_of == sec_index
    delta = (row_hit[:, :, None] & col_hit[None, :, :] & layer_hit[None, :, None]).astype(
        jnp.float32
    )
    delta = (delta * source_amplitude).reshape(rows_here, local_sources * full_cols)
    real_rhs = local_field[0].astype(jnp.float32) + delta
    rhs_field = jnp.stack([real_rhs, local_field[1].astype(jnp.float32)])

    def apply_front(field_in):
        turned = y_transform(real_turned, imag_turned, field_in)
        line_field = lax.all_to_all(turned, "px", split_axis=2, concat_axis=1, tiled=True)
        finished = x_transform(x_block, line_field)
        return lax.all_to_all(finished, "px", split_axis=1, concat_axis=2, tiled=True)

    forward_field = jnp.zeros(local_field.shape, jnp.bfloat16)
    outgoing = pick_batch(forward_field, sec_count, 0)
    for step in range(2 * sec_count - 1):
        incoming = shifted(outgoing, "sec", 1)
        batch_index = step - sec_index
        active = (batch_index >= 0) & (batch_index < sec_count)
        clamped = jnp.clip(batch_index, 0, sec_count - 1)
        rhs_batch = pick_batch(rhs_field, sec_count, clamped)
        reduced = (rhs_batch - scale_rows(incoming, local_weights, full_cols)).astype(jnp.bfloat16)
        candidate = apply_front(reduced)
        previous = pick_batch(forward_field, sec_count, clamped)
        kept = jnp.where(active, candidate, previous)
        forward_field = place_batch(forward_field, kept, sec_count, clamped)
        outgoing = candidate
    sweep_field = forward_field
    for step in range(2 * sec_count - 2):
        send_index = jnp.clip(step - (sec_count - 1 - sec_index), 0, sec_count - 1)
        own_batch = pick_batch(sweep_field, sec_count, send_index)
        sent_field = scale_rows(own_batch, local_weights, full_cols).astype(jnp.bfloat16)
        incoming = shifted(sent_field, "sec", -1)
        batch_index = step - (sec_count - 2 - sec_index)
        active = (batch_index >= 0) & (batch_index < sec_count) & (sec_index <= sec_count - 2)
        clamped = jnp.clip(batch_index, 0, sec_count - 1)
        solved = apply_front(incoming)
        forward_batch = pick_batch(forward_field, sec_count, clamped)
        candidate = (forward_batch.astype(jnp.float32) - solved.astype(jnp.float32)).astype(
            jnp.bfloat16
        )
        previous = pick_batch(sweep_field, sec_count, clamped)
        kept = jnp.where(active, candidate, previous)
        sweep_field = place_batch(sweep_field, kept, sec_count, clamped)
    return sweep_field[:, None]


def start_all(copies):
    for copy in copies:
        copy.start()


def wait_all(copies):
    for copy in copies:
        copy.wait()


def row_chunks(order, step):
    step = min(step, order)
    return [slice(first, first + step) for first in range(0, order, step)]


def pack_kernel(place, field, *rest):
    pieces, sems = rest[:-1], rest[-1]
    copies = []
    for index, piece in enumerate(pieces):
        width = piece.shape[2]
        offset = pl.multiple_of(place[index] * width, width)
        copies.append(
            pltpu.make_async_copy(field.at[:, :, pl.ds(offset, width)], piece, sems.at[index])
        )
    start_all(copies)
    wait_all(copies)


def unpack_kernel(place, *rest):
    pieces, field, sems = rest[:-2], rest[-2], rest[-1]
    copies = []
    for index, piece in enumerate(pieces):
        width = piece.shape[2]
        offset = pl.multiple_of(place[index] * width, width)
        copies.append(
            pltpu.make_async_copy(piece, field.at[:, :, pl.ds(offset, width)], sems.at[index])
        )
    start_all(copies)
    wait_all(copies)


def stack_kernel(info, own, first, second, third, x_column, y_column, sems):
    height = own.shape[1]
    copies = []
    for turn, block in enumerate((own, first, second, third)):
        rows = pl.ds(pl.multiple_of(info[info_block + turn] * height, height), height)
        for which, column in enumerate((x_column, y_column)):
            copies.append(
                pltpu.make_async_copy(
                    block.at[pl.ds(2 * which, 2)], column.at[:, rows, :], sems.at[turn, which]
                )
            )
    start_all(copies)
    wait_all(copies)


def weight_kernel(info, own, first, second, third, weights, sems):
    height = own.shape[1]
    half_height = weights.shape[1] // 2
    copies = []
    for turn, block in enumerate((own, first, second, third)):
        for index in range(block.shape[0]):
            slot, half = info[info_piece + 2 * index], info[info_piece + 2 * index + 1]
            start = half * half_height + info[info_block + turn] * height
            rows = pl.ds(pl.multiple_of(start, height), height)
            copies.append(
                pltpu.make_async_copy(
                    block.at[index], weights.at[slot, rows, :], sems.at[turn, index]
                )
            )
    start_all(copies)
    wait_all(copies)


class Factors:
    def __init__(self, info, columns, plain, crossed, sems):
        order = plain.shape[2]
        self.order, self.plain, self.crossed, self.sems = order, plain, crossed, sems
        self.columns = columns
        left, right = pl.ds(0, order), pl.ds(order, order)
        self.ends = ((0, plain, left), (1, plain, right), (1, crossed, left), (0, crossed, right))
        height = columns[0][0].shape[1]
        for which in (1, 0):
            for index, column in enumerate(columns[which]):
                slot, half = info[info_slot + index // 2], info[info_half + index % 2]
                rows = pl.ds(pl.multiple_of(half * height, height), height)
                for end, (plane, target, side) in enumerate(self.ends):
                    pltpu.make_async_copy(
                        column.at[plane],
                        target.at[slot, which, rows, side],
                        sems.at[slot, which, index % 2, end],
                    ).start()

    def ready(self, slot, which):
        column = self.columns[which][0]
        height = column.shape[1]
        for half in range(2):
            rows = pl.ds(half * height, height)
            for end, (plane, target, side) in enumerate(self.ends):
                pltpu.make_async_copy(
                    column.at[plane],
                    target.at[slot, which, rows, side],
                    self.sems.at[slot, which, half, end],
                ).wait()
        right = slice(self.order, 2 * self.order)
        self.plain[slot, which, :, right] = -self.plain[slot, which, :, right]

    def apply(self, slot, beside, below, store, fresh):
        order = self.order
        turned = (((1,), (1,)), ((), ()))
        if fresh:
            self.ready(slot, 1)
        for plane, ref in enumerate((self.plain, self.crossed)):
            for columns in row_chunks(order, 256):
                part = lax.dot_general(
                    beside[...], ref[slot, 1, columns], turned, preferred_element_type=f32
                )
                below[plane * order : (plane + 1) * order, columns] = part.astype(bf16)
        if fresh:
            self.ready(slot, 0)
        for plane, ref in enumerate((self.plain, self.crossed)):
            for columns in row_chunks(order, 256):
                store(
                    plane,
                    columns,
                    jnp.dot(ref[slot, 0], below[:, columns], preferred_element_type=f32),
                )


def reduce_into(beside, rhs, info, slot, weights, incoming):
    order = beside.shape[0]
    for plane in range(2):
        for rows in row_chunks(order, 128):
            values = rhs[slot, plane, rows].astype(f32)
            if plane == 0:
                row = lax.broadcasted_iota(jnp.int32, values.shape, 0) + rows.start
                column = lax.broadcasted_iota(jnp.int32, values.shape, 1)
                hit = (row == info[1]) & (column == info[2]) & (info[0] == slot)
                values = values + jnp.where(hit, f32(source_amplitude), f32(0.0))
            scaled = weights[slot, rows].astype(f32) * incoming(plane, rows)
            beside[rows, plane * order : (plane + 1) * order] = (values - scaled).astype(bf16)


def sent_into(beside, weights, slot, field):
    order = beside.shape[0]
    for plane in range(2):
        for rows in row_chunks(order, 128):
            scaled = weights[slot, rows].astype(f32) * field(plane, rows)
            beside[rows, plane * order : (plane + 1) * order] = scaled.astype(bf16)


def subtract_into(target, forward):
    def store(plane, columns, values):
        solved = values.astype(bf16).astype(f32)
        target[plane, :, columns] = (forward(plane, columns).astype(f32) - solved).astype(bf16)

    return store


def round_into(target):
    def store(plane, columns, values):
        target[plane, :, columns] = values.astype(bf16)

    return store


def rhs_copies(info, pieces, rhs, sems):
    copies = []
    for index, piece in enumerate(pieces):
        height = piece.shape[1]
        slot, half = info[info_piece + 2 * index], info[info_piece + 2 * index + 1]
        rows = pl.ds(pl.multiple_of(half * height, height), height)
        copies.append(pltpu.make_async_copy(piece, rhs.at[slot, :, rows, :], sems.at[index]))
    return copies


def first_kernel(info, x0, x1, x2, x3, y0, y1, y2, y3, coupling, p0, p1, p2, p3, w_low, w_high,
                 plain, crossed, weights, rhs, beside, below, sems, fsems):
    @pl.when(info[info_member] == 0)
    def _():
        early = rhs_copies(info, (p0, p1, p2, p3), rhs, sems)
        early.append(pltpu.make_async_copy(coupling, weights, sems.at[4]))
        start_all(early)
        factors = Factors(info, ((x0, x1, x2, x3), (y0, y1, y2, y3)), plain, crossed, fsems)
        wait_all(early)
        reduce_into(beside, rhs, info, 0, weights, lambda plane, rows: f32(0.0))
        factors.apply(0, beside, below, round_into(w_low), True)
        reduce_into(
            beside, rhs, info, 1, weights, lambda plane, rows: w_low[plane, rows].astype(f32)
        )
        factors.apply(1, beside, below, round_into(w_high), True)


def last_kernel(info, x0, x1, x2, x3, y0, y1, y2, y3, coupling, p0, p1, p2, p3, incoming, field,
                sent, plain, crossed, weights, rhs, arrived, kept, beside, below, sems, fsems, osems):
    @pl.when(info[info_member] == 1)
    def _():
        early = rhs_copies(info, (p0, p1, p2, p3), rhs, sems)
        early.append(pltpu.make_async_copy(coupling, weights, sems.at[4]))
        early.append(pltpu.make_async_copy(incoming, arrived, sems.at[5]))
        start_all(early)
        factors = Factors(info, ((x0, x1, x2, x3), (y0, y1, y2, y3)), plain, crossed, fsems)
        wait_all(early)
        order = beside.shape[0]
        reduce_into(
            beside, rhs, info, 0, weights, lambda plane, rows: arrived[plane, rows].astype(f32)
        )
        w_low, w_high = kept.at[0], kept.at[1]
        factors.apply(0, beside, below, round_into(w_low), True)
        reduce_into(
            beside, rhs, info, 1, weights, lambda plane, rows: w_low[plane, rows].astype(f32)
        )
        factors.apply(1, beside, below, round_into(w_high), True)
        out_high = pltpu.make_async_copy(w_high, field.at[1], osems.at[1])
        out_high.start()
        sent_into(beside, weights, 1, lambda plane, rows: w_high[plane, rows].astype(f32))
        factors.apply(
            0,
            beside,
            below,
            subtract_into(w_low, lambda plane, columns: w_low[plane, :, columns]),
            False,
        )
        out_low = pltpu.make_async_copy(w_low, field.at[0], osems.at[0])
        out_low.start()
        sent_into(beside, weights, 0, lambda plane, rows: w_low[plane, rows].astype(f32))
        for plane in range(2):
            sent[plane] = beside[:, plane * order : (plane + 1) * order]
        out_high.wait()
        out_low.wait()


def back_kernel(info, x0, x1, x2, x3, y0, y1, y2, y3, coupling, w_low, w_high, incoming, field,
                p0, p1, p2, p3, plain, crossed, weights, kept, beside, below, sems, fsems, osems):
    def piece_copies(source):
        copies = []
        for index, piece in enumerate((p0, p1, p2, p3)):
            height = piece.shape[1]
            slot, half = info[info_piece + 2 * index], info[info_piece + 2 * index + 1]
            rows = pl.ds(pl.multiple_of(half * height, height), height)
            copies.append(
                pltpu.make_async_copy(source.at[slot, :, rows, :], piece, osems.at[index])
            )
        return copies

    @pl.when(info[info_member] == 0)
    def _():
        order = beside.shape[0]
        columns = [pl.ds(plane * order, order) for plane in range(2)]
        early = [
            pltpu.make_async_copy(incoming.at[plane], beside.at[:, columns[plane]], sems.at[plane])
            for plane in range(2)
        ]
        start_all(early)
        factors = Factors(info, ((x0, x1, x2, x3), (y0, y1, y2, y3)), plain, crossed, fsems)
        later = [
            pltpu.make_async_copy(coupling, weights, sems.at[2]),
            pltpu.make_async_copy(w_low, kept.at[0], sems.at[3]),
            pltpu.make_async_copy(w_high, kept.at[1], sems.at[4]),
        ]
        start_all(later)
        wait_all(early)
        wait_all(later)
        u_low, u_high = kept.at[0], kept.at[1]
        factors.apply(
            1,
            beside,
            below,
            subtract_into(u_high, lambda plane, columns: u_high[plane, :, columns]),
            True,
        )
        sent_into(beside, weights, 1, lambda plane, rows: u_high[plane, rows].astype(f32))
        factors.apply(
            0,
            beside,
            below,
            subtract_into(u_low, lambda plane, columns: u_low[plane, :, columns]),
            True,
        )
        copies = piece_copies(kept)
        start_all(copies)
        wait_all(copies)

    @pl.when(info[info_member] != 0)
    def _():
        copies = piece_copies(field)
        start_all(copies)
        wait_all(copies)


def on_device(background, src_pos, coupling, x_factor, y_factor):
    px_count = lax.axis_size("px")
    sec_index, own_x, own_y = (lax.axis_index(axis) for axis in ("sec", "px", "py"))
    group, member = sec_index // 2, sec_index % 2
    groups = lax.axis_size("sec") // 2
    order = y_factor.shape[3]
    field = background[:, 0]
    rows_here = field.shape[1]
    height = x_factor.shape[2]
    params = pltpu.CompilerParams(vmem_limit_bytes=vmem_bytes)
    rounds = [(a, b) for a in range(groups) for b in range(px_count)]

    def pairs(a, b):
        return [
            ((2 * x + c) * px_count + y, (2 * ((c + a) % 2) + x) * px_count + (y + b) % px_count)
            for x in range(groups)
            for c in range(2)
            for y in range(px_count)
        ]

    def back_pairs(a, b):
        return [(target, source) for source, target in pairs(a, b)]

    own_source = src_pos[own_y * groups * px_count + group * px_count + own_x]
    plane_cells = x_factor.shape[3] * order
    layer = own_source // plane_cells
    remainder = own_source % plane_cells
    py_count = lax.axis_size("py")
    entries = [
        jnp.where(layer // 2 == member, layer % 2, -1),
        remainder // order,
        remainder % order,
        member,
    ]
    for a, b in rounds:
        entries += [(group + a) % 2, (own_x - b) % px_count]
    entries += [group, (group + 1) % 2, own_x, (own_x + 1) % 2]
    entries += [(own_y - turn) % py_count for turn in range(py_count)]
    info = jnp.stack([jnp.asarray(entry, jnp.int32) for entry in entries])

    def rotated(block):
        return [block] + [
            lax.ppermute(block, "py", [(z, (z + turn) % py_count) for z in range(py_count)])
            for turn in range(1, py_count)
        ]

    shard = jnp.concatenate([x_factor[0], y_factor[0]], axis=0)
    shards = rotated(shard)
    sends_to = jnp.stack(
        [((member + a) % 2) * px_count + (own_x + b) % px_count for a, b in rounds]
    ).astype(jnp.int32)
    piece_shape = jax.ShapeDtypeStruct((2, rows_here, order), bf16)
    pieces = pl.pallas_call(
        pack_kernel,
        out_shape=[piece_shape] * len(rounds),
        in_specs=[in_smem, anywhere],
        out_specs=[anywhere] * len(rounds),
        scratch_shapes=[pltpu.SemaphoreType.DMA((len(rounds),))],
        compiler_params=params,
    )(sends_to, field)
    pieces = [
        lax.ppermute(piece, ("sec", "px"), pairs(a, b)) for piece, (a, b) in zip(pieces, rounds)
    ]

    column_shape = jax.ShapeDtypeStruct((2, rows_here, order), bf16)
    x_column, y_column = pl.pallas_call(
        stack_kernel,
        out_shape=[column_shape] * 2,
        in_specs=[in_smem] + [anywhere] * 4,
        out_specs=[anywhere] * 2,
        scratch_shapes=[pltpu.SemaphoreType.DMA((4, 2))],
        compiler_params=params,
    )(info, *shards)

    own_weights = lax.dynamic_slice_in_dim(coupling[0], own_y * height, height)
    own_weights = jnp.stack([lax.ppermute(own_weights, ("sec", "px"), pairs(a, b)) for a, b in rounds])
    weights = pl.pallas_call(
        weight_kernel,
        out_shape=jax.ShapeDtypeStruct((2, order, order), bf16),
        in_specs=[in_smem] + [anywhere] * 4,
        out_specs=anywhere,
        scratch_shapes=[pltpu.SemaphoreType.DMA((4, 4))],
        compiler_params=params,
    )(info, *rotated(own_weights))

    def across(block, a):
        return lax.ppermute(block, ("sec", "px"), pairs(a, 0))

    def aside(block):
        return lax.ppermute(block, "px", [(y, (y + 1) % 2) for y in range(2)])

    x_aside = aside(x_column)
    y_near = [across(y_column, a) for a in range(2)]
    x_near = [across(x_column, a) for a in range(2)]
    y_far = [aside(block) for block in y_near]
    x_far = [across(x_aside, a) for a in range(2)]
    factors = []
    for near, far in ((x_near, x_far), (y_near, y_far)):
        factors += [near[0], far[0], near[1], far[1]]

    full_shape = jax.ShapeDtypeStruct((2, order, order), bf16)
    factor_scratch = pltpu.VMEM((2, 2, order, 2 * order), bf16)
    weight_scratch = pltpu.VMEM((2, order, order), bf16)
    field_scratch = pltpu.VMEM((2, 2, order, order), bf16)
    beside_scratch = pltpu.VMEM((order, 2 * order), bf16)
    below_scratch = pltpu.VMEM((2 * order, order), bf16)
    factor_sems = pltpu.SemaphoreType.DMA((2, 2, 2, 4))
    solve_flops = 16 * order**3
    w_low, w_high = pl.pallas_call(
        first_kernel,
        out_shape=[full_shape] * 2,
        in_specs=[in_smem] + [anywhere] * 13,
        out_specs=[in_vmem] * 2,
        scratch_shapes=[
            factor_scratch,
            factor_scratch,
            weight_scratch,
            field_scratch,
            beside_scratch,
            below_scratch,
            pltpu.SemaphoreType.DMA((6,)),
            factor_sems,
        ],
        compiler_params=params,
        cost_estimate=pl.CostEstimate(
            flops=2 * solve_flops, bytes_accessed=16 * order * order * 2, transcendentals=0
        ),
    )(info, *factors, weights, *pieces)

    up = [(2 * x, 2 * x + 1) for x in range(groups)]
    incoming = lax.ppermute(w_high, "sec", up)
    solved, sent = pl.pallas_call(
        last_kernel,
        out_shape=[jax.ShapeDtypeStruct((2, 2, order, order), bf16), full_shape],
        in_specs=[in_smem] + [anywhere] * 14,
        out_specs=[anywhere, in_vmem],
        scratch_shapes=[
            factor_scratch,
            factor_scratch,
            weight_scratch,
            field_scratch,
            pltpu.VMEM((2, order, order), bf16),
            field_scratch,
            beside_scratch,
            below_scratch,
            pltpu.SemaphoreType.DMA((7,)),
            factor_sems,
            pltpu.SemaphoreType.DMA((2,)),
        ],
        compiler_params=params,
        cost_estimate=pl.CostEstimate(
            flops=3 * solve_flops, bytes_accessed=16 * order * order * 2, transcendentals=0
        ),
    )(info, *factors, weights, *pieces, incoming)

    down = [(target, source) for source, target in up]
    incoming = lax.ppermute(sent, "sec", down)
    results = pl.pallas_call(
        back_kernel,
        out_shape=[piece_shape] * len(rounds),
        in_specs=[in_smem] + [anywhere] * 13,
        out_specs=[anywhere] * len(rounds),
        scratch_shapes=[
            factor_scratch,
            factor_scratch,
            weight_scratch,
            field_scratch,
            beside_scratch,
            below_scratch,
            pltpu.SemaphoreType.DMA((6,)),
            factor_sems,
            pltpu.SemaphoreType.DMA((len(rounds),)),
        ],
        compiler_params=params,
        cost_estimate=pl.CostEstimate(
            flops=2 * solve_flops, bytes_accessed=16 * order * order * 2, transcendentals=0
        ),
    )(info, *factors, weights, w_low, w_high, incoming, solved)
    results = [
        lax.ppermute(piece, ("sec", "px"), back_pairs(a, b)) for piece, (a, b) in zip(results, rounds)
    ]
    output = pl.pallas_call(
        unpack_kernel,
        out_shape=jax.ShapeDtypeStruct(field.shape, bf16),
        in_specs=[in_smem] + [anywhere] * len(rounds),
        out_specs=anywhere,
        scratch_shapes=[pltpu.SemaphoreType.DMA((len(rounds),))],
        compiler_params=params,
    )(sends_to, *results)
    return output[:, None]


def chip_plan_fits(mesh):
    return mesh.shape["sec"] == 4 and mesh.shape["px"] == 2 and mesh.shape["py"] == 4


def solution(mesh):
    placed = (
        P(None, "sec", "px", "py"),
        P(),
        P("sec", "px", None),
        P("sec", None, ("px", "py"), None),
        P("sec", None, ("px", "py"), None),
    )
    return jax.shard_map(
        on_device if chip_plan_fits(mesh) else on_device_by_layer,
        mesh=mesh,
        in_specs=placed,
        out_specs=P(None, "sec", "px", "py"),
        check_vma=False,
    )
```

```python
import functools

import jax
import jax.numpy as jnp
from jax import lax
from jax.experimental import pallas as pl
from jax.experimental.pallas import tpu as pltpu
from jax.sharding import PartitionSpec as P

source_amplitude = 8.0
vmem_bytes = 32 * 1024 * 1024
bf16 = jnp.bfloat16
f32 = jnp.float32
anywhere = pl.BlockSpec(memory_space=pl.ANY)
in_smem = pl.BlockSpec(memory_space=pltpu.SMEM)
in_vmem = pl.BlockSpec(memory_space=pltpu.VMEM)

info_member, info_piece, info_slot, info_half, info_block = 3, 4, 12, 14, 16


def shifted(x, axis, by):
    peers = lax.axis_size(axis)
    pairs = [(i, i + by) for i in range(peers) if 0 <= i + by < peers]
    return lax.ppermute(x, axis, pairs)


def complex_block(factor):
    upper = jnp.concatenate([factor[0], -factor[1]], axis=1)
    lower = jnp.concatenate([factor[1], factor[0]], axis=1)
    return jnp.concatenate([upper, lower], axis=0)


def y_transform(real_turned, imag_turned, field_in):
    real_part = jnp.dot(field_in[0], real_turned, preferred_element_type=jnp.float32) - jnp.dot(
        field_in[1], imag_turned, preferred_element_type=jnp.float32
    )
    imag_part = jnp.dot(field_in[0], imag_turned, preferred_element_type=jnp.float32) + jnp.dot(
        field_in[1], real_turned, preferred_element_type=jnp.float32
    )
    return jnp.stack([real_part, imag_part]).astype(jnp.bfloat16)


def x_transform(x_block, field_in):
    planes, rows_all, width = field_in.shape
    output = jnp.dot(
        x_block, field_in.reshape(planes * rows_all, width), preferred_element_type=jnp.float32
    )
    return output.astype(jnp.bfloat16).reshape(planes, rows_all, width)


def scale_rows(field_in, weights, width):
    planes, rows_here, merged = field_in.shape
    spread = field_in.astype(jnp.float32).reshape(planes, rows_here, merged // width, width)
    return (spread * weights.astype(jnp.float32)[None, :, None, :]).reshape(
        planes, rows_here, merged
    )


def pick_batch(field, batch_count, batch_index):
    planes, rows_here, merged = field.shape
    split_field = field.reshape(planes, rows_here, batch_count, merged // batch_count)
    return lax.dynamic_index_in_dim(split_field, batch_index, 2, keepdims=False)


def place_batch(field, piece, batch_count, batch_index):
    planes, rows_here, merged = field.shape
    split_field = field.reshape(planes, rows_here, batch_count, merged // batch_count)
    shaped = piece.reshape(planes, rows_here, 1, merged // batch_count)
    updated = lax.dynamic_update_slice_in_dim(split_field, shaped, batch_index, 2)
    return updated.reshape(planes, rows_here, merged)


def on_device_by_layer(background, src_pos, coupling, x_factor, y_factor):
    source_count = src_pos.shape[0]
    sec_count = lax.axis_size("sec")
    sec_index = lax.axis_index("sec")
    grid_y = lax.axis_size("py")
    own_x = lax.axis_index("px")
    own_y = lax.axis_index("py")
    local_sources = source_count // grid_y
    x_pieces, y_pieces = (
        lax.all_gather(x_factor[0], ("px", "py"), axis=1, tiled=True),
        lax.all_gather(y_factor[0], ("px", "py"), axis=1, tiled=True),
    )
    x_block = complex_block(x_pieces)
    real_turned = y_pieces[0].T
    imag_turned = y_pieces[1].T
    local_field = background[:, 0]
    local_weights = coupling[0]
    rows_here = local_field.shape[1]
    full_cols = y_factor.shape[3]
    plane_cells = x_factor.shape[3] * full_cols
    own_sources = lax.dynamic_slice_in_dim(src_pos, own_y * local_sources, local_sources)
    layer_of = own_sources // plane_cells
    remainder = own_sources % plane_cells
    row_of = remainder // full_cols
    column_of = remainder % full_cols
    row_start = own_x * rows_here
    row_hit = row_of[None, :] == row_start + jnp.arange(rows_here, dtype=jnp.int32)[:, None]
    col_hit = column_of[:, None] == jnp.arange(full_cols, dtype=jnp.int32)[None, :]
    layer_hit = layer_of == sec_index
    delta = (row_hit[:, :, None] & col_hit[None, :, :] & layer_hit[None, :, None]).astype(
        jnp.float32
    )
    delta = (delta * source_amplitude).reshape(rows_here, local_sources * full_cols)
    real_rhs = local_field[0].astype(jnp.float32) + delta
    rhs_field = jnp.stack([real_rhs, local_field[1].astype(jnp.float32)])

    def apply_front(field_in):
        turned = y_transform(real_turned, imag_turned, field_in)
        line_field = lax.all_to_all(turned, "px", split_axis=2, concat_axis=1, tiled=True)
        finished = x_transform(x_block, line_field)
        return lax.all_to_all(finished, "px", split_axis=1, concat_axis=2, tiled=True)

    forward_field = jnp.zeros(local_field.shape, jnp.bfloat16)
    outgoing = pick_batch(forward_field, sec_count, 0)
    for step in range(2 * sec_count - 1):
        incoming = shifted(outgoing, "sec", 1)
        batch_index = step - sec_index
        active = (batch_index >= 0) & (batch_index < sec_count)
        clamped = jnp.clip(batch_index, 0, sec_count - 1)
        rhs_batch = pick_batch(rhs_field, sec_count, clamped)
        reduced = (rhs_batch - scale_rows(incoming, local_weights, full_cols)).astype(jnp.bfloat16)
        candidate = apply_front(reduced)
        previous = pick_batch(forward_field, sec_count, clamped)
        kept = jnp.where(active, candidate, previous)
        forward_field = place_batch(forward_field, kept, sec_count, clamped)
        outgoing = candidate
    sweep_field = forward_field
    for step in range(2 * sec_count - 2):
        send_index = jnp.clip(step - (sec_count - 1 - sec_index), 0, sec_count - 1)
        own_batch = pick_batch(sweep_field, sec_count, send_index)
        sent_field = scale_rows(own_batch, local_weights, full_cols).astype(jnp.bfloat16)
        incoming = shifted(sent_field, "sec", -1)
        batch_index = step - (sec_count - 2 - sec_index)
        active = (batch_index >= 0) & (batch_index < sec_count) & (sec_index <= sec_count - 2)
        clamped = jnp.clip(batch_index, 0, sec_count - 1)
        solved = apply_front(incoming)
        forward_batch = pick_batch(forward_field, sec_count, clamped)
        candidate = (forward_batch.astype(jnp.float32) - solved.astype(jnp.float32)).astype(
            jnp.bfloat16
        )
        previous = pick_batch(sweep_field, sec_count, clamped)
        kept = jnp.where(active, candidate, previous)
        sweep_field = place_batch(sweep_field, kept, sec_count, clamped)
    return sweep_field[:, None]


def start_all(copies):
    for copy in copies:
        copy.start()


def wait_all(copies):
    for copy in copies:
        copy.wait()


def row_chunks(order, step):
    step = min(step, order)
    return [slice(first, first + step) for first in range(0, order, step)]


def pack_kernel(place, field, *rest):
    pieces, sems = rest[:-1], rest[-1]
    copies = []
    for index, piece in enumerate(pieces):
        width = piece.shape[2]
        offset = pl.multiple_of(place[index] * width, width)
        copies.append(
            pltpu.make_async_copy(field.at[:, :, pl.ds(offset, width)], piece, sems.at[index])
        )
    start_all(copies)
    wait_all(copies)


def unpack_kernel(place, *rest):
    pieces, field, sems = rest[:-2], rest[-2], rest[-1]
    copies = []
    for index, piece in enumerate(pieces):
        width = piece.shape[2]
        offset = pl.multiple_of(place[index] * width, width)
        copies.append(
            pltpu.make_async_copy(piece, field.at[:, :, pl.ds(offset, width)], sems.at[index])
        )
    start_all(copies)
    wait_all(copies)


def stack_kernel(info, own, first, second, third, x_column, y_column, sems):
    height = own.shape[1]
    copies = []
    for turn, block in enumerate((own, first, second, third)):
        rows = pl.ds(pl.multiple_of(info[info_block + turn] * height, height), height)
        for which, column in enumerate((x_column, y_column)):
            copies.append(
                pltpu.make_async_copy(
                    block.at[pl.ds(2 * which, 2)], column.at[:, rows, :], sems.at[turn, which]
                )
            )
    start_all(copies)
    wait_all(copies)


def weight_kernel(info, own, first, second, third, weights, sems):
    height = own.shape[1]
    half_height = weights.shape[1] // 2
    copies = []
    for turn, block in enumerate((own, first, second, third)):
        for index in range(block.shape[0]):
            slot, half = info[info_piece + 2 * index], info[info_piece + 2 * index + 1]
            start = half * half_height + info[info_block + turn] * height
            rows = pl.ds(pl.multiple_of(start, height), height)
            copies.append(
                pltpu.make_async_copy(
                    block.at[index], weights.at[slot, rows, :], sems.at[turn, index]
                )
            )
    start_all(copies)
    wait_all(copies)


class Factors:
    def __init__(self, info, columns, held, sems):
        self.order, self.held, self.sems, self.columns = held.shape[2], held, sems, columns
        height = columns[0][0].shape[1]
        for which in (1, 0):
            for index, column in enumerate(columns[which]):
                slot, half = info[info_slot + index // 2], info[info_half + index % 2]
                rows = pl.ds(pl.multiple_of(half * height, height), height)
                for plane in range(2):
                    self.copy(column, plane, slot, which, rows, index % 2).start()

    def copy(self, column, plane, slot, which, rows, half):
        target = self.held.at[slot, which, rows, pl.ds(plane * self.order, self.order)]
        return pltpu.make_async_copy(
            column.at[plane], target, self.sems.at[slot, which, half, plane]
        )

    def ready(self, slot, which):
        column = self.columns[which][0]
        height = column.shape[1]
        for half in range(2):
            for plane in range(2):
                rows = pl.ds(half * height, height)
                self.copy(column, plane, slot, which, rows, half).wait()

    def apply(self, slot, beside, below, store, fresh):
        order = self.order
        turned = (((1,), (1,)), ((), ()))
        if fresh:
            self.ready(slot, 1)
        for columns in row_chunks(order, 256):
            part = lax.dot_general(
                beside[...], self.held[slot, 1, columns], turned, preferred_element_type=f32
            ).astype(bf16)
            real, imag = part[:order], part[order:]
            further = slice(columns.start + order, columns.stop + order)
            below[:order, columns] = real
            below[:order, further] = imag
            below[order:, columns] = -imag
            below[order:, further] = real
        if fresh:
            self.ready(slot, 0)
        for plane in range(2):
            for columns in row_chunks(order, 256):
                along = slice(columns.start + plane * order, columns.stop + plane * order)
                store(
                    plane,
                    columns,
                    jnp.dot(self.held[slot, 0], below[:, along], preferred_element_type=f32),
                )


def put_beside(beside, plane, rows, values):
    order = beside.shape[0] // 2
    left, right = slice(0, order), slice(order, 2 * order)
    lower = slice(rows.start + order, rows.stop + order)
    values = values.astype(bf16)
    if plane == 0:
        beside[rows, left] = values
        beside[lower, right] = values
    else:
        beside[rows, right] = -values
        beside[lower, left] = values


def reduce_into(beside, rhs, info, slot, weights, incoming):
    order = beside.shape[0] // 2
    for plane in range(2):
        for rows in row_chunks(order, 128):
            values = rhs[slot, plane, rows].astype(f32)
            if plane == 0:
                row = lax.broadcasted_iota(jnp.int32, values.shape, 0) + rows.start
                column = lax.broadcasted_iota(jnp.int32, values.shape, 1)
                hit = (row == info[1]) & (column == info[2]) & (info[0] == slot)
                values = values + jnp.where(hit, f32(source_amplitude), f32(0.0))
            scaled = weights[slot, rows].astype(f32) * incoming(plane, rows)
            put_beside(beside, plane, rows, values - scaled)


def sent_into(beside, weights, slot, field):
    order = beside.shape[0] // 2
    for plane in range(2):
        for rows in row_chunks(order, 128):
            scaled = weights[slot, rows].astype(f32) * field(plane, rows)
            put_beside(beside, plane, rows, scaled)


def subtract_into(target, forward):
    def store(plane, columns, values):
        solved = values.astype(bf16).astype(f32)
        target[plane, :, columns] = (forward(plane, columns).astype(f32) - solved).astype(bf16)

    return store


def round_into(target):
    def store(plane, columns, values):
        target[plane, :, columns] = values.astype(bf16)

    return store


def rhs_copies(info, pieces, rhs, sems):
    copies = []
    for index, piece in enumerate(pieces):
        height = piece.shape[1]
        slot, half = info[info_piece + 2 * index], info[info_piece + 2 * index + 1]
        rows = pl.ds(pl.multiple_of(half * height, height), height)
        copies.append(pltpu.make_async_copy(piece, rhs.at[slot, :, rows, :], sems.at[index]))
    return copies


def first_kernel(info, x0, x1, x2, x3, y0, y1, y2, y3, coupling, p0, p1, p2, p3, w_low, w_high,
                 held, weights, rhs, beside, below, sems, fsems):
    @pl.when(info[info_member] == 0)
    def _():
        early = rhs_copies(info, (p0, p1, p2, p3), rhs, sems)
        early.append(pltpu.make_async_copy(coupling, weights, sems.at[4]))
        start_all(early)
        factors = Factors(info, ((x0, x1, x2, x3), (y0, y1, y2, y3)), held, fsems)
        wait_all(early)
        reduce_into(beside, rhs, info, 0, weights, lambda plane, rows: f32(0.0))
        factors.apply(0, beside, below, round_into(w_low), True)
        reduce_into(
            beside, rhs, info, 1, weights, lambda plane, rows: w_low[plane, rows].astype(f32)
        )
        factors.apply(1, beside, below, round_into(w_high), True)


def last_kernel(info, x0, x1, x2, x3, y0, y1, y2, y3, coupling, p0, p1, p2, p3, incoming, field,
                sent, held, weights, rhs, arrived, kept, beside, below, sems, fsems, osems):
    @pl.when(info[info_member] == 1)
    def _():
        early = rhs_copies(info, (p0, p1, p2, p3), rhs, sems)
        early.append(pltpu.make_async_copy(coupling, weights, sems.at[4]))
        early.append(pltpu.make_async_copy(incoming, arrived, sems.at[5]))
        start_all(early)
        factors = Factors(info, ((x0, x1, x2, x3), (y0, y1, y2, y3)), held, fsems)
        wait_all(early)
        order = beside.shape[0] // 2
        reduce_into(
            beside, rhs, info, 0, weights, lambda plane, rows: arrived[plane, rows].astype(f32)
        )
        w_low, w_high = kept.at[0], kept.at[1]
        factors.apply(0, beside, below, round_into(w_low), True)
        reduce_into(
            beside, rhs, info, 1, weights, lambda plane, rows: w_low[plane, rows].astype(f32)
        )
        factors.apply(1, beside, below, round_into(w_high), True)
        out_high = pltpu.make_async_copy(w_high, field.at[1], osems.at[1])
        out_high.start()
        sent_into(beside, weights, 1, lambda plane, rows: w_high[plane, rows].astype(f32))
        factors.apply(
            0,
            beside,
            below,
            subtract_into(w_low, lambda plane, columns: w_low[plane, :, columns]),
            False,
        )
        out_low = pltpu.make_async_copy(w_low, field.at[0], osems.at[0])
        out_low.start()
        sent_into(beside, weights, 0, lambda plane, rows: w_low[plane, rows].astype(f32))
        for plane in range(2):
            sent[plane] = beside[plane * order : (plane + 1) * order, :order]
        out_high.wait()
        out_low.wait()


def back_kernel(info, x0, x1, x2, x3, y0, y1, y2, y3, coupling, w_low, w_high, incoming, field,
                p0, p1, p2, p3, held, weights, kept, arrived, beside, below, sems, fsems, osems):
    @pl.when(info[info_member] == 0)
    def _():
        early = [pltpu.make_async_copy(incoming, arrived, sems.at[0])]
        start_all(early)
        factors = Factors(info, ((x0, x1, x2, x3), (y0, y1, y2, y3)), held, fsems)
        early += [
            pltpu.make_async_copy(coupling, weights, sems.at[1]),
            pltpu.make_async_copy(w_low, kept.at[0], sems.at[2]),
            pltpu.make_async_copy(w_high, kept.at[1], sems.at[3]),
        ]
        start_all(early[1:])
        wait_all(early)
        order = beside.shape[0] // 2
        for plane in range(2):
            for rows in row_chunks(order, 128):
                put_beside(beside, plane, rows, arrived[plane, rows])
        u_low, u_high = kept.at[0], kept.at[1]
        factors.apply(
            1,
            beside,
            below,
            subtract_into(u_high, lambda plane, columns: u_high[plane, :, columns]),
            True,
        )
        sent_into(beside, weights, 1, lambda plane, rows: u_high[plane, rows].astype(f32))
        factors.apply(
            0,
            beside,
            below,
            subtract_into(u_low, lambda plane, columns: u_low[plane, :, columns]),
            True,
        )

    @pl.when(info[info_member] != 0)
    def _():
        finished = pltpu.make_async_copy(field, kept, sems.at[0])
        finished.start()
        finished.wait()

    copies = []
    for index, piece in enumerate((p0, p1, p2, p3)):
        height = piece.shape[1]
        slot, half = info[info_piece + 2 * index], info[info_piece + 2 * index + 1]
        rows = pl.ds(pl.multiple_of(half * height, height), height)
        copies.append(pltpu.make_async_copy(kept.at[slot, :, rows, :], piece, osems.at[index]))
    start_all(copies)
    wait_all(copies)


def on_device(background, src_pos, coupling, x_factor, y_factor):
    px_count = lax.axis_size("px")
    sec_index, own_x, own_y = (lax.axis_index(axis) for axis in ("sec", "px", "py"))
    group, member = sec_index // 2, sec_index % 2
    groups = lax.axis_size("sec") // 2
    order = y_factor.shape[3]
    field = background[:, 0]
    rows_here = field.shape[1]
    height = x_factor.shape[2]
    params = pltpu.CompilerParams(vmem_limit_bytes=vmem_bytes)
    rounds = [(a, b) for a in range(groups) for b in range(px_count)]

    def pairs(a, b):
        return [
            ((2 * x + c) * px_count + y, (2 * ((c + a) % 2) + x) * px_count + (y + b) % px_count)
            for x in range(groups)
            for c in range(2)
            for y in range(px_count)
        ]

    def back_pairs(a, b):
        return [(target, source) for source, target in pairs(a, b)]

    own_source = src_pos[own_y * groups * px_count + group * px_count + own_x]
    plane_cells = x_factor.shape[3] * order
    layer = own_source // plane_cells
    remainder = own_source % plane_cells
    py_count = lax.axis_size("py")
    entries = [
        jnp.where(layer // 2 == member, layer % 2, -1),
        remainder // order,
        remainder % order,
        member,
    ]
    for a, b in rounds:
        entries += [(group + a) % 2, (own_x - b) % px_count]
    entries += [group, (group + 1) % 2, own_x, (own_x + 1) % 2]
    entries += [(own_y - turn) % py_count for turn in range(py_count)]
    info = jnp.stack([jnp.asarray(entry, jnp.int32) for entry in entries])

    def rotated(block):
        return [block] + [
            lax.ppermute(block, "py", [(z, (z + turn) % py_count) for z in range(py_count)])
            for turn in range(1, py_count)
        ]

    shard = jnp.concatenate([x_factor[0], y_factor[0]], axis=0)
    shards = rotated(shard)
    sends_to = jnp.stack(
        [((member + a) % 2) * px_count + (own_x + b) % px_count for a, b in rounds]
    ).astype(jnp.int32)
    piece_shape = jax.ShapeDtypeStruct((2, rows_here, order), bf16)
    pieces = pl.pallas_call(
        pack_kernel,
        out_shape=[piece_shape] * len(rounds),
        in_specs=[in_smem, anywhere],
        out_specs=[in_vmem] * len(rounds),
        scratch_shapes=[pltpu.SemaphoreType.DMA((len(rounds),))],
        compiler_params=params,
    )(sends_to, field)
    pieces = [
        lax.ppermute(piece, ("sec", "px"), pairs(a, b)) for piece, (a, b) in zip(pieces, rounds)
    ]

    column_shape = jax.ShapeDtypeStruct((2, rows_here, order), bf16)
    x_column, y_column = pl.pallas_call(
        stack_kernel,
        out_shape=[column_shape] * 2,
        in_specs=[in_smem] + [anywhere] * 4,
        out_specs=[in_vmem] * 2,
        scratch_shapes=[pltpu.SemaphoreType.DMA((4, 2))],
        compiler_params=params,
    )(info, *shards)

    own_weights = lax.dynamic_slice_in_dim(coupling[0], own_y * height, height)
    own_weights = jnp.stack([lax.ppermute(own_weights, ("sec", "px"), pairs(a, b)) for a, b in rounds])
    weights = pl.pallas_call(
        weight_kernel,
        out_shape=jax.ShapeDtypeStruct((2, order, order), bf16),
        in_specs=[in_smem] + [anywhere] * 4,
        out_specs=in_vmem,
        scratch_shapes=[pltpu.SemaphoreType.DMA((4, 4))],
        compiler_params=params,
    )(info, *rotated(own_weights))

    def across(block, a):
        return lax.ppermute(block, ("sec", "px"), pairs(a, 0))

    def aside(block):
        return lax.ppermute(block, "px", [(y, (y + 1) % 2) for y in range(2)])

    x_aside = aside(x_column)
    y_near = [across(y_column, a) for a in range(2)]
    x_near = [across(x_column, a) for a in range(2)]
    y_far = [aside(block) for block in y_near]
    x_far = [across(x_aside, a) for a in range(2)]
    factors = []
    for near, far in ((x_near, x_far), (y_near, y_far)):
        factors += [near[0], far[0], near[1], far[1]]

    full_shape = jax.ShapeDtypeStruct((2, order, order), bf16)
    factor_scratch = pltpu.VMEM((2, 2, order, 2 * order), bf16)
    arrived_scratch = pltpu.VMEM((2, order, order), bf16)
    weight_scratch = pltpu.VMEM((2, order, order), bf16)
    field_scratch = pltpu.VMEM((2, 2, order, order), bf16)
    beside_scratch = pltpu.VMEM((2 * order, 2 * order), bf16)
    below_scratch = beside_scratch
    factor_sems = pltpu.SemaphoreType.DMA((2, 2, 2, 2))
    solve_flops = 16 * order**3
    w_low, w_high = pl.pallas_call(
        first_kernel,
        out_shape=[full_shape] * 2,
        in_specs=[in_smem] + [anywhere] * 13,
        out_specs=[in_vmem] * 2,
        scratch_shapes=[
            factor_scratch,
            weight_scratch,
            field_scratch,
            beside_scratch,
            below_scratch,
            pltpu.SemaphoreType.DMA((6,)),
            factor_sems,
        ],
        compiler_params=params,
        cost_estimate=pl.CostEstimate(
            flops=2 * solve_flops, bytes_accessed=16 * order * order * 2, transcendentals=0
        ),
    )(info, *factors, weights, *pieces)

    up = [(2 * x, 2 * x + 1) for x in range(groups)]
    incoming = lax.ppermute(w_high, "sec", up)
    solved, sent = pl.pallas_call(
        last_kernel,
        out_shape=[jax.ShapeDtypeStruct((2, 2, order, order), bf16), full_shape],
        in_specs=[in_smem] + [anywhere] * 14,
        out_specs=[anywhere, in_vmem],
        scratch_shapes=[
            factor_scratch,
            weight_scratch,
            field_scratch,
            arrived_scratch,
            field_scratch,
            beside_scratch,
            below_scratch,
            pltpu.SemaphoreType.DMA((7,)),
            factor_sems,
            pltpu.SemaphoreType.DMA((2,)),
        ],
        compiler_params=params,
        cost_estimate=pl.CostEstimate(
            flops=3 * solve_flops, bytes_accessed=16 * order * order * 2, transcendentals=0
        ),
    )(info, *factors, weights, *pieces, incoming)

    down = [(target, source) for source, target in up]
    incoming = lax.ppermute(sent, "sec", down)
    results = pl.pallas_call(
        back_kernel,
        out_shape=[piece_shape] * len(rounds),
        in_specs=[in_smem] + [anywhere] * 13,
        out_specs=[anywhere] * len(rounds),
        scratch_shapes=[
            factor_scratch,
            weight_scratch,
            field_scratch,
            arrived_scratch,
            beside_scratch,
            below_scratch,
            pltpu.SemaphoreType.DMA((6,)),
            factor_sems,
            pltpu.SemaphoreType.DMA((len(rounds),)),
        ],
        compiler_params=params,
        cost_estimate=pl.CostEstimate(
            flops=2 * solve_flops, bytes_accessed=16 * order * order * 2, transcendentals=0
        ),
    )(info, *factors, weights, w_low, w_high, incoming, solved)
    results = [
        lax.ppermute(piece, ("sec", "px"), back_pairs(a, b)) for piece, (a, b) in zip(results, rounds)
    ]
    output = pl.pallas_call(
        unpack_kernel,
        out_shape=jax.ShapeDtypeStruct(field.shape, bf16),
        in_specs=[in_smem] + [anywhere] * len(rounds),
        out_specs=in_vmem,
        scratch_shapes=[pltpu.SemaphoreType.DMA((len(rounds),))],
        compiler_params=params,
    )(sends_to, *results)
    return output[:, None]


def chip_plan_fits(mesh):
    return mesh.shape["sec"] == 4 and mesh.shape["px"] == 2 and mesh.shape["py"] == 4


def solution(mesh):
    placed = (
        P(None, "sec", "px", "py"),
        P(),
        P("sec", "px", None),
        P("sec", None, ("px", "py"), None),
        P("sec", None, ("px", "py"), None),
    )
    return jax.shard_map(
        on_device if chip_plan_fits(mesh) else on_device_by_layer,
        mesh=mesh,
        in_specs=placed,
        out_specs=P(None, "sec", "px", "py"),
        check_vma=False,
    )
```

```python
import functools

import jax
import jax.numpy as jnp
from jax import lax
from jax.experimental import pallas as pl
from jax.experimental.pallas import tpu as pltpu
from jax.sharding import PartitionSpec as P

source_amplitude = 8.0
vmem_bytes = 32 * 1024 * 1024
bf16 = jnp.bfloat16
f32 = jnp.float32
anywhere = pl.BlockSpec(memory_space=pl.ANY)
in_smem = pl.BlockSpec(memory_space=pltpu.SMEM)
in_vmem = pl.BlockSpec(memory_space=pltpu.VMEM)

info_member, info_piece, info_slot, info_half, info_block = 3, 4, 12, 14, 16


def shifted(x, axis, by):
    peers = lax.axis_size(axis)
    pairs = [(i, i + by) for i in range(peers) if 0 <= i + by < peers]
    return lax.ppermute(x, axis, pairs)


def complex_block(factor):
    upper = jnp.concatenate([factor[0], -factor[1]], axis=1)
    lower = jnp.concatenate([factor[1], factor[0]], axis=1)
    return jnp.concatenate([upper, lower], axis=0)


def y_transform(real_turned, imag_turned, field_in):
    real_part = jnp.dot(field_in[0], real_turned, preferred_element_type=jnp.float32) - jnp.dot(
        field_in[1], imag_turned, preferred_element_type=jnp.float32
    )
    imag_part = jnp.dot(field_in[0], imag_turned, preferred_element_type=jnp.float32) + jnp.dot(
        field_in[1], real_turned, preferred_element_type=jnp.float32
    )
    return jnp.stack([real_part, imag_part]).astype(jnp.bfloat16)


def x_transform(x_block, field_in):
    planes, rows_all, width = field_in.shape
    output = jnp.dot(
        x_block, field_in.reshape(planes * rows_all, width), preferred_element_type=jnp.float32
    )
    return output.astype(jnp.bfloat16).reshape(planes, rows_all, width)


def scale_rows(field_in, weights, width):
    planes, rows_here, merged = field_in.shape
    spread = field_in.astype(jnp.float32).reshape(planes, rows_here, merged // width, width)
    return (spread * weights.astype(jnp.float32)[None, :, None, :]).reshape(
        planes, rows_here, merged
    )


def pick_batch(field, batch_count, batch_index):
    planes, rows_here, merged = field.shape
    split_field = field.reshape(planes, rows_here, batch_count, merged // batch_count)
    return lax.dynamic_index_in_dim(split_field, batch_index, 2, keepdims=False)


def place_batch(field, piece, batch_count, batch_index):
    planes, rows_here, merged = field.shape
    split_field = field.reshape(planes, rows_here, batch_count, merged // batch_count)
    shaped = piece.reshape(planes, rows_here, 1, merged // batch_count)
    updated = lax.dynamic_update_slice_in_dim(split_field, shaped, batch_index, 2)
    return updated.reshape(planes, rows_here, merged)


def on_device_by_layer(background, src_pos, coupling, x_factor, y_factor):
    source_count = src_pos.shape[0]
    sec_count = lax.axis_size("sec")
    sec_index = lax.axis_index("sec")
    grid_y = lax.axis_size("py")
    own_x = lax.axis_index("px")
    own_y = lax.axis_index("py")
    local_sources = source_count // grid_y
    x_pieces, y_pieces = (
        lax.all_gather(x_factor[0], ("px", "py"), axis=1, tiled=True),
        lax.all_gather(y_factor[0], ("px", "py"), axis=1, tiled=True),
    )
    x_block = complex_block(x_pieces)
    real_turned = y_pieces[0].T
    imag_turned = y_pieces[1].T
    local_field = background[:, 0]
    local_weights = coupling[0]
    rows_here = local_field.shape[1]
    full_cols = y_factor.shape[3]
    plane_cells = x_factor.shape[3] * full_cols
    own_sources = lax.dynamic_slice_in_dim(src_pos, own_y * local_sources, local_sources)
    layer_of = own_sources // plane_cells
    remainder = own_sources % plane_cells
    row_of = remainder // full_cols
    column_of = remainder % full_cols
    row_start = own_x * rows_here
    row_hit = row_of[None, :] == row_start + jnp.arange(rows_here, dtype=jnp.int32)[:, None]
    col_hit = column_of[:, None] == jnp.arange(full_cols, dtype=jnp.int32)[None, :]
    layer_hit = layer_of == sec_index
    delta = (row_hit[:, :, None] & col_hit[None, :, :] & layer_hit[None, :, None]).astype(
        jnp.float32
    )
    delta = (delta * source_amplitude).reshape(rows_here, local_sources * full_cols)
    real_rhs = local_field[0].astype(jnp.float32) + delta
    rhs_field = jnp.stack([real_rhs, local_field[1].astype(jnp.float32)])

    def apply_front(field_in):
        turned = y_transform(real_turned, imag_turned, field_in)
        line_field = lax.all_to_all(turned, "px", split_axis=2, concat_axis=1, tiled=True)
        finished = x_transform(x_block, line_field)
        return lax.all_to_all(finished, "px", split_axis=1, concat_axis=2, tiled=True)

    forward_field = jnp.zeros(local_field.shape, jnp.bfloat16)
    outgoing = pick_batch(forward_field, sec_count, 0)
    for step in range(2 * sec_count - 1):
        incoming = shifted(outgoing, "sec", 1)
        batch_index = step - sec_index
        active = (batch_index >= 0) & (batch_index < sec_count)
        clamped = jnp.clip(batch_index, 0, sec_count - 1)
        rhs_batch = pick_batch(rhs_field, sec_count, clamped)
        reduced = (rhs_batch - scale_rows(incoming, local_weights, full_cols)).astype(jnp.bfloat16)
        candidate = apply_front(reduced)
        previous = pick_batch(forward_field, sec_count, clamped)
        kept = jnp.where(active, candidate, previous)
        forward_field = place_batch(forward_field, kept, sec_count, clamped)
        outgoing = candidate
    sweep_field = forward_field
    for step in range(2 * sec_count - 2):
        send_index = jnp.clip(step - (sec_count - 1 - sec_index), 0, sec_count - 1)
        own_batch = pick_batch(sweep_field, sec_count, send_index)
        sent_field = scale_rows(own_batch, local_weights, full_cols).astype(jnp.bfloat16)
        incoming = shifted(sent_field, "sec", -1)
        batch_index = step - (sec_count - 2 - sec_index)
        active = (batch_index >= 0) & (batch_index < sec_count) & (sec_index <= sec_count - 2)
        clamped = jnp.clip(batch_index, 0, sec_count - 1)
        solved = apply_front(incoming)
        forward_batch = pick_batch(forward_field, sec_count, clamped)
        candidate = (forward_batch.astype(jnp.float32) - solved.astype(jnp.float32)).astype(
            jnp.bfloat16
        )
        previous = pick_batch(sweep_field, sec_count, clamped)
        kept = jnp.where(active, candidate, previous)
        sweep_field = place_batch(sweep_field, kept, sec_count, clamped)
    return sweep_field[:, None]


def start_all(copies):
    for copy in copies:
        copy.start()


def wait_all(copies):
    for copy in copies:
        copy.wait()


def row_chunks(order, step):
    step = min(step, order)
    return [slice(first, first + step) for first in range(0, order, step)]


def pack_kernel(place, field, coupling, *rest):
    pieces, own_rows, sems = rest[:-2], rest[-2], rest[-1]
    copies = []
    for index, piece in enumerate(pieces):
        width = piece.shape[2]
        offset = pl.multiple_of(place[index] * width, width)
        copies.append(
            pltpu.make_async_copy(field.at[:, :, pl.ds(offset, width)], piece, sems.at[index])
        )
    height = own_rows.shape[0]
    rows = pl.ds(pl.multiple_of(place[len(pieces)] * height, height), height)
    copies.append(pltpu.make_async_copy(coupling.at[rows], own_rows, sems.at[len(pieces)]))
    start_all(copies)
    wait_all(copies)


def unpack_kernel(place, *rest):
    pieces, field, sems = rest[:-2], rest[-2], rest[-1]
    copies = []
    for index, piece in enumerate(pieces):
        width = piece.shape[2]
        offset = pl.multiple_of(place[index] * width, width)
        copies.append(
            pltpu.make_async_copy(piece, field.at[:, :, pl.ds(offset, width)], sems.at[index])
        )
    start_all(copies)
    wait_all(copies)


def stack_kernel(info, own, first, second, third, c0, c1, c2, c3, x_column, y_column, rows_held,
                 sems, csems):
    height = own.shape[1]
    copies = []
    for turn, block in enumerate((own, first, second, third)):
        rows = pl.ds(pl.multiple_of(info[info_block + turn] * height, height), height)
        for which, column in enumerate((x_column, y_column)):
            copies.append(
                pltpu.make_async_copy(
                    block.at[pl.ds(2 * which, 2)], column.at[:, rows, :], sems.at[turn, which]
                )
            )
    for index, rows_of in enumerate((c0, c1, c2, c3)):
        copies.append(pltpu.make_async_copy(rows_of, rows_held.at[index], csems.at[index]))
    start_all(copies)
    wait_all(copies)


def weight_kernel(info, own, first, second, third, weights, sems):
    height = own.shape[1]
    half_height = weights.shape[1] // 2
    copies = []
    for turn, block in enumerate((own, first, second, third)):
        for index in range(block.shape[0]):
            slot, half = info[info_piece + 2 * index], info[info_piece + 2 * index + 1]
            start = half * half_height + info[info_block + turn] * height
            rows = pl.ds(pl.multiple_of(start, height), height)
            copies.append(
                pltpu.make_async_copy(
                    block.at[index], weights.at[slot, rows, :], sems.at[turn, index]
                )
            )
    start_all(copies)
    wait_all(copies)


def halves(*pairs):
    return [pair.at[half] for pair in pairs for half in range(2)]


class Factors:
    def __init__(self, info, columns, held, sems):
        self.order, self.held, self.sems, self.columns = held.shape[2], held, sems, columns
        height = columns[0][0].shape[1]
        for which in (1, 0):
            for index, column in enumerate(columns[which]):
                slot, half = info[info_slot + index // 2], info[info_half + index % 2]
                rows = pl.ds(pl.multiple_of(half * height, height), height)
                for plane in range(2):
                    self.copy(column, plane, slot, which, rows, index % 2).start()

    def copy(self, column, plane, slot, which, rows, half):
        target = self.held.at[slot, which, rows, pl.ds(plane * self.order, self.order)]
        return pltpu.make_async_copy(
            column.at[plane], target, self.sems.at[slot, which, half, plane]
        )

    def ready(self, slot, which):
        column = self.columns[which][0]
        height = column.shape[1]
        for half in range(2):
            for plane in range(2):
                rows = pl.ds(half * height, height)
                self.copy(column, plane, slot, which, rows, half).wait()

    def apply(self, slot, beside, below, store, fresh):
        order = self.order
        turned = (((1,), (1,)), ((), ()))
        if fresh:
            self.ready(slot, 1)
        for columns in row_chunks(order, 512):
            part = lax.dot_general(
                beside[...], self.held[slot, 1, columns], turned, preferred_element_type=f32
            ).astype(bf16)
            real, imag = part[:order], part[order:]
            further = slice(columns.start + order, columns.stop + order)
            below[:order, columns] = real
            below[:order, further] = imag
            below[order:, columns] = -imag
            below[order:, further] = real
        if fresh:
            self.ready(slot, 0)
        for plane in range(2):
            for columns in row_chunks(order, 512):
                along = slice(columns.start + plane * order, columns.stop + plane * order)
                store(
                    plane,
                    columns,
                    jnp.dot(self.held[slot, 0], below[:, along], preferred_element_type=f32),
                )


def put_beside(beside, plane, rows, values):
    order = beside.shape[0] // 2
    left, right = slice(0, order), slice(order, 2 * order)
    lower = slice(rows.start + order, rows.stop + order)
    values = values.astype(bf16)
    if plane == 0:
        beside[rows, left] = values
        beside[lower, right] = values
    else:
        beside[rows, right] = -values
        beside[lower, left] = values


def reduce_into(beside, rhs, info, slot, weights, incoming):
    order = beside.shape[0] // 2
    for plane in range(2):
        for rows in row_chunks(order, 128):
            values = rhs[slot, plane, rows].astype(f32)
            scaled = weights[slot, rows].astype(f32) * incoming(plane, rows, slice(None))
            put_beside(beside, plane, rows, values - scaled)

    @pl.when(info[0] == slot)
    def _():
        tall, wide = 16, 128
        top = pl.multiple_of(info[1] // tall * tall, tall)
        left = pl.multiple_of(info[2] // wide * wide, wide)
        rows, columns = pl.ds(top, tall), pl.ds(left, wide)
        values = rhs[slot, 0, rows, columns].astype(f32)
        row = lax.broadcasted_iota(jnp.int32, values.shape, 0) + top
        column = lax.broadcasted_iota(jnp.int32, values.shape, 1) + left
        hit = (row == info[1]) & (column == info[2])
        values = values + jnp.where(hit, f32(source_amplitude), f32(0.0))
        scaled = weights[slot, rows, columns].astype(f32) * incoming(0, rows, columns)
        values = (values - scaled).astype(bf16)
        beside[rows, columns] = values
        lower = pl.ds(pl.multiple_of(order + top, tall), tall)
        further = pl.ds(pl.multiple_of(order + left, wide), wide)
        beside[lower, further] = values


def sent_into(beside, weights, slot, field):
    order = beside.shape[0] // 2
    for plane in range(2):
        for rows in row_chunks(order, 128):
            scaled = weights[slot, rows].astype(f32) * field(plane, rows)
            put_beside(beside, plane, rows, scaled)


def subtract_into(target, forward):
    def store(plane, columns, values):
        solved = values.astype(bf16).astype(f32)
        target[plane, :, columns] = (forward(plane, columns).astype(f32) - solved).astype(bf16)

    return store


def round_into(target):
    def store(plane, columns, values):
        target[plane, :, columns] = values.astype(bf16)

    return store


def rhs_copies(info, pieces, rhs, sems):
    copies = []
    for index, piece in enumerate(pieces):
        height = piece.shape[1]
        slot, half = info[info_piece + 2 * index], info[info_piece + 2 * index + 1]
        rows = pl.ds(pl.multiple_of(half * height, height), height)
        copies.append(pltpu.make_async_copy(piece, rhs.at[slot, :, rows, :], sems.at[index]))
    return copies


def first_kernel(info, x0, x1, y0, y1, y2, y3, coupling, p0, p1, p2, p3, w_low, w_high,
                 held, weights, rhs, beside, below, sems, fsems):
    @pl.when(info[info_member] == 0)
    def _():
        early = rhs_copies(info, (p0, p1, p2, p3), rhs, sems)
        early.append(pltpu.make_async_copy(coupling, weights, sems.at[4]))
        start_all(early)
        factors = Factors(info, (halves(x0, x1), (y0, y1, y2, y3)), held, fsems)
        wait_all(early)
        reduce_into(beside, rhs, info, 0, weights, lambda *where: f32(0.0))
        factors.apply(0, beside, below, round_into(w_low), True)
        reduce_into(
            beside, rhs, info, 1, weights, lambda *where: w_low[where].astype(f32)
        )
        factors.apply(1, beside, below, round_into(w_high), True)


def last_kernel(info, x0, x1, y0, y1, y2, y3, coupling, p0, p1, p2, p3, incoming, field,
                sent, held, weights, rhs, arrived, kept, beside, below, sems, fsems, osems):
    @pl.when(info[info_member] == 1)
    def _():
        early = rhs_copies(info, (p0, p1, p2, p3), rhs, sems)
        early.append(pltpu.make_async_copy(coupling, weights, sems.at[4]))
        early.append(pltpu.make_async_copy(incoming, arrived, sems.at[5]))
        start_all(early)
        factors = Factors(info, (halves(x0, x1), (y0, y1, y2, y3)), held, fsems)
        wait_all(early)
        order = beside.shape[0] // 2
        reduce_into(
            beside, rhs, info, 0, weights, lambda *where: arrived[where].astype(f32)
        )
        w_low, w_high = kept.at[0], kept.at[1]
        factors.apply(0, beside, below, round_into(w_low), True)
        reduce_into(
            beside, rhs, info, 1, weights, lambda *where: w_low[where].astype(f32)
        )
        factors.apply(1, beside, below, round_into(w_high), True)
        out_high = pltpu.make_async_copy(w_high, field.at[1], osems.at[1])
        out_high.start()
        sent_into(beside, weights, 1, lambda plane, rows: w_high[plane, rows].astype(f32))
        factors.apply(
            0,
            beside,
            below,
            subtract_into(w_low, lambda plane, columns: w_low[plane, :, columns]),
            False,
        )
        out_low = pltpu.make_async_copy(w_low, field.at[0], osems.at[0])
        out_low.start()
        sent_into(beside, weights, 0, lambda plane, rows: w_low[plane, rows].astype(f32))
        for plane in range(2):
            sent[plane] = beside[plane * order : (plane + 1) * order, :order]
        out_high.wait()
        out_low.wait()


def back_kernel(info, x0, x1, y0, y1, y2, y3, coupling, w_low, w_high, incoming, field,
                p0, p1, p2, p3, held, weights, kept, arrived, beside, below, sems, fsems, osems):
    @pl.when(info[info_member] == 0)
    def _():
        early = [pltpu.make_async_copy(incoming, arrived, sems.at[0])]
        start_all(early)
        factors = Factors(info, (halves(x0, x1), (y0, y1, y2, y3)), held, fsems)
        early += [
            pltpu.make_async_copy(coupling, weights, sems.at[1]),
            pltpu.make_async_copy(w_low, kept.at[0], sems.at[2]),
            pltpu.make_async_copy(w_high, kept.at[1], sems.at[3]),
        ]
        start_all(early[1:])
        wait_all(early)
        order = beside.shape[0] // 2
        for plane in range(2):
            for rows in row_chunks(order, 128):
                put_beside(beside, plane, rows, arrived[plane, rows])
        u_low, u_high = kept.at[0], kept.at[1]
        factors.apply(
            1,
            beside,
            below,
            subtract_into(u_high, lambda plane, columns: u_high[plane, :, columns]),
            True,
        )
        sent_into(beside, weights, 1, lambda plane, rows: u_high[plane, rows].astype(f32))
        factors.apply(
            0,
            beside,
            below,
            subtract_into(u_low, lambda plane, columns: u_low[plane, :, columns]),
            True,
        )

    @pl.when(info[info_member] != 0)
    def _():
        finished = pltpu.make_async_copy(field, kept, sems.at[0])
        finished.start()
        finished.wait()

    copies = []
    for index, piece in enumerate((p0, p1, p2, p3)):
        height = piece.shape[1]
        slot, half = info[info_piece + 2 * index], info[info_piece + 2 * index + 1]
        rows = pl.ds(pl.multiple_of(half * height, height), height)
        copies.append(pltpu.make_async_copy(kept.at[slot, :, rows, :], piece, osems.at[index]))
    start_all(copies)
    wait_all(copies)


def on_device(background, src_pos, coupling, x_factor, y_factor):
    px_count = lax.axis_size("px")
    sec_index, own_x, own_y = (lax.axis_index(axis) for axis in ("sec", "px", "py"))
    group, member = sec_index // 2, sec_index % 2
    groups = lax.axis_size("sec") // 2
    order = y_factor.shape[3]
    field = background[:, 0]
    rows_here = field.shape[1]
    height = x_factor.shape[2]
    params = pltpu.CompilerParams(vmem_limit_bytes=vmem_bytes)
    rounds = [(a, b) for a in range(groups) for b in range(px_count)]

    def pairs(a, b):
        return [
            ((2 * x + c) * px_count + y, (2 * ((c + a) % 2) + x) * px_count + (y + b) % px_count)
            for x in range(groups)
            for c in range(2)
            for y in range(px_count)
        ]

    def back_pairs(a, b):
        return [(target, source) for source, target in pairs(a, b)]

    own_source = src_pos[own_y * groups * px_count + group * px_count + own_x]
    plane_cells = x_factor.shape[3] * order
    layer = own_source // plane_cells
    remainder = own_source % plane_cells
    py_count = lax.axis_size("py")
    entries = [
        jnp.where(layer // 2 == member, layer % 2, -1),
        remainder // order,
        remainder % order,
        member,
    ]
    for a, b in rounds:
        entries += [(group + a) % 2, (own_x - b) % px_count]
    entries += [group, (group + 1) % 2, own_x, (own_x + 1) % 2]
    entries += [(own_y - turn) % py_count for turn in range(py_count)]
    info = jnp.stack([jnp.asarray(entry, jnp.int32) for entry in entries])

    def rotated(block):
        return [block] + [
            lax.ppermute(block, "py", [(z, (z + turn) % py_count) for z in range(py_count)])
            for turn in range(1, py_count)
        ]

    shard = jnp.concatenate([x_factor[0], y_factor[0]], axis=0)
    shards = rotated(shard)
    sends_to = jnp.stack(
        [((member + a) % 2) * px_count + (own_x + b) % px_count for a, b in rounds] + [own_y]
    ).astype(jnp.int32)
    piece_shape = jax.ShapeDtypeStruct((2, rows_here, order), bf16)
    *pieces, own_rows = pl.pallas_call(
        pack_kernel,
        out_shape=[piece_shape] * len(rounds) + [jax.ShapeDtypeStruct((height, order), bf16)],
        in_specs=[in_smem, anywhere, anywhere],
        out_specs=[in_vmem] * (len(rounds) + 1),
        scratch_shapes=[pltpu.SemaphoreType.DMA((len(rounds) + 1,))],
        compiler_params=params,
    )(sends_to, field, coupling[0])
    pieces = [
        lax.ppermute(piece, ("sec", "px"), pairs(a, b)) for piece, (a, b) in zip(pieces, rounds)
    ]
    layer_rows = [lax.ppermute(own_rows, ("sec", "px"), pairs(a, b)) for a, b in rounds]

    column_shape = jax.ShapeDtypeStruct((2, rows_here, order), bf16)
    x_column, y_column, rows_held = pl.pallas_call(
        stack_kernel,
        out_shape=[column_shape] * 2 + [jax.ShapeDtypeStruct((4, height, order), bf16)],
        in_specs=[in_smem] + [anywhere] * 8,
        out_specs=[in_vmem] * 3,
        scratch_shapes=[pltpu.SemaphoreType.DMA((4, 2)), pltpu.SemaphoreType.DMA((4,))],
        compiler_params=params,
    )(info, *shards, *layer_rows)

    def across(block, a):
        return lax.ppermute(block, ("sec", "px"), pairs(a, 0))

    def aside(block):
        return lax.ppermute(block, "px", [(y, (y + 1) % 2) for y in range(2)])

    x_aside = aside(x_column)
    y_near = [across(y_column, a) for a in range(2)]
    y_far = [aside(block) for block in y_near]
    x_both = jnp.stack([x_column, x_aside])
    x_across = [across(x_both, a) for a in range(2)]
    factors = x_across + [y_near[0], y_far[0], y_near[1], y_far[1]]
    weights = pl.pallas_call(
        weight_kernel,
        out_shape=jax.ShapeDtypeStruct((2, order, order), bf16),
        in_specs=[in_smem] + [anywhere] * 4,
        out_specs=in_vmem,
        scratch_shapes=[pltpu.SemaphoreType.DMA((4, 4))],
        compiler_params=params,
    )(info, *rotated(rows_held))

    full_shape = jax.ShapeDtypeStruct((2, order, order), bf16)
    factor_scratch = pltpu.VMEM((2, 2, order, 2 * order), bf16)
    arrived_scratch = pltpu.VMEM((2, order, order), bf16)
    weight_scratch = pltpu.VMEM((2, order, order), bf16)
    field_scratch = pltpu.VMEM((2, 2, order, order), bf16)
    beside_scratch = pltpu.VMEM((2 * order, 2 * order), bf16)
    below_scratch = beside_scratch
    factor_sems = pltpu.SemaphoreType.DMA((2, 2, 2, 2))
    solve_flops = 16 * order**3
    w_low, w_high = pl.pallas_call(
        first_kernel,
        out_shape=[full_shape] * 2,
        in_specs=[in_smem] + [anywhere] * 11,
        out_specs=[in_vmem] * 2,
        scratch_shapes=[
            factor_scratch,
            weight_scratch,
            field_scratch,
            beside_scratch,
            below_scratch,
            pltpu.SemaphoreType.DMA((6,)),
            factor_sems,
        ],
        compiler_params=params,
        cost_estimate=pl.CostEstimate(
            flops=2 * solve_flops, bytes_accessed=16 * order * order * 2, transcendentals=0
        ),
    )(info, *factors, weights, *pieces)

    up = [(2 * x, 2 * x + 1) for x in range(groups)]
    incoming = lax.ppermute(w_high, "sec", up)
    solved, sent = pl.pallas_call(
        last_kernel,
        out_shape=[jax.ShapeDtypeStruct((2, 2, order, order), bf16), full_shape],
        in_specs=[in_smem] + [anywhere] * 12,
        out_specs=[anywhere, in_vmem],
        scratch_shapes=[
            factor_scratch,
            weight_scratch,
            field_scratch,
            arrived_scratch,
            field_scratch,
            beside_scratch,
            below_scratch,
            pltpu.SemaphoreType.DMA((7,)),
            factor_sems,
            pltpu.SemaphoreType.DMA((2,)),
        ],
        compiler_params=params,
        cost_estimate=pl.CostEstimate(
            flops=3 * solve_flops, bytes_accessed=16 * order * order * 2, transcendentals=0
        ),
    )(info, *factors, weights, *pieces, incoming)

    down = [(target, source) for source, target in up]
    incoming = lax.ppermute(sent, "sec", down)
    results = pl.pallas_call(
        back_kernel,
        out_shape=[piece_shape] * len(rounds),
        in_specs=[in_smem] + [anywhere] * 11,
        out_specs=[anywhere] * len(rounds),
        scratch_shapes=[
            factor_scratch,
            weight_scratch,
            field_scratch,
            arrived_scratch,
            beside_scratch,
            below_scratch,
            pltpu.SemaphoreType.DMA((6,)),
            factor_sems,
            pltpu.SemaphoreType.DMA((len(rounds),)),
        ],
        compiler_params=params,
        cost_estimate=pl.CostEstimate(
            flops=2 * solve_flops, bytes_accessed=16 * order * order * 2, transcendentals=0
        ),
    )(info, *factors, weights, w_low, w_high, incoming, solved)
    results = [
        lax.ppermute(piece, ("sec", "px"), back_pairs(a, b)) for piece, (a, b) in zip(results, rounds)
    ]
    output = pl.pallas_call(
        unpack_kernel,
        out_shape=jax.ShapeDtypeStruct(field.shape, bf16),
        in_specs=[in_smem] + [anywhere] * len(rounds),
        out_specs=in_vmem,
        scratch_shapes=[pltpu.SemaphoreType.DMA((len(rounds),))],
        compiler_params=params,
    )(sends_to, *results)
    return output[:, None]


def chip_plan_fits(mesh):
    return mesh.shape["sec"] == 4 and mesh.shape["px"] == 2 and mesh.shape["py"] == 4


def solution(mesh):
    placed = (
        P(None, "sec", "px", "py"),
        P(),
        P("sec", "px", None),
        P("sec", None, ("px", "py"), None),
        P("sec", None, ("px", "py"), None),
    )
    return jax.shard_map(
        on_device if chip_plan_fits(mesh) else on_device_by_layer,
        mesh=mesh,
        in_specs=placed,
        out_specs=P(None, "sec", "px", "py"),
        check_vma=False,
    )
```

```python
import functools

import jax
import jax.numpy as jnp
from jax import lax
from jax.experimental import pallas as pl
from jax.experimental.pallas import tpu as pltpu
from jax.sharding import PartitionSpec as P

source_amplitude = 8.0
vmem_bytes = 32 * 1024 * 1024
bf16 = jnp.bfloat16
f32 = jnp.float32
anywhere = pl.BlockSpec(memory_space=pl.ANY)
in_smem = pl.BlockSpec(memory_space=pltpu.SMEM)
in_vmem = pl.BlockSpec(memory_space=pltpu.VMEM)

info_member, info_piece, info_slot, info_half = 3, 4, 12, 14


def shifted(x, axis, by):
    peers = lax.axis_size(axis)
    pairs = [(i, i + by) for i in range(peers) if 0 <= i + by < peers]
    return lax.ppermute(x, axis, pairs)


def complex_block(factor):
    upper = jnp.concatenate([factor[0], -factor[1]], axis=1)
    lower = jnp.concatenate([factor[1], factor[0]], axis=1)
    return jnp.concatenate([upper, lower], axis=0)


def y_transform(real_turned, imag_turned, field_in):
    real_part = jnp.dot(field_in[0], real_turned, preferred_element_type=jnp.float32) - jnp.dot(
        field_in[1], imag_turned, preferred_element_type=jnp.float32
    )
    imag_part = jnp.dot(field_in[0], imag_turned, preferred_element_type=jnp.float32) + jnp.dot(
        field_in[1], real_turned, preferred_element_type=jnp.float32
    )
    return jnp.stack([real_part, imag_part]).astype(jnp.bfloat16)


def x_transform(x_block, field_in):
    planes, rows_all, width = field_in.shape
    output = jnp.dot(
        x_block, field_in.reshape(planes * rows_all, width), preferred_element_type=jnp.float32
    )
    return output.astype(jnp.bfloat16).reshape(planes, rows_all, width)


def scale_rows(field_in, weights, width):
    planes, rows_here, merged = field_in.shape
    spread = field_in.astype(jnp.float32).reshape(planes, rows_here, merged // width, width)
    return (spread * weights.astype(jnp.float32)[None, :, None, :]).reshape(
        planes, rows_here, merged
    )


def pick_batch(field, batch_count, batch_index):
    planes, rows_here, merged = field.shape
    split_field = field.reshape(planes, rows_here, batch_count, merged // batch_count)
    return lax.dynamic_index_in_dim(split_field, batch_index, 2, keepdims=False)


def place_batch(field, piece, batch_count, batch_index):
    planes, rows_here, merged = field.shape
    split_field = field.reshape(planes, rows_here, batch_count, merged // batch_count)
    shaped = piece.reshape(planes, rows_here, 1, merged // batch_count)
    updated = lax.dynamic_update_slice_in_dim(split_field, shaped, batch_index, 2)
    return updated.reshape(planes, rows_here, merged)


def on_device_by_layer(background, src_pos, coupling, x_factor, y_factor):
    source_count = src_pos.shape[0]
    sec_count = lax.axis_size("sec")
    sec_index = lax.axis_index("sec")
    grid_y = lax.axis_size("py")
    own_x = lax.axis_index("px")
    own_y = lax.axis_index("py")
    local_sources = source_count // grid_y
    x_pieces, y_pieces = (
        lax.all_gather(x_factor[0], ("px", "py"), axis=1, tiled=True),
        lax.all_gather(y_factor[0], ("px", "py"), axis=1, tiled=True),
    )
    x_block = complex_block(x_pieces)
    real_turned = y_pieces[0].T
    imag_turned = y_pieces[1].T
    local_field = background[:, 0]
    local_weights = coupling[0]
    rows_here = local_field.shape[1]
    full_cols = y_factor.shape[3]
    plane_cells = x_factor.shape[3] * full_cols
    own_sources = lax.dynamic_slice_in_dim(src_pos, own_y * local_sources, local_sources)
    layer_of = own_sources // plane_cells
    remainder = own_sources % plane_cells
    row_of = remainder // full_cols
    column_of = remainder % full_cols
    row_start = own_x * rows_here
    row_hit = row_of[None, :] == row_start + jnp.arange(rows_here, dtype=jnp.int32)[:, None]
    col_hit = column_of[:, None] == jnp.arange(full_cols, dtype=jnp.int32)[None, :]
    layer_hit = layer_of == sec_index
    delta = (row_hit[:, :, None] & col_hit[None, :, :] & layer_hit[None, :, None]).astype(
        jnp.float32
    )
    delta = (delta * source_amplitude).reshape(rows_here, local_sources * full_cols)
    real_rhs = local_field[0].astype(jnp.float32) + delta
    rhs_field = jnp.stack([real_rhs, local_field[1].astype(jnp.float32)])

    def apply_front(field_in):
        turned = y_transform(real_turned, imag_turned, field_in)
        line_field = lax.all_to_all(turned, "px", split_axis=2, concat_axis=1, tiled=True)
        finished = x_transform(x_block, line_field)
        return lax.all_to_all(finished, "px", split_axis=1, concat_axis=2, tiled=True)

    forward_field = jnp.zeros(local_field.shape, jnp.bfloat16)
    outgoing = pick_batch(forward_field, sec_count, 0)
    for step in range(2 * sec_count - 1):
        incoming = shifted(outgoing, "sec", 1)
        batch_index = step - sec_index
        active = (batch_index >= 0) & (batch_index < sec_count)
        clamped = jnp.clip(batch_index, 0, sec_count - 1)
        rhs_batch = pick_batch(rhs_field, sec_count, clamped)
        reduced = (rhs_batch - scale_rows(incoming, local_weights, full_cols)).astype(jnp.bfloat16)
        candidate = apply_front(reduced)
        previous = pick_batch(forward_field, sec_count, clamped)
        kept = jnp.where(active, candidate, previous)
        forward_field = place_batch(forward_field, kept, sec_count, clamped)
        outgoing = candidate
    sweep_field = forward_field
    for step in range(2 * sec_count - 2):
        send_index = jnp.clip(step - (sec_count - 1 - sec_index), 0, sec_count - 1)
        own_batch = pick_batch(sweep_field, sec_count, send_index)
        sent_field = scale_rows(own_batch, local_weights, full_cols).astype(jnp.bfloat16)
        incoming = shifted(sent_field, "sec", -1)
        batch_index = step - (sec_count - 2 - sec_index)
        active = (batch_index >= 0) & (batch_index < sec_count) & (sec_index <= sec_count - 2)
        clamped = jnp.clip(batch_index, 0, sec_count - 1)
        solved = apply_front(incoming)
        forward_batch = pick_batch(forward_field, sec_count, clamped)
        candidate = (forward_batch.astype(jnp.float32) - solved.astype(jnp.float32)).astype(
            jnp.bfloat16
        )
        previous = pick_batch(sweep_field, sec_count, clamped)
        kept = jnp.where(active, candidate, previous)
        sweep_field = place_batch(sweep_field, kept, sec_count, clamped)
    return sweep_field[:, None]


def start_all(copies):
    for copy in copies:
        copy.start()


def wait_all(copies):
    for copy in copies:
        copy.wait()


def row_chunks(order, step):
    step = min(step, order)
    return [slice(first, first + step) for first in range(0, order, step)]


def pack_kernel(place, field, coupling, x_factor, y_factor, *rest):
    pieces, (blocks, sems, csems, fsems) = rest[:-4], rest[-4:]
    copies = []
    height = x_factor.shape[1]
    own = pl.ds(pl.multiple_of(place[len(pieces)] * height, height), height)
    for index, piece in enumerate(pieces):
        width = piece.shape[1]
        offset = pl.multiple_of(place[index] * width, width)
        rows_here = field.shape[1]
        for plane in range(2):
            copies.append(
                pltpu.make_async_copy(
                    field.at[plane, :, pl.ds(offset, width)],
                    piece.at[pl.ds(plane * rows_here, rows_here)],
                    sems.at[index, plane],
                )
            )
        copies.append(
            pltpu.make_async_copy(
                coupling.at[own], piece.at[pl.ds(2 * rows_here, height)], csems.at[index]
            )
        )
    for target in range(blocks.shape[0]):
        for which, factor in enumerate((x_factor, y_factor)):
            copies.append(
                pltpu.make_async_copy(
                    factor, blocks.at[target, pl.ds(2 * which, 2)], fsems.at[target, which]
                )
            )
    start_all(copies)
    wait_all(copies)


def unpack_kernel(place, *rest):
    pieces, field, sems = rest[:-2], rest[-2], rest[-1]
    copies = []
    for index, piece in enumerate(pieces):
        width = piece.shape[2]
        offset = pl.multiple_of(place[index] * width, width)
        copies.append(
            pltpu.make_async_copy(piece, field.at[:, :, pl.ds(offset, width)], sems.at[index])
        )
    start_all(copies)
    wait_all(copies)


def column_kernel(blocks, p0, p1, p2, p3, x_column, y_column, sems):
    height = blocks.shape[2]
    copies = []
    for index in range(blocks.shape[0]):
        rows = pl.ds(index * height, height)
        for which, column in enumerate((x_column, y_column)):
            copies.append(
                pltpu.make_async_copy(
                    blocks.at[index, pl.ds(2 * which, 2)],
                    column.at[:, rows, :],
                    sems.at[index, which],
                )
            )
    start_all(copies)
    wait_all(copies)


def both_kernel(x_column, x_aside, y0, y1, p0, p1, p2, p3, x_both, rows_held, sems, csems):
    copies = [
        pltpu.make_async_copy(x_column, x_both.at[0], sems.at[0]),
        pltpu.make_async_copy(x_aside, x_both.at[1], sems.at[1]),
    ]
    height = rows_held.shape[2]
    for target in range(rows_held.shape[0]):
        for index, piece in enumerate((p0, p1, p2, p3)):
            copies.append(
                pltpu.make_async_copy(
                    piece.at[pl.ds(piece.shape[0] - height, height)],
                    rows_held.at[target, index],
                    csems.at[target, index],
                )
            )
    start_all(copies)
    wait_all(copies)


def weight_copies(info, blocks, weights, sems):
    height = blocks.shape[2]
    half_height = weights.shape[1] // 2
    copies = []
    for index in range(blocks.shape[0]):
        for turn in range(blocks.shape[1]):
            slot, half = info[info_piece + 2 * turn], info[info_piece + 2 * turn + 1]
            rows = pl.ds(pl.multiple_of(half * half_height + index * height, height), height)
            copies.append(
                pltpu.make_async_copy(
                    blocks.at[index, turn], weights.at[slot, rows, :], sems.at[index, turn]
                )
            )
    return copies


def halves(*pairs):
    return [pair.at[half] for pair in pairs for half in range(2)]


class Factors:
    def __init__(self, info, columns, held, sems):
        self.order, self.held, self.sems, self.columns = held.shape[2], held, sems, columns
        height = columns[0][0].shape[1]
        for which in (1, 0):
            for index, column in enumerate(columns[which]):
                slot, half = info[info_slot + index // 2], info[info_half + index % 2]
                rows = pl.ds(pl.multiple_of(half * height, height), height)
                for plane in range(2):
                    self.copy(column, plane, slot, which, rows, index % 2).start()

    def copy(self, column, plane, slot, which, rows, half):
        target = self.held.at[slot, which, rows, pl.ds(plane * self.order, self.order)]
        return pltpu.make_async_copy(
            column.at[plane], target, self.sems.at[slot, which, half, plane]
        )

    def ready(self, slot, which):
        column = self.columns[which][0]
        height = column.shape[1]
        for half in range(2):
            for plane in range(2):
                rows = pl.ds(half * height, height)
                self.copy(column, plane, slot, which, rows, half).wait()

    def apply(self, slot, beside, below, store, fresh):
        order = self.order
        turned = (((1,), (1,)), ((), ()))
        if fresh:
            self.ready(slot, 1)
        for columns in row_chunks(order, 512):
            part = lax.dot_general(
                beside[...], self.held[slot, 1, columns], turned, preferred_element_type=f32
            ).astype(bf16)
            real, imag = part[:order], part[order:]
            further = slice(columns.start + order, columns.stop + order)
            below[:order, columns] = real
            below[:order, further] = imag
            below[order:, columns] = -imag
            below[order:, further] = real
        if fresh:
            self.ready(slot, 0)
        for plane in range(2):
            for columns in row_chunks(order, 512):
                along = slice(columns.start + plane * order, columns.stop + plane * order)
                store(
                    plane,
                    columns,
                    jnp.dot(self.held[slot, 0], below[:, along], preferred_element_type=f32),
                )


def put_beside(beside, plane, rows, values):
    order = beside.shape[0] // 2
    left, right = slice(0, order), slice(order, 2 * order)
    lower = slice(rows.start + order, rows.stop + order)
    values = values.astype(bf16)
    if plane == 0:
        beside[rows, left] = values
        beside[lower, right] = values
    else:
        beside[rows, right] = -values
        beside[lower, left] = values


def reduce_into(beside, rhs, info, slot, weights, incoming):
    order = beside.shape[0] // 2
    for plane in range(2):
        for rows in row_chunks(order, 128):
            values = rhs[slot, plane, rows].astype(f32)
            scaled = weights[slot, rows].astype(f32) * incoming(plane, rows, slice(None))
            put_beside(beside, plane, rows, values - scaled)

    @pl.when(info[0] == slot)
    def _():
        tall, wide = 16, 128
        top = pl.multiple_of(info[1] // tall * tall, tall)
        left = pl.multiple_of(info[2] // wide * wide, wide)
        rows, columns = pl.ds(top, tall), pl.ds(left, wide)
        values = rhs[slot, 0, rows, columns].astype(f32)
        row = lax.broadcasted_iota(jnp.int32, values.shape, 0) + top
        column = lax.broadcasted_iota(jnp.int32, values.shape, 1) + left
        hit = (row == info[1]) & (column == info[2])
        values = values + jnp.where(hit, f32(source_amplitude), f32(0.0))
        scaled = weights[slot, rows, columns].astype(f32) * incoming(0, rows, columns)
        values = (values - scaled).astype(bf16)
        beside[rows, columns] = values
        lower = pl.ds(pl.multiple_of(order + top, tall), tall)
        further = pl.ds(pl.multiple_of(order + left, wide), wide)
        beside[lower, further] = values


def sent_into(beside, weights, slot, field):
    order = beside.shape[0] // 2
    for plane in range(2):
        for rows in row_chunks(order, 128):
            scaled = weights[slot, rows].astype(f32) * field(plane, rows)
            put_beside(beside, plane, rows, scaled)


def subtract_into(target, forward):
    def store(plane, columns, values):
        solved = values.astype(bf16).astype(f32)
        target[plane, :, columns] = (forward(plane, columns).astype(f32) - solved).astype(bf16)

    return store


def round_into(target):
    def store(plane, columns, values):
        target[plane, :, columns] = values.astype(bf16)

    return store


def rhs_copies(info, pieces, rhs, sems):
    copies = []
    height = rhs.shape[2] // 2
    for index, piece in enumerate(pieces):
        slot, half = info[info_piece + 2 * index], info[info_piece + 2 * index + 1]
        rows = pl.ds(pl.multiple_of(half * height, height), height)
        for plane in range(2):
            copies.append(
                pltpu.make_async_copy(
                    piece.at[pl.ds(plane * height, height)],
                    rhs.at[slot, plane, rows, :],
                    sems.at[2 * index + plane],
                )
            )
    return copies


def first_kernel(info, x0, x1, y0, y1, y2, y3, coupling, p0, p1, p2, p3, w_low, w_high,
                 held, weights, rhs, beside, below, sems, csems, fsems):
    @pl.when(info[info_member] == 0)
    def _():
        early = rhs_copies(info, (p0, p1, p2, p3), rhs, sems)
        early += weight_copies(info, coupling, weights, csems)
        start_all(early)
        factors = Factors(info, (halves(x0, x1), (y0, y1, y2, y3)), held, fsems)
        wait_all(early)
        reduce_into(beside, rhs, info, 0, weights, lambda *where: f32(0.0))
        factors.apply(0, beside, below, round_into(w_low), True)
        reduce_into(
            beside, rhs, info, 1, weights, lambda *where: w_low[where].astype(f32)
        )
        factors.apply(1, beside, below, round_into(w_high), True)


def last_kernel(info, x0, x1, y0, y1, y2, y3, coupling, p0, p1, p2, p3, incoming, field,
                sent, held, weights, rhs, arrived, kept, beside, below, sems, csems, fsems,
                osems):
    @pl.when(info[info_member] == 1)
    def _():
        early = rhs_copies(info, (p0, p1, p2, p3), rhs, sems)
        early += weight_copies(info, coupling, weights, csems)
        early.append(pltpu.make_async_copy(incoming, arrived, sems.at[8]))
        start_all(early)
        factors = Factors(info, (halves(x0, x1), (y0, y1, y2, y3)), held, fsems)
        wait_all(early)
        order = beside.shape[0] // 2
        reduce_into(
            beside, rhs, info, 0, weights, lambda *where: arrived[where].astype(f32)
        )
        w_low, w_high = kept.at[0], kept.at[1]
        factors.apply(0, beside, below, round_into(w_low), True)
        reduce_into(
            beside, rhs, info, 1, weights, lambda *where: w_low[where].astype(f32)
        )
        factors.apply(1, beside, below, round_into(w_high), True)
        out_high = pltpu.make_async_copy(w_high, field.at[1], osems.at[1])
        out_high.start()
        sent_into(beside, weights, 1, lambda plane, rows: w_high[plane, rows].astype(f32))
        factors.apply(
            0,
            beside,
            below,
            subtract_into(w_low, lambda plane, columns: w_low[plane, :, columns]),
            False,
        )
        out_low = pltpu.make_async_copy(w_low, field.at[0], osems.at[0])
        out_low.start()
        sent_into(beside, weights, 0, lambda plane, rows: w_low[plane, rows].astype(f32))
        for plane in range(2):
            sent[plane] = beside[plane * order : (plane + 1) * order, :order]
        out_high.wait()
        out_low.wait()


def back_kernel(info, x0, x1, y0, y1, y2, y3, coupling, w_low, w_high, incoming, field,
                p0, p1, p2, p3, held, weights, kept, arrived, beside, below, sems, csems, fsems,
                osems):
    @pl.when(info[info_member] == 0)
    def _():
        early = [pltpu.make_async_copy(incoming, arrived, sems.at[0])]
        start_all(early)
        factors = Factors(info, (halves(x0, x1), (y0, y1, y2, y3)), held, fsems)
        early += weight_copies(info, coupling, weights, csems)
        early += [
            pltpu.make_async_copy(w_low, kept.at[0], sems.at[2]),
            pltpu.make_async_copy(w_high, kept.at[1], sems.at[3]),
        ]
        start_all(early[1:])
        wait_all(early)
        order = beside.shape[0] // 2
        for plane in range(2):
            for rows in row_chunks(order, 128):
                put_beside(beside, plane, rows, arrived[plane, rows])
        u_low, u_high = kept.at[0], kept.at[1]
        factors.apply(
            1,
            beside,
            below,
            subtract_into(u_high, lambda plane, columns: u_high[plane, :, columns]),
            True,
        )
        sent_into(beside, weights, 1, lambda plane, rows: u_high[plane, rows].astype(f32))
        factors.apply(
            0,
            beside,
            below,
            subtract_into(u_low, lambda plane, columns: u_low[plane, :, columns]),
            True,
        )

    @pl.when(info[info_member] != 0)
    def _():
        finished = pltpu.make_async_copy(field, kept, sems.at[0])
        finished.start()
        finished.wait()

    copies = []
    for index, piece in enumerate((p0, p1, p2, p3)):
        height = piece.shape[1]
        slot, half = info[info_piece + 2 * index], info[info_piece + 2 * index + 1]
        rows = pl.ds(pl.multiple_of(half * height, height), height)
        copies.append(pltpu.make_async_copy(kept.at[slot, :, rows, :], piece, osems.at[index]))
    start_all(copies)
    wait_all(copies)


def on_device(background, src_pos, coupling, x_factor, y_factor):
    px_count = lax.axis_size("px")
    sec_index, own_x, own_y = (lax.axis_index(axis) for axis in ("sec", "px", "py"))
    group, member = sec_index // 2, sec_index % 2
    groups = lax.axis_size("sec") // 2
    order = y_factor.shape[3]
    field = background[:, 0]
    rows_here = field.shape[1]
    height = x_factor.shape[2]
    params = pltpu.CompilerParams(vmem_limit_bytes=vmem_bytes)
    rounds = [(a, b) for a in range(groups) for b in range(px_count)]

    def pairs(a, b):
        return [
            ((2 * x + c) * px_count + y, (2 * ((c + a) % 2) + x) * px_count + (y + b) % px_count)
            for x in range(groups)
            for c in range(2)
            for y in range(px_count)
        ]

    def back_pairs(a, b):
        return [(target, source) for source, target in pairs(a, b)]

    own_source = src_pos[own_y * groups * px_count + group * px_count + own_x]
    plane_cells = x_factor.shape[3] * order
    layer = own_source // plane_cells
    remainder = own_source % plane_cells
    py_count = lax.axis_size("py")
    entries = [
        jnp.where(layer // 2 == member, layer % 2, -1),
        remainder // order,
        remainder % order,
        member,
    ]
    for a, b in rounds:
        entries += [(group + a) % 2, (own_x - b) % px_count]
    entries += [group, (group + 1) % 2, own_x, (own_x + 1) % 2]
    info = jnp.stack([jnp.asarray(entry, jnp.int32) for entry in entries])

    sends_to = jnp.stack(
        [((member + a) % 2) * px_count + (own_x + b) % px_count for a, b in rounds] + [own_y]
    ).astype(jnp.int32)
    piece_shape = jax.ShapeDtypeStruct((2, rows_here, order), bf16)
    *pieces, blocks = pl.pallas_call(
        pack_kernel,
        out_shape=[jax.ShapeDtypeStruct((2 * rows_here + height, order), bf16)] * len(rounds)
        + [jax.ShapeDtypeStruct((py_count, 4, height, order), bf16)],
        in_specs=[in_smem] + [anywhere] * 4,
        out_specs=[in_vmem] * (len(rounds) + 1),
        scratch_shapes=[
            pltpu.SemaphoreType.DMA((len(rounds), 2)),
            pltpu.SemaphoreType.DMA((len(rounds),)),
            pltpu.SemaphoreType.DMA((py_count, 2)),
        ],
        compiler_params=params,
    )(sends_to, field, coupling[0], x_factor[0], y_factor[0])
    pieces = [
        lax.ppermute(piece, ("sec", "px"), pairs(a, b)) for piece, (a, b) in zip(pieces, rounds)
    ]
    blocks = lax.all_to_all(blocks, "py", split_axis=0, concat_axis=0, tiled=True)

    column_shape = jax.ShapeDtypeStruct((2, rows_here, order), bf16)
    x_column, y_column = pl.pallas_call(
        column_kernel,
        out_shape=[column_shape] * 2,
        in_specs=[anywhere] * 5,
        out_specs=[in_vmem] * 2,
        scratch_shapes=[pltpu.SemaphoreType.DMA((py_count, 2))],
        compiler_params=params,
    )(blocks, *pieces)

    def across(block, a):
        return lax.ppermute(block, ("sec", "px"), pairs(a, 0))

    def aside(block):
        return lax.ppermute(block, "px", [(y, (y + 1) % 2) for y in range(2)])

    x_aside = aside(x_column)
    y_near = [across(y_column, a) for a in range(2)]
    x_both, rows_held = pl.pallas_call(
        both_kernel,
        out_shape=[
            jax.ShapeDtypeStruct((2, 2, rows_here, order), bf16),
            jax.ShapeDtypeStruct((py_count, len(rounds), height, order), bf16),
        ],
        in_specs=[anywhere] * 8,
        out_specs=[in_vmem] * 2,
        scratch_shapes=[
            pltpu.SemaphoreType.DMA((2,)),
            pltpu.SemaphoreType.DMA((py_count, len(rounds))),
        ],
        compiler_params=params,
    )(x_column, x_aside, *y_near, *pieces)
    y_far = [aside(block) for block in y_near]
    x_across = [across(x_both, a) for a in range(2)]
    weights = lax.all_to_all(rows_held, "py", split_axis=0, concat_axis=0, tiled=True)
    factors = x_across + [y_near[0], y_far[0], y_near[1], y_far[1]]

    full_shape = jax.ShapeDtypeStruct((2, order, order), bf16)
    factor_scratch = pltpu.VMEM((2, 2, order, 2 * order), bf16)
    arrived_scratch = pltpu.VMEM((2, order, order), bf16)
    weight_scratch = pltpu.VMEM((2, order, order), bf16)
    field_scratch = pltpu.VMEM((2, 2, order, order), bf16)
    beside_scratch = pltpu.VMEM((2 * order, 2 * order), bf16)
    below_scratch = beside_scratch
    factor_sems = pltpu.SemaphoreType.DMA((2, 2, 2, 2))
    solve_flops = 16 * order**3
    w_low, w_high = pl.pallas_call(
        first_kernel,
        out_shape=[full_shape] * 2,
        in_specs=[in_smem] + [anywhere] * 11,
        out_specs=[in_vmem] * 2,
        scratch_shapes=[
            factor_scratch,
            weight_scratch,
            field_scratch,
            beside_scratch,
            below_scratch,
            pltpu.SemaphoreType.DMA((9,)),
            pltpu.SemaphoreType.DMA((4, 4)),
            factor_sems,
        ],
        compiler_params=params,
        cost_estimate=pl.CostEstimate(
            flops=2 * solve_flops, bytes_accessed=16 * order * order * 2, transcendentals=0
        ),
    )(info, *factors, weights, *pieces)

    up = [(2 * x, 2 * x + 1) for x in range(groups)]
    incoming = lax.ppermute(w_high, "sec", up)
    solved, sent = pl.pallas_call(
        last_kernel,
        out_shape=[jax.ShapeDtypeStruct((2, 2, order, order), bf16), full_shape],
        in_specs=[in_smem] + [anywhere] * 12,
        out_specs=[anywhere, in_vmem],
        scratch_shapes=[
            factor_scratch,
            weight_scratch,
            field_scratch,
            arrived_scratch,
            field_scratch,
            beside_scratch,
            below_scratch,
            pltpu.SemaphoreType.DMA((9,)),
            pltpu.SemaphoreType.DMA((4, 4)),
            factor_sems,
            pltpu.SemaphoreType.DMA((2,)),
        ],
        compiler_params=params,
        cost_estimate=pl.CostEstimate(
            flops=3 * solve_flops, bytes_accessed=16 * order * order * 2, transcendentals=0
        ),
    )(info, *factors, weights, *pieces, incoming)

    down = [(target, source) for source, target in up]
    incoming = lax.ppermute(sent, "sec", down)
    results = pl.pallas_call(
        back_kernel,
        out_shape=[piece_shape] * len(rounds),
        in_specs=[in_smem] + [anywhere] * 11,
        out_specs=[anywhere] * len(rounds),
        scratch_shapes=[
            factor_scratch,
            weight_scratch,
            field_scratch,
            arrived_scratch,
            beside_scratch,
            below_scratch,
            pltpu.SemaphoreType.DMA((9,)),
            pltpu.SemaphoreType.DMA((4, 4)),
            factor_sems,
            pltpu.SemaphoreType.DMA((len(rounds),)),
        ],
        compiler_params=params,
        cost_estimate=pl.CostEstimate(
            flops=2 * solve_flops, bytes_accessed=16 * order * order * 2, transcendentals=0
        ),
    )(info, *factors, weights, w_low, w_high, incoming, solved)
    results = [
        lax.ppermute(piece, ("sec", "px"), back_pairs(a, b)) for piece, (a, b) in zip(results, rounds)
    ]
    output = pl.pallas_call(
        unpack_kernel,
        out_shape=jax.ShapeDtypeStruct(field.shape, bf16),
        in_specs=[in_smem] + [anywhere] * len(rounds),
        out_specs=in_vmem,
        scratch_shapes=[pltpu.SemaphoreType.DMA((len(rounds),))],
        compiler_params=params,
    )(sends_to, *results)
    return output[:, None]


def chip_plan_fits(mesh):
    return mesh.shape["sec"] == 4 and mesh.shape["px"] == 2 and mesh.shape["py"] == 4


def solution(mesh):
    placed = (
        P(None, "sec", "px", "py"),
        P(),
        P("sec", "px", None),
        P("sec", None, ("px", "py"), None),
        P("sec", None, ("px", "py"), None),
    )
    return jax.shard_map(
        on_device if chip_plan_fits(mesh) else on_device_by_layer,
        mesh=mesh,
        in_specs=placed,
        out_specs=P(None, "sec", "px", "py"),
        check_vma=False,
    )
```

```python
import functools

import jax
import jax.numpy as jnp
from jax import lax
from jax.experimental import pallas as pl
from jax.experimental.pallas import tpu as pltpu
from jax.sharding import PartitionSpec as P

source_amplitude = 8.0
vmem_bytes = 32 * 1024 * 1024
bf16 = jnp.bfloat16
f32 = jnp.float32
anywhere = pl.BlockSpec(memory_space=pl.ANY)
in_smem = pl.BlockSpec(memory_space=pltpu.SMEM)
in_vmem = pl.BlockSpec(memory_space=pltpu.VMEM)

info_member, info_piece, info_slot, info_half, info_block = 3, 4, 12, 14, 16


def shifted(x, axis, by):
    peers = lax.axis_size(axis)
    pairs = [(i, i + by) for i in range(peers) if 0 <= i + by < peers]
    return lax.ppermute(x, axis, pairs)


def complex_block(factor):
    upper = jnp.concatenate([factor[0], -factor[1]], axis=1)
    lower = jnp.concatenate([factor[1], factor[0]], axis=1)
    return jnp.concatenate([upper, lower], axis=0)


def y_transform(real_turned, imag_turned, field_in):
    real_part = jnp.dot(field_in[0], real_turned, preferred_element_type=jnp.float32) - jnp.dot(
        field_in[1], imag_turned, preferred_element_type=jnp.float32
    )
    imag_part = jnp.dot(field_in[0], imag_turned, preferred_element_type=jnp.float32) + jnp.dot(
        field_in[1], real_turned, preferred_element_type=jnp.float32
    )
    return jnp.stack([real_part, imag_part]).astype(jnp.bfloat16)


def x_transform(x_block, field_in):
    planes, rows_all, width = field_in.shape
    output = jnp.dot(
        x_block, field_in.reshape(planes * rows_all, width), preferred_element_type=jnp.float32
    )
    return output.astype(jnp.bfloat16).reshape(planes, rows_all, width)


def scale_rows(field_in, weights, width):
    planes, rows_here, merged = field_in.shape
    spread = field_in.astype(jnp.float32).reshape(planes, rows_here, merged // width, width)
    return (spread * weights.astype(jnp.float32)[None, :, None, :]).reshape(
        planes, rows_here, merged
    )


def pick_batch(field, batch_count, batch_index):
    planes, rows_here, merged = field.shape
    split_field = field.reshape(planes, rows_here, batch_count, merged // batch_count)
    return lax.dynamic_index_in_dim(split_field, batch_index, 2, keepdims=False)


def place_batch(field, piece, batch_count, batch_index):
    planes, rows_here, merged = field.shape
    split_field = field.reshape(planes, rows_here, batch_count, merged // batch_count)
    shaped = piece.reshape(planes, rows_here, 1, merged // batch_count)
    updated = lax.dynamic_update_slice_in_dim(split_field, shaped, batch_index, 2)
    return updated.reshape(planes, rows_here, merged)


def on_device_by_layer(background, src_pos, coupling, x_factor, y_factor):
    source_count = src_pos.shape[0]
    sec_count = lax.axis_size("sec")
    sec_index = lax.axis_index("sec")
    grid_y = lax.axis_size("py")
    own_x = lax.axis_index("px")
    own_y = lax.axis_index("py")
    local_sources = source_count // grid_y
    x_pieces, y_pieces = (
        lax.all_gather(x_factor[0], ("px", "py"), axis=1, tiled=True),
        lax.all_gather(y_factor[0], ("px", "py"), axis=1, tiled=True),
    )
    x_block = complex_block(x_pieces)
    real_turned = y_pieces[0].T
    imag_turned = y_pieces[1].T
    local_field = background[:, 0]
    local_weights = coupling[0]
    rows_here = local_field.shape[1]
    full_cols = y_factor.shape[3]
    plane_cells = x_factor.shape[3] * full_cols
    own_sources = lax.dynamic_slice_in_dim(src_pos, own_y * local_sources, local_sources)
    layer_of = own_sources // plane_cells
    remainder = own_sources % plane_cells
    row_of = remainder // full_cols
    column_of = remainder % full_cols
    row_start = own_x * rows_here
    row_hit = row_of[None, :] == row_start + jnp.arange(rows_here, dtype=jnp.int32)[:, None]
    col_hit = column_of[:, None] == jnp.arange(full_cols, dtype=jnp.int32)[None, :]
    layer_hit = layer_of == sec_index
    delta = (row_hit[:, :, None] & col_hit[None, :, :] & layer_hit[None, :, None]).astype(
        jnp.float32
    )
    delta = (delta * source_amplitude).reshape(rows_here, local_sources * full_cols)
    real_rhs = local_field[0].astype(jnp.float32) + delta
    rhs_field = jnp.stack([real_rhs, local_field[1].astype(jnp.float32)])

    def apply_front(field_in):
        turned = y_transform(real_turned, imag_turned, field_in)
        line_field = lax.all_to_all(turned, "px", split_axis=2, concat_axis=1, tiled=True)
        finished = x_transform(x_block, line_field)
        return lax.all_to_all(finished, "px", split_axis=1, concat_axis=2, tiled=True)

    forward_field = jnp.zeros(local_field.shape, jnp.bfloat16)
    outgoing = pick_batch(forward_field, sec_count, 0)
    for step in range(2 * sec_count - 1):
        incoming = shifted(outgoing, "sec", 1)
        batch_index = step - sec_index
        active = (batch_index >= 0) & (batch_index < sec_count)
        clamped = jnp.clip(batch_index, 0, sec_count - 1)
        rhs_batch = pick_batch(rhs_field, sec_count, clamped)
        reduced = (rhs_batch - scale_rows(incoming, local_weights, full_cols)).astype(jnp.bfloat16)
        candidate = apply_front(reduced)
        previous = pick_batch(forward_field, sec_count, clamped)
        kept = jnp.where(active, candidate, previous)
        forward_field = place_batch(forward_field, kept, sec_count, clamped)
        outgoing = candidate
    sweep_field = forward_field
    for step in range(2 * sec_count - 2):
        send_index = jnp.clip(step - (sec_count - 1 - sec_index), 0, sec_count - 1)
        own_batch = pick_batch(sweep_field, sec_count, send_index)
        sent_field = scale_rows(own_batch, local_weights, full_cols).astype(jnp.bfloat16)
        incoming = shifted(sent_field, "sec", -1)
        batch_index = step - (sec_count - 2 - sec_index)
        active = (batch_index >= 0) & (batch_index < sec_count) & (sec_index <= sec_count - 2)
        clamped = jnp.clip(batch_index, 0, sec_count - 1)
        solved = apply_front(incoming)
        forward_batch = pick_batch(forward_field, sec_count, clamped)
        candidate = (forward_batch.astype(jnp.float32) - solved.astype(jnp.float32)).astype(
            jnp.bfloat16
        )
        previous = pick_batch(sweep_field, sec_count, clamped)
        kept = jnp.where(active, candidate, previous)
        sweep_field = place_batch(sweep_field, kept, sec_count, clamped)
    return sweep_field[:, None]


def start_all(copies):
    for copy in copies:
        copy.start()


def wait_all(copies):
    for copy in copies:
        copy.wait()


def row_chunks(order, step):
    step = min(step, order)
    return [slice(first, first + step) for first in range(0, order, step)]


def pack_kernel(place, field, coupling, *rest):
    pieces, (sems, csems) = rest[:-2], rest[-2:]
    copies = []
    for index, piece in enumerate(pieces):
        width = piece.shape[1]
        offset = pl.multiple_of(place[index] * width, width)
        rows_here = field.shape[1]
        height = piece.shape[0] - 2 * rows_here
        own = pl.ds(pl.multiple_of(place[len(pieces)] * height, height), height)
        for plane in range(2):
            copies.append(
                pltpu.make_async_copy(
                    field.at[plane, :, pl.ds(offset, width)],
                    piece.at[pl.ds(plane * rows_here, rows_here)],
                    sems.at[index, plane],
                )
            )
        copies.append(
            pltpu.make_async_copy(
                coupling.at[own], piece.at[pl.ds(2 * rows_here, height)], csems.at[index]
            )
        )
    start_all(copies)
    wait_all(copies)


def unpack_kernel(place, *rest):
    pieces, field, sems = rest[:-2], rest[-2], rest[-1]
    copies = []
    for index, piece in enumerate(pieces):
        width = piece.shape[2]
        offset = pl.multiple_of(place[index] * width, width)
        copies.append(
            pltpu.make_async_copy(piece, field.at[:, :, pl.ds(offset, width)], sems.at[index])
        )
    start_all(copies)
    wait_all(copies)


def column_kernel(blocks, p0, p1, p2, p3, x_column, y_turned, rows_held, sems, csems):
    count, planes, height, order = blocks.shape
    copies = []
    for index in range(count):
        copies.append(
            pltpu.make_async_copy(
                blocks.at[index, pl.ds(0, 2)],
                x_column.at[:, pl.ds(index * height, height), :],
                sems.at[index],
            )
        )
    for index, piece in enumerate((p0, p1, p2, p3)):
        copies.append(
            pltpu.make_async_copy(
                piece.at[pl.ds(piece.shape[0] - height, height)], rows_held.at[index], csems.at[index]
            )
        )
    start_all(copies)
    for plane in range(2):
        column = blocks[:, 2 + plane].reshape(count * height, order)
        y_turned[plane] = column.astype(f32).T.astype(bf16)
    wait_all(copies)


def both_kernel(x_column, x_aside, y0, y1, rows_held, rows_next, x_both, y_both, rows_both, sems):
    copies = []
    for target, parts in ((x_both, (x_column, x_aside)), (y_both, (y0, y1)), (rows_both, (rows_held, rows_next))):
        for index, part in enumerate(parts):
            copies.append(pltpu.make_async_copy(part, target.at[index], sems.at[len(copies)]))
    start_all(copies)
    wait_all(copies)


def weight_copies(info, near, far, weights, sems):
    height = near.shape[2]
    half_height = weights.shape[1] // 2
    copies = []
    for index in range(4):
        block = (near if index < 2 else far).at[index % 2]
        for turn in range(near.shape[1]):
            slot, half = info[info_piece + 2 * turn], info[info_piece + 2 * turn + 1]
            start = half * half_height + info[info_block + index] * height
            rows = pl.ds(pl.multiple_of(start, height), height)
            copies.append(
                pltpu.make_async_copy(
                    block.at[turn], weights.at[slot, rows, :], sems.at[index, turn]
                )
            )
    return copies


def halves(*pairs):
    return [pair.at[half] for pair in pairs for half in range(2)]


class Factors:
    def __init__(self, info, x_columns, y_columns, held_x, held_y, sems):
        self.order, self.held_x, self.held_y = held_x.shape[1], held_x, held_y
        self.sems, self.columns = sems, (x_columns, y_columns)
        for which in (1, 0):
            for index, column in enumerate(self.columns[which]):
                slot, half = info[info_slot + index // 2], info[info_half + index % 2]
                for plane in range(2):
                    self.copy(column, which, plane, slot, half, index % 2).start()

    def copy(self, column, which, plane, slot, half, place):
        size = self.order // 2
        part = pl.ds(half * size if isinstance(half, int) else pl.multiple_of(half * size, size), size)
        across = pl.ds(plane * self.order, self.order)
        target = self.held_y.at[slot, across, part] if which else self.held_x.at[slot, part, across]
        return pltpu.make_async_copy(
            column.at[plane], target, self.sems.at[slot, which, place, plane]
        )

    def ready(self, slot, which):
        for place in range(2):
            for plane in range(2):
                self.copy(self.columns[which][0], which, plane, slot, place, place).wait()

    def apply(self, slot, beside, below, store, fresh):
        order = self.order
        if fresh:
            self.ready(slot, 1)
        for columns in row_chunks(order, 256):
            part = jnp.dot(
                beside[...], self.held_y[slot, :, columns], preferred_element_type=f32
            ).astype(bf16)
            real, imag = part[:order], part[order:]
            further = slice(columns.start + order, columns.stop + order)
            below[:order, columns] = real
            below[:order, further] = imag
            below[order:, columns] = -imag
            below[order:, further] = real
        if fresh:
            self.ready(slot, 0)
        for plane in range(2):
            for columns in row_chunks(order, 256):
                along = slice(columns.start + plane * order, columns.stop + plane * order)
                store(
                    plane,
                    columns,
                    jnp.dot(self.held_x[slot], below[:, along], preferred_element_type=f32),
                )


def put_beside(beside, plane, rows, values):
    order = beside.shape[0] // 2
    left, right = slice(0, order), slice(order, 2 * order)
    lower = slice(rows.start + order, rows.stop + order)
    values = values.astype(bf16)
    if plane == 0:
        beside[rows, left] = values
        beside[lower, right] = values
    else:
        beside[rows, right] = -values
        beside[lower, left] = values


def reduce_into(beside, rhs, info, slot, weights, incoming):
    order = beside.shape[0] // 2
    for plane in range(2):
        for rows in row_chunks(order, 128):
            values = rhs[slot, plane, rows].astype(f32)
            scaled = weights[slot, rows].astype(f32) * incoming(plane, rows, slice(None))
            put_beside(beside, plane, rows, values - scaled)

    @pl.when(info[0] == slot)
    def _():
        tall, wide = 16, 128
        top = pl.multiple_of(info[1] // tall * tall, tall)
        left = pl.multiple_of(info[2] // wide * wide, wide)
        rows, columns = pl.ds(top, tall), pl.ds(left, wide)
        values = rhs[slot, 0, rows, columns].astype(f32)
        row = lax.broadcasted_iota(jnp.int32, values.shape, 0) + top
        column = lax.broadcasted_iota(jnp.int32, values.shape, 1) + left
        hit = (row == info[1]) & (column == info[2])
        values = values + jnp.where(hit, f32(source_amplitude), f32(0.0))
        scaled = weights[slot, rows, columns].astype(f32) * incoming(0, rows, columns)
        values = (values - scaled).astype(bf16)
        beside[rows, columns] = values
        lower = pl.ds(pl.multiple_of(order + top, tall), tall)
        further = pl.ds(pl.multiple_of(order + left, wide), wide)
        beside[lower, further] = values


def sent_into(beside, weights, slot, field):
    order = beside.shape[0] // 2
    for plane in range(2):
        for rows in row_chunks(order, 128):
            scaled = weights[slot, rows].astype(f32) * field(plane, rows)
            put_beside(beside, plane, rows, scaled)


def subtract_into(target, forward):
    def store(plane, columns, values):
        solved = values.astype(bf16).astype(f32)
        target[plane, :, columns] = (forward(plane, columns).astype(f32) - solved).astype(bf16)

    return store


def round_into(target):
    def store(plane, columns, values):
        target[plane, :, columns] = values.astype(bf16)

    return store


def rhs_copies(info, pieces, rhs, sems):
    copies = []
    height = rhs.shape[2] // 2
    for index, piece in enumerate(pieces):
        slot, half = info[info_piece + 2 * index], info[info_piece + 2 * index + 1]
        rows = pl.ds(pl.multiple_of(half * height, height), height)
        for plane in range(2):
            copies.append(
                pltpu.make_async_copy(
                    piece.at[pl.ds(plane * height, height)],
                    rhs.at[slot, plane, rows, :],
                    sems.at[2 * index + plane],
                )
            )
    return copies


def first_kernel(info, x0, x1, y0, y1, y2, near, far, p0, p1, p2, p3, w_low, w_high,
                 held_x, held_y, weights, rhs, beside, below, sems, csems, fsems):
    @pl.when(info[info_member] == 0)
    def _():
        early = rhs_copies(info, (p0, p1, p2, p3), rhs, sems)
        early += weight_copies(info, near, far, weights, csems)
        start_all(early)
        factors = Factors(
            info, halves(x0, x1), (y0, y2.at[0], y1, y2.at[1]), held_x, held_y, fsems
        )
        wait_all(early)
        reduce_into(beside, rhs, info, 0, weights, lambda *where: f32(0.0))
        factors.apply(0, beside, below, round_into(w_low), True)
        reduce_into(
            beside, rhs, info, 1, weights, lambda *where: w_low[where].astype(f32)
        )
        factors.apply(1, beside, below, round_into(w_high), True)


def last_kernel(info, x0, x1, y0, y1, y2, near, far, p0, p1, p2, p3, incoming, field,
                sent, held_x, held_y, weights, rhs, arrived, kept, beside, below, sems, csems, fsems,
                osems):
    @pl.when(info[info_member] == 1)
    def _():
        early = rhs_copies(info, (p0, p1, p2, p3), rhs, sems)
        early += weight_copies(info, near, far, weights, csems)
        early.append(pltpu.make_async_copy(incoming, arrived, sems.at[8]))
        start_all(early)
        factors = Factors(
            info, halves(x0, x1), (y0, y2.at[0], y1, y2.at[1]), held_x, held_y, fsems
        )
        wait_all(early)
        order = beside.shape[0] // 2
        reduce_into(
            beside, rhs, info, 0, weights, lambda *where: arrived[where].astype(f32)
        )
        w_low, w_high = kept.at[0], kept.at[1]
        factors.apply(0, beside, below, round_into(w_low), True)
        reduce_into(
            beside, rhs, info, 1, weights, lambda *where: w_low[where].astype(f32)
        )
        factors.apply(1, beside, below, round_into(w_high), True)
        out_high = pltpu.make_async_copy(w_high, field.at[1], osems.at[1])
        out_high.start()
        sent_into(beside, weights, 1, lambda plane, rows: w_high[plane, rows].astype(f32))
        factors.apply(
            0,
            beside,
            below,
            subtract_into(w_low, lambda plane, columns: w_low[plane, :, columns]),
            False,
        )
        out_low = pltpu.make_async_copy(w_low, field.at[0], osems.at[0])
        out_low.start()
        sent_into(beside, weights, 0, lambda plane, rows: w_low[plane, rows].astype(f32))
        for plane in range(2):
            sent[plane] = beside[plane * order : (plane + 1) * order, :order]
        out_high.wait()
        out_low.wait()


def back_kernel(info, x0, x1, y0, y1, y2, near, far, w_low, w_high, incoming, field,
                p0, p1, p2, p3, held_x, held_y, weights, kept, arrived, beside, below, sems, csems, fsems,
                osems):
    @pl.when(info[info_member] == 0)
    def _():
        early = [pltpu.make_async_copy(incoming, arrived, sems.at[0])]
        start_all(early)
        factors = Factors(
            info, halves(x0, x1), (y0, y2.at[0], y1, y2.at[1]), held_x, held_y, fsems
        )
        early += weight_copies(info, near, far, weights, csems)
        early += [
            pltpu.make_async_copy(w_low, kept.at[0], sems.at[2]),
            pltpu.make_async_copy(w_high, kept.at[1], sems.at[3]),
        ]
        start_all(early[1:])
        wait_all(early)
        order = beside.shape[0] // 2
        for plane in range(2):
            for rows in row_chunks(order, 128):
                put_beside(beside, plane, rows, arrived[plane, rows])
        u_low, u_high = kept.at[0], kept.at[1]
        factors.apply(
            1,
            beside,
            below,
            subtract_into(u_high, lambda plane, columns: u_high[plane, :, columns]),
            True,
        )
        sent_into(beside, weights, 1, lambda plane, rows: u_high[plane, rows].astype(f32))
        factors.apply(
            0,
            beside,
            below,
            subtract_into(u_low, lambda plane, columns: u_low[plane, :, columns]),
            True,
        )

    @pl.when(info[info_member] != 0)
    def _():
        finished = pltpu.make_async_copy(field, kept, sems.at[0])
        finished.start()
        finished.wait()

    copies = []
    for index, piece in enumerate((p0, p1, p2, p3)):
        height = piece.shape[1]
        slot, half = info[info_piece + 2 * index], info[info_piece + 2 * index + 1]
        rows = pl.ds(pl.multiple_of(half * height, height), height)
        copies.append(pltpu.make_async_copy(kept.at[slot, :, rows, :], piece, osems.at[index]))
    start_all(copies)
    wait_all(copies)


def on_device(background, src_pos, coupling, x_factor, y_factor):
    px_count = lax.axis_size("px")
    sec_index, own_x, own_y = (lax.axis_index(axis) for axis in ("sec", "px", "py"))
    group, member = sec_index // 2, sec_index % 2
    groups = lax.axis_size("sec") // 2
    order = y_factor.shape[3]
    field = background[:, 0]
    rows_here = field.shape[1]
    height = x_factor.shape[2]
    params = pltpu.CompilerParams(vmem_limit_bytes=vmem_bytes)
    rounds = [(a, b) for a in range(groups) for b in range(px_count)]

    def pairs(a, b):
        return [
            ((2 * x + c) * px_count + y, (2 * ((c + a) % 2) + x) * px_count + (y + b) % px_count)
            for x in range(groups)
            for c in range(2)
            for y in range(px_count)
        ]

    def back_pairs(a, b):
        return [(target, source) for source, target in pairs(a, b)]

    own_source = src_pos[own_y * groups * px_count + group * px_count + own_x]
    plane_cells = x_factor.shape[3] * order
    layer = own_source // plane_cells
    remainder = own_source % plane_cells
    py_count = lax.axis_size("py")
    entries = [
        jnp.where(layer // 2 == member, layer % 2, -1),
        remainder // order,
        remainder % order,
        member,
    ]
    for a, b in rounds:
        entries += [(group + a) % 2, (own_x - b) % px_count]
    entries += [group, (group + 1) % 2, own_x, (own_x + 1) % 2]
    pair = own_y // 2 * 2
    entries += [own_y, pair + (own_y + 1) % 2, (own_y + 2) % 4, (pair + 2) % 4 + (own_y + 1) % 2]
    info = jnp.stack([jnp.asarray(entry, jnp.int32) for entry in entries])

    sends_to = jnp.stack(
        [((member + a) % 2) * px_count + (own_x + b) % px_count for a, b in rounds] + [own_y]
    ).astype(jnp.int32)
    piece_shape = jax.ShapeDtypeStruct((2, rows_here, order), bf16)
    shard = jnp.concatenate([x_factor[0], y_factor[0]], axis=0)
    blocks = jnp.broadcast_to(shard[None], (py_count,) + shard.shape)
    blocks = lax.all_to_all(blocks, "py", split_axis=0, concat_axis=0, tiled=True)
    pieces = pl.pallas_call(
        pack_kernel,
        out_shape=[jax.ShapeDtypeStruct((2 * rows_here + height, order), bf16)] * len(rounds),
        in_specs=[in_smem] + [anywhere] * 2,
        out_specs=[in_vmem] * len(rounds),
        scratch_shapes=[
            pltpu.SemaphoreType.DMA((len(rounds), 2)),
            pltpu.SemaphoreType.DMA((len(rounds),)),
        ],
        compiler_params=pltpu.CompilerParams(vmem_limit_bytes=60 * 1024 * 1024),
    )(sends_to, field, coupling[0])
    pieces = [
        lax.ppermute(piece, ("sec", "px"), pairs(a, b)) for piece, (a, b) in zip(pieces, rounds)
    ]

    column_shape = jax.ShapeDtypeStruct((2, rows_here, order), bf16)
    turned_shape = jax.ShapeDtypeStruct((2, order, rows_here), bf16)
    rows_shape = jax.ShapeDtypeStruct((len(rounds), height, order), bf16)
    x_column, y_turned, rows_held = pl.pallas_call(
        column_kernel,
        out_shape=[column_shape, turned_shape, rows_shape],
        in_specs=[in_vmem] + [anywhere] * 4,
        out_specs=[in_vmem] * 3,
        scratch_shapes=[
            pltpu.SemaphoreType.DMA((py_count,)),
            pltpu.SemaphoreType.DMA((len(rounds),)),
        ],
        compiler_params=params,
    )(blocks, *pieces)

    def across(block, a):
        return lax.ppermute(block, ("sec", "px"), pairs(a, 0))

    def aside(block):
        return lax.ppermute(block, "px", [(y, (y + 1) % 2) for y in range(2)])

    def over_z(block, bit):
        return lax.ppermute(block, "py", [(z, z ^ bit) for z in range(py_count)])

    y_near = [across(y_turned, a) for a in range(2)]
    x_aside = aside(x_column)
    rows_next = over_z(rows_held, 1)
    twice = [
        jax.ShapeDtypeStruct((2,) + one.shape, bf16) for one in (column_shape, turned_shape, rows_shape)
    ]
    x_both, y_both, rows_both = pl.pallas_call(
        both_kernel,
        out_shape=twice,
        in_specs=[anywhere] * 6,
        out_specs=[in_vmem] * 3,
        scratch_shapes=[pltpu.SemaphoreType.DMA((6,))],
        compiler_params=params,
    )(x_column, x_aside, *y_near, rows_held, rows_next)
    y_far = aside(y_both)
    x_across = [across(x_both, a) for a in range(2)]
    rows_far = over_z(rows_both, 2)
    factors = x_across + [*y_near, y_far, rows_both, rows_far]

    full_shape = jax.ShapeDtypeStruct((2, order, order), bf16)
    x_scratch = pltpu.VMEM((2, order, 2 * order), bf16)
    y_scratch = pltpu.VMEM((2, 2 * order, order), bf16)
    arrived_scratch = pltpu.VMEM((2, order, order), bf16)
    weight_scratch = pltpu.VMEM((2, order, order), bf16)
    field_scratch = pltpu.VMEM((2, 2, order, order), bf16)
    beside_scratch = pltpu.VMEM((2 * order, 2 * order), bf16)
    below_scratch = beside_scratch
    factor_sems = pltpu.SemaphoreType.DMA((2, 2, 2, 2))
    solve_flops = 16 * order**3
    w_low, w_high = pl.pallas_call(
        first_kernel,
        out_shape=[full_shape] * 2,
        in_specs=[in_smem] + [anywhere] * 11,
        out_specs=[in_vmem] * 2,
        scratch_shapes=[
            x_scratch,
            y_scratch,
            weight_scratch,
            field_scratch,
            beside_scratch,
            below_scratch,
            pltpu.SemaphoreType.DMA((9,)),
            pltpu.SemaphoreType.DMA((4, 4)),
            factor_sems,
        ],
        compiler_params=params,
        cost_estimate=pl.CostEstimate(
            flops=2 * solve_flops, bytes_accessed=16 * order * order * 2, transcendentals=0
        ),
    )(info, *factors, *pieces)

    up = [(2 * x, 2 * x + 1) for x in range(groups)]
    incoming = lax.ppermute(w_high, "sec", up)
    solved, sent = pl.pallas_call(
        last_kernel,
        out_shape=[jax.ShapeDtypeStruct((2, 2, order, order), bf16), full_shape],
        in_specs=[in_smem] + [anywhere] * 12,
        out_specs=[anywhere, in_vmem],
        scratch_shapes=[
            x_scratch,
            y_scratch,
            weight_scratch,
            field_scratch,
            arrived_scratch,
            field_scratch,
            beside_scratch,
            below_scratch,
            pltpu.SemaphoreType.DMA((9,)),
            pltpu.SemaphoreType.DMA((4, 4)),
            factor_sems,
            pltpu.SemaphoreType.DMA((2,)),
        ],
        compiler_params=params,
        cost_estimate=pl.CostEstimate(
            flops=3 * solve_flops, bytes_accessed=16 * order * order * 2, transcendentals=0
        ),
    )(info, *factors, *pieces, incoming)

    down = [(target, source) for source, target in up]
    incoming = lax.ppermute(sent, "sec", down)
    results = pl.pallas_call(
        back_kernel,
        out_shape=[piece_shape] * len(rounds),
        in_specs=[in_smem] + [anywhere] * 11,
        out_specs=[anywhere] * len(rounds),
        scratch_shapes=[
            x_scratch,
            y_scratch,
            weight_scratch,
            field_scratch,
            arrived_scratch,
            beside_scratch,
            below_scratch,
            pltpu.SemaphoreType.DMA((9,)),
            pltpu.SemaphoreType.DMA((4, 4)),
            factor_sems,
            pltpu.SemaphoreType.DMA((len(rounds),)),
        ],
        compiler_params=params,
        cost_estimate=pl.CostEstimate(
            flops=2 * solve_flops, bytes_accessed=16 * order * order * 2, transcendentals=0
        ),
    )(info, *factors, w_low, w_high, incoming, solved)
    results = [
        lax.ppermute(piece, ("sec", "px"), back_pairs(a, b)) for piece, (a, b) in zip(results, rounds)
    ]
    output = pl.pallas_call(
        unpack_kernel,
        out_shape=jax.ShapeDtypeStruct(field.shape, bf16),
        in_specs=[in_smem] + [anywhere] * len(rounds),
        out_specs=in_vmem,
        scratch_shapes=[pltpu.SemaphoreType.DMA((len(rounds),))],
        compiler_params=params,
    )(sends_to, *results)
    return output[:, None]


def chip_plan_fits(mesh):
    return mesh.shape["sec"] == 4 and mesh.shape["px"] == 2 and mesh.shape["py"] == 4


def solution(mesh):
    placed = (
        P(None, "sec", "px", "py"),
        P(),
        P("sec", "px", None),
        P("sec", None, ("px", "py"), None),
        P("sec", None, ("px", "py"), None),
    )
    return jax.shard_map(
        on_device if chip_plan_fits(mesh) else on_device_by_layer,
        mesh=mesh,
        in_specs=placed,
        out_specs=P(None, "sec", "px", "py"),
        check_vma=False,
    )
```

```python
import functools

import jax
import jax.numpy as jnp
from jax import lax
from jax.experimental import pallas as pl
from jax.experimental.pallas import tpu as pltpu
from jax.sharding import PartitionSpec as P

source_amplitude = 8.0
vmem_bytes = 32 * 1024 * 1024
bf16 = jnp.bfloat16
f32 = jnp.float32
anywhere = pl.BlockSpec(memory_space=pl.ANY)
in_smem = pl.BlockSpec(memory_space=pltpu.SMEM)
in_vmem = pl.BlockSpec(memory_space=pltpu.VMEM)

info_member, info_piece, info_slot, info_half, info_block, info_self = 3, 4, 12, 14, 16, 20


def shifted(x, axis, by):
    peers = lax.axis_size(axis)
    pairs = [(i, i + by) for i in range(peers) if 0 <= i + by < peers]
    return lax.ppermute(x, axis, pairs)


def complex_block(factor):
    upper = jnp.concatenate([factor[0], -factor[1]], axis=1)
    lower = jnp.concatenate([factor[1], factor[0]], axis=1)
    return jnp.concatenate([upper, lower], axis=0)


def y_transform(real_turned, imag_turned, field_in):
    real_part = jnp.dot(field_in[0], real_turned, preferred_element_type=jnp.float32) - jnp.dot(
        field_in[1], imag_turned, preferred_element_type=jnp.float32
    )
    imag_part = jnp.dot(field_in[0], imag_turned, preferred_element_type=jnp.float32) + jnp.dot(
        field_in[1], real_turned, preferred_element_type=jnp.float32
    )
    return jnp.stack([real_part, imag_part]).astype(jnp.bfloat16)


def x_transform(x_block, field_in):
    planes, rows_all, width = field_in.shape
    output = jnp.dot(
        x_block, field_in.reshape(planes * rows_all, width), preferred_element_type=jnp.float32
    )
    return output.astype(jnp.bfloat16).reshape(planes, rows_all, width)


def scale_rows(field_in, weights, width):
    planes, rows_here, merged = field_in.shape
    spread = field_in.astype(jnp.float32).reshape(planes, rows_here, merged // width, width)
    return (spread * weights.astype(jnp.float32)[None, :, None, :]).reshape(
        planes, rows_here, merged
    )


def pick_batch(field, batch_count, batch_index):
    planes, rows_here, merged = field.shape
    split_field = field.reshape(planes, rows_here, batch_count, merged // batch_count)
    return lax.dynamic_index_in_dim(split_field, batch_index, 2, keepdims=False)


def place_batch(field, piece, batch_count, batch_index):
    planes, rows_here, merged = field.shape
    split_field = field.reshape(planes, rows_here, batch_count, merged // batch_count)
    shaped = piece.reshape(planes, rows_here, 1, merged // batch_count)
    updated = lax.dynamic_update_slice_in_dim(split_field, shaped, batch_index, 2)
    return updated.reshape(planes, rows_here, merged)


def on_device_by_layer(background, src_pos, coupling, x_factor, y_factor):
    source_count = src_pos.shape[0]
    sec_count = lax.axis_size("sec")
    sec_index = lax.axis_index("sec")
    grid_y = lax.axis_size("py")
    own_x = lax.axis_index("px")
    own_y = lax.axis_index("py")
    local_sources = source_count // grid_y
    x_pieces, y_pieces = (
        lax.all_gather(x_factor[0], ("px", "py"), axis=1, tiled=True),
        lax.all_gather(y_factor[0], ("px", "py"), axis=1, tiled=True),
    )
    x_block = complex_block(x_pieces)
    real_turned = y_pieces[0].T
    imag_turned = y_pieces[1].T
    local_field = background[:, 0]
    local_weights = coupling[0]
    rows_here = local_field.shape[1]
    full_cols = y_factor.shape[3]
    plane_cells = x_factor.shape[3] * full_cols
    own_sources = lax.dynamic_slice_in_dim(src_pos, own_y * local_sources, local_sources)
    layer_of = own_sources // plane_cells
    remainder = own_sources % plane_cells
    row_of = remainder // full_cols
    column_of = remainder % full_cols
    row_start = own_x * rows_here
    row_hit = row_of[None, :] == row_start + jnp.arange(rows_here, dtype=jnp.int32)[:, None]
    col_hit = column_of[:, None] == jnp.arange(full_cols, dtype=jnp.int32)[None, :]
    layer_hit = layer_of == sec_index
    delta = (row_hit[:, :, None] & col_hit[None, :, :] & layer_hit[None, :, None]).astype(
        jnp.float32
    )
    delta = (delta * source_amplitude).reshape(rows_here, local_sources * full_cols)
    real_rhs = local_field[0].astype(jnp.float32) + delta
    rhs_field = jnp.stack([real_rhs, local_field[1].astype(jnp.float32)])

    def apply_front(field_in):
        turned = y_transform(real_turned, imag_turned, field_in)
        line_field = lax.all_to_all(turned, "px", split_axis=2, concat_axis=1, tiled=True)
        finished = x_transform(x_block, line_field)
        return lax.all_to_all(finished, "px", split_axis=1, concat_axis=2, tiled=True)

    forward_field = jnp.zeros(local_field.shape, jnp.bfloat16)
    outgoing = pick_batch(forward_field, sec_count, 0)
    for step in range(2 * sec_count - 1):
        incoming = shifted(outgoing, "sec", 1)
        batch_index = step - sec_index
        active = (batch_index >= 0) & (batch_index < sec_count)
        clamped = jnp.clip(batch_index, 0, sec_count - 1)
        rhs_batch = pick_batch(rhs_field, sec_count, clamped)
        reduced = (rhs_batch - scale_rows(incoming, local_weights, full_cols)).astype(jnp.bfloat16)
        candidate = apply_front(reduced)
        previous = pick_batch(forward_field, sec_count, clamped)
        kept = jnp.where(active, candidate, previous)
        forward_field = place_batch(forward_field, kept, sec_count, clamped)
        outgoing = candidate
    sweep_field = forward_field
    for step in range(2 * sec_count - 2):
        send_index = jnp.clip(step - (sec_count - 1 - sec_index), 0, sec_count - 1)
        own_batch = pick_batch(sweep_field, sec_count, send_index)
        sent_field = scale_rows(own_batch, local_weights, full_cols).astype(jnp.bfloat16)
        incoming = shifted(sent_field, "sec", -1)
        batch_index = step - (sec_count - 2 - sec_index)
        active = (batch_index >= 0) & (batch_index < sec_count) & (sec_index <= sec_count - 2)
        clamped = jnp.clip(batch_index, 0, sec_count - 1)
        solved = apply_front(incoming)
        forward_batch = pick_batch(forward_field, sec_count, clamped)
        candidate = (forward_batch.astype(jnp.float32) - solved.astype(jnp.float32)).astype(
            jnp.bfloat16
        )
        previous = pick_batch(sweep_field, sec_count, clamped)
        kept = jnp.where(active, candidate, previous)
        sweep_field = place_batch(sweep_field, kept, sec_count, clamped)
    return sweep_field[:, None]


def start_all(copies):
    for copy in copies:
        copy.start()


def wait_all(copies):
    for copy in copies:
        copy.wait()


def row_chunks(order, step):
    step = min(step, order)
    return [slice(first, first + step) for first in range(0, order, step)]


class Either:
    def __init__(self, flag, own, received, target, sem):
        self.flag = flag
        self.own = pltpu.make_async_copy(own, target, sem)
        self.received = pltpu.make_async_copy(received, target, sem)

    def start(self):
        @pl.when(self.flag != 0)
        def _():
            self.own.start()

        @pl.when(self.flag == 0)
        def _():
            self.received.start()

    def wait(self):
        self.received.wait()


def pack_kernel(place, field, coupling, x_factor, y_factor, *rest):
    pieces, (blocks, held, shard, sems, csems, osems, fsems) = rest[:-7], rest[-7:]
    rows_here = field.shape[1]
    height = x_factor.shape[1]
    own = pl.ds(pl.multiple_of(place[len(pieces)] * height, height), height)
    factors = [
        pltpu.make_async_copy(factor, shard.at[pl.ds(2 * which, 2)], fsems.at[which])
        for which, factor in enumerate((x_factor, y_factor))
    ]
    start_all(factors)
    incoming = []
    for index, piece in enumerate(pieces):
        width = piece.shape[1]
        offset = pl.multiple_of(place[index] * width, width)
        copies = [
            pltpu.make_async_copy(
                field.at[plane, :, pl.ds(offset, width)],
                held.at[index, pl.ds(plane * rows_here, rows_here)],
                sems.at[index, plane],
            )
            for plane in range(2)
        ]
        copies.append(
            pltpu.make_async_copy(
                coupling.at[own], held.at[index, pl.ds(2 * rows_here, height)], csems.at[index]
            )
        )
        start_all(copies)
        incoming.append(copies)
    outgoing = []
    wait_all(factors)
    for target in range(blocks.shape[0]):
        outgoing.append(pltpu.make_async_copy(shard, blocks.at[target], fsems.at[2 + target]))
        outgoing[-1].start()
    for index, piece in enumerate(pieces):
        wait_all(incoming[index])
        outgoing.append(pltpu.make_async_copy(held.at[index], piece, osems.at[index]))
        outgoing[-1].start()
    wait_all(outgoing)


def unpack_kernel(place, own, *rest):
    pieces, field, sems = rest[:-2], rest[-2], rest[-1]
    copies = []
    for index, piece in enumerate(pieces):
        width = piece.shape[2]
        offset = pl.multiple_of(place[index] * width, width)
        target = field.at[:, :, pl.ds(offset, width)]
        if index:
            copies.append(pltpu.make_async_copy(piece, target, sems.at[index]))
        else:
            copies.append(Either(place[len(pieces) + 1], own, piece, target, sems.at[index]))
    start_all(copies)
    wait_all(copies)


def column_kernel(info, blocks, own, p0, p1, p2, p3, x_column, y_column, rows_held, sems, csems):
    count, planes, height, order = blocks.shape
    copies = []
    for index in range(count):
        for which, column in enumerate((x_column, y_column)):
            copies.append(
                pltpu.make_async_copy(
                    blocks.at[index, pl.ds(2 * which, 2)],
                    column.at[:, pl.ds(index * height, height), :],
                    sems.at[index, which],
                )
            )
    last = pl.ds(own.shape[0] - height, height)
    copies.append(Either(info[info_self], own.at[last], p0.at[last], rows_held.at[0], csems.at[0]))
    for index, piece in enumerate((p1, p2, p3)):
        copies.append(
            pltpu.make_async_copy(piece.at[last], rows_held.at[index + 1], csems.at[index + 1])
        )
    start_all(copies)
    wait_all(copies)


def both_kernel(info, x_column, x_aside, y_column, y0, y1, rows_held, rows_next, x_both, y_both,
                rows_both, sems):
    copies = [
        pltpu.make_async_copy(x_column, x_both.at[0], sems.at[0]),
        pltpu.make_async_copy(x_aside, x_both.at[1], sems.at[1]),
        Either(info[info_self], y_column, y0, y_both.at[0], sems.at[2]),
        pltpu.make_async_copy(y1, y_both.at[1], sems.at[3]),
        pltpu.make_async_copy(rows_held, rows_both.at[0], sems.at[4]),
        pltpu.make_async_copy(rows_next, rows_both.at[1], sems.at[5]),
    ]
    start_all(copies)
    wait_all(copies)


def weight_copies(info, near, far, weights, sems):
    height = near.shape[2]
    half_height = weights.shape[1] // 2
    copies = []
    for index in range(4):
        block = (near if index < 2 else far).at[index % 2]
        for turn in range(near.shape[1]):
            slot, half = info[info_piece + 2 * turn], info[info_piece + 2 * turn + 1]
            start = half * half_height + info[info_block + index] * height
            rows = pl.ds(pl.multiple_of(start, height), height)
            copies.append(
                pltpu.make_async_copy(
                    block.at[turn], weights.at[slot, rows, :], sems.at[index, turn]
                )
            )
    return copies


class Factors:
    def __init__(self, info, x_both, x0, x1, y_both, y_far, held, sems):
        self.order, self.held, self.sems = held.shape[2], held, sems
        self.column = x_both.at[0]
        for which in (1, 0):
            for turn in range(2):
                for far in range(2):
                    slot, half = info[info_slot + turn], info[info_half + far]
                    for plane in range(2):
                        ends = self.ends(which, plane, slot, half, far)
                        if which:
                            source = (y_far if far else y_both).at[turn, plane]
                            pltpu.make_async_copy(source, *ends).start()
                        elif turn:
                            pltpu.make_async_copy(x1.at[far, plane], *ends).start()
                        else:
                            own, received = x_both.at[far, plane], x0.at[far, plane]
                            Either(info[info_self], own, received, *ends).start()

    def ends(self, which, plane, slot, half, far):
        height = self.order // 2
        rows = pl.ds(pl.multiple_of(half * height, height), height)
        target = self.held.at[slot, which, rows, pl.ds(plane * self.order, self.order)]
        return target, self.sems.at[slot, which, far, plane]

    def ready(self, slot, which):
        for far in range(2):
            for plane in range(2):
                ends = self.ends(which, plane, slot, far, far)
                pltpu.make_async_copy(self.column.at[plane], *ends).wait()

    def apply(self, slot, source, below, store, fresh):
        order = self.order
        turned = (((1,), (1,)), ((), ()))
        if fresh:
            self.ready(slot, 1)
        for rows in row_chunks(order, 256):
            real, imag = source(0, rows), source(1, rows)
            upper = jnp.concatenate([real, -imag], axis=1)
            lower = jnp.concatenate([imag, real], axis=1)
            part = lax.dot_general(
                jnp.concatenate([upper, lower], axis=0),
                self.held[slot, 1],
                turned,
                preferred_element_type=f32,
            ).astype(bf16)
            height = rows.stop - rows.start
            real, imag = part[:height], part[height:]
            further = slice(rows.start + order, rows.stop + order)
            below[rows, :order] = real
            below[rows, order:] = imag
            below[further, :order] = -imag
            below[further, order:] = real
        if fresh:
            self.ready(slot, 0)
        for plane in range(2):
            for columns in row_chunks(order, 256):
                along = slice(columns.start + plane * order, columns.stop + plane * order)
                store(
                    plane,
                    columns,
                    jnp.dot(self.held[slot, 0], below[:, along], preferred_element_type=f32),
                )


def reduced(rhs, info, slot, weights, incoming):
    def source(plane, rows):
        values = rhs[slot, plane, rows].astype(f32)
        if plane == 0:
            row = lax.broadcasted_iota(jnp.int32, values.shape, 0) + rows.start
            column = lax.broadcasted_iota(jnp.int32, (1, values.shape[1]), 1)
            hit = (column == info[2]) & (info[0] == slot)
            cell = jnp.where(hit, f32(source_amplitude), f32(0.0))
            values = values + jnp.where(row == info[1], cell, f32(0.0))
        scaled = weights[slot, rows].astype(f32) * incoming(plane, rows)
        return (values - scaled).astype(bf16)

    return source


def sent(weights, slot, field):
    def source(plane, rows):
        scaled = weights[slot, rows].astype(f32) * field[plane, rows].astype(f32)
        return scaled.astype(bf16)

    return source


def subtract_into(target):
    def store(plane, columns, values):
        solved = values.astype(bf16).astype(f32)
        forward = target[plane, :, columns].astype(f32)
        target[plane, :, columns] = (forward - solved).astype(bf16)

    return store


def round_into(target):
    def store(plane, columns, values):
        target[plane, :, columns] = values.astype(bf16)

    return store


def rhs_copies(info, own, pieces, rhs, sems):
    copies = []
    height = rhs.shape[2] // 2
    for index, piece in enumerate(pieces):
        slot, half = info[info_piece + 2 * index], info[info_piece + 2 * index + 1]
        rows = pl.ds(pl.multiple_of(half * height, height), height)
        for plane in range(2):
            part = pl.ds(plane * height, height)
            ends = (rhs.at[slot, plane, rows, :], sems.at[2 * index + plane])
            if index:
                copies.append(pltpu.make_async_copy(piece.at[part], *ends))
            else:
                copies.append(Either(info[info_self], own.at[part], piece.at[part], *ends))
    return copies


def first_kernel(info, xb, x0, x1, yb, yf, near, far, own, p0, p1, p2, p3, w_low, w_high, held,
                 weights, rhs, below, sems, csems, fsems):
    @pl.when(info[info_member] == 0)
    def _():
        early = rhs_copies(info, own, (p0, p1, p2, p3), rhs, sems)
        early += weight_copies(info, near, far, weights, csems)
        start_all(early)
        factors = Factors(info, xb, x0, x1, yb, yf, held, fsems)
        wait_all(early)
        zero = reduced(rhs, info, 0, weights, lambda plane, rows: f32(0.0))
        factors.apply(0, zero, below, round_into(w_low), True)
        one = reduced(rhs, info, 1, weights, lambda plane, rows: w_low[plane, rows].astype(f32))
        factors.apply(1, one, below, round_into(w_high), True)


def last_kernel(info, xb, x0, x1, yb, yf, near, far, own, p0, p1, p2, p3, incoming, field, back,
                held, weights, rhs, arrived, kept, below, sems, csems, fsems, osems):
    @pl.when(info[info_member] == 1)
    def _():
        early = rhs_copies(info, own, (p0, p1, p2, p3), rhs, sems)
        early += weight_copies(info, near, far, weights, csems)
        early.append(pltpu.make_async_copy(incoming, arrived, sems.at[8]))
        start_all(early)
        factors = Factors(info, xb, x0, x1, yb, yf, held, fsems)
        wait_all(early)
        low, high = kept.at[0], kept.at[1]
        two = reduced(rhs, info, 0, weights, lambda plane, rows: arrived[plane, rows].astype(f32))
        factors.apply(0, two, below, round_into(low), True)
        three = reduced(rhs, info, 1, weights, lambda plane, rows: low[plane, rows].astype(f32))
        factors.apply(1, three, below, round_into(high), True)
        out_high = pltpu.make_async_copy(high, field.at[1], osems.at[1])
        out_high.start()
        factors.apply(0, sent(weights, 1, high), below, subtract_into(low), False)
        out_low = pltpu.make_async_copy(low, field.at[0], osems.at[0])
        out_low.start()
        last = sent(weights, 0, low)
        for plane in range(2):
            for rows in row_chunks(weights.shape[1], 256):
                back[plane, rows] = last(plane, rows)
        out_high.wait()
        out_low.wait()


def back_kernel(info, xb, x0, x1, yb, yf, near, far, w_low, w_high, incoming, field, p0, p1, p2, p3,
                held, weights, kept, arrived, below, sems, csems, fsems, osems):
    @pl.when(info[info_member] == 0)
    def _():
        early = [pltpu.make_async_copy(incoming, arrived, sems.at[0])]
        start_all(early)
        factors = Factors(info, xb, x0, x1, yb, yf, held, fsems)
        early += weight_copies(info, near, far, weights, csems)
        early += [
            pltpu.make_async_copy(w_low, kept.at[0], sems.at[2]),
            pltpu.make_async_copy(w_high, kept.at[1], sems.at[3]),
        ]
        start_all(early[1:])
        wait_all(early)
        low, high = kept.at[0], kept.at[1]
        one = lambda plane, rows: arrived[plane, rows]
        factors.apply(1, one, below, subtract_into(high), True)
        factors.apply(0, sent(weights, 1, high), below, subtract_into(low), True)

    @pl.when(info[info_member] != 0)
    def _():
        finished = pltpu.make_async_copy(field, kept, sems.at[0])
        finished.start()
        finished.wait()

    copies = []
    for index, piece in enumerate((p0, p1, p2, p3)):
        height = piece.shape[1]
        slot, half = info[info_piece + 2 * index], info[info_piece + 2 * index + 1]
        rows = pl.ds(pl.multiple_of(half * height, height), height)
        copies.append(pltpu.make_async_copy(kept.at[slot, :, rows, :], piece, osems.at[index]))
    start_all(copies)
    wait_all(copies)


def on_device(background, src_pos, coupling, x_factor, y_factor):
    px_count = lax.axis_size("px")
    sec_index, own_x, own_y = (lax.axis_index(axis) for axis in ("sec", "px", "py"))
    group, member = sec_index // 2, sec_index % 2
    groups = lax.axis_size("sec") // 2
    order = y_factor.shape[3]
    field = background[:, 0]
    rows_here = field.shape[1]
    height = x_factor.shape[2]
    params = pltpu.CompilerParams(vmem_limit_bytes=vmem_bytes)
    rounds = [(a, b) for a in range(groups) for b in range(px_count)]

    def pairs(a, b):
        return [
            ((2 * x + c) * px_count + y, (2 * ((c + a) % 2) + x) * px_count + (y + b) % px_count)
            for x in range(groups)
            for c in range(2)
            for y in range(px_count)
            if (a, b, x) != (0, 0, c)
        ]

    def back_pairs(a, b):
        return [(target, source) for source, target in pairs(a, b)]

    own_source = src_pos[own_y * groups * px_count + group * px_count + own_x]
    plane_cells = x_factor.shape[3] * order
    layer = own_source // plane_cells
    remainder = own_source % plane_cells
    py_count = lax.axis_size("py")
    entries = [
        jnp.where(layer // 2 == member, layer % 2, -1),
        remainder // order,
        remainder % order,
        member,
    ]
    for a, b in rounds:
        entries += [(group + a) % 2, (own_x - b) % px_count]
    entries += [group, (group + 1) % 2, own_x, (own_x + 1) % 2]
    pair = own_y // 2 * 2
    entries += [own_y, pair + (own_y + 1) % 2, (own_y + 2) % 4, (pair + 2) % 4 + (own_y + 1) % 2]
    entries += [group == member]
    info = jnp.stack([jnp.asarray(entry, jnp.int32) for entry in entries])

    sends_to = jnp.stack(
        [((member + a) % 2) * px_count + (own_x + b) % px_count for a, b in rounds]
        + [own_y, group == member]
    ).astype(jnp.int32)
    piece_shape = jax.ShapeDtypeStruct((2, rows_here, order), bf16)
    *packed, blocks = pl.pallas_call(
        pack_kernel,
        out_shape=[jax.ShapeDtypeStruct((2 * rows_here + height, order), bf16)] * len(rounds)
        + [jax.ShapeDtypeStruct((py_count, 4, height, order), bf16)],
        in_specs=[in_smem] + [anywhere] * 4,
        out_specs=[anywhere] * (len(rounds) + 1),
        scratch_shapes=[
            pltpu.VMEM((len(rounds), 2 * rows_here + height, order), bf16),
            pltpu.VMEM((4, height, order), bf16),
            pltpu.SemaphoreType.DMA((len(rounds), 2)),
            pltpu.SemaphoreType.DMA((len(rounds),)),
            pltpu.SemaphoreType.DMA((len(rounds),)),
            pltpu.SemaphoreType.DMA((2 + py_count,)),
        ],
        compiler_params=pltpu.CompilerParams(vmem_limit_bytes=60 * 1024 * 1024),
    )(sends_to, field, coupling[0], x_factor[0], y_factor[0])
    pieces = [
        lax.ppermute(piece, ("sec", "px"), pairs(a, b)) for piece, (a, b) in zip(packed, rounds)
    ]
    blocks = lax.all_to_all(blocks, "py", split_axis=0, concat_axis=0, tiled=True)

    column_shape = jax.ShapeDtypeStruct((2, rows_here, order), bf16)
    rows_shape = jax.ShapeDtypeStruct((len(rounds), height, order), bf16)
    x_column, y_column, rows_held = pl.pallas_call(
        column_kernel,
        out_shape=[column_shape, column_shape, rows_shape],
        in_specs=[in_smem] + [anywhere] * 6,
        out_specs=[in_vmem] * 3,
        scratch_shapes=[
            pltpu.SemaphoreType.DMA((py_count, 2)),
            pltpu.SemaphoreType.DMA((len(rounds),)),
        ],
        compiler_params=params,
    )(info, blocks, packed[0], *pieces)

    def across(block, a):
        return lax.ppermute(block, ("sec", "px"), pairs(a, 0))

    def aside(block):
        return lax.ppermute(block, "px", [(y, (y + 1) % 2) for y in range(2)])

    def over_z(block, bit):
        return lax.ppermute(block, "py", [(z, z ^ bit) for z in range(py_count)])

    y_near = [across(y_column, a) for a in range(2)]
    x_aside = aside(x_column)
    rows_next = over_z(rows_held, 1)
    twice = [
        jax.ShapeDtypeStruct((2,) + one.shape, bf16) for one in (column_shape, column_shape, rows_shape)
    ]
    x_both, y_both, rows_both = pl.pallas_call(
        both_kernel,
        out_shape=twice,
        in_specs=[in_smem] + [anywhere] * 7,
        out_specs=[in_vmem] * 3,
        scratch_shapes=[pltpu.SemaphoreType.DMA((6,))],
        compiler_params=params,
    )(info, x_column, x_aside, y_column, *y_near, rows_held, rows_next)
    y_far = aside(y_both)
    x_across = [across(x_both, a) for a in range(2)]
    rows_far = over_z(rows_both, 2)
    factors = [x_both, *x_across, y_both, y_far, rows_both, rows_far]

    full_shape = jax.ShapeDtypeStruct((2, order, order), bf16)
    factor_scratch = pltpu.VMEM((2, 2, order, 2 * order), bf16)
    arrived_scratch = pltpu.VMEM((2, order, order), bf16)
    weight_scratch = pltpu.VMEM((2, order, order), bf16)
    field_scratch = pltpu.VMEM((2, 2, order, order), bf16)
    below_scratch = pltpu.VMEM((2 * order, 2 * order), bf16)
    factor_sems = pltpu.SemaphoreType.DMA((2, 2, 2, 2))
    solve_flops = 16 * order**3
    w_low, w_high = pl.pallas_call(
        first_kernel,
        out_shape=[full_shape] * 2,
        in_specs=[in_smem] + [anywhere] * 12,
        out_specs=[in_vmem] * 2,
        scratch_shapes=[
            factor_scratch,
            weight_scratch,
            field_scratch,
            below_scratch,
            pltpu.SemaphoreType.DMA((9,)),
            pltpu.SemaphoreType.DMA((4, 4)),
            factor_sems,
        ],
        compiler_params=params,
        cost_estimate=pl.CostEstimate(
            flops=2 * solve_flops, bytes_accessed=16 * order * order * 2, transcendentals=0
        ),
    )(info, *factors, packed[0], *pieces)

    up = [(2 * x, 2 * x + 1) for x in range(groups)]
    incoming = lax.ppermute(w_high, "sec", up)
    solved, back = pl.pallas_call(
        last_kernel,
        out_shape=[jax.ShapeDtypeStruct((2, 2, order, order), bf16), full_shape],
        in_specs=[in_smem] + [anywhere] * 13,
        out_specs=[anywhere, in_vmem],
        scratch_shapes=[
            factor_scratch,
            weight_scratch,
            field_scratch,
            arrived_scratch,
            field_scratch,
            below_scratch,
            pltpu.SemaphoreType.DMA((9,)),
            pltpu.SemaphoreType.DMA((4, 4)),
            factor_sems,
            pltpu.SemaphoreType.DMA((2,)),
        ],
        compiler_params=params,
        cost_estimate=pl.CostEstimate(
            flops=3 * solve_flops, bytes_accessed=16 * order * order * 2, transcendentals=0
        ),
    )(info, *factors, packed[0], *pieces, incoming)

    down = [(target, source) for source, target in up]
    incoming = lax.ppermute(back, "sec", down)
    results = pl.pallas_call(
        back_kernel,
        out_shape=[piece_shape] * len(rounds),
        in_specs=[in_smem] + [anywhere] * 11,
        out_specs=[anywhere] * len(rounds),
        scratch_shapes=[
            factor_scratch,
            weight_scratch,
            field_scratch,
            arrived_scratch,
            below_scratch,
            pltpu.SemaphoreType.DMA((9,)),
            pltpu.SemaphoreType.DMA((4, 4)),
            factor_sems,
            pltpu.SemaphoreType.DMA((len(rounds),)),
        ],
        compiler_params=params,
        cost_estimate=pl.CostEstimate(
            flops=2 * solve_flops, bytes_accessed=16 * order * order * 2, transcendentals=0
        ),
    )(info, *factors, w_low, w_high, incoming, solved)
    received = [
        lax.ppermute(piece, ("sec", "px"), back_pairs(a, b)) for piece, (a, b) in zip(results, rounds)
    ]
    output = pl.pallas_call(
        unpack_kernel,
        out_shape=jax.ShapeDtypeStruct(field.shape, bf16),
        in_specs=[in_smem] + [anywhere] * (len(rounds) + 1),
        out_specs=in_vmem,
        scratch_shapes=[pltpu.SemaphoreType.DMA((len(rounds),))],
        compiler_params=params,
    )(sends_to, results[0], *received)
    return output[:, None]


def chip_plan_fits(mesh):
    return mesh.shape["sec"] == 4 and mesh.shape["px"] == 2 and mesh.shape["py"] == 4


def solution(mesh):
    placed = (
        P(None, "sec", "px", "py"),
        P(),
        P("sec", "px", None),
        P("sec", None, ("px", "py"), None),
        P("sec", None, ("px", "py"), None),
    )
    return jax.shard_map(
        on_device if chip_plan_fits(mesh) else on_device_by_layer,
        mesh=mesh,
        in_specs=placed,
        out_specs=P(None, "sec", "px", "py"),
        check_vma=False,
    )
```

```python
import functools

import jax
import jax.numpy as jnp
from jax import lax
from jax.experimental import pallas as pl
from jax.experimental.pallas import tpu as pltpu
from jax.sharding import PartitionSpec as P

source_amplitude = 8.0
vmem_bytes = 32 * 1024 * 1024
bf16 = jnp.bfloat16
f32 = jnp.float32
anywhere = pl.BlockSpec(memory_space=pl.ANY)
in_smem = pl.BlockSpec(memory_space=pltpu.SMEM)
in_vmem = pl.BlockSpec(memory_space=pltpu.VMEM)

info_member, info_piece, info_slot, info_half, info_block, info_self = 3, 4, 12, 14, 16, 20


def shifted(x, axis, by):
    peers = lax.axis_size(axis)
    pairs = [(i, i + by) for i in range(peers) if 0 <= i + by < peers]
    return lax.ppermute(x, axis, pairs)


def complex_block(factor):
    upper = jnp.concatenate([factor[0], -factor[1]], axis=1)
    lower = jnp.concatenate([factor[1], factor[0]], axis=1)
    return jnp.concatenate([upper, lower], axis=0)


def y_transform(real_turned, imag_turned, field_in):
    real_part = jnp.dot(field_in[0], real_turned, preferred_element_type=jnp.float32) - jnp.dot(
        field_in[1], imag_turned, preferred_element_type=jnp.float32
    )
    imag_part = jnp.dot(field_in[0], imag_turned, preferred_element_type=jnp.float32) + jnp.dot(
        field_in[1], real_turned, preferred_element_type=jnp.float32
    )
    return jnp.stack([real_part, imag_part]).astype(jnp.bfloat16)


def x_transform(x_block, field_in):
    planes, rows_all, width = field_in.shape
    output = jnp.dot(
        x_block, field_in.reshape(planes * rows_all, width), preferred_element_type=jnp.float32
    )
    return output.astype(jnp.bfloat16).reshape(planes, rows_all, width)


def scale_rows(field_in, weights, width):
    planes, rows_here, merged = field_in.shape
    spread = field_in.astype(jnp.float32).reshape(planes, rows_here, merged // width, width)
    return (spread * weights.astype(jnp.float32)[None, :, None, :]).reshape(
        planes, rows_here, merged
    )


def pick_batch(field, batch_count, batch_index):
    planes, rows_here, merged = field.shape
    split_field = field.reshape(planes, rows_here, batch_count, merged // batch_count)
    return lax.dynamic_index_in_dim(split_field, batch_index, 2, keepdims=False)


def place_batch(field, piece, batch_count, batch_index):
    planes, rows_here, merged = field.shape
    split_field = field.reshape(planes, rows_here, batch_count, merged // batch_count)
    shaped = piece.reshape(planes, rows_here, 1, merged // batch_count)
    updated = lax.dynamic_update_slice_in_dim(split_field, shaped, batch_index, 2)
    return updated.reshape(planes, rows_here, merged)


def on_device_by_layer(background, src_pos, coupling, x_factor, y_factor):
    source_count = src_pos.shape[0]
    sec_count = lax.axis_size("sec")
    sec_index = lax.axis_index("sec")
    grid_y = lax.axis_size("py")
    own_x = lax.axis_index("px")
    own_y = lax.axis_index("py")
    local_sources = source_count // grid_y
    x_pieces, y_pieces = (
        lax.all_gather(x_factor[0], ("px", "py"), axis=1, tiled=True),
        lax.all_gather(y_factor[0], ("px", "py"), axis=1, tiled=True),
    )
    x_block = complex_block(x_pieces)
    real_turned = y_pieces[0].T
    imag_turned = y_pieces[1].T
    local_field = background[:, 0]
    local_weights = coupling[0]
    rows_here = local_field.shape[1]
    full_cols = y_factor.shape[3]
    plane_cells = x_factor.shape[3] * full_cols
    own_sources = lax.dynamic_slice_in_dim(src_pos, own_y * local_sources, local_sources)
    layer_of = own_sources // plane_cells
    remainder = own_sources % plane_cells
    row_of = remainder // full_cols
    column_of = remainder % full_cols
    row_start = own_x * rows_here
    row_hit = row_of[None, :] == row_start + jnp.arange(rows_here, dtype=jnp.int32)[:, None]
    col_hit = column_of[:, None] == jnp.arange(full_cols, dtype=jnp.int32)[None, :]
    layer_hit = layer_of == sec_index
    delta = (row_hit[:, :, None] & col_hit[None, :, :] & layer_hit[None, :, None]).astype(
        jnp.float32
    )
    delta = (delta * source_amplitude).reshape(rows_here, local_sources * full_cols)
    real_rhs = local_field[0].astype(jnp.float32) + delta
    rhs_field = jnp.stack([real_rhs, local_field[1].astype(jnp.float32)])

    def apply_front(field_in):
        turned = y_transform(real_turned, imag_turned, field_in)
        line_field = lax.all_to_all(turned, "px", split_axis=2, concat_axis=1, tiled=True)
        finished = x_transform(x_block, line_field)
        return lax.all_to_all(finished, "px", split_axis=1, concat_axis=2, tiled=True)

    forward_field = jnp.zeros(local_field.shape, jnp.bfloat16)
    outgoing = pick_batch(forward_field, sec_count, 0)
    for step in range(2 * sec_count - 1):
        incoming = shifted(outgoing, "sec", 1)
        batch_index = step - sec_index
        active = (batch_index >= 0) & (batch_index < sec_count)
        clamped = jnp.clip(batch_index, 0, sec_count - 1)
        rhs_batch = pick_batch(rhs_field, sec_count, clamped)
        reduced = (rhs_batch - scale_rows(incoming, local_weights, full_cols)).astype(jnp.bfloat16)
        candidate = apply_front(reduced)
        previous = pick_batch(forward_field, sec_count, clamped)
        kept = jnp.where(active, candidate, previous)
        forward_field = place_batch(forward_field, kept, sec_count, clamped)
        outgoing = candidate
    sweep_field = forward_field
    for step in range(2 * sec_count - 2):
        send_index = jnp.clip(step - (sec_count - 1 - sec_index), 0, sec_count - 1)
        own_batch = pick_batch(sweep_field, sec_count, send_index)
        sent_field = scale_rows(own_batch, local_weights, full_cols).astype(jnp.bfloat16)
        incoming = shifted(sent_field, "sec", -1)
        batch_index = step - (sec_count - 2 - sec_index)
        active = (batch_index >= 0) & (batch_index < sec_count) & (sec_index <= sec_count - 2)
        clamped = jnp.clip(batch_index, 0, sec_count - 1)
        solved = apply_front(incoming)
        forward_batch = pick_batch(forward_field, sec_count, clamped)
        candidate = (forward_batch.astype(jnp.float32) - solved.astype(jnp.float32)).astype(
            jnp.bfloat16
        )
        previous = pick_batch(sweep_field, sec_count, clamped)
        kept = jnp.where(active, candidate, previous)
        sweep_field = place_batch(sweep_field, kept, sec_count, clamped)
    return sweep_field[:, None]


def start_all(copies):
    for copy in copies:
        copy.start()


def wait_all(copies):
    for copy in copies:
        copy.wait()


def row_chunks(order, step):
    step = min(step, order)
    return [slice(first, first + step) for first in range(0, order, step)]


class Either:
    def __init__(self, flag, own, received, target, sem):
        self.flag = flag
        self.own = pltpu.make_async_copy(own, target, sem)
        self.received = pltpu.make_async_copy(received, target, sem)

    def start(self):
        @pl.when(self.flag != 0)
        def _():
            self.own.start()

        @pl.when(self.flag == 0)
        def _():
            self.received.start()

    def wait(self):
        self.received.wait()


def pack_kernel(place, field, coupling, x_factor, y_factor, *rest):
    pieces, (blocks, held, shard, sems, csems, osems, fsems) = rest[:-7], rest[-7:]
    rows_here = field.shape[1]
    height = x_factor.shape[1]
    own = pl.ds(pl.multiple_of(place[len(pieces)] * height, height), height)
    factors = [
        pltpu.make_async_copy(factor, shard.at[pl.ds(2 * which, 2)], fsems.at[which])
        for which, factor in enumerate((x_factor, y_factor))
    ]
    start_all(factors)
    incoming = []
    for index, piece in enumerate(pieces):
        width = piece.shape[1]
        offset = pl.multiple_of(place[index] * width, width)
        copies = [
            pltpu.make_async_copy(
                field.at[plane, :, pl.ds(offset, width)],
                held.at[index, pl.ds(plane * rows_here, rows_here)],
                sems.at[index, plane],
            )
            for plane in range(2)
        ]
        copies.append(
            pltpu.make_async_copy(
                coupling.at[own], held.at[index, pl.ds(2 * rows_here, height)], csems.at[index]
            )
        )
        start_all(copies)
        incoming.append(copies)
    outgoing = []
    wait_all(factors)
    for target in range(blocks.shape[0]):
        outgoing.append(pltpu.make_async_copy(shard, blocks.at[target], fsems.at[2 + target]))
        outgoing[-1].start()
    for index, piece in enumerate(pieces):
        wait_all(incoming[index])
        outgoing.append(pltpu.make_async_copy(held.at[index], piece, osems.at[index]))
        outgoing[-1].start()
    wait_all(outgoing)


def unpack_kernel(place, own, *rest):
    pieces, field, sems = rest[:-2], rest[-2], rest[-1]
    copies = []
    for index, piece in enumerate(pieces):
        width = piece.shape[2]
        offset = pl.multiple_of(place[index] * width, width)
        target = field.at[:, :, pl.ds(offset, width)]
        if index:
            copies.append(pltpu.make_async_copy(piece, target, sems.at[index]))
        else:
            copies.append(Either(place[len(pieces) + 1], own, piece, target, sems.at[index]))
    start_all(copies)
    wait_all(copies)


def column_kernel(info, blocks, own, p0, p1, p2, p3, x_column, y_column, rows_held, sems, csems):
    count, planes, height, order = blocks.shape
    copies = []
    for index in range(count):
        for which, column in enumerate((x_column, y_column)):
            copies.append(
                pltpu.make_async_copy(
                    blocks.at[index, pl.ds(2 * which, 2)],
                    column.at[:, pl.ds(index * height, height), :],
                    sems.at[index, which],
                )
            )
    last = pl.ds(own.shape[0] - height, height)
    copies.append(Either(info[info_self], own.at[last], p0.at[last], rows_held.at[0], csems.at[0]))
    for index, piece in enumerate((p1, p2, p3)):
        copies.append(
            pltpu.make_async_copy(piece.at[last], rows_held.at[index + 1], csems.at[index + 1])
        )
    start_all(copies)
    wait_all(copies)


def both_kernel(info, x_column, x_aside, y_column, y0, y1, rows_next, x_both, y_both, sems):
    copies = [
        pltpu.make_async_copy(x_column, x_both.at[0], sems.at[0]),
        pltpu.make_async_copy(x_aside, x_both.at[1], sems.at[1]),
        Either(info[info_self], y_column, y0, y_both.at[0], sems.at[2]),
        pltpu.make_async_copy(y1, y_both.at[1], sems.at[3]),
    ]
    start_all(copies)
    wait_all(copies)


class Layers:
    def __init__(self, info, x_parts, y_parts, row_blocks, held, weights, sems, csems):
        self.info, self.order = info, held.shape[2]
        self.x_parts, self.y_parts, self.row_blocks = x_parts, y_parts, row_blocks
        self.held, self.weights, self.sems, self.csems = held, weights, sems, csems

    def half_rows(self, far):
        height = self.order // 2
        return pl.ds(pl.multiple_of(self.info[info_half + far] * height, height), height)

    def factor_copies(self, slot, which, parts):
        return [
            pltpu.make_async_copy(
                part.at[plane],
                self.held.at[
                    slot, which, self.half_rows(far), pl.ds(plane * self.order, self.order)
                ],
                self.sems.at[slot, which, far, plane],
            )
            for far, part in enumerate(parts)
            for plane in range(2)
        ]

    def y_copies(self, slot):
        turn = self.info[info_slot + slot]
        return self.factor_copies(slot, 1, [part.at[turn] for part in self.y_parts])

    def start_y(self, slot):
        start_all(self.y_copies(slot))

    def start_x(self, slot):
        own, first, second = self.x_parts
        turn, same = self.info[info_slot + slot], self.info[info_self]
        for hit, part in (
            ((turn == 0) & (same != 0), own),
            ((turn == 0) & (same == 0), first),
            (turn == 1, second),
        ):

            @pl.when(hit)
            def _():
                start_all(self.factor_copies(slot, 0, [part.at[0], part.at[1]]))

    def ready(self, slot, which):
        part = self.x_parts[0].at[0]
        wait_all(self.factor_copies(slot, which, [part, part]))

    def weight_copies(self, slot):
        height = self.row_blocks[0].shape[1]
        copies = []
        for index, block in enumerate(self.row_blocks):
            for far in range(2):
                turn = 2 * self.info[info_slot + slot] + far
                start = self.info[info_half + far] * (self.order // 2)
                start = start + self.info[info_block + index] * height
                rows = pl.ds(pl.multiple_of(start, height), height)
                copies.append(
                    pltpu.make_async_copy(
                        block.at[turn], self.weights.at[slot, rows, :], self.csems.at[slot, index, far]
                    )
                )
        return copies

    def rhs_copies(self, slot, pair, rhs, sems):
        height = self.order // 2
        return [
            pltpu.make_async_copy(
                piece.at[pl.ds(plane * height, height)],
                rhs.at[slot, plane, self.half_rows(far), :],
                sems.at[slot, far, plane],
            )
            for far, piece in enumerate(pair)
            for plane in range(2)
        ]

    def start_rhs(self, slot, own, pieces, rhs, sems):
        turn, same = self.info[info_slot + slot], self.info[info_self]
        for hit, pair in (
            ((turn == 0) & (same != 0), (own, pieces[1])),
            ((turn == 0) & (same == 0), pieces[:2]),
            (turn == 1, pieces[2:]),
        ):

            @pl.when(hit)
            def _():
                start_all(self.rhs_copies(slot, pair, rhs, sems))

    def start(self, slot, own, pieces, rhs, sems):
        self.start_y(slot)
        self.start_rhs(slot, own, pieces, rhs, sems)
        start_all(self.weight_copies(slot))
        self.start_x(slot)

    def wait(self, slot, own, pieces, rhs, sems):
        wait_all(self.rhs_copies(slot, pieces[:2], rhs, sems))
        wait_all(self.weight_copies(slot))

    def apply(self, slot, source, below, store, fresh):
        order = self.order
        turned = (((1,), (1,)), ((), ()))
        if fresh:
            self.ready(slot, 1)
        for rows in row_chunks(order, 256):
            real, imag = source(0, rows), source(1, rows)
            upper = jnp.concatenate([real, -imag], axis=1)
            lower = jnp.concatenate([imag, real], axis=1)
            part = lax.dot_general(
                jnp.concatenate([upper, lower], axis=0),
                self.held[slot, 1],
                turned,
                preferred_element_type=f32,
            ).astype(bf16)
            height = rows.stop - rows.start
            real, imag = part[:height], part[height:]
            further = slice(rows.start + order, rows.stop + order)
            below[rows, :order] = real
            below[rows, order:] = imag
            below[further, :order] = -imag
            below[further, order:] = real
        if fresh:
            self.ready(slot, 0)
        for plane in range(2):
            for columns in row_chunks(order, 256):
                along = slice(columns.start + plane * order, columns.stop + plane * order)
                store(
                    plane,
                    columns,
                    jnp.dot(self.held[slot, 0], below[:, along], preferred_element_type=f32),
                )


def reduced(rhs, info, slot, weights, incoming):
    def source(plane, rows):
        values = rhs[slot, plane, rows].astype(f32)
        if plane == 0:
            row = lax.broadcasted_iota(jnp.int32, values.shape, 0) + rows.start
            column = lax.broadcasted_iota(jnp.int32, (1, values.shape[1]), 1)
            hit = (column == info[2]) & (info[0] == slot)
            cell = jnp.where(hit, f32(source_amplitude), f32(0.0))
            values = values + jnp.where(row == info[1], cell, f32(0.0))
        scaled = weights[slot, rows].astype(f32) * incoming(plane, rows)
        return (values - scaled).astype(bf16)

    return source


def sent(weights, slot, field):
    def source(plane, rows):
        scaled = weights[slot, rows].astype(f32) * field[plane, rows].astype(f32)
        return scaled.astype(bf16)

    return source


def subtract_into(target, forward):
    def store(plane, columns, values):
        solved = values.astype(bf16).astype(f32)
        target[plane, :, columns] = (forward[plane, :, columns].astype(f32) - solved).astype(bf16)

    return store


def round_into(target):
    def store(plane, columns, values):
        target[plane, :, columns] = values.astype(bf16)

    return store


def first_kernel(info, xb, x0, x1, yb, yf, c0, c1, c2, c3, own, p0, p1, p2, p3, w_low, w_high,
                 held, weights, rhs, below, sems, csems, fsems):
    @pl.when(info[info_member] == 0)
    def _():
        layers = Layers(info, (xb, x0, x1), (yb, yf), (c0, c1, c2, c3), held, weights, fsems, csems)
        fields = (own, (p0, p1, p2, p3), rhs, sems)
        layers.start(0, *fields)
        layers.start(1, *fields)
        layers.wait(0, *fields)
        zero = reduced(rhs, info, 0, weights, lambda plane, rows: f32(0.0))
        layers.apply(0, zero, below, round_into(w_low), True)
        layers.wait(1, *fields)
        one = reduced(rhs, info, 1, weights, lambda plane, rows: w_low[plane, rows].astype(f32))
        layers.apply(1, one, below, round_into(w_high), True)


def last_kernel(info, xb, x0, x1, yb, yf, c0, c1, c2, c3, own, p0, p1, p2, p3, arrived, field, back,
                held, weights, rhs, forward, below, sems, csems, fsems):
    @pl.when(info[info_member] == 1)
    def _():
        layers = Layers(info, (xb, x0, x1), (yb, yf), (c0, c1, c2, c3), held, weights, fsems, csems)
        fields = (own, (p0, p1, p2, p3), rhs, sems)
        layers.start(0, *fields)
        layers.start(1, *fields)
        layers.wait(0, *fields)
        low, high = field.at[0], field.at[1]
        two = reduced(rhs, info, 0, weights, lambda plane, rows: arrived[plane, rows].astype(f32))
        layers.apply(0, two, below, round_into(forward), True)
        layers.wait(1, *fields)
        three = reduced(rhs, info, 1, weights, lambda plane, rows: forward[plane, rows].astype(f32))
        layers.apply(1, three, below, round_into(high), True)
        layers.apply(0, sent(weights, 1, high), below, subtract_into(low, forward), False)
        last = sent(weights, 0, low)
        for plane in range(2):
            for rows in row_chunks(weights.shape[1], 256):
                back[plane, rows] = last(plane, rows)


def back_kernel(info, xb, x0, x1, yb, yf, c0, c1, c2, c3, w_low, w_high, arrived, field,
                p0, p1, p2, p3, held, weights, kept, below, csems, fsems, osems):
    def start_pieces(source, slot):
        for index, piece in enumerate((p0, p1, p2, p3)):
            height = piece.shape[1]
            half = info[info_piece + 2 * index + 1]
            rows = pl.ds(pl.multiple_of(half * height, height), height)

            @pl.when(info[info_piece + 2 * index] == slot)
            def _():
                pltpu.make_async_copy(source.at[slot, :, rows, :], piece, osems.at[index]).start()

    @pl.when(info[info_member] == 0)
    def _():
        layers = Layers(info, (xb, x0, x1), (yb, yf), (c0, c1, c2, c3), held, weights, fsems, csems)
        layers.start_y(1)
        layers.start_x(1)
        high_rows = layers.weight_copies(1)
        start_all(high_rows)
        layers.start_y(0)
        layers.start_x(0)
        low, high = kept.at[0], kept.at[1]
        layers.apply(
            1, lambda plane, rows: arrived[plane, rows], below, subtract_into(high, w_high), True
        )
        start_pieces(kept, 1)
        wait_all(high_rows)
        layers.apply(0, sent(weights, 1, high), below, subtract_into(low, w_low), True)
        start_pieces(kept, 0)

    @pl.when(info[info_member] != 0)
    def _():
        start_pieces(field, 1)
        start_pieces(field, 0)

    for index, piece in enumerate((p0, p1, p2, p3)):
        part = kept.at[0, :, pl.ds(0, piece.shape[1]), :]
        pltpu.make_async_copy(part, piece, osems.at[index]).wait()


def on_device(background, src_pos, coupling, x_factor, y_factor):
    px_count = lax.axis_size("px")
    sec_index, own_x, own_y = (lax.axis_index(axis) for axis in ("sec", "px", "py"))
    group, member = sec_index // 2, sec_index % 2
    groups = lax.axis_size("sec") // 2
    order = y_factor.shape[3]
    field = background[:, 0]
    rows_here = field.shape[1]
    height = x_factor.shape[2]
    params = pltpu.CompilerParams(vmem_limit_bytes=vmem_bytes)
    rounds = [(a, b) for a in range(groups) for b in range(px_count)]

    def pairs(a, b):
        return [
            ((2 * x + c) * px_count + y, (2 * ((c + a) % 2) + x) * px_count + (y + b) % px_count)
            for x in range(groups)
            for c in range(2)
            for y in range(px_count)
            if (a, b, x) != (0, 0, c)
        ]

    def back_pairs(a, b):
        return [(target, source) for source, target in pairs(a, b)]

    own_source = src_pos[own_y * groups * px_count + group * px_count + own_x]
    plane_cells = x_factor.shape[3] * order
    layer = own_source // plane_cells
    remainder = own_source % plane_cells
    py_count = lax.axis_size("py")
    entries = [
        jnp.where(layer // 2 == member, layer % 2, -1),
        remainder // order,
        remainder % order,
        member,
    ]
    for a, b in rounds:
        entries += [(group + a) % 2, (own_x - b) % px_count]
    entries += [group, (group + 1) % 2, own_x, (own_x + 1) % 2]
    pair = own_y // 2 * 2
    entries += [own_y, pair + (own_y + 1) % 2, (own_y + 2) % 4, (pair + 2) % 4 + (own_y + 1) % 2]
    entries += [group == member]
    info = jnp.stack([jnp.asarray(entry, jnp.int32) for entry in entries])

    sends_to = jnp.stack(
        [((member + a) % 2) * px_count + (own_x + b) % px_count for a, b in rounds]
        + [own_y, group == member]
    ).astype(jnp.int32)
    piece_shape = jax.ShapeDtypeStruct((2, rows_here, order), bf16)
    *packed, blocks = pl.pallas_call(
        pack_kernel,
        out_shape=[jax.ShapeDtypeStruct((2 * rows_here + height, order), bf16)] * len(rounds)
        + [jax.ShapeDtypeStruct((py_count, 4, height, order), bf16)],
        in_specs=[in_smem] + [anywhere] * 4,
        out_specs=[anywhere] * (len(rounds) + 1),
        scratch_shapes=[
            pltpu.VMEM((len(rounds), 2 * rows_here + height, order), bf16),
            pltpu.VMEM((4, height, order), bf16),
            pltpu.SemaphoreType.DMA((len(rounds), 2)),
            pltpu.SemaphoreType.DMA((len(rounds),)),
            pltpu.SemaphoreType.DMA((len(rounds),)),
            pltpu.SemaphoreType.DMA((2 + py_count,)),
        ],
        compiler_params=pltpu.CompilerParams(vmem_limit_bytes=60 * 1024 * 1024),
    )(sends_to, field, coupling[0], x_factor[0], y_factor[0])
    pieces = [
        lax.ppermute(piece, ("sec", "px"), pairs(a, b)) for piece, (a, b) in zip(packed, rounds)
    ]
    blocks = lax.all_to_all(blocks, "py", split_axis=0, concat_axis=0, tiled=True)

    column_shape = jax.ShapeDtypeStruct((2, rows_here, order), bf16)
    rows_shape = jax.ShapeDtypeStruct((len(rounds), height, order), bf16)
    x_column, y_column, rows_held = pl.pallas_call(
        column_kernel,
        out_shape=[column_shape, column_shape, rows_shape],
        in_specs=[in_smem] + [anywhere] * 6,
        out_specs=[in_vmem] * 3,
        scratch_shapes=[
            pltpu.SemaphoreType.DMA((py_count, 2)),
            pltpu.SemaphoreType.DMA((len(rounds),)),
        ],
        compiler_params=params,
    )(info, blocks, packed[0], *pieces)

    def across(block, a):
        return lax.ppermute(block, ("sec", "px"), pairs(a, 0))

    def aside(block):
        return lax.ppermute(block, "px", [(y, (y + 1) % 2) for y in range(2)])

    def over_z(block, bit):
        return lax.ppermute(block, "py", [(z, z ^ bit) for z in range(py_count)])

    y_near = [across(y_column, a) for a in range(2)]
    x_aside = aside(x_column)
    rows_next = over_z(rows_held, 1)
    rows_far = over_z(rows_held, 2)
    x_both, y_both = pl.pallas_call(
        both_kernel,
        out_shape=[jax.ShapeDtypeStruct((2,) + column_shape.shape, bf16)] * 2,
        in_specs=[in_smem] + [anywhere] * 6,
        out_specs=[in_vmem] * 2,
        scratch_shapes=[pltpu.SemaphoreType.DMA((4,))],
        compiler_params=params,
    )(info, x_column, x_aside, y_column, *y_near, rows_next)
    y_far = aside(y_both)
    x_across = [across(x_both, a) for a in range(2)]
    factors = [x_both, *x_across, y_both, y_far, rows_held, rows_next, rows_far, over_z(rows_next, 2)]

    full_shape = jax.ShapeDtypeStruct((2, order, order), bf16)
    factor_scratch = pltpu.VMEM((2, 2, order, 2 * order), bf16)
    weight_scratch = pltpu.VMEM((2, order, order), bf16)
    field_scratch = pltpu.VMEM((2, 2, order, order), bf16)
    below_scratch = pltpu.VMEM((2 * order, 2 * order), bf16)
    factor_sems = pltpu.SemaphoreType.DMA((2, 2, 2, 2))
    weight_sems = pltpu.SemaphoreType.DMA((2, py_count, 2))
    field_sems = pltpu.SemaphoreType.DMA((2, 2, 2))
    solve_flops = 16 * order**3
    fields = (packed[0], *pieces)

    def cost(solves):
        return pl.CostEstimate(
            flops=solves * solve_flops, bytes_accessed=16 * order * order * 2, transcendentals=0
        )

    w_low, w_high = pl.pallas_call(
        first_kernel,
        out_shape=[full_shape] * 2,
        in_specs=[in_smem] + [anywhere] * 14,
        out_specs=[in_vmem] * 2,
        scratch_shapes=[
            factor_scratch,
            weight_scratch,
            field_scratch,
            below_scratch,
            field_sems,
            weight_sems,
            factor_sems,
        ],
        compiler_params=params,
        cost_estimate=cost(2),
    )(info, *factors, *fields)

    up = [(2 * x, 2 * x + 1) for x in range(groups)]
    incoming = lax.ppermute(w_high, "sec", up)
    solved, back = pl.pallas_call(
        last_kernel,
        out_shape=[jax.ShapeDtypeStruct((2, 2, order, order), bf16), full_shape],
        in_specs=[in_smem] + [anywhere] * 14 + [in_vmem],
        out_specs=[in_vmem] * 2,
        scratch_shapes=[
            factor_scratch,
            weight_scratch,
            field_scratch,
            pltpu.VMEM((2, order, order), bf16),
            below_scratch,
            field_sems,
            weight_sems,
            factor_sems,
        ],
        compiler_params=params,
        cost_estimate=cost(3),
    )(info, *factors, *fields, incoming)

    down = [(target, source) for source, target in up]
    incoming = lax.ppermute(back, "sec", down)
    results = pl.pallas_call(
        back_kernel,
        out_shape=[piece_shape] * len(rounds),
        in_specs=[in_smem] + [anywhere] * 9 + [in_vmem] * 3 + [anywhere],
        out_specs=[anywhere] * len(rounds),
        scratch_shapes=[
            factor_scratch,
            weight_scratch,
            field_scratch,
            below_scratch,
            weight_sems,
            factor_sems,
            pltpu.SemaphoreType.DMA((len(rounds),)),
        ],
        compiler_params=params,
        cost_estimate=cost(2),
    )(info, *factors, w_low, w_high, incoming, solved)
    received = [
        lax.ppermute(piece, ("sec", "px"), back_pairs(a, b)) for piece, (a, b) in zip(results, rounds)
    ]
    output = pl.pallas_call(
        unpack_kernel,
        out_shape=jax.ShapeDtypeStruct(field.shape, bf16),
        in_specs=[in_smem] + [anywhere] * (len(rounds) + 1),
        out_specs=in_vmem,
        scratch_shapes=[pltpu.SemaphoreType.DMA((len(rounds),))],
        compiler_params=params,
    )(sends_to, results[0], *received)
    return output[:, None]


def chip_plan_fits(mesh):
    return mesh.shape["sec"] == 4 and mesh.shape["px"] == 2 and mesh.shape["py"] == 4


def solution(mesh):
    placed = (
        P(None, "sec", "px", "py"),
        P(),
        P("sec", "px", None),
        P("sec", None, ("px", "py"), None),
        P("sec", None, ("px", "py"), None),
    )
    return jax.shard_map(
        on_device if chip_plan_fits(mesh) else on_device_by_layer,
        mesh=mesh,
        in_specs=placed,
        out_specs=P(None, "sec", "px", "py"),
        check_vma=False,
    )
```

```python
import functools

import jax
import jax.numpy as jnp
from jax import lax
from jax.experimental import pallas as pl
from jax.experimental.pallas import tpu as pltpu
from jax.sharding import PartitionSpec as P

source_amplitude = 8.0
vmem_bytes = 32 * 1024 * 1024
bf16 = jnp.bfloat16
f32 = jnp.float32
anywhere = pl.BlockSpec(memory_space=pl.ANY)
in_smem = pl.BlockSpec(memory_space=pltpu.SMEM)
in_vmem = pl.BlockSpec(memory_space=pltpu.VMEM)

info_member, info_piece, info_slot, info_half, info_block, info_self = 3, 4, 12, 14, 16, 20


def shifted(x, axis, by):
    peers = lax.axis_size(axis)
    pairs = [(i, i + by) for i in range(peers) if 0 <= i + by < peers]
    return lax.ppermute(x, axis, pairs)


def complex_block(factor):
    upper = jnp.concatenate([factor[0], -factor[1]], axis=1)
    lower = jnp.concatenate([factor[1], factor[0]], axis=1)
    return jnp.concatenate([upper, lower], axis=0)


def y_transform(real_turned, imag_turned, field_in):
    real_part = jnp.dot(field_in[0], real_turned, preferred_element_type=jnp.float32) - jnp.dot(
        field_in[1], imag_turned, preferred_element_type=jnp.float32
    )
    imag_part = jnp.dot(field_in[0], imag_turned, preferred_element_type=jnp.float32) + jnp.dot(
        field_in[1], real_turned, preferred_element_type=jnp.float32
    )
    return jnp.stack([real_part, imag_part]).astype(jnp.bfloat16)


def x_transform(x_block, field_in):
    planes, rows_all, width = field_in.shape
    output = jnp.dot(
        x_block, field_in.reshape(planes * rows_all, width), preferred_element_type=jnp.float32
    )
    return output.astype(jnp.bfloat16).reshape(planes, rows_all, width)


def scale_rows(field_in, weights, width):
    planes, rows_here, merged = field_in.shape
    spread = field_in.astype(jnp.float32).reshape(planes, rows_here, merged // width, width)
    return (spread * weights.astype(jnp.float32)[None, :, None, :]).reshape(
        planes, rows_here, merged
    )


def pick_batch(field, batch_count, batch_index):
    planes, rows_here, merged = field.shape
    split_field = field.reshape(planes, rows_here, batch_count, merged // batch_count)
    return lax.dynamic_index_in_dim(split_field, batch_index, 2, keepdims=False)


def place_batch(field, piece, batch_count, batch_index):
    planes, rows_here, merged = field.shape
    split_field = field.reshape(planes, rows_here, batch_count, merged // batch_count)
    shaped = piece.reshape(planes, rows_here, 1, merged // batch_count)
    updated = lax.dynamic_update_slice_in_dim(split_field, shaped, batch_index, 2)
    return updated.reshape(planes, rows_here, merged)


def on_device_by_layer(background, src_pos, coupling, x_factor, y_factor):
    source_count = src_pos.shape[0]
    sec_count = lax.axis_size("sec")
    sec_index = lax.axis_index("sec")
    grid_y = lax.axis_size("py")
    own_x = lax.axis_index("px")
    own_y = lax.axis_index("py")
    local_sources = source_count // grid_y
    x_pieces, y_pieces = (
        lax.all_gather(x_factor[0], ("px", "py"), axis=1, tiled=True),
        lax.all_gather(y_factor[0], ("px", "py"), axis=1, tiled=True),
    )
    x_block = complex_block(x_pieces)
    real_turned = y_pieces[0].T
    imag_turned = y_pieces[1].T
    local_field = background[:, 0]
    local_weights = coupling[0]
    rows_here = local_field.shape[1]
    full_cols = y_factor.shape[3]
    plane_cells = x_factor.shape[3] * full_cols
    own_sources = lax.dynamic_slice_in_dim(src_pos, own_y * local_sources, local_sources)
    layer_of = own_sources // plane_cells
    remainder = own_sources % plane_cells
    row_of = remainder // full_cols
    column_of = remainder % full_cols
    row_start = own_x * rows_here
    row_hit = row_of[None, :] == row_start + jnp.arange(rows_here, dtype=jnp.int32)[:, None]
    col_hit = column_of[:, None] == jnp.arange(full_cols, dtype=jnp.int32)[None, :]
    layer_hit = layer_of == sec_index
    delta = (row_hit[:, :, None] & col_hit[None, :, :] & layer_hit[None, :, None]).astype(
        jnp.float32
    )
    delta = (delta * source_amplitude).reshape(rows_here, local_sources * full_cols)
    real_rhs = local_field[0].astype(jnp.float32) + delta
    rhs_field = jnp.stack([real_rhs, local_field[1].astype(jnp.float32)])

    def apply_front(field_in):
        turned = y_transform(real_turned, imag_turned, field_in)
        line_field = lax.all_to_all(turned, "px", split_axis=2, concat_axis=1, tiled=True)
        finished = x_transform(x_block, line_field)
        return lax.all_to_all(finished, "px", split_axis=1, concat_axis=2, tiled=True)

    forward_field = jnp.zeros(local_field.shape, jnp.bfloat16)
    outgoing = pick_batch(forward_field, sec_count, 0)
    for step in range(2 * sec_count - 1):
        incoming = shifted(outgoing, "sec", 1)
        batch_index = step - sec_index
        active = (batch_index >= 0) & (batch_index < sec_count)
        clamped = jnp.clip(batch_index, 0, sec_count - 1)
        rhs_batch = pick_batch(rhs_field, sec_count, clamped)
        reduced = (rhs_batch - scale_rows(incoming, local_weights, full_cols)).astype(jnp.bfloat16)
        candidate = apply_front(reduced)
        previous = pick_batch(forward_field, sec_count, clamped)
        kept = jnp.where(active, candidate, previous)
        forward_field = place_batch(forward_field, kept, sec_count, clamped)
        outgoing = candidate
    sweep_field = forward_field
    for step in range(2 * sec_count - 2):
        send_index = jnp.clip(step - (sec_count - 1 - sec_index), 0, sec_count - 1)
        own_batch = pick_batch(sweep_field, sec_count, send_index)
        sent_field = scale_rows(own_batch, local_weights, full_cols).astype(jnp.bfloat16)
        incoming = shifted(sent_field, "sec", -1)
        batch_index = step - (sec_count - 2 - sec_index)
        active = (batch_index >= 0) & (batch_index < sec_count) & (sec_index <= sec_count - 2)
        clamped = jnp.clip(batch_index, 0, sec_count - 1)
        solved = apply_front(incoming)
        forward_batch = pick_batch(forward_field, sec_count, clamped)
        candidate = (forward_batch.astype(jnp.float32) - solved.astype(jnp.float32)).astype(
            jnp.bfloat16
        )
        previous = pick_batch(sweep_field, sec_count, clamped)
        kept = jnp.where(active, candidate, previous)
        sweep_field = place_batch(sweep_field, kept, sec_count, clamped)
    return sweep_field[:, None]


def start_all(copies):
    for copy in copies:
        copy.start()


def wait_all(copies):
    for copy in copies:
        copy.wait()


def row_chunks(order, step):
    step = min(step, order)
    return [slice(first, first + step) for first in range(0, order, step)]


class Either:
    def __init__(self, flag, own, received, target, sem):
        self.flag = flag
        self.own = pltpu.make_async_copy(own, target, sem)
        self.received = pltpu.make_async_copy(received, target, sem)

    def start(self):
        @pl.when(self.flag != 0)
        def _():
            self.own.start()

        @pl.when(self.flag == 0)
        def _():
            self.received.start()

    def wait(self):
        self.received.wait()


def pack_kernel(place, field, coupling, *rest):
    pieces, (sems, csems) = rest[:-2], rest[-2:]
    rows_here = field.shape[1]
    height = pieces[0].shape[0] - 2 * rows_here
    own = pl.ds(pl.multiple_of(place[len(pieces)] * height, height), height)
    copies = []
    for index, piece in enumerate(pieces):
        width = piece.shape[1]
        offset = pl.multiple_of(place[index] * width, width)
        for plane in range(2):
            copies.append(
                pltpu.make_async_copy(
                    field.at[plane, :, pl.ds(offset, width)],
                    piece.at[pl.ds(plane * rows_here, rows_here)],
                    sems.at[index, plane],
                )
            )
        copies.append(
            pltpu.make_async_copy(
                coupling.at[own], piece.at[pl.ds(2 * rows_here, height)], csems.at[index]
            )
        )
    start_all(copies)
    wait_all(copies)


def unpack_kernel(place, own, *rest):
    pieces, field, sems = rest[:-2], rest[-2], rest[-1]
    copies = []
    for index, piece in enumerate(pieces):
        width = piece.shape[2]
        offset = pl.multiple_of(place[index] * width, width)
        target = field.at[:, :, pl.ds(offset, width)]
        if index:
            copies.append(pltpu.make_async_copy(piece, target, sems.at[index]))
        else:
            copies.append(Either(place[len(pieces) + 1], own, piece, target, sems.at[index]))
    start_all(copies)
    wait_all(copies)


def column_kernel(info, blocks, own, p0, p1, p2, p3, x_column, y_column, rows_held, sems, csems):
    count, planes, height, order = blocks.shape
    copies = []
    for index in range(count):
        for which, column in enumerate((x_column, y_column)):
            copies.append(
                pltpu.make_async_copy(
                    blocks.at[index, pl.ds(2 * which, 2)],
                    column.at[:, pl.ds(index * height, height), :],
                    sems.at[index, which],
                )
            )
    last = pl.ds(own.shape[0] - height, height)
    copies.append(Either(info[info_self], own.at[last], p0.at[last], rows_held.at[0], csems.at[0]))
    for index, piece in enumerate((p1, p2, p3)):
        copies.append(
            pltpu.make_async_copy(piece.at[last], rows_held.at[index + 1], csems.at[index + 1])
        )
    start_all(copies)
    wait_all(copies)


def both_kernel(info, x_column, x_aside, y_column, y0, y1, rows_next, rows_far, x_both, y_both, sems):
    copies = [
        pltpu.make_async_copy(x_column, x_both.at[0], sems.at[0]),
        pltpu.make_async_copy(x_aside, x_both.at[1], sems.at[1]),
        Either(info[info_self], y_column, y0, y_both.at[0], sems.at[2]),
        pltpu.make_async_copy(y1, y_both.at[1], sems.at[3]),
    ]
    start_all(copies)
    wait_all(copies)


class Layers:
    def __init__(self, info, x_parts, y_parts, row_blocks, held, weights, sems, csems):
        self.info, self.order = info, held.shape[2]
        self.x_parts, self.y_parts, self.row_blocks = x_parts, y_parts, row_blocks
        self.held, self.weights, self.sems, self.csems = held, weights, sems, csems

    def half_rows(self, far):
        height = self.order // 2
        return pl.ds(pl.multiple_of(self.info[info_half + far] * height, height), height)

    def factor_copies(self, slot, which, parts):
        return [
            pltpu.make_async_copy(
                part.at[plane],
                self.held.at[
                    slot, which, self.half_rows(far), pl.ds(plane * self.order, self.order)
                ],
                self.sems.at[slot, which, far, plane],
            )
            for far, part in enumerate(parts)
            for plane in range(2)
        ]

    def y_copies(self, slot):
        turn = self.info[info_slot + slot]
        return self.factor_copies(slot, 1, [part.at[turn] for part in self.y_parts])

    def start_y(self, slot):
        start_all(self.y_copies(slot))

    def start_x(self, slot):
        own, first, second = self.x_parts
        turn, same = self.info[info_slot + slot], self.info[info_self]
        for hit, part in (
            ((turn == 0) & (same != 0), own),
            ((turn == 0) & (same == 0), first),
            (turn == 1, second),
        ):

            @pl.when(hit)
            def _():
                start_all(self.factor_copies(slot, 0, [part.at[0], part.at[1]]))

    def ready(self, slot, which):
        part = self.x_parts[0].at[0]
        wait_all(self.factor_copies(slot, which, [part, part]))

    def weight_copies(self, slot):
        height = self.row_blocks[0].shape[1]
        copies = []
        for index, block in enumerate(self.row_blocks):
            for far in range(2):
                turn = 2 * self.info[info_slot + slot] + far
                start = self.info[info_half + far] * (self.order // 2)
                start = start + self.info[info_block + index] * height
                rows = pl.ds(pl.multiple_of(start, height), height)
                copies.append(
                    pltpu.make_async_copy(
                        block.at[turn], self.weights.at[slot, rows, :], self.csems.at[slot, index, far]
                    )
                )
        return copies

    def rhs_copies(self, slot, pair, rhs, sems):
        height = self.order // 2
        return [
            pltpu.make_async_copy(
                piece.at[pl.ds(plane * height, height)],
                rhs.at[slot, plane, self.half_rows(far), :],
                sems.at[slot, far, plane],
            )
            for far, piece in enumerate(pair)
            for plane in range(2)
        ]

    def start_rhs(self, slot, own, pieces, rhs, sems):
        turn, same = self.info[info_slot + slot], self.info[info_self]
        for hit, pair in (
            ((turn == 0) & (same != 0), (own, pieces[1])),
            ((turn == 0) & (same == 0), pieces[:2]),
            (turn == 1, pieces[2:]),
        ):

            @pl.when(hit)
            def _():
                start_all(self.rhs_copies(slot, pair, rhs, sems))

    def start(self, slot, own, pieces, rhs, sems):
        self.start_y(slot)
        self.start_rhs(slot, own, pieces, rhs, sems)
        start_all(self.weight_copies(slot))
        self.start_x(slot)

    def wait(self, slot, own, pieces, rhs, sems):
        wait_all(self.rhs_copies(slot, pieces[:2], rhs, sems))
        wait_all(self.weight_copies(slot))

    def apply(self, slot, source, below, store, fresh):
        order = self.order
        turned = (((1,), (1,)), ((), ()))
        if 1 in fresh:
            self.ready(slot, 1)
        for rows in row_chunks(order, 256):
            real, imag = source(0, rows), source(1, rows)
            upper = jnp.concatenate([real, -imag], axis=1)
            lower = jnp.concatenate([imag, real], axis=1)
            part = lax.dot_general(
                jnp.concatenate([upper, lower], axis=0),
                self.held[slot, 1],
                turned,
                preferred_element_type=f32,
            ).astype(bf16)
            height = rows.stop - rows.start
            real, imag = part[:height], part[height:]
            further = slice(rows.start + order, rows.stop + order)
            below[rows, :order] = real
            below[rows, order:] = imag
            below[further, :order] = -imag
            below[further, order:] = real
        if 0 in fresh:
            self.ready(slot, 0)
        for plane in range(2):
            for columns in row_chunks(order, 256):
                along = slice(columns.start + plane * order, columns.stop + plane * order)
                store(
                    plane,
                    columns,
                    jnp.dot(self.held[slot, 0], below[:, along], preferred_element_type=f32),
                )


def reduced(rhs, info, slot, weights, incoming):
    def source(plane, rows):
        values = rhs[slot, plane, rows].astype(f32)
        if plane == 0:
            row = lax.broadcasted_iota(jnp.int32, values.shape, 0) + rows.start
            column = lax.broadcasted_iota(jnp.int32, (1, values.shape[1]), 1)
            hit = (column == info[2]) & (info[0] == slot)
            cell = jnp.where(hit, f32(source_amplitude), f32(0.0))
            values = values + jnp.where(row == info[1], cell, f32(0.0))
        scaled = weights[slot, rows].astype(f32) * incoming(plane, rows)
        return (values - scaled).astype(bf16)

    return source


def sent(weights, slot, field):
    def source(plane, rows):
        scaled = weights[slot, rows].astype(f32) * field[plane, rows].astype(f32)
        return scaled.astype(bf16)

    return source


def subtract_into(target, forward):
    def store(plane, columns, values):
        solved = values.astype(bf16).astype(f32)
        target[plane, :, columns] = (forward[plane, :, columns].astype(f32) - solved).astype(bf16)

    return store


def round_into(target):
    def store(plane, columns, values):
        target[plane, :, columns] = values.astype(bf16)

    return store


def first_kernel(info, xb, x0, x1, yb, yf, c0, c1, c2, c3, own, p0, p1, p2, p3, w_low, w_high,
                 held, weights, rhs, below, sems, csems, fsems):
    @pl.when(info[info_member] == 0)
    def _():
        layers = Layers(info, (xb, x0, x1), (yb, yf), (c0, c1, c2, c3), held, weights, fsems, csems)
        fields = (own, (p0, p1, p2, p3), rhs, sems)
        layers.start(0, *fields)
        layers.wait(0, *fields)
        layers.ready(0, 1)
        layers.start(1, *fields)
        zero = reduced(rhs, info, 0, weights, lambda plane, rows: f32(0.0))
        layers.apply(0, zero, below, round_into(w_low), (0,))
        layers.wait(1, *fields)
        one = reduced(rhs, info, 1, weights, lambda plane, rows: w_low[plane, rows].astype(f32))
        layers.apply(1, one, below, round_into(w_high), (0, 1))


def last_kernel(info, xb, x0, x1, yb, yf, c0, c1, c2, c3, own, p0, p1, p2, p3, arrived, field, back,
                held, weights, rhs, forward, below, sems, csems, fsems):
    @pl.when(info[info_member] == 1)
    def _():
        layers = Layers(info, (xb, x0, x1), (yb, yf), (c0, c1, c2, c3), held, weights, fsems, csems)
        fields = (own, (p0, p1, p2, p3), rhs, sems)
        layers.start(0, *fields)
        layers.wait(0, *fields)
        layers.ready(0, 1)
        layers.start(1, *fields)
        low, high = field.at[0], field.at[1]
        two = reduced(rhs, info, 0, weights, lambda plane, rows: arrived[plane, rows].astype(f32))
        layers.apply(0, two, below, round_into(forward), (0,))
        layers.wait(1, *fields)
        three = reduced(rhs, info, 1, weights, lambda plane, rows: forward[plane, rows].astype(f32))
        layers.apply(1, three, below, round_into(high), (0, 1))
        layers.apply(0, sent(weights, 1, high), below, subtract_into(low, forward), ())
        last = sent(weights, 0, low)
        for plane in range(2):
            for rows in row_chunks(weights.shape[1], 256):
                back[plane, rows] = last(plane, rows)


def back_kernel(info, xb, x0, x1, yb, yf, c0, c1, c2, c3, w_low, w_high, arrived, field,
                p0, p1, p2, p3, held, weights, kept, below, csems, fsems, osems):
    def start_pieces(source, slot):
        for index, piece in enumerate((p0, p1, p2, p3)):
            height = piece.shape[1]
            half = info[info_piece + 2 * index + 1]
            rows = pl.ds(pl.multiple_of(half * height, height), height)

            @pl.when(info[info_piece + 2 * index] == slot)
            def _():
                pltpu.make_async_copy(source.at[slot, :, rows, :], piece, osems.at[index]).start()

    @pl.when(info[info_member] == 0)
    def _():
        layers = Layers(info, (xb, x0, x1), (yb, yf), (c0, c1, c2, c3), held, weights, fsems, csems)
        layers.start_y(1)
        layers.start_x(1)
        layers.ready(1, 1)
        high_rows = layers.weight_copies(1)
        start_all(high_rows)
        layers.start_y(0)
        layers.start_x(0)
        low, high = kept.at[0], kept.at[1]
        layers.apply(
            1, lambda plane, rows: arrived[plane, rows], below, subtract_into(high, w_high), (0,)
        )
        start_pieces(kept, 1)
        wait_all(high_rows)
        layers.apply(0, sent(weights, 1, high), below, subtract_into(low, w_low), (0, 1))
        start_pieces(kept, 0)

    @pl.when(info[info_member] != 0)
    def _():
        start_pieces(field, 1)
        start_pieces(field, 0)

    for index, piece in enumerate((p0, p1, p2, p3)):
        part = kept.at[0, :, pl.ds(0, piece.shape[1]), :]
        pltpu.make_async_copy(part, piece, osems.at[index]).wait()


def on_device(background, src_pos, coupling, x_factor, y_factor):
    px_count = lax.axis_size("px")
    sec_index, own_x, own_y = (lax.axis_index(axis) for axis in ("sec", "px", "py"))
    group, member = sec_index // 2, sec_index % 2
    groups = lax.axis_size("sec") // 2
    order = y_factor.shape[3]
    field = background[:, 0]
    rows_here = field.shape[1]
    height = x_factor.shape[2]
    params = pltpu.CompilerParams(vmem_limit_bytes=vmem_bytes)
    rounds = [(a, b) for a in range(groups) for b in range(px_count)]

    def pairs(a, b):
        return [
            ((2 * x + c) * px_count + y, (2 * ((c + a) % 2) + x) * px_count + (y + b) % px_count)
            for x in range(groups)
            for c in range(2)
            for y in range(px_count)
            if (a, b, x) != (0, 0, c)
        ]

    def back_pairs(a, b):
        return [(target, source) for source, target in pairs(a, b)]

    own_source = src_pos[own_y * groups * px_count + group * px_count + own_x]
    plane_cells = x_factor.shape[3] * order
    layer = own_source // plane_cells
    remainder = own_source % plane_cells
    py_count = lax.axis_size("py")
    entries = [
        jnp.where(layer // 2 == member, layer % 2, -1),
        remainder // order,
        remainder % order,
        member,
    ]
    for a, b in rounds:
        entries += [(group + a) % 2, (own_x - b) % px_count]
    entries += [group, (group + 1) % 2, own_x, (own_x + 1) % 2]
    pair = own_y // 2 * 2
    entries += [own_y, pair + (own_y + 1) % 2, (own_y + 2) % 4, (pair + 2) % 4 + (own_y + 1) % 2]
    entries += [group == member]
    info = jnp.stack([jnp.asarray(entry, jnp.int32) for entry in entries])

    sends_to = jnp.stack(
        [((member + a) % 2) * px_count + (own_x + b) % px_count for a, b in rounds]
        + [own_y, group == member]
    ).astype(jnp.int32)
    piece_shape = jax.ShapeDtypeStruct((2, rows_here, order), bf16)
    shard = jnp.concatenate([x_factor[0], y_factor[0]], axis=0)
    blocks = jnp.broadcast_to(shard[None], (py_count,) + shard.shape)
    packed = pl.pallas_call(
        pack_kernel,
        out_shape=[jax.ShapeDtypeStruct((2 * rows_here + height, order), bf16)] * len(rounds),
        in_specs=[in_smem] + [anywhere] * 2,
        out_specs=[in_vmem] * len(rounds),
        scratch_shapes=[
            pltpu.SemaphoreType.DMA((len(rounds), 2)),
            pltpu.SemaphoreType.DMA((len(rounds),)),
        ],
        compiler_params=params,
    )(sends_to, field, coupling[0])
    pieces = [
        lax.ppermute(piece, ("sec", "px"), pairs(a, b)) for piece, (a, b) in zip(packed, rounds)
    ]
    blocks = lax.all_to_all(blocks, "py", split_axis=0, concat_axis=0, tiled=True)

    column_shape = jax.ShapeDtypeStruct((2, rows_here, order), bf16)
    rows_shape = jax.ShapeDtypeStruct((len(rounds), height, order), bf16)
    x_column, y_column, rows_held = pl.pallas_call(
        column_kernel,
        out_shape=[column_shape, column_shape, rows_shape],
        in_specs=[in_smem] + [anywhere] * 6,
        out_specs=[in_vmem] * 3,
        scratch_shapes=[
            pltpu.SemaphoreType.DMA((py_count, 2)),
            pltpu.SemaphoreType.DMA((len(rounds),)),
        ],
        compiler_params=params,
    )(info, blocks, packed[0], *pieces)

    def across(block, a):
        return lax.ppermute(block, ("sec", "px"), pairs(a, 0))

    def aside(block):
        return lax.ppermute(block, "px", [(y, (y + 1) % 2) for y in range(2)])

    def over_z(block, bit):
        return lax.ppermute(block, "py", [(z, z ^ bit) for z in range(py_count)])

    y_near = [across(y_column, a) for a in range(2)]
    x_aside = aside(x_column)
    rows_next = over_z(rows_held, 1)
    rows_far = over_z(rows_held, 2)
    x_both, y_both = pl.pallas_call(
        both_kernel,
        out_shape=[jax.ShapeDtypeStruct((2,) + column_shape.shape, bf16)] * 2,
        in_specs=[in_smem] + [anywhere] * 7,
        out_specs=[in_vmem] * 2,
        scratch_shapes=[pltpu.SemaphoreType.DMA((4,))],
        compiler_params=params,
    )(info, x_column, x_aside, y_column, *y_near, rows_next, rows_far)
    y_far = aside(y_both)
    x_across = [across(x_both, a) for a in range(2)]
    factors = [x_both, *x_across, y_both, y_far, rows_held, rows_next, rows_far, over_z(rows_next, 2)]

    full_shape = jax.ShapeDtypeStruct((2, order, order), bf16)
    factor_scratch = pltpu.VMEM((2, 2, order, 2 * order), bf16)
    weight_scratch = pltpu.VMEM((2, order, order), bf16)
    field_scratch = pltpu.VMEM((2, 2, order, order), bf16)
    below_scratch = pltpu.VMEM((2 * order, 2 * order), bf16)
    factor_sems = pltpu.SemaphoreType.DMA((2, 2, 2, 2))
    weight_sems = pltpu.SemaphoreType.DMA((2, py_count, 2))
    field_sems = pltpu.SemaphoreType.DMA((2, 2, 2))
    solve_flops = 16 * order**3
    fields = (packed[0], *pieces)

    def cost(solves):
        return pl.CostEstimate(
            flops=solves * solve_flops, bytes_accessed=16 * order * order * 2, transcendentals=0
        )

    w_low, w_high = pl.pallas_call(
        first_kernel,
        out_shape=[full_shape] * 2,
        in_specs=[in_smem] + [anywhere] * 14,
        out_specs=[in_vmem] * 2,
        scratch_shapes=[
            factor_scratch,
            weight_scratch,
            field_scratch,
            below_scratch,
            field_sems,
            weight_sems,
            factor_sems,
        ],
        compiler_params=params,
        cost_estimate=cost(2),
    )(info, *factors, *fields)

    up = [(2 * x, 2 * x + 1) for x in range(groups)]
    incoming = lax.ppermute(w_high, "sec", up)
    solved, back = pl.pallas_call(
        last_kernel,
        out_shape=[jax.ShapeDtypeStruct((2, 2, order, order), bf16), full_shape],
        in_specs=[in_smem] + [anywhere] * 14 + [in_vmem],
        out_specs=[in_vmem] * 2,
        scratch_shapes=[
            factor_scratch,
            weight_scratch,
            field_scratch,
            pltpu.VMEM((2, order, order), bf16),
            below_scratch,
            field_sems,
            weight_sems,
            factor_sems,
        ],
        compiler_params=params,
        cost_estimate=cost(3),
    )(info, *factors, *fields, incoming)

    down = [(target, source) for source, target in up]
    incoming = lax.ppermute(back, "sec", down)
    results = pl.pallas_call(
        back_kernel,
        out_shape=[piece_shape] * len(rounds),
        in_specs=[in_smem] + [anywhere] * 9 + [in_vmem] * 3 + [anywhere],
        out_specs=[anywhere] * len(rounds),
        scratch_shapes=[
            factor_scratch,
            weight_scratch,
            field_scratch,
            below_scratch,
            weight_sems,
            factor_sems,
            pltpu.SemaphoreType.DMA((len(rounds),)),
        ],
        compiler_params=params,
        cost_estimate=cost(2),
    )(info, *factors, w_low, w_high, incoming, solved)
    received = [
        lax.ppermute(piece, ("sec", "px"), back_pairs(a, b)) for piece, (a, b) in zip(results, rounds)
    ]
    output = pl.pallas_call(
        unpack_kernel,
        out_shape=jax.ShapeDtypeStruct(field.shape, bf16),
        in_specs=[in_smem] + [anywhere] * (len(rounds) + 1),
        out_specs=anywhere,
        scratch_shapes=[pltpu.SemaphoreType.DMA((len(rounds),))],
        compiler_params=params,
    )(sends_to, results[0], *received)
    return output[:, None]


def chip_plan_fits(mesh):
    return mesh.shape["sec"] == 4 and mesh.shape["px"] == 2 and mesh.shape["py"] == 4


def solution(mesh):
    placed = (
        P(None, "sec", "px", "py"),
        P(),
        P("sec", "px", None),
        P("sec", None, ("px", "py"), None),
        P("sec", None, ("px", "py"), None),
    )
    return jax.shard_map(
        on_device if chip_plan_fits(mesh) else on_device_by_layer,
        mesh=mesh,
        in_specs=placed,
        out_specs=P(None, "sec", "px", "py"),
        check_vma=False,
    )
```

```python
import functools

import jax
import jax.numpy as jnp
from jax import lax
from jax.experimental import pallas as pl
from jax.experimental.pallas import tpu as pltpu
from jax.sharding import PartitionSpec as P

source_amplitude = 8.0
vmem_bytes = 32 * 1024 * 1024
bf16 = jnp.bfloat16
f32 = jnp.float32
anywhere = pl.BlockSpec(memory_space=pl.ANY)
in_smem = pl.BlockSpec(memory_space=pltpu.SMEM)
in_vmem = pl.BlockSpec(memory_space=pltpu.VMEM)

info_member, info_piece, info_slot, info_half, info_block, info_self = 3, 4, 12, 14, 16, 18


def shifted(x, axis, by):
    peers = lax.axis_size(axis)
    pairs = [(i, i + by) for i in range(peers) if 0 <= i + by < peers]
    return lax.ppermute(x, axis, pairs)


def complex_block(factor):
    upper = jnp.concatenate([factor[0], -factor[1]], axis=1)
    lower = jnp.concatenate([factor[1], factor[0]], axis=1)
    return jnp.concatenate([upper, lower], axis=0)


def y_transform(real_turned, imag_turned, field_in):
    real_part = jnp.dot(field_in[0], real_turned, preferred_element_type=jnp.float32) - jnp.dot(
        field_in[1], imag_turned, preferred_element_type=jnp.float32
    )
    imag_part = jnp.dot(field_in[0], imag_turned, preferred_element_type=jnp.float32) + jnp.dot(
        field_in[1], real_turned, preferred_element_type=jnp.float32
    )
    return jnp.stack([real_part, imag_part]).astype(jnp.bfloat16)


def x_transform(x_block, field_in):
    planes, rows_all, width = field_in.shape
    output = jnp.dot(
        x_block, field_in.reshape(planes * rows_all, width), preferred_element_type=jnp.float32
    )
    return output.astype(jnp.bfloat16).reshape(planes, rows_all, width)


def scale_rows(field_in, weights, width):
    planes, rows_here, merged = field_in.shape
    spread = field_in.astype(jnp.float32).reshape(planes, rows_here, merged // width, width)
    return (spread * weights.astype(jnp.float32)[None, :, None, :]).reshape(
        planes, rows_here, merged
    )


def pick_batch(field, batch_count, batch_index):
    planes, rows_here, merged = field.shape
    split_field = field.reshape(planes, rows_here, batch_count, merged // batch_count)
    return lax.dynamic_index_in_dim(split_field, batch_index, 2, keepdims=False)


def place_batch(field, piece, batch_count, batch_index):
    planes, rows_here, merged = field.shape
    split_field = field.reshape(planes, rows_here, batch_count, merged // batch_count)
    shaped = piece.reshape(planes, rows_here, 1, merged // batch_count)
    updated = lax.dynamic_update_slice_in_dim(split_field, shaped, batch_index, 2)
    return updated.reshape(planes, rows_here, merged)


def on_device_by_layer(background, src_pos, coupling, x_factor, y_factor):
    source_count = src_pos.shape[0]
    sec_count = lax.axis_size("sec")
    sec_index = lax.axis_index("sec")
    grid_y = lax.axis_size("py")
    own_x = lax.axis_index("px")
    own_y = lax.axis_index("py")
    local_sources = source_count // grid_y
    x_pieces, y_pieces = (
        lax.all_gather(x_factor[0], ("px", "py"), axis=1, tiled=True),
        lax.all_gather(y_factor[0], ("px", "py"), axis=1, tiled=True),
    )
    x_block = complex_block(x_pieces)
    real_turned = y_pieces[0].T
    imag_turned = y_pieces[1].T
    local_field = background[:, 0]
    local_weights = coupling[0]
    rows_here = local_field.shape[1]
    full_cols = y_factor.shape[3]
    plane_cells = x_factor.shape[3] * full_cols
    own_sources = lax.dynamic_slice_in_dim(src_pos, own_y * local_sources, local_sources)
    layer_of = own_sources // plane_cells
    remainder = own_sources % plane_cells
    row_of = remainder // full_cols
    column_of = remainder % full_cols
    row_start = own_x * rows_here
    row_hit = row_of[None, :] == row_start + jnp.arange(rows_here, dtype=jnp.int32)[:, None]
    col_hit = column_of[:, None] == jnp.arange(full_cols, dtype=jnp.int32)[None, :]
    layer_hit = layer_of == sec_index
    delta = (row_hit[:, :, None] & col_hit[None, :, :] & layer_hit[None, :, None]).astype(
        jnp.float32
    )
    delta = (delta * source_amplitude).reshape(rows_here, local_sources * full_cols)
    real_rhs = local_field[0].astype(jnp.float32) + delta
    rhs_field = jnp.stack([real_rhs, local_field[1].astype(jnp.float32)])

    def apply_front(field_in):
        turned = y_transform(real_turned, imag_turned, field_in)
        line_field = lax.all_to_all(turned, "px", split_axis=2, concat_axis=1, tiled=True)
        finished = x_transform(x_block, line_field)
        return lax.all_to_all(finished, "px", split_axis=1, concat_axis=2, tiled=True)

    forward_field = jnp.zeros(local_field.shape, jnp.bfloat16)
    outgoing = pick_batch(forward_field, sec_count, 0)
    for step in range(2 * sec_count - 1):
        incoming = shifted(outgoing, "sec", 1)
        batch_index = step - sec_index
        active = (batch_index >= 0) & (batch_index < sec_count)
        clamped = jnp.clip(batch_index, 0, sec_count - 1)
        rhs_batch = pick_batch(rhs_field, sec_count, clamped)
        reduced = (rhs_batch - scale_rows(incoming, local_weights, full_cols)).astype(jnp.bfloat16)
        candidate = apply_front(reduced)
        previous = pick_batch(forward_field, sec_count, clamped)
        kept = jnp.where(active, candidate, previous)
        forward_field = place_batch(forward_field, kept, sec_count, clamped)
        outgoing = candidate
    sweep_field = forward_field
    for step in range(2 * sec_count - 2):
        send_index = jnp.clip(step - (sec_count - 1 - sec_index), 0, sec_count - 1)
        own_batch = pick_batch(sweep_field, sec_count, send_index)
        sent_field = scale_rows(own_batch, local_weights, full_cols).astype(jnp.bfloat16)
        incoming = shifted(sent_field, "sec", -1)
        batch_index = step - (sec_count - 2 - sec_index)
        active = (batch_index >= 0) & (batch_index < sec_count) & (sec_index <= sec_count - 2)
        clamped = jnp.clip(batch_index, 0, sec_count - 1)
        solved = apply_front(incoming)
        forward_batch = pick_batch(forward_field, sec_count, clamped)
        candidate = (forward_batch.astype(jnp.float32) - solved.astype(jnp.float32)).astype(
            jnp.bfloat16
        )
        previous = pick_batch(sweep_field, sec_count, clamped)
        kept = jnp.where(active, candidate, previous)
        sweep_field = place_batch(sweep_field, kept, sec_count, clamped)
    return sweep_field[:, None]


def start_all(copies):
    for copy in copies:
        copy.start()


def wait_all(copies):
    for copy in copies:
        copy.wait()


def row_chunks(order, step):
    step = min(step, order)
    return [slice(first, first + step) for first in range(0, order, step)]


class Either:
    def __init__(self, flag, own, received, target, sem):
        self.flag = flag
        self.own = pltpu.make_async_copy(own, target, sem)
        self.received = pltpu.make_async_copy(received, target, sem)

    def start(self):
        @pl.when(self.flag != 0)
        def _():
            self.own.start()

        @pl.when(self.flag == 0)
        def _():
            self.received.start()

    def wait(self):
        self.received.wait()


def pack_kernel(place, field, coupling, *rest):
    pieces, (sems, csems) = rest[:-2], rest[-2:]
    rows_here = field.shape[1]
    height = pieces[0].shape[0] - 2 * rows_here
    own = pl.ds(pl.multiple_of(place[len(pieces)] * height, height), height)
    copies = []
    for index, piece in enumerate(pieces):
        width = piece.shape[1]
        offset = pl.multiple_of(place[index] * width, width)
        for plane in range(2):
            copies.append(
                pltpu.make_async_copy(
                    field.at[plane, :, pl.ds(offset, width)],
                    piece.at[pl.ds(plane * rows_here, rows_here)],
                    sems.at[index, plane],
                )
            )
        copies.append(
            pltpu.make_async_copy(
                coupling.at[own], piece.at[pl.ds(2 * rows_here, height)], csems.at[index]
            )
        )
    start_all(copies)
    wait_all(copies)


def unpack_kernel(place, own, *rest):
    pieces, field, sems = rest[:-2], rest[-2], rest[-1]
    copies = []
    for index, piece in enumerate(pieces):
        width = piece.shape[2]
        offset = pl.multiple_of(place[index] * width, width)
        target = field.at[:, :, pl.ds(offset, width)]
        if index:
            copies.append(pltpu.make_async_copy(piece, target, sems.at[index]))
        else:
            copies.append(Either(place[len(pieces) + 1], own, piece, target, sems.at[index]))
    start_all(copies)
    wait_all(copies)


def column_kernel(info, blocks, own, p0, p1, p2, p3, x_column, y_column, rows_held, sems, csems):
    count, planes, height, order = blocks.shape
    copies = []
    for index in range(count):
        for which, column in enumerate((x_column, y_column)):
            copies.append(
                pltpu.make_async_copy(
                    blocks.at[index, pl.ds(2 * which, 2)],
                    column.at[:, pl.ds(index * height, height), :],
                    sems.at[index, which],
                )
            )
    tall = rows_held.shape[1]
    last = pl.ds(own.shape[0] - tall, tall)
    copies.append(Either(info[info_self], own.at[last], p0.at[last], rows_held.at[0], csems.at[0]))
    for index, piece in enumerate((p1, p2, p3)):
        copies.append(
            pltpu.make_async_copy(piece.at[last], rows_held.at[index + 1], csems.at[index + 1])
        )
    start_all(copies)
    wait_all(copies)


def both_kernel(info, x_column, x_aside, y_column, y0, y1, rows_next, x_both, y_both, sems):
    copies = [
        pltpu.make_async_copy(x_column, x_both.at[0], sems.at[0]),
        pltpu.make_async_copy(x_aside, x_both.at[1], sems.at[1]),
        Either(info[info_self], y_column, y0, y_both.at[0], sems.at[2]),
        pltpu.make_async_copy(y1, y_both.at[1], sems.at[3]),
    ]
    start_all(copies)
    wait_all(copies)


class Layers:
    def __init__(self, info, x_parts, y_parts, row_blocks, held, weights, sems, csems):
        self.info, self.order = info, held.shape[1]
        self.x_parts, self.y_parts, self.row_blocks = x_parts, y_parts, row_blocks
        self.held, self.weights, self.sems, self.csems = held, weights, sems, csems

    def half_rows(self, far):
        height = self.order // 2
        return pl.ds(pl.multiple_of(self.info[info_half + far] * height, height), height)

    def x_copies(self, slot, part):
        return [
            pltpu.make_async_copy(
                part.at[far, plane],
                self.held.at[slot, self.half_rows(far), pl.ds(plane * self.order, self.order)],
                self.sems.at[slot, far, plane],
            )
            for far in range(2)
            for plane in range(2)
        ]

    def start_x(self, slot):
        own, first, second = self.x_parts
        turn, same = self.info[info_slot + slot], self.info[info_self]
        for hit, part in (
            ((turn == 0) & (same != 0), own),
            ((turn == 0) & (same == 0), first),
            (turn == 1, second),
        ):

            @pl.when(hit)
            def _():
                start_all(self.x_copies(slot, part))

    def ready_x(self, slot):
        wait_all(self.x_copies(slot, self.x_parts[0]))

    def weight_copies(self, slot):
        height = self.row_blocks[0].shape[1]
        copies = []
        for index, block in enumerate(self.row_blocks):
            for far in range(2):
                turn = 2 * self.info[info_slot + slot] + far
                start = self.info[info_half + far] * (self.order // 2)
                start = start + self.info[info_block + index] * height
                rows = pl.ds(pl.multiple_of(start, height), height)
                copies.append(
                    pltpu.make_async_copy(
                        block.at[turn], self.weights.at[slot, rows, :], self.csems.at[slot, index, far]
                    )
                )
        return copies

    def rhs_copies(self, slot, pair, rhs, sems):
        height = self.order // 2
        return [
            pltpu.make_async_copy(
                piece.at[pl.ds(plane * height, height)],
                rhs.at[slot, plane, self.half_rows(far), :],
                sems.at[slot, far, plane],
            )
            for far, piece in enumerate(pair)
            for plane in range(2)
        ]

    def start_rhs(self, slot, own, pieces, rhs, sems):
        turn, same = self.info[info_slot + slot], self.info[info_self]
        for hit, pair in (
            ((turn == 0) & (same != 0), (own, pieces[1])),
            ((turn == 0) & (same == 0), pieces[:2]),
            (turn == 1, pieces[2:]),
        ):

            @pl.when(hit)
            def _():
                start_all(self.rhs_copies(slot, pair, rhs, sems))

    def start(self, slot, own, pieces, rhs, sems):
        self.start_rhs(slot, own, pieces, rhs, sems)
        start_all(self.weight_copies(slot))
        self.start_x(slot)

    def wait(self, slot, own, pieces, rhs, sems):
        wait_all(self.rhs_copies(slot, pieces[:2], rhs, sems))
        wait_all(self.weight_copies(slot))

    def apply(self, slot, source, below, store, fresh):
        order = self.order
        turned = (((1,), (1,)), ((), ()))
        turn = self.info[info_slot + slot]
        for rows in row_chunks(order, 256):
            real, imag = source(0, rows), source(1, rows)
            upper = jnp.concatenate([real, -imag], axis=1)
            lower = jnp.concatenate([imag, real], axis=1)
            both = jnp.concatenate([upper, lower], axis=0)
            height = rows.stop - rows.start
            further = slice(rows.start + order, rows.stop + order)
            for far, part in enumerate(self.y_parts):
                right = jnp.concatenate([part[turn, 0], part[turn, 1]], axis=1)
                product = lax.dot_general(
                    both, right, turned, preferred_element_type=f32
                ).astype(bf16)
                start = self.info[info_half + far] * (order // 2)
                columns = pl.ds(pl.multiple_of(start, order // 2), order // 2)
                beyond = pl.ds(pl.multiple_of(order + start, order // 2), order // 2)
                below[rows, columns] = product[:height]
                below[rows, beyond] = product[height:]
                below[further, columns] = -product[height:]
                below[further, beyond] = product[:height]
        if fresh:
            self.ready_x(slot)
        for plane in range(2):
            for columns in row_chunks(order, 256):
                along = slice(columns.start + plane * order, columns.stop + plane * order)
                store(
                    plane,
                    columns,
                    jnp.dot(self.held[slot], below[:, along], preferred_element_type=f32),
                )


def reduced(rhs, info, slot, weights, incoming):
    def source(plane, rows):
        values = rhs[slot, plane, rows].astype(f32)
        if plane == 0:
            row = lax.broadcasted_iota(jnp.int32, values.shape, 0) + rows.start
            column = lax.broadcasted_iota(jnp.int32, (1, values.shape[1]), 1)
            hit = (column == info[2]) & (info[0] == slot)
            cell = jnp.where(hit, f32(source_amplitude), f32(0.0))
            values = values + jnp.where(row == info[1], cell, f32(0.0))
        scaled = weights[slot, rows].astype(f32) * incoming(plane, rows)
        return (values - scaled).astype(bf16)

    return source


def sent(weights, slot, field):
    def source(plane, rows):
        scaled = weights[slot, rows].astype(f32) * field[plane, rows].astype(f32)
        return scaled.astype(bf16)

    return source


def subtract_into(target, forward):
    def store(plane, columns, values):
        solved = values.astype(bf16).astype(f32)
        target[plane, :, columns] = (forward[plane, :, columns].astype(f32) - solved).astype(bf16)

    return store


def round_into(target):
    def store(plane, columns, values):
        target[plane, :, columns] = values.astype(bf16)

    return store


def first_kernel(info, xb, x0, x1, yb, yf, c0, c1, own, p0, p1, p2, p3, w_low, w_high,
                 held, weights, rhs, below, sems, csems, fsems):
    @pl.when(info[info_member] == 0)
    def _():
        layers = Layers(info, (xb, x0, x1), (yb, yf), (c0, c1), held, weights, fsems, csems)
        fields = (own, (p0, p1, p2, p3), rhs, sems)
        layers.start(0, *fields)
        layers.wait(0, *fields)
        layers.start(1, *fields)
        zero = reduced(rhs, info, 0, weights, lambda plane, rows: f32(0.0))
        layers.apply(0, zero, below, round_into(w_low), True)
        layers.wait(1, *fields)
        one = reduced(rhs, info, 1, weights, lambda plane, rows: w_low[plane, rows].astype(f32))
        layers.apply(1, one, below, round_into(w_high), True)


def last_kernel(info, xb, x0, x1, yb, yf, c0, c1, own, p0, p1, p2, p3, arrived, field, back,
                held, weights, rhs, forward, below, sems, csems, fsems):
    @pl.when(info[info_member] == 1)
    def _():
        layers = Layers(info, (xb, x0, x1), (yb, yf), (c0, c1), held, weights, fsems, csems)
        fields = (own, (p0, p1, p2, p3), rhs, sems)
        layers.start(0, *fields)
        layers.wait(0, *fields)
        layers.start(1, *fields)
        low, high = field.at[0], field.at[1]
        two = reduced(rhs, info, 0, weights, lambda plane, rows: arrived[plane, rows].astype(f32))
        layers.apply(0, two, below, round_into(forward), True)
        layers.wait(1, *fields)
        three = reduced(rhs, info, 1, weights, lambda plane, rows: forward[plane, rows].astype(f32))
        layers.apply(1, three, below, round_into(high), True)
        layers.apply(0, sent(weights, 1, high), below, subtract_into(low, forward), False)
        last = sent(weights, 0, low)
        for plane in range(2):
            for rows in row_chunks(weights.shape[1], 256):
                back[plane, rows] = last(plane, rows)


def back_kernel(info, xb, x0, x1, yb, yf, c0, c1, w_low, w_high, arrived, field,
                p0, p1, p2, p3, held, weights, kept, below, csems, fsems, osems):
    def start_pieces(source, slot):
        for index, piece in enumerate((p0, p1, p2, p3)):
            height = piece.shape[1]
            half = info[info_piece + 2 * index + 1]
            rows = pl.ds(pl.multiple_of(half * height, height), height)

            @pl.when(info[info_piece + 2 * index] == slot)
            def _():
                pltpu.make_async_copy(source.at[slot, :, rows, :], piece, osems.at[index]).start()

    @pl.when(info[info_member] == 0)
    def _():
        layers = Layers(info, (xb, x0, x1), (yb, yf), (c0, c1), held, weights, fsems, csems)
        layers.start_x(1)
        high_rows = layers.weight_copies(1)
        start_all(high_rows)
        layers.start_x(0)
        low, high = kept.at[0], kept.at[1]
        layers.apply(
            1, lambda plane, rows: arrived[plane, rows], below, subtract_into(high, w_high), True
        )
        start_pieces(kept, 1)
        wait_all(high_rows)
        layers.apply(0, sent(weights, 1, high), below, subtract_into(low, w_low), True)
        start_pieces(kept, 0)

    @pl.when(info[info_member] != 0)
    def _():
        start_pieces(field, 1)
        start_pieces(field, 0)

    for index, piece in enumerate((p0, p1, p2, p3)):
        part = kept.at[0, :, pl.ds(0, piece.shape[1]), :]
        pltpu.make_async_copy(part, piece, osems.at[index]).wait()


def on_device(background, src_pos, coupling, x_factor, y_factor):
    px_count = lax.axis_size("px")
    sec_index, own_x, own_y = (lax.axis_index(axis) for axis in ("sec", "px", "py"))
    group, member = sec_index // 2, sec_index % 2
    groups = lax.axis_size("sec") // 2
    order = y_factor.shape[3]
    field = background[:, 0]
    rows_here = field.shape[1]
    height = x_factor.shape[2]
    params = pltpu.CompilerParams(vmem_limit_bytes=vmem_bytes)
    rounds = [(a, b) for a in range(groups) for b in range(px_count)]

    def pairs(a, b):
        return [
            ((2 * x + c) * px_count + y, (2 * ((c + a) % 2) + x) * px_count + (y + b) % px_count)
            for x in range(groups)
            for c in range(2)
            for y in range(px_count)
            if (a, b, x) != (0, 0, c)
        ]

    def back_pairs(a, b):
        return [(target, source) for source, target in pairs(a, b)]

    own_source = src_pos[own_y * groups * px_count + group * px_count + own_x]
    plane_cells = x_factor.shape[3] * order
    layer = own_source // plane_cells
    remainder = own_source % plane_cells
    py_count = lax.axis_size("py")
    entries = [
        jnp.where(layer // 2 == member, layer % 2, -1),
        remainder // order,
        remainder % order,
        member,
    ]
    for a, b in rounds:
        entries += [(group + a) % 2, (own_x - b) % px_count]
    entries += [group, (group + 1) % 2, own_x, (own_x + 1) % 2]
    entries += [own_y % 2, (own_y + 1) % 2, group == member]
    info = jnp.stack([jnp.asarray(entry, jnp.int32) for entry in entries])

    sends_to = jnp.stack(
        [((member + a) % 2) * px_count + (own_x + b) % px_count for a, b in rounds]
        + [own_y % 2, group == member]
    ).astype(jnp.int32)
    piece_shape = jax.ShapeDtypeStruct((2, rows_here, order), bf16)
    shard = jnp.concatenate([x_factor[0], y_factor[0]], axis=0)
    blocks = jnp.broadcast_to(shard[None], (py_count,) + shard.shape)
    packed = pl.pallas_call(
        pack_kernel,
        out_shape=[jax.ShapeDtypeStruct((2 * rows_here + rows_here // 2, order), bf16)] * len(rounds),
        in_specs=[in_smem] + [anywhere] * 2,
        out_specs=[in_vmem] * len(rounds),
        scratch_shapes=[
            pltpu.SemaphoreType.DMA((len(rounds), 2)),
            pltpu.SemaphoreType.DMA((len(rounds),)),
        ],
        compiler_params=params,
    )(sends_to, field, coupling[0])
    pieces = [
        lax.ppermute(piece, ("sec", "px"), pairs(a, b)) for piece, (a, b) in zip(packed, rounds)
    ]
    blocks = lax.all_to_all(blocks, "py", split_axis=0, concat_axis=0, tiled=True)

    column_shape = jax.ShapeDtypeStruct((2, rows_here, order), bf16)
    rows_shape = jax.ShapeDtypeStruct((len(rounds), rows_here // 2, order), bf16)
    x_column, y_column, rows_held = pl.pallas_call(
        column_kernel,
        out_shape=[column_shape, column_shape, rows_shape],
        in_specs=[in_smem] + [anywhere] * 6,
        out_specs=[in_vmem] * 3,
        scratch_shapes=[
            pltpu.SemaphoreType.DMA((py_count, 2)),
            pltpu.SemaphoreType.DMA((len(rounds),)),
        ],
        compiler_params=params,
    )(info, blocks, packed[0], *pieces)

    def across(block, a):
        return lax.ppermute(block, ("sec", "px"), pairs(a, 0))

    def aside(block):
        return lax.ppermute(block, "px", [(y, (y + 1) % 2) for y in range(2)])

    def over_z(block, bit):
        return lax.ppermute(block, "py", [(z, z ^ bit) for z in range(py_count)])

    y_near = [across(y_column, a) for a in range(2)]
    x_aside = aside(x_column)
    rows_next = over_z(rows_held, 1)
    x_both, y_both = pl.pallas_call(
        both_kernel,
        out_shape=[jax.ShapeDtypeStruct((2,) + column_shape.shape, bf16)] * 2,
        in_specs=[in_smem] + [anywhere] * 6,
        out_specs=[in_vmem] * 2,
        scratch_shapes=[pltpu.SemaphoreType.DMA((4,))],
        compiler_params=params,
    )(info, x_column, x_aside, y_column, *y_near, rows_next)
    y_far = aside(y_both)
    x_across = [across(x_both, a) for a in range(2)]
    factors = [x_both, *x_across, y_both, y_far, rows_held, rows_next]

    full_shape = jax.ShapeDtypeStruct((2, order, order), bf16)
    factor_scratch = pltpu.VMEM((2, order, 2 * order), bf16)
    weight_scratch = pltpu.VMEM((2, order, order), bf16)
    field_scratch = pltpu.VMEM((2, 2, order, order), bf16)
    below_scratch = pltpu.VMEM((2 * order, 2 * order), bf16)
    factor_sems = pltpu.SemaphoreType.DMA((2, 2, 2))
    weight_sems = pltpu.SemaphoreType.DMA((2, 2, 2))
    field_sems = pltpu.SemaphoreType.DMA((2, 2, 2))
    solver_specs = [in_smem] + [anywhere] * 3 + [in_vmem] * 2 + [anywhere] * 2
    solve_flops = 16 * order**3
    fields = (packed[0], *pieces)

    def cost(solves):
        return pl.CostEstimate(
            flops=solves * solve_flops, bytes_accessed=16 * order * order * 2, transcendentals=0
        )

    w_low, w_high = pl.pallas_call(
        first_kernel,
        out_shape=[full_shape] * 2,
        in_specs=solver_specs + [anywhere] * 5,
        out_specs=[in_vmem] * 2,
        scratch_shapes=[
            factor_scratch,
            weight_scratch,
            field_scratch,
            below_scratch,
            field_sems,
            weight_sems,
            factor_sems,
        ],
        compiler_params=params,
        cost_estimate=cost(2),
    )(info, *factors, *fields)

    up = [(2 * x, 2 * x + 1) for x in range(groups)]
    incoming = lax.ppermute(w_high, "sec", up)
    solved, back = pl.pallas_call(
        last_kernel,
        out_shape=[jax.ShapeDtypeStruct((2, 2, order, order), bf16), full_shape],
        in_specs=solver_specs + [anywhere] * 5 + [in_vmem],
        out_specs=[in_vmem] * 2,
        scratch_shapes=[
            factor_scratch,
            weight_scratch,
            field_scratch,
            pltpu.VMEM((2, order, order), bf16),
            below_scratch,
            field_sems,
            weight_sems,
            factor_sems,
        ],
        compiler_params=params,
        cost_estimate=cost(3),
    )(info, *factors, *fields, incoming)

    down = [(target, source) for source, target in up]
    incoming = lax.ppermute(back, "sec", down)
    results = pl.pallas_call(
        back_kernel,
        out_shape=[piece_shape] * len(rounds),
        in_specs=solver_specs + [in_vmem] * 3 + [anywhere],
        out_specs=[anywhere] * len(rounds),
        scratch_shapes=[
            factor_scratch,
            weight_scratch,
            field_scratch,
            below_scratch,
            weight_sems,
            factor_sems,
            pltpu.SemaphoreType.DMA((len(rounds),)),
        ],
        compiler_params=params,
        cost_estimate=cost(2),
    )(info, *factors, w_low, w_high, incoming, solved)
    received = [
        lax.ppermute(piece, ("sec", "px"), back_pairs(a, b)) for piece, (a, b) in zip(results, rounds)
    ]
    output = pl.pallas_call(
        unpack_kernel,
        out_shape=jax.ShapeDtypeStruct(field.shape, bf16),
        in_specs=[in_smem] + [anywhere] * (len(rounds) + 1),
        out_specs=anywhere,
        scratch_shapes=[pltpu.SemaphoreType.DMA((len(rounds),))],
        compiler_params=params,
    )(sends_to, results[0], *received)
    return output[:, None]


def chip_plan_fits(mesh):
    return mesh.shape["sec"] == 4 and mesh.shape["px"] == 2 and mesh.shape["py"] == 4


def solution(mesh):
    placed = (
        P(None, "sec", "px", "py"),
        P(),
        P("sec", "px", None),
        P("sec", None, ("px", "py"), None),
        P("sec", None, ("px", "py"), None),
    )
    return jax.shard_map(
        on_device if chip_plan_fits(mesh) else on_device_by_layer,
        mesh=mesh,
        in_specs=placed,
        out_specs=P(None, "sec", "px", "py"),
        check_vma=False,
    )
```

```python
import functools

import jax
import jax.numpy as jnp
from jax import lax
from jax.experimental import pallas as pl
from jax.experimental.pallas import tpu as pltpu
from jax.sharding import PartitionSpec as P

source_amplitude = 8.0
vmem_bytes = 32 * 1024 * 1024
bf16 = jnp.bfloat16
f32 = jnp.float32
anywhere = pl.BlockSpec(memory_space=pl.ANY)
in_smem = pl.BlockSpec(memory_space=pltpu.SMEM)
in_vmem = pl.BlockSpec(memory_space=pltpu.VMEM)

info_member, info_piece, info_slot, info_half, info_self = 3, 4, 12, 14, 16


def shifted(x, axis, by):
    peers = lax.axis_size(axis)
    pairs = [(i, i + by) for i in range(peers) if 0 <= i + by < peers]
    return lax.ppermute(x, axis, pairs)


def complex_block(factor):
    upper = jnp.concatenate([factor[0], -factor[1]], axis=1)
    lower = jnp.concatenate([factor[1], factor[0]], axis=1)
    return jnp.concatenate([upper, lower], axis=0)


def y_transform(real_turned, imag_turned, field_in):
    real_part = jnp.dot(field_in[0], real_turned, preferred_element_type=jnp.float32) - jnp.dot(
        field_in[1], imag_turned, preferred_element_type=jnp.float32
    )
    imag_part = jnp.dot(field_in[0], imag_turned, preferred_element_type=jnp.float32) + jnp.dot(
        field_in[1], real_turned, preferred_element_type=jnp.float32
    )
    return jnp.stack([real_part, imag_part]).astype(jnp.bfloat16)


def x_transform(x_block, field_in):
    planes, rows_all, width = field_in.shape
    output = jnp.dot(
        x_block, field_in.reshape(planes * rows_all, width), preferred_element_type=jnp.float32
    )
    return output.astype(jnp.bfloat16).reshape(planes, rows_all, width)


def scale_rows(field_in, weights, width):
    planes, rows_here, merged = field_in.shape
    spread = field_in.astype(jnp.float32).reshape(planes, rows_here, merged // width, width)
    return (spread * weights.astype(jnp.float32)[None, :, None, :]).reshape(
        planes, rows_here, merged
    )


def pick_batch(field, batch_count, batch_index):
    planes, rows_here, merged = field.shape
    split_field = field.reshape(planes, rows_here, batch_count, merged // batch_count)
    return lax.dynamic_index_in_dim(split_field, batch_index, 2, keepdims=False)


def place_batch(field, piece, batch_count, batch_index):
    planes, rows_here, merged = field.shape
    split_field = field.reshape(planes, rows_here, batch_count, merged // batch_count)
    shaped = piece.reshape(planes, rows_here, 1, merged // batch_count)
    updated = lax.dynamic_update_slice_in_dim(split_field, shaped, batch_index, 2)
    return updated.reshape(planes, rows_here, merged)


def on_device_by_layer(background, src_pos, coupling, x_factor, y_factor):
    source_count = src_pos.shape[0]
    sec_count = lax.axis_size("sec")
    sec_index = lax.axis_index("sec")
    grid_y = lax.axis_size("py")
    own_x = lax.axis_index("px")
    own_y = lax.axis_index("py")
    local_sources = source_count // grid_y
    x_pieces, y_pieces = (
        lax.all_gather(x_factor[0], ("px", "py"), axis=1, tiled=True),
        lax.all_gather(y_factor[0], ("px", "py"), axis=1, tiled=True),
    )
    x_block = complex_block(x_pieces)
    real_turned = y_pieces[0].T
    imag_turned = y_pieces[1].T
    local_field = background[:, 0]
    local_weights = coupling[0]
    rows_here = local_field.shape[1]
    full_cols = y_factor.shape[3]
    plane_cells = x_factor.shape[3] * full_cols
    own_sources = lax.dynamic_slice_in_dim(src_pos, own_y * local_sources, local_sources)
    layer_of = own_sources // plane_cells
    remainder = own_sources % plane_cells
    row_of = remainder // full_cols
    column_of = remainder % full_cols
    row_start = own_x * rows_here
    row_hit = row_of[None, :] == row_start + jnp.arange(rows_here, dtype=jnp.int32)[:, None]
    col_hit = column_of[:, None] == jnp.arange(full_cols, dtype=jnp.int32)[None, :]
    layer_hit = layer_of == sec_index
    delta = (row_hit[:, :, None] & col_hit[None, :, :] & layer_hit[None, :, None]).astype(
        jnp.float32
    )
    delta = (delta * source_amplitude).reshape(rows_here, local_sources * full_cols)
    real_rhs = local_field[0].astype(jnp.float32) + delta
    rhs_field = jnp.stack([real_rhs, local_field[1].astype(jnp.float32)])

    def apply_front(field_in):
        turned = y_transform(real_turned, imag_turned, field_in)
        line_field = lax.all_to_all(turned, "px", split_axis=2, concat_axis=1, tiled=True)
        finished = x_transform(x_block, line_field)
        return lax.all_to_all(finished, "px", split_axis=1, concat_axis=2, tiled=True)

    forward_field = jnp.zeros(local_field.shape, jnp.bfloat16)
    outgoing = pick_batch(forward_field, sec_count, 0)
    for step in range(2 * sec_count - 1):
        incoming = shifted(outgoing, "sec", 1)
        batch_index = step - sec_index
        active = (batch_index >= 0) & (batch_index < sec_count)
        clamped = jnp.clip(batch_index, 0, sec_count - 1)
        rhs_batch = pick_batch(rhs_field, sec_count, clamped)
        reduced = (rhs_batch - scale_rows(incoming, local_weights, full_cols)).astype(jnp.bfloat16)
        candidate = apply_front(reduced)
        previous = pick_batch(forward_field, sec_count, clamped)
        kept = jnp.where(active, candidate, previous)
        forward_field = place_batch(forward_field, kept, sec_count, clamped)
        outgoing = candidate
    sweep_field = forward_field
    for step in range(2 * sec_count - 2):
        send_index = jnp.clip(step - (sec_count - 1 - sec_index), 0, sec_count - 1)
        own_batch = pick_batch(sweep_field, sec_count, send_index)
        sent_field = scale_rows(own_batch, local_weights, full_cols).astype(jnp.bfloat16)
        incoming = shifted(sent_field, "sec", -1)
        batch_index = step - (sec_count - 2 - sec_index)
        active = (batch_index >= 0) & (batch_index < sec_count) & (sec_index <= sec_count - 2)
        clamped = jnp.clip(batch_index, 0, sec_count - 1)
        solved = apply_front(incoming)
        forward_batch = pick_batch(forward_field, sec_count, clamped)
        candidate = (forward_batch.astype(jnp.float32) - solved.astype(jnp.float32)).astype(
            jnp.bfloat16
        )
        previous = pick_batch(sweep_field, sec_count, clamped)
        kept = jnp.where(active, candidate, previous)
        sweep_field = place_batch(sweep_field, kept, sec_count, clamped)
    return sweep_field[:, None]


def start_all(copies):
    for copy in copies:
        copy.start()


def wait_all(copies):
    for copy in copies:
        copy.wait()


def row_chunks(order, step):
    step = min(step, order)
    return [slice(first, first + step) for first in range(0, order, step)]


class Either:
    def __init__(self, flag, own, received, target, sem):
        self.flag = flag
        self.own = pltpu.make_async_copy(own, target, sem)
        self.received = pltpu.make_async_copy(received, target, sem)

    def start(self):
        @pl.when(self.flag != 0)
        def _():
            self.own.start()

        @pl.when(self.flag == 0)
        def _():
            self.received.start()

    def wait(self):
        self.received.wait()


def pack_kernel(place, field, *rest):
    pieces, sems = rest[:-1], rest[-1]
    copies = []
    for index, piece in enumerate(pieces):
        width = piece.shape[2]
        offset = pl.multiple_of(place[index] * width, width)
        copies.append(
            pltpu.make_async_copy(field.at[:, :, pl.ds(offset, width)], piece, sems.at[index])
        )
    start_all(copies)
    wait_all(copies)


def unpack_kernel(place, own, *rest):
    pieces, field, sems = rest[:-2], rest[-2], rest[-1]
    copies = []
    for index, piece in enumerate(pieces):
        width = piece.shape[2]
        offset = pl.multiple_of(place[index] * width, width)
        target = field.at[:, :, pl.ds(offset, width)]
        if index:
            copies.append(pltpu.make_async_copy(piece, target, sems.at[index]))
        else:
            copies.append(Either(place[len(pieces)], own, piece, target, sems.at[index]))
    start_all(copies)
    wait_all(copies)


def column_kernel(blocks, coupling, p0, p1, p2, p3, x_column, y_column, sems, csems):
    count, planes, height, order = blocks.shape
    copies = []
    rows_here = coupling.shape[0]
    for index in range(count):
        for which, column in enumerate((x_column, y_column)):
            for plane in range(2):
                copies.append(
                    pltpu.make_async_copy(
                        blocks.at[index, 2 * which + plane],
                        column.at[pl.ds(plane * rows_here + index * height, height)],
                        sems.at[index, which, plane],
                    )
                )
    part = rows_here // 2
    for which, column in enumerate((x_column, y_column)):
        copies.append(
            pltpu.make_async_copy(
                coupling.at[pl.ds(which * part, part)],
                column.at[pl.ds(2 * rows_here, part)],
                csems.at[which],
            )
        )
    start_all(copies)
    wait_all(copies)


def both_kernel(info, x_column, x_aside, y_column, y0, y1, x_both, y_both, sems):
    copies = [
        pltpu.make_async_copy(x_column, x_both.at[0], sems.at[0]),
        pltpu.make_async_copy(x_aside, x_both.at[1], sems.at[1]),
        Either(info[info_self], y_column, y0, y_both.at[0], sems.at[2]),
        pltpu.make_async_copy(y1, y_both.at[1], sems.at[3]),
    ]
    start_all(copies)
    wait_all(copies)


class Layers:
    def __init__(self, info, x_parts, y_parts, held, weights, sems, csems):
        self.info, self.order = info, held.shape[2]
        self.x_parts, self.y_parts = x_parts, y_parts
        self.held, self.weights, self.sems, self.csems = held, weights, sems, csems

    def half_rows(self, far):
        height = self.order // 2
        return pl.ds(pl.multiple_of(self.info[info_half + far] * height, height), height)

    def factor_copies(self, slot, which, parts):
        height = self.order // 2
        return [
            pltpu.make_async_copy(
                part.at[pl.ds(plane * height, height)],
                self.held.at[
                    slot, which, self.half_rows(far), pl.ds(plane * self.order, self.order)
                ],
                self.sems.at[slot, which, far, plane],
            )
            for far, part in enumerate(parts)
            for plane in range(2)
        ]

    def weight_copies(self, slot, which, parts):
        height = self.order // 2
        tall = height // 2
        copies = []
        for far, part in enumerate(parts):
            start = self.info[info_half + far] * height + which * tall
            rows = pl.ds(pl.multiple_of(start, tall), tall)
            copies.append(
                pltpu.make_async_copy(
                    part.at[pl.ds(2 * height, tall)],
                    self.weights.at[slot, rows, :],
                    self.csems.at[slot, which, far],
                )
            )
        return copies

    def start_y(self, slot, with_weights=True):
        turn = self.info[info_slot + slot]
        parts = [part.at[turn] for part in self.y_parts]
        start_all(self.factor_copies(slot, 1, parts))
        if with_weights:
            start_all(self.weight_copies(slot, 1, parts))

    def start_x(self, slot, with_weights=True):
        own, first, second = self.x_parts
        turn, same = self.info[info_slot + slot], self.info[info_self]
        for hit, part in (
            ((turn == 0) & (same != 0), own),
            ((turn == 0) & (same == 0), first),
            (turn == 1, second),
        ):

            @pl.when(hit)
            def _():
                parts = [part.at[0], part.at[1]]
                if with_weights:
                    start_all(self.weight_copies(slot, 0, parts))
                start_all(self.factor_copies(slot, 0, parts))

    def ready(self, slot, which):
        part = self.x_parts[0].at[0]
        wait_all(self.factor_copies(slot, which, [part, part]))

    def ready_weights(self, slot):
        part = self.x_parts[0].at[0]
        for which in range(2):
            wait_all(self.weight_copies(slot, which, [part, part]))

    def rhs_copies(self, slot, pair, rhs, sems):
        return [
            pltpu.make_async_copy(
                piece, rhs.at[slot, :, self.half_rows(far), :], sems.at[slot, far]
            )
            for far, piece in enumerate(pair)
        ]

    def start_rhs(self, slot, own, pieces, rhs, sems):
        turn, same = self.info[info_slot + slot], self.info[info_self]
        for hit, pair in (
            ((turn == 0) & (same != 0), (own, pieces[1])),
            ((turn == 0) & (same == 0), pieces[:2]),
            (turn == 1, pieces[2:]),
        ):

            @pl.when(hit)
            def _():
                start_all(self.rhs_copies(slot, pair, rhs, sems))

    def start(self, slot, own, pieces, rhs, sems):
        self.start_y(slot)
        self.start_rhs(slot, own, pieces, rhs, sems)
        self.start_x(slot)

    def wait(self, slot, own, pieces, rhs, sems):
        wait_all(self.rhs_copies(slot, pieces[:2], rhs, sems))
        self.ready_weights(slot)

    def apply(self, slot, source, below, store, fresh):
        order = self.order
        turned = (((1,), (1,)), ((), ()))
        if 1 in fresh:
            self.ready(slot, 1)
        for rows in row_chunks(order, 256):
            real, imag = source(0, rows), source(1, rows)
            upper = jnp.concatenate([real, -imag], axis=1)
            lower = jnp.concatenate([imag, real], axis=1)
            part = lax.dot_general(
                jnp.concatenate([upper, lower], axis=0),
                self.held[slot, 1],
                turned,
                preferred_element_type=f32,
            ).astype(bf16)
            height = rows.stop - rows.start
            real, imag = part[:height], part[height:]
            further = slice(rows.start + order, rows.stop + order)
            below[rows, :order] = real
            below[rows, order:] = imag
            below[further, :order] = -imag
            below[further, order:] = real
        if 0 in fresh:
            self.ready(slot, 0)
        for plane in range(2):
            for columns in row_chunks(order, 256):
                along = slice(columns.start + plane * order, columns.stop + plane * order)
                store(
                    plane,
                    columns,
                    jnp.dot(self.held[slot, 0], below[:, along], preferred_element_type=f32),
                )


def reduced(rhs, info, slot, weights, incoming):
    def source(plane, rows):
        values = rhs[slot, plane, rows]
        if plane == 0:
            row = lax.broadcasted_iota(jnp.int32, values.shape, 0) + rows.start
            column = lax.broadcasted_iota(jnp.int32, values.shape, 1)
            hit = (row == info[1]) & (column == info[2]) & (info[0] == slot)
            values = values + jnp.where(hit, f32(source_amplitude), f32(0.0)).astype(bf16)
        return values - weights[slot, rows] * incoming(plane, rows)

    return source


def sent(weights, slot, field):
    return lambda plane, rows: weights[slot, rows] * field[plane, rows]


def subtract_into(target, forward):
    def store(plane, columns, values):
        target[plane, :, columns] = forward[plane, :, columns] - values.astype(bf16)

    return store


def round_into(target):
    def store(plane, columns, values):
        target[plane, :, columns] = values.astype(bf16)

    return store


def first_kernel(info, xb, x0, x1, yb, yf, own, p0, p1, p2, p3, w_low, w_high,
                 held, weights, rhs, below, sems, csems, fsems):
    @pl.when(info[info_member] == 0)
    def _():
        layers = Layers(info, (xb, x0, x1), (yb, yf), held, weights, fsems, csems)
        fields = (own, (p0, p1, p2, p3), rhs, sems)
        layers.start(0, *fields)
        layers.wait(0, *fields)
        layers.ready(0, 1)
        layers.start(1, *fields)
        zero = reduced(rhs, info, 0, weights, lambda plane, rows: bf16(0.0))
        layers.apply(0, zero, below, round_into(w_low), (0,))
        layers.wait(1, *fields)
        one = reduced(rhs, info, 1, weights, lambda plane, rows: w_low[plane, rows])
        layers.apply(1, one, below, round_into(w_high), (0, 1))


def last_kernel(info, xb, x0, x1, yb, yf, own, p0, p1, p2, p3, arrived, field, back,
                held, weights, rhs, forward, below, sems, csems, fsems):
    @pl.when(info[info_member] == 1)
    def _():
        layers = Layers(info, (xb, x0, x1), (yb, yf), held, weights, fsems, csems)
        fields = (own, (p0, p1, p2, p3), rhs, sems)
        layers.start(0, *fields)
        layers.wait(0, *fields)
        layers.ready(0, 1)
        layers.start(1, *fields)
        low, high = field.at[0], field.at[1]
        two = reduced(rhs, info, 0, weights, lambda plane, rows: arrived[plane, rows])
        layers.apply(0, two, below, round_into(forward), (0,))
        layers.wait(1, *fields)
        three = reduced(rhs, info, 1, weights, lambda plane, rows: forward[plane, rows])
        layers.apply(1, three, below, round_into(high), (0, 1))
        layers.apply(0, sent(weights, 1, high), below, subtract_into(low, forward), ())
        last = sent(weights, 0, low)
        for plane in range(2):
            for rows in row_chunks(weights.shape[1], 256):
                back[plane, rows] = last(plane, rows)


def back_kernel(info, xb, x0, x1, yb, yf, w_low, w_high, arrived, field,
                p0, p1, p2, p3, held, weights, kept, below, csems, fsems, osems):
    def start_pieces(source, slot):
        for index, piece in enumerate((p0, p1, p2, p3)):
            height = piece.shape[1]
            half = info[info_piece + 2 * index + 1]
            rows = pl.ds(pl.multiple_of(half * height, height), height)

            @pl.when(info[info_piece + 2 * index] == slot)
            def _():
                pltpu.make_async_copy(source.at[slot, :, rows, :], piece, osems.at[index]).start()

    @pl.when(info[info_member] == 0)
    def _():
        layers = Layers(info, (xb, x0, x1), (yb, yf), held, weights, fsems, csems)
        layers.start_y(1)
        layers.start_x(1)
        layers.ready(1, 1)
        layers.start_y(0, False)
        layers.start_x(0, False)
        low, high = kept.at[0], kept.at[1]
        layers.apply(
            1, lambda plane, rows: arrived[plane, rows], below, subtract_into(high, w_high), (0,)
        )
        start_pieces(kept, 1)
        layers.ready_weights(1)
        layers.apply(0, sent(weights, 1, high), below, subtract_into(low, w_low), (0, 1))
        start_pieces(kept, 0)

    @pl.when(info[info_member] != 0)
    def _():
        start_pieces(field, 1)
        start_pieces(field, 0)

    for index, piece in enumerate((p0, p1, p2, p3)):
        part = kept.at[0, :, pl.ds(0, piece.shape[1]), :]
        pltpu.make_async_copy(part, piece, osems.at[index]).wait()


def on_device(background, src_pos, coupling, x_factor, y_factor):
    px_count = lax.axis_size("px")
    sec_index, own_x, own_y = (lax.axis_index(axis) for axis in ("sec", "px", "py"))
    group, member = sec_index // 2, sec_index % 2
    groups = lax.axis_size("sec") // 2
    order = y_factor.shape[3]
    field = background[:, 0]
    rows_here = field.shape[1]
    height = x_factor.shape[2]
    params = pltpu.CompilerParams(vmem_limit_bytes=vmem_bytes)
    rounds = [(a, b) for a in range(groups) for b in range(px_count)]

    def pairs(a, b):
        return [
            ((2 * x + c) * px_count + y, (2 * ((c + a) % 2) + x) * px_count + (y + b) % px_count)
            for x in range(groups)
            for c in range(2)
            for y in range(px_count)
            if (a, b, x) != (0, 0, c)
        ]

    def back_pairs(a, b):
        return [(target, source) for source, target in pairs(a, b)]

    own_source = src_pos[own_y * groups * px_count + group * px_count + own_x]
    plane_cells = x_factor.shape[3] * order
    layer = own_source // plane_cells
    remainder = own_source % plane_cells
    py_count = lax.axis_size("py")
    entries = [
        jnp.where(layer // 2 == member, layer % 2, -1),
        remainder // order,
        remainder % order,
        member,
    ]
    for a, b in rounds:
        entries += [(group + a) % 2, (own_x - b) % px_count]
    entries += [group, (group + 1) % 2, own_x, (own_x + 1) % 2]
    entries += [group == member]
    info = jnp.stack([jnp.asarray(entry, jnp.int32) for entry in entries])

    sends_to = jnp.stack(
        [((member + a) % 2) * px_count + (own_x + b) % px_count for a, b in rounds]
        + [group == member]
    ).astype(jnp.int32)
    piece_shape = jax.ShapeDtypeStruct((2, rows_here, order), bf16)
    shard = jnp.concatenate([x_factor[0], y_factor[0]], axis=0)
    blocks = jnp.broadcast_to(shard[None], (py_count,) + shard.shape)
    packed = pl.pallas_call(
        pack_kernel,
        out_shape=[piece_shape] * len(rounds),
        in_specs=[in_smem, anywhere],
        out_specs=[in_vmem] * len(rounds),
        scratch_shapes=[pltpu.SemaphoreType.DMA((len(rounds),))],
        compiler_params=params,
    )(sends_to, field)
    pieces = [
        lax.ppermute(piece, ("sec", "px"), pairs(a, b)) for piece, (a, b) in zip(packed, rounds)
    ]
    blocks = lax.all_to_all(blocks, "py", split_axis=0, concat_axis=0, tiled=True)

    column_shape = jax.ShapeDtypeStruct((2 * rows_here + rows_here // 2, order), bf16)
    x_column, y_column = pl.pallas_call(
        column_kernel,
        out_shape=[column_shape] * 2,
        in_specs=[anywhere] * 6,
        out_specs=[in_vmem] * 2,
        scratch_shapes=[
            pltpu.SemaphoreType.DMA((py_count, 2, 2)),
            pltpu.SemaphoreType.DMA((2,)),
        ],
        compiler_params=params,
    )(blocks, coupling[0], *pieces)

    def across(block, a):
        return lax.ppermute(block, ("sec", "px"), pairs(a, 0))

    def aside(block):
        return lax.ppermute(block, "px", [(y, (y + 1) % 2) for y in range(2)])

    y_near = [across(y_column, a) for a in range(2)]
    x_aside = aside(x_column)
    x_both, y_both = pl.pallas_call(
        both_kernel,
        out_shape=[jax.ShapeDtypeStruct((2,) + column_shape.shape, bf16)] * 2,
        in_specs=[in_smem] + [anywhere] * 5,
        out_specs=[in_vmem] * 2,
        scratch_shapes=[pltpu.SemaphoreType.DMA((4,))],
        compiler_params=params,
    )(info, x_column, x_aside, y_column, *y_near)
    y_far = aside(y_both)
    x_across = [across(x_both, a) for a in range(2)]
    factors = [x_both, *x_across, y_both, y_far]

    full_shape = jax.ShapeDtypeStruct((2, order, order), bf16)
    factor_scratch = pltpu.VMEM((2, 2, order, 2 * order), bf16)
    weight_scratch = pltpu.VMEM((2, order, order), bf16)
    field_scratch = pltpu.VMEM((2, 2, order, order), bf16)
    below_scratch = pltpu.VMEM((2 * order, 2 * order), bf16)
    factor_sems = pltpu.SemaphoreType.DMA((2, 2, 2, 2))
    weight_sems = pltpu.SemaphoreType.DMA((2, 2, 2))
    field_sems = pltpu.SemaphoreType.DMA((2, 2))
    solve_flops = 16 * order**3
    fields = (packed[0], *pieces)

    def cost(solves):
        return pl.CostEstimate(
            flops=solves * solve_flops, bytes_accessed=16 * order * order * 2, transcendentals=0
        )

    w_low, w_high = pl.pallas_call(
        first_kernel,
        out_shape=[full_shape] * 2,
        in_specs=[in_smem] + [anywhere] * 10,
        out_specs=[in_vmem] * 2,
        scratch_shapes=[
            factor_scratch,
            weight_scratch,
            field_scratch,
            below_scratch,
            field_sems,
            weight_sems,
            factor_sems,
        ],
        compiler_params=params,
        cost_estimate=cost(2),
    )(info, *factors, *fields)

    up = [(2 * x, 2 * x + 1) for x in range(groups)]
    incoming = lax.ppermute(w_high, "sec", up)
    solved, back = pl.pallas_call(
        last_kernel,
        out_shape=[jax.ShapeDtypeStruct((2, 2, order, order), bf16), full_shape],
        in_specs=[in_smem] + [anywhere] * 10 + [in_vmem],
        out_specs=[in_vmem] * 2,
        scratch_shapes=[
            factor_scratch,
            weight_scratch,
            field_scratch,
            pltpu.VMEM((2, order, order), bf16),
            below_scratch,
            field_sems,
            weight_sems,
            factor_sems,
        ],
        compiler_params=params,
        cost_estimate=cost(3),
    )(info, *factors, *fields, incoming)

    down = [(target, source) for source, target in up]
    incoming = lax.ppermute(back, "sec", down)
    results = pl.pallas_call(
        back_kernel,
        out_shape=[piece_shape] * len(rounds),
        in_specs=[in_smem] + [anywhere] * 5 + [in_vmem] * 3 + [anywhere],
        out_specs=[anywhere] * len(rounds),
        scratch_shapes=[
            factor_scratch,
            weight_scratch,
            field_scratch,
            below_scratch,
            weight_sems,
            factor_sems,
            pltpu.SemaphoreType.DMA((len(rounds),)),
        ],
        compiler_params=params,
        cost_estimate=cost(2),
    )(info, *factors, w_low, w_high, incoming, solved)
    received = [
        lax.ppermute(piece, ("sec", "px"), back_pairs(a, b)) for piece, (a, b) in zip(results, rounds)
    ]
    output = pl.pallas_call(
        unpack_kernel,
        out_shape=jax.ShapeDtypeStruct(field.shape, bf16),
        in_specs=[in_smem] + [anywhere] * (len(rounds) + 1),
        out_specs=anywhere,
        scratch_shapes=[pltpu.SemaphoreType.DMA((len(rounds),))],
        compiler_params=params,
    )(sends_to, results[0], *received)
    return output[:, None]


def chip_plan_fits(mesh):
    return mesh.shape["sec"] == 4 and mesh.shape["px"] == 2 and mesh.shape["py"] == 4


def solution(mesh):
    placed = (
        P(None, "sec", "px", "py"),
        P(),
        P("sec", "px", None),
        P("sec", None, ("px", "py"), None),
        P("sec", None, ("px", "py"), None),
    )
    return jax.shard_map(
        on_device if chip_plan_fits(mesh) else on_device_by_layer,
        mesh=mesh,
        in_specs=placed,
        out_specs=P(None, "sec", "px", "py"),
        check_vma=False,
    )
```

```python
import functools

import jax
import jax.numpy as jnp
from jax import lax
from jax.experimental import pallas as pl
from jax.experimental.pallas import tpu as pltpu
from jax.sharding import PartitionSpec as P

source_amplitude = 8.0
vmem_bytes = 32 * 1024 * 1024
bf16 = jnp.bfloat16
f32 = jnp.float32
anywhere = pl.BlockSpec(memory_space=pl.ANY)
in_smem = pl.BlockSpec(memory_space=pltpu.SMEM)
in_vmem = pl.BlockSpec(memory_space=pltpu.VMEM)

info_member, info_piece, info_slot, info_half, info_block, info_self = 3, 4, 12, 14, 16, 20


def shifted(x, axis, by):
    peers = lax.axis_size(axis)
    pairs = [(i, i + by) for i in range(peers) if 0 <= i + by < peers]
    return lax.ppermute(x, axis, pairs)


def complex_block(factor):
    upper = jnp.concatenate([factor[0], -factor[1]], axis=1)
    lower = jnp.concatenate([factor[1], factor[0]], axis=1)
    return jnp.concatenate([upper, lower], axis=0)


def y_transform(real_turned, imag_turned, field_in):
    real_part = jnp.dot(field_in[0], real_turned, preferred_element_type=jnp.float32) - jnp.dot(
        field_in[1], imag_turned, preferred_element_type=jnp.float32
    )
    imag_part = jnp.dot(field_in[0], imag_turned, preferred_element_type=jnp.float32) + jnp.dot(
        field_in[1], real_turned, preferred_element_type=jnp.float32
    )
    return jnp.stack([real_part, imag_part]).astype(jnp.bfloat16)


def x_transform(x_block, field_in):
    planes, rows_all, width = field_in.shape
    output = jnp.dot(
        x_block, field_in.reshape(planes * rows_all, width), preferred_element_type=jnp.float32
    )
    return output.astype(jnp.bfloat16).reshape(planes, rows_all, width)


def scale_rows(field_in, weights, width):
    planes, rows_here, merged = field_in.shape
    spread = field_in.astype(jnp.float32).reshape(planes, rows_here, merged // width, width)
    return (spread * weights.astype(jnp.float32)[None, :, None, :]).reshape(
        planes, rows_here, merged
    )


def pick_batch(field, batch_count, batch_index):
    planes, rows_here, merged = field.shape
    split_field = field.reshape(planes, rows_here, batch_count, merged // batch_count)
    return lax.dynamic_index_in_dim(split_field, batch_index, 2, keepdims=False)


def place_batch(field, piece, batch_count, batch_index):
    planes, rows_here, merged = field.shape
    split_field = field.reshape(planes, rows_here, batch_count, merged // batch_count)
    shaped = piece.reshape(planes, rows_here, 1, merged // batch_count)
    updated = lax.dynamic_update_slice_in_dim(split_field, shaped, batch_index, 2)
    return updated.reshape(planes, rows_here, merged)


def on_device_by_layer(background, src_pos, coupling, x_factor, y_factor):
    source_count = src_pos.shape[0]
    sec_count = lax.axis_size("sec")
    sec_index = lax.axis_index("sec")
    grid_y = lax.axis_size("py")
    own_x = lax.axis_index("px")
    own_y = lax.axis_index("py")
    local_sources = source_count // grid_y
    x_pieces, y_pieces = (
        lax.all_gather(x_factor[0], ("px", "py"), axis=1, tiled=True),
        lax.all_gather(y_factor[0], ("px", "py"), axis=1, tiled=True),
    )
    x_block = complex_block(x_pieces)
    real_turned = y_pieces[0].T
    imag_turned = y_pieces[1].T
    local_field = background[:, 0]
    local_weights = coupling[0]
    rows_here = local_field.shape[1]
    full_cols = y_factor.shape[3]
    plane_cells = x_factor.shape[3] * full_cols
    own_sources = lax.dynamic_slice_in_dim(src_pos, own_y * local_sources, local_sources)
    layer_of = own_sources // plane_cells
    remainder = own_sources % plane_cells
    row_of = remainder // full_cols
    column_of = remainder % full_cols
    row_start = own_x * rows_here
    row_hit = row_of[None, :] == row_start + jnp.arange(rows_here, dtype=jnp.int32)[:, None]
    col_hit = column_of[:, None] == jnp.arange(full_cols, dtype=jnp.int32)[None, :]
    layer_hit = layer_of == sec_index
    delta = (row_hit[:, :, None] & col_hit[None, :, :] & layer_hit[None, :, None]).astype(
        jnp.float32
    )
    delta = (delta * source_amplitude).reshape(rows_here, local_sources * full_cols)
    real_rhs = local_field[0].astype(jnp.float32) + delta
    rhs_field = jnp.stack([real_rhs, local_field[1].astype(jnp.float32)])

    def apply_front(field_in):
        turned = y_transform(real_turned, imag_turned, field_in)
        line_field = lax.all_to_all(turned, "px", split_axis=2, concat_axis=1, tiled=True)
        finished = x_transform(x_block, line_field)
        return lax.all_to_all(finished, "px", split_axis=1, concat_axis=2, tiled=True)

    forward_field = jnp.zeros(local_field.shape, jnp.bfloat16)
    outgoing = pick_batch(forward_field, sec_count, 0)
    for step in range(2 * sec_count - 1):
        incoming = shifted(outgoing, "sec", 1)
        batch_index = step - sec_index
        active = (batch_index >= 0) & (batch_index < sec_count)
        clamped = jnp.clip(batch_index, 0, sec_count - 1)
        rhs_batch = pick_batch(rhs_field, sec_count, clamped)
        reduced = (rhs_batch - scale_rows(incoming, local_weights, full_cols)).astype(jnp.bfloat16)
        candidate = apply_front(reduced)
        previous = pick_batch(forward_field, sec_count, clamped)
        kept = jnp.where(active, candidate, previous)
        forward_field = place_batch(forward_field, kept, sec_count, clamped)
        outgoing = candidate
    sweep_field = forward_field
    for step in range(2 * sec_count - 2):
        send_index = jnp.clip(step - (sec_count - 1 - sec_index), 0, sec_count - 1)
        own_batch = pick_batch(sweep_field, sec_count, send_index)
        sent_field = scale_rows(own_batch, local_weights, full_cols).astype(jnp.bfloat16)
        incoming = shifted(sent_field, "sec", -1)
        batch_index = step - (sec_count - 2 - sec_index)
        active = (batch_index >= 0) & (batch_index < sec_count) & (sec_index <= sec_count - 2)
        clamped = jnp.clip(batch_index, 0, sec_count - 1)
        solved = apply_front(incoming)
        forward_batch = pick_batch(forward_field, sec_count, clamped)
        candidate = (forward_batch.astype(jnp.float32) - solved.astype(jnp.float32)).astype(
            jnp.bfloat16
        )
        previous = pick_batch(sweep_field, sec_count, clamped)
        kept = jnp.where(active, candidate, previous)
        sweep_field = place_batch(sweep_field, kept, sec_count, clamped)
    return sweep_field[:, None]


def start_all(copies):
    for copy in copies:
        copy.start()


def wait_all(copies):
    for copy in copies:
        copy.wait()


def row_chunks(order, step):
    step = min(step, order)
    return [slice(first, first + step) for first in range(0, order, step)]


class Either:
    def __init__(self, flag, own, received, target, sem):
        self.flag = flag
        self.own = pltpu.make_async_copy(own, target, sem)
        self.received = pltpu.make_async_copy(received, target, sem)

    def start(self):
        @pl.when(self.flag != 0)
        def _():
            self.own.start()

        @pl.when(self.flag == 0)
        def _():
            self.received.start()

    def wait(self):
        self.received.wait()


def pack_kernel(place, field, coupling, *rest):
    pieces, (sems, csems) = rest[:-2], rest[-2:]
    rows_here = field.shape[1]
    height = pieces[0].shape[0] - 2 * rows_here
    own = pl.ds(pl.multiple_of(place[len(pieces)] * height, height), height)
    copies = []
    for index, piece in enumerate(pieces):
        width = piece.shape[1]
        offset = pl.multiple_of(place[index] * width, width)
        for plane in range(2):
            copies.append(
                pltpu.make_async_copy(
                    field.at[plane, :, pl.ds(offset, width)],
                    piece.at[pl.ds(plane * rows_here, rows_here)],
                    sems.at[index, plane],
                )
            )
        copies.append(
            pltpu.make_async_copy(
                coupling.at[own], piece.at[pl.ds(2 * rows_here, height)], csems.at[index]
            )
        )
    start_all(copies)
    wait_all(copies)


def unpack_kernel(place, own, *rest):
    pieces, field, sems = rest[:-2], rest[-2], rest[-1]
    copies = []
    for index, piece in enumerate(pieces):
        width = piece.shape[2]
        offset = pl.multiple_of(place[index] * width, width)
        target = field.at[:, :, pl.ds(offset, width)]
        if index:
            copies.append(pltpu.make_async_copy(piece, target, sems.at[index]))
        else:
            copies.append(Either(place[len(pieces) + 1], own, piece, target, sems.at[index]))
    start_all(copies)
    wait_all(copies)


def column_kernel(info, blocks, own, p0, p1, p2, p3, x_column, y_column, rows_held, sems, csems):
    count, planes, height, order = blocks.shape
    copies = []
    for index in range(count):
        for which, column in enumerate((x_column, y_column)):
            copies.append(
                pltpu.make_async_copy(
                    blocks.at[index, pl.ds(2 * which, 2)],
                    column.at[:, pl.ds(index * height, height), :],
                    sems.at[index, which],
                )
            )
    last = pl.ds(own.shape[0] - height, height)
    copies.append(Either(info[info_self], own.at[last], p0.at[last], rows_held.at[0], csems.at[0]))
    for index, piece in enumerate((p1, p2, p3)):
        copies.append(
            pltpu.make_async_copy(piece.at[last], rows_held.at[index + 1], csems.at[index + 1])
        )
    start_all(copies)
    wait_all(copies)


def both_kernel(info, x_column, x_aside, y_column, y0, y1, rows_next, rows_far, x_both, y_both, sems):
    copies = [
        pltpu.make_async_copy(x_column, x_both.at[0], sems.at[0]),
        pltpu.make_async_copy(x_aside, x_both.at[1], sems.at[1]),
        Either(info[info_self], y_column, y0, y_both.at[0], sems.at[2]),
        pltpu.make_async_copy(y1, y_both.at[1], sems.at[3]),
    ]
    start_all(copies)
    wait_all(copies)


class Layers:
    def __init__(self, info, x_parts, y_parts, row_blocks, held_x, held_y, weights, sems, csems):
        self.info, self.order = info, held_y.shape[1]
        self.x_parts, self.y_parts, self.row_blocks = x_parts, y_parts, row_blocks
        self.held_x, self.held_y, self.weights = held_x, held_y, weights
        self.sems, self.csems = sems, csems

    def half_rows(self, far):
        height = self.order // 2
        return pl.ds(pl.multiple_of(self.info[info_half + far] * height, height), height)

    def y_copies(self, slot, parts):
        return [
            pltpu.make_async_copy(
                part.at[plane],
                self.held_y.at[slot, self.half_rows(far), pl.ds(plane * self.order, self.order)],
                self.sems.at[slot, far, plane],
            )
            for far, part in enumerate(parts)
            for plane in range(2)
        ]

    def x_copies(self, slot, part):
        height = self.order // 2
        copies = []
        for far in range(2):
            start = self.info[info_half + far] * height
            for index, (plane, lower, right) in enumerate(((0, 0, 0), (1, 0, 1), (1, 1, 0), (0, 1, 1))):
                rows = pl.ds(pl.multiple_of(lower * self.order + start, height), height)
                copies.append(
                    pltpu.make_async_copy(
                        part.at[far, plane],
                        self.held_x.at[slot, rows, pl.ds(right * self.order, self.order)],
                        self.sems.at[slot, far, 2 + index],
                    )
                )
        return copies

    def start_y(self, slot):
        turn = self.info[info_slot + slot]
        start_all(self.y_copies(slot, [part.at[turn] for part in self.y_parts]))

    def start_x(self, slot):
        own, first, second = self.x_parts
        turn, same = self.info[info_slot + slot], self.info[info_self]
        for hit, part in (
            ((turn == 0) & (same != 0), own),
            ((turn == 0) & (same == 0), first),
            (turn == 1, second),
        ):

            @pl.when(hit)
            def _():
                start_all(self.x_copies(slot, part))

    def ready_y(self, slot):
        wait_all(self.y_copies(slot, [part.at[0] for part in self.y_parts]))

    def ready_x(self, slot):
        wait_all(self.x_copies(slot, self.x_parts[0]))
        order = self.order
        self.held_x[slot, :order, order:] = -self.held_x[slot, :order, order:]

    def weight_copies(self, slot):
        height = self.row_blocks[0].shape[1]
        copies = []
        for index, block in enumerate(self.row_blocks):
            for far in range(2):
                turn = 2 * self.info[info_slot + slot] + far
                start = self.info[info_half + far] * (self.order // 2)
                start = start + self.info[info_block + index] * height
                rows = pl.ds(pl.multiple_of(start, height), height)
                copies.append(
                    pltpu.make_async_copy(
                        block.at[turn], self.weights.at[slot, rows, :], self.csems.at[slot, index, far]
                    )
                )
        return copies

    def rhs_copies(self, slot, pair, rhs, sems):
        height = self.order // 2
        return [
            pltpu.make_async_copy(
                piece.at[pl.ds(plane * height, height)],
                rhs.at[slot, plane, self.half_rows(far), :],
                sems.at[slot, far, plane],
            )
            for far, piece in enumerate(pair)
            for plane in range(2)
        ]

    def start_rhs(self, slot, own, pieces, rhs, sems):
        turn, same = self.info[info_slot + slot], self.info[info_self]
        for hit, pair in (
            ((turn == 0) & (same != 0), (own, pieces[1])),
            ((turn == 0) & (same == 0), pieces[:2]),
            (turn == 1, pieces[2:]),
        ):

            @pl.when(hit)
            def _():
                start_all(self.rhs_copies(slot, pair, rhs, sems))

    def start(self, slot, own, pieces, rhs, sems):
        self.start_y(slot)
        self.start_rhs(slot, own, pieces, rhs, sems)
        start_all(self.weight_copies(slot))
        self.start_x(slot)

    def wait(self, slot, own, pieces, rhs, sems):
        wait_all(self.rhs_copies(slot, pieces[:2], rhs, sems))
        wait_all(self.weight_copies(slot))

    def apply(self, slot, source, beside, below, store, fresh):
        order = self.order
        turned = (((1,), (1,)), ((), ()))
        for rows in row_chunks(order, 256):
            further = slice(rows.start + order, rows.stop + order)
            real, imag = source(0, rows), source(1, rows)
            beside[rows, :order] = real
            beside[rows, order:] = -imag
            beside[further, :order] = imag
            beside[further, order:] = real
        for columns in row_chunks(order, 256):
            product = lax.dot_general(
                beside[...], self.held_y[slot, columns], turned, preferred_element_type=f32
            )
            below[:, columns] = product.astype(bf16)
        if fresh:
            self.ready_x(slot)
        for columns in row_chunks(order, 256):
            product = jnp.dot(self.held_x[slot], below[:, columns], preferred_element_type=f32)
            store(0, columns, product[:order])
            store(1, columns, product[order:])


def reduced(rhs, info, slot, weights, incoming):
    def source(plane, rows):
        values = rhs[slot, plane, rows]
        if plane == 0:
            row = lax.broadcasted_iota(jnp.int32, values.shape, 0) + rows.start
            column = lax.broadcasted_iota(jnp.int32, values.shape, 1)
            hit = (row == info[1]) & (column == info[2]) & (info[0] == slot)
            values = values + jnp.where(hit, f32(source_amplitude), f32(0.0)).astype(bf16)
        return values - weights[slot, rows] * incoming(plane, rows)

    return source


def sent(weights, slot, field):
    return lambda plane, rows: weights[slot, rows] * field[plane, rows]


def subtract_into(target, forward):
    def store(plane, columns, values):
        target[plane, :, columns] = forward[plane, :, columns] - values.astype(bf16)

    return store


def round_into(target):
    def store(plane, columns, values):
        target[plane, :, columns] = values.astype(bf16)

    return store


def first_kernel(info, xb, x0, x1, yb, yf, c0, c1, c2, c3, own, p0, p1, p2, p3, w_low, w_high,
                 held_x, held_y, weights, rhs, beside, below, sems, csems, fsems):
    @pl.when(info[info_member] == 0)
    def _():
        layers = Layers(info, (xb, x0, x1), (yb, yf), (c0, c1, c2, c3), held_x, held_y, weights, fsems, csems)
        fields = (own, (p0, p1, p2, p3), rhs, sems)
        layers.start(0, *fields)
        layers.wait(0, *fields)
        layers.ready_y(0)
        layers.start(1, *fields)
        zero = reduced(rhs, info, 0, weights, lambda plane, rows: bf16(0.0))
        layers.apply(0, zero, beside, below, round_into(w_low), True)
        layers.wait(1, *fields)
        one = reduced(rhs, info, 1, weights, lambda plane, rows: w_low[plane, rows])
        layers.ready_y(1)
        layers.apply(1, one, beside, below, round_into(w_high), True)


def last_kernel(info, xb, x0, x1, yb, yf, c0, c1, c2, c3, own, p0, p1, p2, p3, arrived, field, back,
                held_x, held_y, weights, rhs, forward, beside, below, sems, csems, fsems):
    @pl.when(info[info_member] == 1)
    def _():
        layers = Layers(info, (xb, x0, x1), (yb, yf), (c0, c1, c2, c3), held_x, held_y, weights, fsems, csems)
        fields = (own, (p0, p1, p2, p3), rhs, sems)
        layers.start(0, *fields)
        layers.wait(0, *fields)
        layers.ready_y(0)
        layers.start(1, *fields)
        low, high = field.at[0], field.at[1]
        two = reduced(rhs, info, 0, weights, lambda plane, rows: arrived[plane, rows])
        layers.apply(0, two, beside, below, round_into(forward), True)
        layers.wait(1, *fields)
        three = reduced(rhs, info, 1, weights, lambda plane, rows: forward[plane, rows])
        layers.ready_y(1)
        layers.apply(1, three, beside, below, round_into(high), True)
        layers.apply(0, sent(weights, 1, high), beside, below, subtract_into(low, forward), False)
        last = sent(weights, 0, low)
        for plane in range(2):
            for rows in row_chunks(weights.shape[1], 256):
                back[plane, rows] = last(plane, rows)


def back_kernel(info, xb, x0, x1, yb, yf, c0, c1, c2, c3, w_low, w_high, arrived, field,
                p0, p1, p2, p3, held_x, held_y, weights, kept, beside, below, csems, fsems, osems):
    def start_pieces(source, slot):
        for index, piece in enumerate((p0, p1, p2, p3)):
            height = piece.shape[1]
            half = info[info_piece + 2 * index + 1]
            rows = pl.ds(pl.multiple_of(half * height, height), height)

            @pl.when(info[info_piece + 2 * index] == slot)
            def _():
                pltpu.make_async_copy(source.at[slot, :, rows, :], piece, osems.at[index]).start()

    @pl.when(info[info_member] == 0)
    def _():
        layers = Layers(info, (xb, x0, x1), (yb, yf), (c0, c1, c2, c3), held_x, held_y, weights, fsems, csems)
        layers.start_y(1)
        layers.start_x(1)
        layers.ready_y(1)
        high_rows = layers.weight_copies(1)
        start_all(high_rows)
        layers.start_y(0)
        layers.start_x(0)
        low, high = kept.at[0], kept.at[1]
        layers.apply(
            1, lambda plane, rows: arrived[plane, rows], beside, below, subtract_into(high, w_high), True
        )
        start_pieces(kept, 1)
        wait_all(high_rows)
        layers.ready_y(0)
        layers.apply(0, sent(weights, 1, high), beside, below, subtract_into(low, w_low), True)
        start_pieces(kept, 0)

    @pl.when(info[info_member] != 0)
    def _():
        start_pieces(field, 1)
        start_pieces(field, 0)

    for index, piece in enumerate((p0, p1, p2, p3)):
        part = kept.at[0, :, pl.ds(0, piece.shape[1]), :]
        pltpu.make_async_copy(part, piece, osems.at[index]).wait()


def on_device(background, src_pos, coupling, x_factor, y_factor):
    px_count = lax.axis_size("px")
    sec_index, own_x, own_y = (lax.axis_index(axis) for axis in ("sec", "px", "py"))
    group, member = sec_index // 2, sec_index % 2
    groups = lax.axis_size("sec") // 2
    order = y_factor.shape[3]
    field = background[:, 0]
    rows_here = field.shape[1]
    height = x_factor.shape[2]
    params = pltpu.CompilerParams(vmem_limit_bytes=vmem_bytes)
    rounds = [(a, b) for a in range(groups) for b in range(px_count)]

    def pairs(a, b):
        return [
            ((2 * x + c) * px_count + y, (2 * ((c + a) % 2) + x) * px_count + (y + b) % px_count)
            for x in range(groups)
            for c in range(2)
            for y in range(px_count)
            if (a, b, x) != (0, 0, c)
        ]

    def back_pairs(a, b):
        return [(target, source) for source, target in pairs(a, b)]

    own_source = src_pos[own_y * groups * px_count + group * px_count + own_x]
    plane_cells = x_factor.shape[3] * order
    layer = own_source // plane_cells
    remainder = own_source % plane_cells
    py_count = lax.axis_size("py")
    entries = [
        jnp.where(layer // 2 == member, layer % 2, -1),
        remainder // order,
        remainder % order,
        member,
    ]
    for a, b in rounds:
        entries += [(group + a) % 2, (own_x - b) % px_count]
    entries += [group, (group + 1) % 2, own_x, (own_x + 1) % 2]
    pair = own_y // 2 * 2
    entries += [own_y, pair + (own_y + 1) % 2, (own_y + 2) % 4, (pair + 2) % 4 + (own_y + 1) % 2]
    entries += [group == member]
    info = jnp.stack([jnp.asarray(entry, jnp.int32) for entry in entries])

    sends_to = jnp.stack(
        [((member + a) % 2) * px_count + (own_x + b) % px_count for a, b in rounds]
        + [own_y, group == member]
    ).astype(jnp.int32)
    piece_shape = jax.ShapeDtypeStruct((2, rows_here, order), bf16)
    shard = jnp.concatenate([x_factor[0], y_factor[0]], axis=0)
    blocks = jnp.broadcast_to(shard[None], (py_count,) + shard.shape)
    packed = pl.pallas_call(
        pack_kernel,
        out_shape=[jax.ShapeDtypeStruct((2 * rows_here + height, order), bf16)] * len(rounds),
        in_specs=[in_smem] + [anywhere] * 2,
        out_specs=[in_vmem] * len(rounds),
        scratch_shapes=[
            pltpu.SemaphoreType.DMA((len(rounds), 2)),
            pltpu.SemaphoreType.DMA((len(rounds),)),
        ],
        compiler_params=params,
    )(sends_to, field, coupling[0])
    pieces = [
        lax.ppermute(piece, ("sec", "px"), pairs(a, b)) for piece, (a, b) in zip(packed, rounds)
    ]
    blocks = lax.all_to_all(blocks, "py", split_axis=0, concat_axis=0, tiled=True)

    column_shape = jax.ShapeDtypeStruct((2, rows_here, order), bf16)
    rows_shape = jax.ShapeDtypeStruct((len(rounds), height, order), bf16)
    x_column, y_column, rows_held = pl.pallas_call(
        column_kernel,
        out_shape=[column_shape, column_shape, rows_shape],
        in_specs=[in_smem] + [anywhere] * 6,
        out_specs=[in_vmem] * 3,
        scratch_shapes=[
            pltpu.SemaphoreType.DMA((py_count, 2)),
            pltpu.SemaphoreType.DMA((len(rounds),)),
        ],
        compiler_params=params,
    )(info, blocks, packed[0], *pieces)

    def across(block, a):
        return lax.ppermute(block, ("sec", "px"), pairs(a, 0))

    def aside(block):
        return lax.ppermute(block, "px", [(y, (y + 1) % 2) for y in range(2)])

    def over_z(block, bit):
        return lax.ppermute(block, "py", [(z, z ^ bit) for z in range(py_count)])

    y_near = [across(y_column, a) for a in range(2)]
    x_aside = aside(x_column)
    rows_next = over_z(rows_held, 1)
    rows_far = over_z(rows_held, 2)
    x_both, y_both = pl.pallas_call(
        both_kernel,
        out_shape=[jax.ShapeDtypeStruct((2,) + column_shape.shape, bf16)] * 2,
        in_specs=[in_smem] + [anywhere] * 7,
        out_specs=[in_vmem] * 2,
        scratch_shapes=[pltpu.SemaphoreType.DMA((4,))],
        compiler_params=params,
    )(info, x_column, x_aside, y_column, *y_near, rows_next, rows_far)
    y_far = aside(y_both)
    x_across = [across(x_both, a) for a in range(2)]
    factors = [x_both, *x_across, y_both, y_far, rows_held, rows_next, rows_far, over_z(rows_next, 2)]

    full_shape = jax.ShapeDtypeStruct((2, order, order), bf16)
    x_scratch = pltpu.VMEM((2, 2 * order, 2 * order), bf16)
    y_scratch = pltpu.VMEM((2, order, 2 * order), bf16)
    beside_scratch = pltpu.VMEM((2 * order, 2 * order), bf16)
    weight_scratch = pltpu.VMEM((2, order, order), bf16)
    field_scratch = pltpu.VMEM((2, 2, order, order), bf16)
    below_scratch = pltpu.VMEM((2 * order, order), bf16)
    factor_sems = pltpu.SemaphoreType.DMA((2, 2, 6))
    weight_sems = pltpu.SemaphoreType.DMA((2, py_count, 2))
    field_sems = pltpu.SemaphoreType.DMA((2, 2, 2))
    solve_flops = 16 * order**3
    fields = (packed[0], *pieces)

    def cost(solves):
        return pl.CostEstimate(
            flops=solves * solve_flops, bytes_accessed=16 * order * order * 2, transcendentals=0
        )

    w_low, w_high = pl.pallas_call(
        first_kernel,
        out_shape=[full_shape] * 2,
        in_specs=[in_smem] + [anywhere] * 14,
        out_specs=[in_vmem] * 2,
        scratch_shapes=[
            x_scratch,
            y_scratch,
            weight_scratch,
            field_scratch,
            beside_scratch,
            below_scratch,
            field_sems,
            weight_sems,
            factor_sems,
        ],
        compiler_params=params,
        cost_estimate=cost(2),
    )(info, *factors, *fields)

    up = [(2 * x, 2 * x + 1) for x in range(groups)]
    incoming = lax.ppermute(w_high, "sec", up)
    solved, back = pl.pallas_call(
        last_kernel,
        out_shape=[jax.ShapeDtypeStruct((2, 2, order, order), bf16), full_shape],
        in_specs=[in_smem] + [anywhere] * 14 + [in_vmem],
        out_specs=[in_vmem] * 2,
        scratch_shapes=[
            x_scratch,
            y_scratch,
            weight_scratch,
            field_scratch,
            pltpu.VMEM((2, order, order), bf16),
            beside_scratch,
            below_scratch,
            field_sems,
            weight_sems,
            factor_sems,
        ],
        compiler_params=params,
        cost_estimate=cost(3),
    )(info, *factors, *fields, incoming)

    down = [(target, source) for source, target in up]
    incoming = lax.ppermute(back, "sec", down)
    results = pl.pallas_call(
        back_kernel,
        out_shape=[piece_shape] * len(rounds),
        in_specs=[in_smem] + [anywhere] * 9 + [in_vmem] * 3 + [anywhere],
        out_specs=[anywhere] * len(rounds),
        scratch_shapes=[
            x_scratch,
            y_scratch,
            weight_scratch,
            field_scratch,
            beside_scratch,
            below_scratch,
            weight_sems,
            factor_sems,
            pltpu.SemaphoreType.DMA((len(rounds),)),
        ],
        compiler_params=params,
        cost_estimate=cost(2),
    )(info, *factors, w_low, w_high, incoming, solved)
    received = [
        lax.ppermute(piece, ("sec", "px"), back_pairs(a, b)) for piece, (a, b) in zip(results, rounds)
    ]
    output = pl.pallas_call(
        unpack_kernel,
        out_shape=jax.ShapeDtypeStruct(field.shape, bf16),
        in_specs=[in_smem] + [anywhere] * (len(rounds) + 1),
        out_specs=in_vmem,
        scratch_shapes=[pltpu.SemaphoreType.DMA((len(rounds),))],
        compiler_params=params,
    )(sends_to, results[0], *received)
    return output[:, None]


def chip_plan_fits(mesh):
    return mesh.shape["sec"] == 4 and mesh.shape["px"] == 2 and mesh.shape["py"] == 4


def solution(mesh):
    placed = (
        P(None, "sec", "px", "py"),
        P(),
        P("sec", "px", None),
        P("sec", None, ("px", "py"), None),
        P("sec", None, ("px", "py"), None),
    )
    return jax.shard_map(
        on_device if chip_plan_fits(mesh) else on_device_by_layer,
        mesh=mesh,
        in_specs=placed,
        out_specs=P(None, "sec", "px", "py"),
        check_vma=False,
    )
```

```python
import functools

import jax
import jax.numpy as jnp
from jax import lax
from jax.experimental import pallas as pl
from jax.experimental.pallas import tpu as pltpu
from jax.sharding import PartitionSpec as P

source_amplitude = 8.0
vmem_bytes = 32 * 1024 * 1024
bf16 = jnp.bfloat16
f32 = jnp.float32
anywhere = pl.BlockSpec(memory_space=pl.ANY)
in_smem = pl.BlockSpec(memory_space=pltpu.SMEM)
in_vmem = pl.BlockSpec(memory_space=pltpu.VMEM)

info_member, info_piece, info_slot, info_half, info_block, info_self = 3, 4, 12, 14, 16, 20


def shifted(x, axis, by):
    peers = lax.axis_size(axis)
    pairs = [(i, i + by) for i in range(peers) if 0 <= i + by < peers]
    return lax.ppermute(x, axis, pairs)


def complex_block(factor):
    upper = jnp.concatenate([factor[0], -factor[1]], axis=1)
    lower = jnp.concatenate([factor[1], factor[0]], axis=1)
    return jnp.concatenate([upper, lower], axis=0)


def y_transform(real_turned, imag_turned, field_in):
    real_part = jnp.dot(field_in[0], real_turned, preferred_element_type=jnp.float32) - jnp.dot(
        field_in[1], imag_turned, preferred_element_type=jnp.float32
    )
    imag_part = jnp.dot(field_in[0], imag_turned, preferred_element_type=jnp.float32) + jnp.dot(
        field_in[1], real_turned, preferred_element_type=jnp.float32
    )
    return jnp.stack([real_part, imag_part]).astype(jnp.bfloat16)


def x_transform(x_block, field_in):
    planes, rows_all, width = field_in.shape
    output = jnp.dot(
        x_block, field_in.reshape(planes * rows_all, width), preferred_element_type=jnp.float32
    )
    return output.astype(jnp.bfloat16).reshape(planes, rows_all, width)


def scale_rows(field_in, weights, width):
    planes, rows_here, merged = field_in.shape
    spread = field_in.astype(jnp.float32).reshape(planes, rows_here, merged // width, width)
    return (spread * weights.astype(jnp.float32)[None, :, None, :]).reshape(
        planes, rows_here, merged
    )


def pick_batch(field, batch_count, batch_index):
    planes, rows_here, merged = field.shape
    split_field = field.reshape(planes, rows_here, batch_count, merged // batch_count)
    return lax.dynamic_index_in_dim(split_field, batch_index, 2, keepdims=False)


def place_batch(field, piece, batch_count, batch_index):
    planes, rows_here, merged = field.shape
    split_field = field.reshape(planes, rows_here, batch_count, merged // batch_count)
    shaped = piece.reshape(planes, rows_here, 1, merged // batch_count)
    updated = lax.dynamic_update_slice_in_dim(split_field, shaped, batch_index, 2)
    return updated.reshape(planes, rows_here, merged)


def on_device_by_layer(background, src_pos, coupling, x_factor, y_factor):
    source_count = src_pos.shape[0]
    sec_count = lax.axis_size("sec")
    sec_index = lax.axis_index("sec")
    grid_y = lax.axis_size("py")
    own_x = lax.axis_index("px")
    own_y = lax.axis_index("py")
    local_sources = source_count // grid_y
    x_pieces, y_pieces = (
        lax.all_gather(x_factor[0], ("px", "py"), axis=1, tiled=True),
        lax.all_gather(y_factor[0], ("px", "py"), axis=1, tiled=True),
    )
    x_block = complex_block(x_pieces)
    real_turned = y_pieces[0].T
    imag_turned = y_pieces[1].T
    local_field = background[:, 0]
    local_weights = coupling[0]
    rows_here = local_field.shape[1]
    full_cols = y_factor.shape[3]
    plane_cells = x_factor.shape[3] * full_cols
    own_sources = lax.dynamic_slice_in_dim(src_pos, own_y * local_sources, local_sources)
    layer_of = own_sources // plane_cells
    remainder = own_sources % plane_cells
    row_of = remainder // full_cols
    column_of = remainder % full_cols
    row_start = own_x * rows_here
    row_hit = row_of[None, :] == row_start + jnp.arange(rows_here, dtype=jnp.int32)[:, None]
    col_hit = column_of[:, None] == jnp.arange(full_cols, dtype=jnp.int32)[None, :]
    layer_hit = layer_of == sec_index
    delta = (row_hit[:, :, None] & col_hit[None, :, :] & layer_hit[None, :, None]).astype(
        jnp.float32
    )
    delta = (delta * source_amplitude).reshape(rows_here, local_sources * full_cols)
    real_rhs = local_field[0].astype(jnp.float32) + delta
    rhs_field = jnp.stack([real_rhs, local_field[1].astype(jnp.float32)])

    def apply_front(field_in):
        turned = y_transform(real_turned, imag_turned, field_in)
        line_field = lax.all_to_all(turned, "px", split_axis=2, concat_axis=1, tiled=True)
        finished = x_transform(x_block, line_field)
        return lax.all_to_all(finished, "px", split_axis=1, concat_axis=2, tiled=True)

    forward_field = jnp.zeros(local_field.shape, jnp.bfloat16)
    outgoing = pick_batch(forward_field, sec_count, 0)
    for step in range(2 * sec_count - 1):
        incoming = shifted(outgoing, "sec", 1)
        batch_index = step - sec_index
        active = (batch_index >= 0) & (batch_index < sec_count)
        clamped = jnp.clip(batch_index, 0, sec_count - 1)
        rhs_batch = pick_batch(rhs_field, sec_count, clamped)
        reduced = (rhs_batch - scale_rows(incoming, local_weights, full_cols)).astype(jnp.bfloat16)
        candidate = apply_front(reduced)
        previous = pick_batch(forward_field, sec_count, clamped)
        kept = jnp.where(active, candidate, previous)
        forward_field = place_batch(forward_field, kept, sec_count, clamped)
        outgoing = candidate
    sweep_field = forward_field
    for step in range(2 * sec_count - 2):
        send_index = jnp.clip(step - (sec_count - 1 - sec_index), 0, sec_count - 1)
        own_batch = pick_batch(sweep_field, sec_count, send_index)
        sent_field = scale_rows(own_batch, local_weights, full_cols).astype(jnp.bfloat16)
        incoming = shifted(sent_field, "sec", -1)
        batch_index = step - (sec_count - 2 - sec_index)
        active = (batch_index >= 0) & (batch_index < sec_count) & (sec_index <= sec_count - 2)
        clamped = jnp.clip(batch_index, 0, sec_count - 1)
        solved = apply_front(incoming)
        forward_batch = pick_batch(forward_field, sec_count, clamped)
        candidate = (forward_batch.astype(jnp.float32) - solved.astype(jnp.float32)).astype(
            jnp.bfloat16
        )
        previous = pick_batch(sweep_field, sec_count, clamped)
        kept = jnp.where(active, candidate, previous)
        sweep_field = place_batch(sweep_field, kept, sec_count, clamped)
    return sweep_field[:, None]


def start_all(copies):
    for copy in copies:
        copy.start()


def wait_all(copies):
    for copy in copies:
        copy.wait()


def row_chunks(order, step):
    step = min(step, order)
    return [slice(first, first + step) for first in range(0, order, step)]


class Either:
    def __init__(self, flag, own, received, target, sem):
        self.flag = flag
        self.own = pltpu.make_async_copy(own, target, sem)
        self.received = pltpu.make_async_copy(received, target, sem)

    def start(self):
        @pl.when(self.flag != 0)
        def _():
            self.own.start()

        @pl.when(self.flag == 0)
        def _():
            self.received.start()

    def wait(self):
        self.received.wait()


def pack_kernel(place, field, coupling, *rest):
    pieces, (sems, csems) = rest[:-2], rest[-2:]
    rows_here = field.shape[1]
    height = pieces[0].shape[0] - 2 * rows_here
    own = pl.ds(pl.multiple_of(place[len(pieces)] * height, height), height)
    copies = []
    for index, piece in enumerate(pieces):
        width = piece.shape[1]
        offset = pl.multiple_of(place[index] * width, width)
        for plane in range(2):
            copies.append(
                pltpu.make_async_copy(
                    field.at[plane, :, pl.ds(offset, width)],
                    piece.at[pl.ds(plane * rows_here, rows_here)],
                    sems.at[index, plane],
                )
            )
        copies.append(
            pltpu.make_async_copy(
                coupling.at[own], piece.at[pl.ds(2 * rows_here, height)], csems.at[index]
            )
        )
    start_all(copies)
    wait_all(copies)


def unpack_kernel(place, own, *rest):
    pieces, field, sems = rest[:-2], rest[-2], rest[-1]
    copies = []
    for index, piece in enumerate(pieces):
        width = piece.shape[2]
        offset = pl.multiple_of(place[index] * width, width)
        target = field.at[:, :, pl.ds(offset, width)]
        if index:
            copies.append(pltpu.make_async_copy(piece, target, sems.at[index]))
        else:
            copies.append(Either(place[len(pieces) + 1], own, piece, target, sems.at[index]))
    start_all(copies)
    wait_all(copies)


def column_kernel(info, blocks, own, p0, p1, p2, p3, x_column, y_column, rows_held, sems, csems):
    count, factors, height, width = blocks.shape
    copies = []
    for index in range(count):
        for which, column in enumerate((x_column, y_column)):
            copies.append(
                pltpu.make_async_copy(
                    blocks.at[index, which],
                    column.at[pl.ds(index * height, height)],
                    sems.at[index, which],
                )
            )
    last = pl.ds(own.shape[0] - height, height)
    copies.append(Either(info[info_self], own.at[last], p0.at[last], rows_held.at[0], csems.at[0]))
    for index, piece in enumerate((p1, p2, p3)):
        copies.append(
            pltpu.make_async_copy(piece.at[last], rows_held.at[index + 1], csems.at[index + 1])
        )
    start_all(copies)
    wait_all(copies)


def field_kernel(info, own, p0, p1, p2, p3, rhs, sems):
    height = rhs.shape[2] // 2
    copies = []
    for index, piece in enumerate((p0, p1, p2, p3)):
        slot, half = info[info_piece + 2 * index], info[info_piece + 2 * index + 1]
        rows = pl.ds(pl.multiple_of(half * height, height), height)
        for plane in range(2):
            part = pl.ds(plane * height, height)
            ends = (rhs.at[slot, plane, rows, :], sems.at[index, plane])
            if index:
                copies.append(pltpu.make_async_copy(piece.at[part], *ends))
            else:
                copies.append(Either(info[info_self], own.at[part], piece.at[part], *ends))
    start_all(copies)
    wait_all(copies)


def weight_kernel(info, c0, c1, c2, c3, weights, sems):
    height = c0.shape[1]
    half_height = weights.shape[1] // 2
    copies = []
    for index, block in enumerate((c0, c1, c2, c3)):
        for turn in range(block.shape[0]):
            slot, half = info[info_piece + 2 * turn], info[info_piece + 2 * turn + 1]
            start = half * half_height + info[info_block + index] * height
            rows = pl.ds(pl.multiple_of(start, height), height)
            copies.append(
                pltpu.make_async_copy(
                    block.at[turn], weights.at[slot, rows, :], sems.at[index, turn]
                )
            )
    start_all(copies)
    wait_all(copies)


def both_kernel(info, x_column, x_aside, y_column, y0, y1, rows_next, rows_far, rhs, x_both, y_both,
                sems):
    copies = [
        pltpu.make_async_copy(x_column, x_both.at[0], sems.at[0]),
        pltpu.make_async_copy(x_aside, x_both.at[1], sems.at[1]),
        Either(info[info_self], y_column, y0, y_both.at[0], sems.at[2]),
        pltpu.make_async_copy(y1, y_both.at[1], sems.at[3]),
    ]
    start_all(copies)
    wait_all(copies)


class Layers:
    def __init__(self, info, x_parts, y_parts, held, beside, below, sems):
        self.info, self.order = info, held.shape[1]
        self.x_parts, self.y_parts, self.held = x_parts, y_parts, held
        self.beside, self.below, self.sems = beside, below, sems

    def x_copies(self, slot, part):
        height = self.order // 2
        copies = []
        for far in range(2):
            rows = pl.ds(pl.multiple_of(self.info[info_half + far] * height, height), height)
            copies.append(
                pltpu.make_async_copy(
                    part.at[far], self.held.at[slot, rows], self.sems.at[slot, far]
                )
            )
        return copies

    def start(self, slot):
        own, first, second = self.x_parts
        turn, same = self.info[info_slot + slot], self.info[info_self]
        for hit, part in (
            ((turn == 0) & (same != 0), own),
            ((turn == 0) & (same == 0), first),
            (turn == 1, second),
        ):

            @pl.when(hit)
            def _():
                start_all(self.x_copies(slot, part))

    def apply(self, slot, source, store, fresh):
        order, beside, below = self.order, self.beside, self.below
        turned = (((1,), (1,)), ((), ()))
        turn = self.info[info_slot + slot]
        for rows in row_chunks(order, 256):
            further = slice(rows.start + order, rows.stop + order)
            real, imag = source(0, rows), source(1, rows)
            beside[rows, :order] = real
            beside[rows, order:] = -imag
            beside[further, :order] = imag
            beside[further, order:] = real
        height = order // 2
        for far, part in enumerate(self.y_parts):
            product = lax.dot_general(
                beside[...], part[turn], turned, preferred_element_type=f32
            ).astype(bf16)
            start = self.info[info_half + far] * height
            columns = pl.ds(pl.multiple_of(start, height), height)
            beyond = pl.ds(pl.multiple_of(order + start, height), height)
            below[:order, columns] = product[:order]
            below[:order, beyond] = product[order:]
            below[order:, columns] = -product[order:]
            below[order:, beyond] = product[:order]
        if fresh:
            wait_all(self.x_copies(slot, self.x_parts[0]))
        for plane in range(2):
            for columns in row_chunks(order, 256):
                along = slice(columns.start + plane * order, columns.stop + plane * order)
                store(
                    plane,
                    columns,
                    jnp.dot(self.held[slot], below[:, along], preferred_element_type=f32),
                )


def reduced(rhs, info, slot, weights, incoming):
    def source(plane, rows):
        values = rhs[slot, plane, rows]
        if plane == 0:
            row = lax.broadcasted_iota(jnp.int32, values.shape, 0) + rows.start
            column = lax.broadcasted_iota(jnp.int32, values.shape, 1)
            hit = (row == info[1]) & (column == info[2]) & (info[0] == slot)
            values = values + jnp.where(hit, f32(source_amplitude), f32(0.0)).astype(bf16)
        return values - weights[slot, rows] * incoming(plane, rows)

    return source


def sent(weights, slot, field):
    return lambda plane, rows: weights[slot, rows] * field[plane, rows]


def subtract_into(target, forward):
    def store(plane, columns, values):
        target[plane, :, columns] = forward[plane, :, columns] - values.astype(bf16)

    return store


def round_into(target):
    def store(plane, columns, values):
        target[plane, :, columns] = values.astype(bf16)

    return store


def first_kernel(info, xb, x0, x1, yb, yf, weights, rhs, w_low, w_high, held, beside, below, sems):
    @pl.when(info[info_member] == 0)
    def _():
        layers = Layers(info, (xb, x0, x1), (yb, yf), held, beside, below, sems)
        layers.start(0)
        layers.start(1)
        zero = reduced(rhs, info, 0, weights, lambda plane, rows: bf16(0.0))
        layers.apply(0, zero, round_into(w_low), True)
        one = reduced(rhs, info, 1, weights, lambda plane, rows: w_low[plane, rows])
        layers.apply(1, one, round_into(w_high), True)


def last_kernel(info, xb, x0, x1, yb, yf, weights, rhs, arrived, field, back, forward, held, beside,
                below, sems):
    @pl.when(info[info_member] == 1)
    def _():
        layers = Layers(info, (xb, x0, x1), (yb, yf), held, beside, below, sems)
        layers.start(0)
        layers.start(1)
        low, high = field.at[0], field.at[1]
        two = reduced(rhs, info, 0, weights, lambda plane, rows: arrived[plane, rows])
        layers.apply(0, two, round_into(forward), True)
        three = reduced(rhs, info, 1, weights, lambda plane, rows: forward[plane, rows])
        layers.apply(1, three, round_into(high), True)
        layers.apply(0, sent(weights, 1, high), subtract_into(low, forward), False)
        last = sent(weights, 0, low)
        for plane in range(2):
            for rows in row_chunks(weights.shape[1], 256):
                back[plane, rows] = last(plane, rows)


def back_kernel(info, xb, x0, x1, yb, yf, weights, w_low, w_high, arrived, field, p0, p1, p2, p3,
                kept, held, beside, below, sems, osems):
    def start_pieces(source, slot):
        for index, piece in enumerate((p0, p1, p2, p3)):
            height = piece.shape[1]
            half = info[info_piece + 2 * index + 1]
            rows = pl.ds(pl.multiple_of(half * height, height), height)

            @pl.when(info[info_piece + 2 * index] == slot)
            def _():
                pltpu.make_async_copy(source.at[slot, :, rows, :], piece, osems.at[index]).start()

    @pl.when(info[info_member] == 0)
    def _():
        layers = Layers(info, (xb, x0, x1), (yb, yf), held, beside, below, sems)
        layers.start(1)
        layers.start(0)
        low, high = kept.at[0], kept.at[1]
        layers.apply(
            1, lambda plane, rows: arrived[plane, rows], subtract_into(high, w_high), True
        )
        start_pieces(kept, 1)
        layers.apply(0, sent(weights, 1, high), subtract_into(low, w_low), True)
        start_pieces(kept, 0)

    @pl.when(info[info_member] != 0)
    def _():
        start_pieces(field, 1)
        start_pieces(field, 0)

    for index, piece in enumerate((p0, p1, p2, p3)):
        part = kept.at[0, :, pl.ds(0, piece.shape[1]), :]
        pltpu.make_async_copy(part, piece, osems.at[index]).wait()


def on_device(background, src_pos, coupling, x_factor, y_factor):
    px_count = lax.axis_size("px")
    sec_index, own_x, own_y = (lax.axis_index(axis) for axis in ("sec", "px", "py"))
    group, member = sec_index // 2, sec_index % 2
    groups = lax.axis_size("sec") // 2
    order = y_factor.shape[3]
    field = background[:, 0]
    rows_here = field.shape[1]
    height = x_factor.shape[2]
    params = pltpu.CompilerParams(vmem_limit_bytes=vmem_bytes)
    rounds = [(a, b) for a in range(groups) for b in range(px_count)]

    def pairs(a, b):
        return [
            ((2 * x + c) * px_count + y, (2 * ((c + a) % 2) + x) * px_count + (y + b) % px_count)
            for x in range(groups)
            for c in range(2)
            for y in range(px_count)
            if (a, b, x) != (0, 0, c)
        ]

    def back_pairs(a, b):
        return [(target, source) for source, target in pairs(a, b)]

    own_source = src_pos[own_y * groups * px_count + group * px_count + own_x]
    plane_cells = x_factor.shape[3] * order
    layer = own_source // plane_cells
    remainder = own_source % plane_cells
    py_count = lax.axis_size("py")
    entries = [
        jnp.where(layer // 2 == member, layer % 2, -1),
        remainder // order,
        remainder % order,
        member,
    ]
    for a, b in rounds:
        entries += [(group + a) % 2, (own_x - b) % px_count]
    entries += [group, (group + 1) % 2, own_x, (own_x + 1) % 2]
    pair = own_y // 2 * 2
    entries += [own_y, pair + (own_y + 1) % 2, (own_y + 2) % 4, (pair + 2) % 4 + (own_y + 1) % 2]
    entries += [group == member]
    info = jnp.stack([jnp.asarray(entry, jnp.int32) for entry in entries])

    sends_to = jnp.stack(
        [((member + a) % 2) * px_count + (own_x + b) % px_count for a, b in rounds]
        + [own_y, group == member]
    ).astype(jnp.int32)
    piece_shape = jax.ShapeDtypeStruct((2, rows_here, order), bf16)
    shard = jnp.stack(
        [jnp.concatenate([factor[0, 0], factor[0, 1]], axis=1) for factor in (x_factor, y_factor)]
    )
    blocks = jnp.broadcast_to(shard[None], (py_count,) + shard.shape)
    packed = pl.pallas_call(
        pack_kernel,
        out_shape=[jax.ShapeDtypeStruct((2 * rows_here + height, order), bf16)] * len(rounds),
        in_specs=[in_smem] + [anywhere] * 2,
        out_specs=[in_vmem] * len(rounds),
        scratch_shapes=[
            pltpu.SemaphoreType.DMA((len(rounds), 2)),
            pltpu.SemaphoreType.DMA((len(rounds),)),
        ],
        compiler_params=params,
    )(sends_to, field, coupling[0])
    pieces = [
        lax.ppermute(piece, ("sec", "px"), pairs(a, b)) for piece, (a, b) in zip(packed, rounds)
    ]
    blocks = lax.all_to_all(blocks, "py", split_axis=0, concat_axis=0, tiled=True)

    column_shape = jax.ShapeDtypeStruct((rows_here, 2 * order), bf16)
    rows_shape = jax.ShapeDtypeStruct((len(rounds), height, order), bf16)
    x_column, y_column, rows_held = pl.pallas_call(
        column_kernel,
        out_shape=[column_shape, column_shape, rows_shape],
        in_specs=[in_smem] + [anywhere] * 6,
        out_specs=[in_vmem] * 3,
        scratch_shapes=[
            pltpu.SemaphoreType.DMA((py_count, 2)),
            pltpu.SemaphoreType.DMA((len(rounds),)),
        ],
        compiler_params=params,
    )(info, blocks, packed[0], *pieces)

    def across(block, a):
        return lax.ppermute(block, ("sec", "px"), pairs(a, 0))

    def aside(block):
        return lax.ppermute(block, "px", [(y, (y + 1) % 2) for y in range(2)])

    def over_z(block, bit):
        return lax.ppermute(block, "py", [(z, z ^ bit) for z in range(py_count)])

    y_near = [across(y_column, a) for a in range(2)]
    x_aside = aside(x_column)
    rows_next = over_z(rows_held, 1)
    rows_far = over_z(rows_held, 2)
    full_shape = jax.ShapeDtypeStruct((2, order, order), bf16)
    double_shape = jax.ShapeDtypeStruct((2, 2, order, order), bf16)
    rhs = pl.pallas_call(
        field_kernel,
        out_shape=double_shape,
        in_specs=[in_smem] + [anywhere] * 5,
        out_specs=in_vmem,
        scratch_shapes=[pltpu.SemaphoreType.DMA((len(rounds), 2))],
        compiler_params=params,
    )(info, packed[0], *pieces)
    x_both, y_both = pl.pallas_call(
        both_kernel,
        out_shape=[jax.ShapeDtypeStruct((2,) + column_shape.shape, bf16)] * 2,
        in_specs=[in_smem] + [anywhere] * 8,
        out_specs=[in_vmem] * 2,
        scratch_shapes=[pltpu.SemaphoreType.DMA((4,))],
        compiler_params=params,
    )(info, x_column, x_aside, y_column, *y_near, rows_next, rows_far, rhs)
    y_far = aside(y_both)
    x_across = [across(x_both, a) for a in range(2)]
    weights = pl.pallas_call(
        weight_kernel,
        out_shape=full_shape,
        in_specs=[in_smem] + [anywhere] * 4,
        out_specs=in_vmem,
        scratch_shapes=[pltpu.SemaphoreType.DMA((4, len(rounds)))],
        compiler_params=params,
    )(info, rows_held, rows_next, rows_far, over_z(rows_next, 2))
    layers = (info, x_both, *x_across, y_both, y_far, weights)
    layer_specs = [in_smem] + [anywhere] * 3 + [in_vmem] * 3
    solver_scratch = [
        pltpu.VMEM((2, order, 2 * order), bf16),
        pltpu.VMEM((2 * order, 2 * order), bf16),
        pltpu.VMEM((2 * order, 2 * order), bf16),
        pltpu.SemaphoreType.DMA((2, 2)),
    ]

    def cost(solves):
        return pl.CostEstimate(
            flops=solves * 16 * order**3, bytes_accessed=16 * order**2 * 2, transcendentals=0
        )

    w_low, w_high = pl.pallas_call(
        first_kernel,
        out_shape=[full_shape] * 2,
        in_specs=layer_specs + [in_vmem],
        out_specs=[in_vmem] * 2,
        scratch_shapes=solver_scratch,
        compiler_params=params,
        cost_estimate=cost(2),
    )(*layers, rhs)

    up = [(2 * x, 2 * x + 1) for x in range(groups)]
    incoming = lax.ppermute(w_high, "sec", up)
    solved, back = pl.pallas_call(
        last_kernel,
        out_shape=[double_shape, full_shape],
        in_specs=layer_specs + [in_vmem] * 2,
        out_specs=[in_vmem] * 2,
        scratch_shapes=[pltpu.VMEM((2, order, order), bf16)] + solver_scratch,
        compiler_params=params,
        cost_estimate=cost(3),
    )(*layers, rhs, incoming)

    down = [(target, source) for source, target in up]
    incoming = lax.ppermute(back, "sec", down)
    results = pl.pallas_call(
        back_kernel,
        out_shape=[piece_shape] * len(rounds),
        in_specs=layer_specs + [in_vmem] * 3 + [anywhere],
        out_specs=[anywhere] * len(rounds),
        scratch_shapes=[pltpu.VMEM((2, 2, order, order), bf16)]
        + solver_scratch
        + [pltpu.SemaphoreType.DMA((len(rounds),))],
        compiler_params=params,
        cost_estimate=cost(2),
    )(*layers, w_low, w_high, incoming, solved)
    received = [
        lax.ppermute(piece, ("sec", "px"), back_pairs(a, b)) for piece, (a, b) in zip(results, rounds)
    ]
    output = pl.pallas_call(
        unpack_kernel,
        out_shape=jax.ShapeDtypeStruct(field.shape, bf16),
        in_specs=[in_smem] + [anywhere] * (len(rounds) + 1),
        out_specs=in_vmem,
        scratch_shapes=[pltpu.SemaphoreType.DMA((len(rounds),))],
        compiler_params=params,
    )(sends_to, results[0], *received)
    return output[:, None]


def chip_plan_fits(mesh):
    return mesh.shape["sec"] == 4 and mesh.shape["px"] == 2 and mesh.shape["py"] == 4


def solution(mesh):
    placed = (
        P(None, "sec", "px", "py"),
        P(),
        P("sec", "px", None),
        P("sec", None, ("px", "py"), None),
        P("sec", None, ("px", "py"), None),
    )
    return jax.shard_map(
        on_device if chip_plan_fits(mesh) else on_device_by_layer,
        mesh=mesh,
        in_specs=placed,
        out_specs=P(None, "sec", "px", "py"),
        check_vma=False,
    )
```

```python
import functools

import jax
import jax.numpy as jnp
from jax import lax
from jax.experimental import pallas as pl
from jax.experimental.pallas import tpu as pltpu
from jax.sharding import PartitionSpec as P

source_amplitude = 8.0
vmem_bytes = 32 * 1024 * 1024
bf16 = jnp.bfloat16
f32 = jnp.float32
anywhere = pl.BlockSpec(memory_space=pl.ANY)
in_hbm = pl.BlockSpec(memory_space=pltpu.HBM)
in_smem = pl.BlockSpec(memory_space=pltpu.SMEM)
in_vmem = pl.BlockSpec(memory_space=pltpu.VMEM)

info_member, info_piece, info_slot, info_half, info_block, info_self = 3, 4, 12, 14, 16, 20


def shifted(x, axis, by):
    peers = lax.axis_size(axis)
    pairs = [(i, i + by) for i in range(peers) if 0 <= i + by < peers]
    return lax.ppermute(x, axis, pairs)


def complex_block(factor):
    upper = jnp.concatenate([factor[0], -factor[1]], axis=1)
    lower = jnp.concatenate([factor[1], factor[0]], axis=1)
    return jnp.concatenate([upper, lower], axis=0)


def y_transform(real_turned, imag_turned, field_in):
    real_part = jnp.dot(field_in[0], real_turned, preferred_element_type=jnp.float32) - jnp.dot(
        field_in[1], imag_turned, preferred_element_type=jnp.float32
    )
    imag_part = jnp.dot(field_in[0], imag_turned, preferred_element_type=jnp.float32) + jnp.dot(
        field_in[1], real_turned, preferred_element_type=jnp.float32
    )
    return jnp.stack([real_part, imag_part]).astype(jnp.bfloat16)


def x_transform(x_block, field_in):
    planes, rows_all, width = field_in.shape
    output = jnp.dot(
        x_block, field_in.reshape(planes * rows_all, width), preferred_element_type=jnp.float32
    )
    return output.astype(jnp.bfloat16).reshape(planes, rows_all, width)


def scale_rows(field_in, weights, width):
    planes, rows_here, merged = field_in.shape
    spread = field_in.astype(jnp.float32).reshape(planes, rows_here, merged // width, width)
    return (spread * weights.astype(jnp.float32)[None, :, None, :]).reshape(
        planes, rows_here, merged
    )


def pick_batch(field, batch_count, batch_index):
    planes, rows_here, merged = field.shape
    split_field = field.reshape(planes, rows_here, batch_count, merged // batch_count)
    return lax.dynamic_index_in_dim(split_field, batch_index, 2, keepdims=False)


def place_batch(field, piece, batch_count, batch_index):
    planes, rows_here, merged = field.shape
    split_field = field.reshape(planes, rows_here, batch_count, merged // batch_count)
    shaped = piece.reshape(planes, rows_here, 1, merged // batch_count)
    updated = lax.dynamic_update_slice_in_dim(split_field, shaped, batch_index, 2)
    return updated.reshape(planes, rows_here, merged)


def on_device_by_layer(background, src_pos, coupling, x_factor, y_factor):
    source_count = src_pos.shape[0]
    sec_count = lax.axis_size("sec")
    sec_index = lax.axis_index("sec")
    grid_y = lax.axis_size("py")
    own_x = lax.axis_index("px")
    own_y = lax.axis_index("py")
    local_sources = source_count // grid_y
    x_pieces, y_pieces = (
        lax.all_gather(x_factor[0], ("px", "py"), axis=1, tiled=True),
        lax.all_gather(y_factor[0], ("px", "py"), axis=1, tiled=True),
    )
    x_block = complex_block(x_pieces)
    real_turned = y_pieces[0].T
    imag_turned = y_pieces[1].T
    local_field = background[:, 0]
    local_weights = coupling[0]
    rows_here = local_field.shape[1]
    full_cols = y_factor.shape[3]
    plane_cells = x_factor.shape[3] * full_cols
    own_sources = lax.dynamic_slice_in_dim(src_pos, own_y * local_sources, local_sources)
    layer_of = own_sources // plane_cells
    remainder = own_sources % plane_cells
    row_of = remainder // full_cols
    column_of = remainder % full_cols
    row_start = own_x * rows_here
    row_hit = row_of[None, :] == row_start + jnp.arange(rows_here, dtype=jnp.int32)[:, None]
    col_hit = column_of[:, None] == jnp.arange(full_cols, dtype=jnp.int32)[None, :]
    layer_hit = layer_of == sec_index
    delta = (row_hit[:, :, None] & col_hit[None, :, :] & layer_hit[None, :, None]).astype(
        jnp.float32
    )
    delta = (delta * source_amplitude).reshape(rows_here, local_sources * full_cols)
    real_rhs = local_field[0].astype(jnp.float32) + delta
    rhs_field = jnp.stack([real_rhs, local_field[1].astype(jnp.float32)])

    def apply_front(field_in):
        turned = y_transform(real_turned, imag_turned, field_in)
        line_field = lax.all_to_all(turned, "px", split_axis=2, concat_axis=1, tiled=True)
        finished = x_transform(x_block, line_field)
        return lax.all_to_all(finished, "px", split_axis=1, concat_axis=2, tiled=True)

    forward_field = jnp.zeros(local_field.shape, jnp.bfloat16)
    outgoing = pick_batch(forward_field, sec_count, 0)
    for step in range(2 * sec_count - 1):
        incoming = shifted(outgoing, "sec", 1)
        batch_index = step - sec_index
        active = (batch_index >= 0) & (batch_index < sec_count)
        clamped = jnp.clip(batch_index, 0, sec_count - 1)
        rhs_batch = pick_batch(rhs_field, sec_count, clamped)
        reduced = (rhs_batch - scale_rows(incoming, local_weights, full_cols)).astype(jnp.bfloat16)
        candidate = apply_front(reduced)
        previous = pick_batch(forward_field, sec_count, clamped)
        kept = jnp.where(active, candidate, previous)
        forward_field = place_batch(forward_field, kept, sec_count, clamped)
        outgoing = candidate
    sweep_field = forward_field
    for step in range(2 * sec_count - 2):
        send_index = jnp.clip(step - (sec_count - 1 - sec_index), 0, sec_count - 1)
        own_batch = pick_batch(sweep_field, sec_count, send_index)
        sent_field = scale_rows(own_batch, local_weights, full_cols).astype(jnp.bfloat16)
        incoming = shifted(sent_field, "sec", -1)
        batch_index = step - (sec_count - 2 - sec_index)
        active = (batch_index >= 0) & (batch_index < sec_count) & (sec_index <= sec_count - 2)
        clamped = jnp.clip(batch_index, 0, sec_count - 1)
        solved = apply_front(incoming)
        forward_batch = pick_batch(forward_field, sec_count, clamped)
        candidate = (forward_batch.astype(jnp.float32) - solved.astype(jnp.float32)).astype(
            jnp.bfloat16
        )
        previous = pick_batch(sweep_field, sec_count, clamped)
        kept = jnp.where(active, candidate, previous)
        sweep_field = place_batch(sweep_field, kept, sec_count, clamped)
    return sweep_field[:, None]


def start_all(copies):
    for copy in copies:
        copy.start()


def wait_all(copies):
    for copy in copies:
        copy.wait()


def row_chunks(order, step):
    step = min(step, order)
    return [slice(first, first + step) for first in range(0, order, step)]


class Either:
    def __init__(self, flag, own, received, target, sem):
        self.flag = flag
        self.own = pltpu.make_async_copy(own, target, sem)
        self.received = pltpu.make_async_copy(received, target, sem)

    def start(self):
        @pl.when(self.flag != 0)
        def _():
            self.own.start()

        @pl.when(self.flag == 0)
        def _():
            self.received.start()

    def wait(self):
        self.received.wait()


def block_kernel(x_factor, y_factor, blocks, sems):
    order = x_factor.shape[2]
    copies = []
    for target in range(blocks.shape[0]):
        for which, factor in enumerate((x_factor, y_factor)):
            for plane in range(2):
                copies.append(
                    pltpu.make_async_copy(
                        factor.at[plane],
                        blocks.at[target, which, :, pl.ds(plane * order, order)],
                        sems.at[target, which, plane],
                    )
                )
    start_all(copies)
    wait_all(copies)


def pack_kernel(place, field, coupling, *rest):
    pieces, sems = rest[:-1], rest[-1]
    rows_here = field.shape[1]
    tall = coupling.shape[1]
    own = pl.ds(2 * place[len(pieces)], 2)
    copies = []
    for index, piece in enumerate(pieces):
        width = piece.shape[2]
        offset = pl.multiple_of(place[index] * width, width)
        copies += [
            pltpu.make_async_copy(
                field.at[:, :, pl.ds(offset, width)],
                piece.at[:, pl.ds(0, rows_here), :],
                sems.at[index, 0],
            ),
            pltpu.make_async_copy(
                coupling.at[own], piece.at[:, pl.ds(rows_here, tall), :], sems.at[index, 1]
            ),
        ]
    start_all(copies)
    wait_all(copies)


def early_unpack_kernel(place, own, p0, p1, p2, field, sems):
    copies = []
    for index, piece in enumerate((p0, p1, p2)):
        width = piece.shape[2]
        offset = pl.multiple_of(place[index] * width, width)
        target = field.at[:, :, pl.ds(offset, width)]
        if index:
            copies.append(pltpu.make_async_copy(piece, target, sems.at[index]))
        else:
            copies.append(Either(place[5], own, piece, target, sems.at[index]))
    start_all(copies)
    wait_all(copies)


def late_unpack_kernel(place, piece, started, field, sem):
    width = piece.shape[2]
    offset = pl.multiple_of(place[3] * width, width)
    copy = pltpu.make_async_copy(piece, field.at[:, :, pl.ds(offset, width)], sem)
    copy.start()
    copy.wait()


def column_kernel(info, blocks, own, p0, p1, p2, p3, x_column, y_turned, rows_held, sems):
    count, factors, height, width = blocks.shape
    last = pl.ds(own.shape[1] - rows_held.shape[2], rows_held.shape[2])
    parts = [piece.at[:, last, :] for piece in (p0, p1, p2, p3)]
    copies = [Either(info[info_self], own.at[:, last, :], parts[0], rows_held.at[0], sems.at[0])]
    for index in range(1, len(parts)):
        copies.append(pltpu.make_async_copy(parts[index], rows_held.at[index], sems.at[index]))
    start_all(copies)
    for index in range(count):
        x_column[index * height : (index + 1) * height] = blocks[index, 0]
    column = blocks[:, 1].reshape(count * height, width)
    y_turned[...] = column.astype(f32).T.astype(bf16)
    wait_all(copies)


def field_kernel(info, own, p0, p1, p2, p3, rhs, sems):
    height = rhs.shape[2] // 2
    copies = []
    for index, piece in enumerate((p0, p1, p2, p3)):
        slot, half = info[info_piece + 2 * index], info[info_piece + 2 * index + 1]
        rows = pl.ds(pl.multiple_of(half * height, height), height)
        part = (slice(None), pl.ds(0, height), slice(None))
        ends = (rhs.at[slot, :, rows, :], sems.at[index])
        if index:
            copies.append(pltpu.make_async_copy(piece.at[part], *ends))
        else:
            copies.append(Either(info[info_self], own.at[part], piece.at[part], *ends))
    start_all(copies)
    wait_all(copies)


def weight_kernel(info, c0, c1, c2, c3, weights, sems):
    height = c0.shape[1]
    half_height = weights.shape[1] // 2
    copies = []
    for index, block in enumerate((c0, c1, c2, c3)):
        for turn in range(block.shape[0]):
            slot, half = info[info_piece + 2 * turn], info[info_piece + 2 * turn + 1]
            start = half * half_height + info[info_block + index] * height
            rows = pl.ds(pl.multiple_of(start, height), height)
            copies.append(
                pltpu.make_async_copy(
                    block.at[turn], weights.at[slot, rows, :], sems.at[index, turn]
                )
            )
    start_all(copies)
    wait_all(copies)


def both_kernel(info, x_column, x_aside, y_column, y0, y1, rows_next, rows_far, rhs, x_both, y_both,
                sems):
    copies = [
        pltpu.make_async_copy(x_column, x_both.at[0], sems.at[0]),
        pltpu.make_async_copy(x_aside, x_both.at[1], sems.at[1]),
        Either(info[info_self], y_column, y0, y_both.at[0], sems.at[2]),
        pltpu.make_async_copy(y1, y_both.at[1], sems.at[3]),
    ]
    start_all(copies)
    wait_all(copies)


class Layers:
    def __init__(self, info, x_parts, y_parts, held, beside, below, sems):
        self.info, self.order = info, held.shape[1]
        self.x_parts, self.y_parts, self.held = x_parts, y_parts, held
        self.beside, self.below, self.sems = beside, below, sems

    def x_copies(self, slot, part):
        height = self.order // 2
        copies = []
        for far in range(2):
            rows = pl.ds(pl.multiple_of(self.info[info_half + far] * height, height), height)
            copies.append(
                pltpu.make_async_copy(
                    part.at[far], self.held.at[slot, rows], self.sems.at[slot, far]
                )
            )
        return copies

    def start(self, slot):
        own, first, second = self.x_parts
        turn, same = self.info[info_slot + slot], self.info[info_self]
        for hit, part in (
            ((turn == 0) & (same != 0), own),
            ((turn == 0) & (same == 0), first),
            (turn == 1, second),
        ):

            @pl.when(hit)
            def _():
                start_all(self.x_copies(slot, part))

    def apply(self, slot, source, store, fresh):
        order, beside, below = self.order, self.beside, self.below
        turn = self.info[info_slot + slot]
        for rows in row_chunks(order, 256):
            further = slice(rows.start + order, rows.stop + order)
            real, imag = source(0, rows), source(1, rows)
            beside[rows, :order] = real
            beside[rows, order:] = -imag
            beside[further, :order] = imag
            beside[further, order:] = real
        height = order // 2
        for far, part in enumerate(self.y_parts):
            product = jnp.dot(beside[...], part[turn], preferred_element_type=f32).astype(bf16)
            start = self.info[info_half + far] * height
            columns = pl.ds(pl.multiple_of(start, height), height)
            beyond = pl.ds(pl.multiple_of(order + start, height), height)
            below[:order, columns] = product[:order]
            below[:order, beyond] = product[order:]
            below[order:, columns] = -product[order:]
            below[order:, beyond] = product[:order]
        if fresh:
            wait_all(self.x_copies(slot, self.x_parts[0]))
        for plane in range(2):
            for columns in row_chunks(order, 256):
                along = slice(columns.start + plane * order, columns.stop + plane * order)
                store(
                    plane,
                    columns,
                    jnp.dot(self.held[slot], below[:, along], preferred_element_type=f32),
                )


def reduced(rhs, info, slot, weights, incoming):
    def source(plane, rows):
        values = rhs[slot, plane, rows]
        if plane == 0:
            row = lax.broadcasted_iota(jnp.int32, values.shape, 0) + rows.start
            column = lax.broadcasted_iota(jnp.int32, values.shape, 1)
            hit = (row == info[1]) & (column == info[2]) & (info[0] == slot)
            values = values + jnp.where(hit, f32(source_amplitude), f32(0.0)).astype(bf16)
        return values - weights[slot, rows] * incoming(plane, rows)

    return source


def sent(weights, slot, field):
    return lambda plane, rows: weights[slot, rows] * field[plane, rows]


def subtract_into(target, forward):
    def store(plane, columns, values):
        target[plane, :, columns] = forward[plane, :, columns] - values.astype(bf16)

    return store


def round_into(target):
    def store(plane, columns, values):
        target[plane, :, columns] = values.astype(bf16)

    return store


def first_kernel(info, xb, x0, x1, yb, yf, weights, rhs, w_low, w_high, held, beside, below, sems):
    @pl.when(info[info_member] == 0)
    def _():
        layers = Layers(info, (xb, x0, x1), (yb, yf), held, beside, below, sems)
        layers.start(0)
        layers.start(1)
        zero = reduced(rhs, info, 0, weights, lambda plane, rows: bf16(0.0))
        layers.apply(0, zero, round_into(w_low), True)
        one = reduced(rhs, info, 1, weights, lambda plane, rows: w_low[plane, rows])
        layers.apply(1, one, round_into(w_high), True)


def last_kernel(info, xb, x0, x1, yb, yf, weights, rhs, arrived, field, back, forward, held, beside,
                below, sems):
    @pl.when(info[info_member] == 1)
    def _():
        layers = Layers(info, (xb, x0, x1), (yb, yf), held, beside, below, sems)
        layers.start(0)
        layers.start(1)
        low, high = field.at[0], field.at[1]
        two = reduced(rhs, info, 0, weights, lambda plane, rows: arrived[plane, rows])
        layers.apply(0, two, round_into(forward), True)
        three = reduced(rhs, info, 1, weights, lambda plane, rows: forward[plane, rows])
        layers.apply(1, three, round_into(high), True)
        layers.apply(0, sent(weights, 1, high), subtract_into(low, forward), False)
        last = sent(weights, 0, low)
        for plane in range(2):
            for rows in row_chunks(weights.shape[1], 256):
                back[plane, rows] = last(plane, rows)


def back_kernel(info, xb, x0, x1, yb, yf, weights, w_low, w_high, arrived, field, p0, p1, p2, p3,
                kept, held, beside, below, sems, osems):
    def start_pieces(source, slot):
        for index, piece in enumerate((p0, p1, p2, p3)):
            height = piece.shape[1]
            half = info[info_piece + 2 * index + 1]
            rows = pl.ds(pl.multiple_of(half * height, height), height)

            @pl.when(info[info_piece + 2 * index] == slot)
            def _():
                pltpu.make_async_copy(source.at[slot, :, rows, :], piece, osems.at[index]).start()

    @pl.when(info[info_member] == 0)
    def _():
        layers = Layers(info, (xb, x0, x1), (yb, yf), held, beside, below, sems)
        layers.start(1)
        layers.start(0)
        low, high = kept.at[0], kept.at[1]
        layers.apply(
            1, lambda plane, rows: arrived[plane, rows], subtract_into(high, w_high), True
        )
        start_pieces(kept, 1)
        layers.apply(0, sent(weights, 1, high), subtract_into(low, w_low), True)
        start_pieces(kept, 0)

    @pl.when(info[info_member] != 0)
    def _():
        start_pieces(field, 1)
        start_pieces(field, 0)

    for index, piece in enumerate((p0, p1, p2, p3)):
        part = kept.at[0, :, pl.ds(0, piece.shape[1]), :]
        pltpu.make_async_copy(part, piece, osems.at[index]).wait()


def on_device(background, src_pos, coupling, x_factor, y_factor):
    px_count = lax.axis_size("px")
    sec_index, own_x, own_y = (lax.axis_index(axis) for axis in ("sec", "px", "py"))
    group, member = sec_index // 2, sec_index % 2
    groups = lax.axis_size("sec") // 2
    order = y_factor.shape[3]
    field = background[:, 0]
    rows_here = field.shape[1]
    height = x_factor.shape[2]
    params = pltpu.CompilerParams(vmem_limit_bytes=vmem_bytes)
    rounds = [(a, b) for a in range(groups) for b in range(px_count)]

    def pairs(a, b):
        return [
            ((2 * x + c) * px_count + y, (2 * ((c + a) % 2) + x) * px_count + (y + b) % px_count)
            for x in range(groups)
            for c in range(2)
            for y in range(px_count)
            if (a, b, x) != (0, 0, c)
        ]

    def back_pairs(a, b):
        return [(target, source) for source, target in pairs(a, b)]

    own_source = src_pos[own_y * groups * px_count + group * px_count + own_x]
    plane_cells = x_factor.shape[3] * order
    layer = own_source // plane_cells
    remainder = own_source % plane_cells
    py_count = lax.axis_size("py")
    entries = [
        jnp.where(layer // 2 == member, layer % 2, -1),
        remainder // order,
        remainder % order,
        member,
    ]
    for a, b in rounds:
        entries += [(group + a) % 2, (own_x - b) % px_count]
    entries += [group, (group + 1) % 2, own_x, (own_x + 1) % 2]
    pair = own_y // 2 * 2
    entries += [own_y, pair + (own_y + 1) % 2, (own_y + 2) % 4, (pair + 2) % 4 + (own_y + 1) % 2]
    entries += [group == member]
    info = jnp.stack([jnp.asarray(entry, jnp.int32) for entry in entries])

    sends_to = jnp.stack(
        [((member + a) % 2) * px_count + (own_x + b) % px_count for a, b in rounds]
        + [own_y, group == member]
    ).astype(jnp.int32)
    piece_shape = jax.ShapeDtypeStruct((2, rows_here, order), bf16)
    blocks = pl.pallas_call(
        block_kernel,
        out_shape=jax.ShapeDtypeStruct((py_count, 2, height, 2 * order), bf16),
        in_specs=[in_hbm] * 2,
        out_specs=in_vmem,
        scratch_shapes=[pltpu.SemaphoreType.DMA((py_count, 2, 2))],
        compiler_params=params,
    )(x_factor[0], y_factor[0])
    tall = height // 2
    packed = pl.pallas_call(
        pack_kernel,
        out_shape=[jax.ShapeDtypeStruct((2, rows_here + tall, order), bf16)] * len(rounds),
        in_specs=[in_smem] + [in_hbm] * 2,
        out_specs=[in_vmem] * len(rounds),
        scratch_shapes=[pltpu.SemaphoreType.DMA((len(rounds), 2))],
        compiler_params=params,
    )(sends_to, field, coupling[0].reshape(rows_here // tall, tall, order))
    pieces = [
        lax.ppermute(piece, ("sec", "px"), pairs(a, b)) for piece, (a, b) in zip(packed, rounds)
    ]
    blocks = lax.all_to_all(blocks, "py", split_axis=0, concat_axis=0, tiled=True)

    column_shape = jax.ShapeDtypeStruct((rows_here, 2 * order), bf16)
    turned_shape = jax.ShapeDtypeStruct((2 * order, rows_here), bf16)
    x_column, y_turned, rows_held = pl.pallas_call(
        column_kernel,
        out_shape=[
            column_shape,
            turned_shape,
            jax.ShapeDtypeStruct((len(rounds), 2, tall, order), bf16),
        ],
        in_specs=[in_smem, in_vmem] + [anywhere] * 5,
        out_specs=[in_vmem] * 3,
        scratch_shapes=[pltpu.SemaphoreType.DMA((len(rounds),))],
        compiler_params=params,
    )(info, blocks, packed[0], *pieces)
    rows_held = rows_held.reshape(len(rounds), height, order)

    def across(block, a):
        return lax.ppermute(block, ("sec", "px"), pairs(a, 0))

    def aside(block):
        return lax.ppermute(block, "px", [(y, (y + 1) % 2) for y in range(2)])

    def over_z(block, bit):
        return lax.ppermute(block, "py", [(z, z ^ bit) for z in range(py_count)])

    y_near = [across(y_turned, a) for a in range(2)]
    x_aside = aside(x_column)
    rows_next = over_z(rows_held, 1)
    rows_far = over_z(rows_held, 2)
    full_shape = jax.ShapeDtypeStruct((2, order, order), bf16)
    double_shape = jax.ShapeDtypeStruct((2, 2, order, order), bf16)
    rhs = pl.pallas_call(
        field_kernel,
        out_shape=double_shape,
        in_specs=[in_smem] + [anywhere] * 5,
        out_specs=in_vmem,
        scratch_shapes=[pltpu.SemaphoreType.DMA((len(rounds),))],
        compiler_params=params,
    )(info, packed[0], *pieces)
    x_both, y_both = pl.pallas_call(
        both_kernel,
        out_shape=[
            jax.ShapeDtypeStruct((2,) + one.shape, bf16) for one in (column_shape, turned_shape)
        ],
        in_specs=[in_smem] + [anywhere] * 8,
        out_specs=[in_vmem] * 2,
        scratch_shapes=[pltpu.SemaphoreType.DMA((4,))],
        compiler_params=params,
    )(info, x_column, x_aside, y_turned, *y_near, rows_next, rows_far, rhs)
    y_far = aside(y_both)
    x_across = [across(x_both, a) for a in range(2)]
    weights = pl.pallas_call(
        weight_kernel,
        out_shape=full_shape,
        in_specs=[in_smem] + [anywhere] * 4,
        out_specs=in_vmem,
        scratch_shapes=[pltpu.SemaphoreType.DMA((4, len(rounds)))],
        compiler_params=params,
    )(info, rows_held, rows_next, rows_far, over_z(rows_next, 2))
    layers = (info, x_both, *x_across, y_both, y_far, weights)
    layer_specs = [in_smem] + [anywhere] * 3 + [in_vmem] * 3
    solver_scratch = [
        pltpu.VMEM((2, order, 2 * order), bf16),
        pltpu.VMEM((2 * order, 2 * order), bf16),
        pltpu.VMEM((2 * order, 2 * order), bf16),
        pltpu.SemaphoreType.DMA((2, 2)),
    ]

    def cost(solves):
        return pl.CostEstimate(
            flops=solves * 16 * order**3, bytes_accessed=16 * order**2 * 2, transcendentals=0
        )

    w_low, w_high = pl.pallas_call(
        first_kernel,
        out_shape=[full_shape] * 2,
        in_specs=layer_specs + [in_vmem],
        out_specs=[in_vmem] * 2,
        scratch_shapes=solver_scratch,
        compiler_params=params,
        cost_estimate=cost(2),
    )(*layers, rhs)

    up = [(2 * x, 2 * x + 1) for x in range(groups)]
    incoming = lax.ppermute(w_high, "sec", up)
    solved, back = pl.pallas_call(
        last_kernel,
        out_shape=[double_shape, full_shape],
        in_specs=layer_specs + [in_vmem] * 2,
        out_specs=[in_vmem] * 2,
        scratch_shapes=[pltpu.VMEM((2, order, order), bf16)] + solver_scratch,
        compiler_params=params,
        cost_estimate=cost(3),
    )(*layers, rhs, incoming)

    down = [(target, source) for source, target in up]
    incoming = lax.ppermute(back, "sec", down)
    results = pl.pallas_call(
        back_kernel,
        out_shape=[piece_shape] * len(rounds),
        in_specs=layer_specs + [in_vmem] * 3 + [anywhere],
        out_specs=[anywhere] * len(rounds),
        scratch_shapes=[pltpu.VMEM((2, 2, order, order), bf16)]
        + solver_scratch
        + [pltpu.SemaphoreType.DMA((len(rounds),))],
        compiler_params=params,
        cost_estimate=cost(2),
    )(*layers, w_low, w_high, incoming, solved)
    received = [
        lax.ppermute(piece, ("sec", "px"), back_pairs(a, b)) for piece, (a, b) in zip(results, rounds)
    ]
    whole_shape = jax.ShapeDtypeStruct(field.shape, bf16)
    started = pl.pallas_call(
        early_unpack_kernel,
        out_shape=whole_shape,
        in_specs=[in_smem] + [in_vmem] * 4,
        out_specs=in_hbm,
        scratch_shapes=[pltpu.SemaphoreType.DMA((3,))],
        compiler_params=params,
    )(sends_to, results[0], *received[:3])
    output = pl.pallas_call(
        late_unpack_kernel,
        out_shape=whole_shape,
        in_specs=[in_smem, in_vmem, in_hbm],
        out_specs=in_hbm,
        scratch_shapes=[pltpu.SemaphoreType.DMA(())],
        input_output_aliases={2: 0},
        compiler_params=params,
    )(sends_to, received[3], started)
    return output[:, None]


def chip_plan_fits(mesh):
    return mesh.shape["sec"] == 4 and mesh.shape["px"] == 2 and mesh.shape["py"] == 4


def solution(mesh):
    placed = (
        P(None, "sec", "px", "py"),
        P(),
        P("sec", "px", None),
        P("sec", None, ("px", "py"), None),
        P("sec", None, ("px", "py"), None),
    )
    return jax.shard_map(
        on_device if chip_plan_fits(mesh) else on_device_by_layer,
        mesh=mesh,
        in_specs=placed,
        out_specs=P(None, "sec", "px", "py"),
        check_vma=False,
    )
```

```python
import functools

import jax
import jax.numpy as jnp
from jax import lax
from jax.experimental import pallas as pl
from jax.experimental.pallas import tpu as pltpu
from jax.sharding import PartitionSpec as P

source_amplitude = 8.0
vmem_bytes = 32 * 1024 * 1024
bf16 = jnp.bfloat16
f32 = jnp.float32
anywhere = pl.BlockSpec(memory_space=pl.ANY)
in_hbm = pl.BlockSpec(memory_space=pltpu.HBM)
in_smem = pl.BlockSpec(memory_space=pltpu.SMEM)
in_vmem = pl.BlockSpec(memory_space=pltpu.VMEM)

info_member, info_piece, info_slot, info_half, info_self = 3, 4, 12, 14, 16


def shifted(x, axis, by):
    peers = lax.axis_size(axis)
    pairs = [(i, i + by) for i in range(peers) if 0 <= i + by < peers]
    return lax.ppermute(x, axis, pairs)


def complex_block(factor):
    upper = jnp.concatenate([factor[0], -factor[1]], axis=1)
    lower = jnp.concatenate([factor[1], factor[0]], axis=1)
    return jnp.concatenate([upper, lower], axis=0)


def y_transform(real_turned, imag_turned, field_in):
    real_part = jnp.dot(field_in[0], real_turned, preferred_element_type=jnp.float32) - jnp.dot(
        field_in[1], imag_turned, preferred_element_type=jnp.float32
    )
    imag_part = jnp.dot(field_in[0], imag_turned, preferred_element_type=jnp.float32) + jnp.dot(
        field_in[1], real_turned, preferred_element_type=jnp.float32
    )
    return jnp.stack([real_part, imag_part]).astype(jnp.bfloat16)


def x_transform(x_block, field_in):
    planes, rows_all, width = field_in.shape
    output = jnp.dot(
        x_block, field_in.reshape(planes * rows_all, width), preferred_element_type=jnp.float32
    )
    return output.astype(jnp.bfloat16).reshape(planes, rows_all, width)


def scale_rows(field_in, weights, width):
    planes, rows_here, merged = field_in.shape
    spread = field_in.astype(jnp.float32).reshape(planes, rows_here, merged // width, width)
    return (spread * weights.astype(jnp.float32)[None, :, None, :]).reshape(
        planes, rows_here, merged
    )


def pick_batch(field, batch_count, batch_index):
    planes, rows_here, merged = field.shape
    split_field = field.reshape(planes, rows_here, batch_count, merged // batch_count)
    return lax.dynamic_index_in_dim(split_field, batch_index, 2, keepdims=False)


def place_batch(field, piece, batch_count, batch_index):
    planes, rows_here, merged = field.shape
    split_field = field.reshape(planes, rows_here, batch_count, merged // batch_count)
    shaped = piece.reshape(planes, rows_here, 1, merged // batch_count)
    updated = lax.dynamic_update_slice_in_dim(split_field, shaped, batch_index, 2)
    return updated.reshape(planes, rows_here, merged)


def on_device_by_layer(background, src_pos, coupling, x_factor, y_factor):
    source_count = src_pos.shape[0]
    sec_count = lax.axis_size("sec")
    sec_index = lax.axis_index("sec")
    grid_y = lax.axis_size("py")
    own_x = lax.axis_index("px")
    own_y = lax.axis_index("py")
    local_sources = source_count // grid_y
    x_pieces, y_pieces = (
        lax.all_gather(x_factor[0], ("px", "py"), axis=1, tiled=True),
        lax.all_gather(y_factor[0], ("px", "py"), axis=1, tiled=True),
    )
    x_block = complex_block(x_pieces)
    real_turned = y_pieces[0].T
    imag_turned = y_pieces[1].T
    local_field = background[:, 0]
    local_weights = coupling[0]
    rows_here = local_field.shape[1]
    full_cols = y_factor.shape[3]
    plane_cells = x_factor.shape[3] * full_cols
    own_sources = lax.dynamic_slice_in_dim(src_pos, own_y * local_sources, local_sources)
    layer_of = own_sources // plane_cells
    remainder = own_sources % plane_cells
    row_of = remainder // full_cols
    column_of = remainder % full_cols
    row_start = own_x * rows_here
    row_hit = row_of[None, :] == row_start + jnp.arange(rows_here, dtype=jnp.int32)[:, None]
    col_hit = column_of[:, None] == jnp.arange(full_cols, dtype=jnp.int32)[None, :]
    layer_hit = layer_of == sec_index
    delta = (row_hit[:, :, None] & col_hit[None, :, :] & layer_hit[None, :, None]).astype(
        jnp.float32
    )
    delta = (delta * source_amplitude).reshape(rows_here, local_sources * full_cols)
    real_rhs = local_field[0].astype(jnp.float32) + delta
    rhs_field = jnp.stack([real_rhs, local_field[1].astype(jnp.float32)])

    def apply_front(field_in):
        turned = y_transform(real_turned, imag_turned, field_in)
        line_field = lax.all_to_all(turned, "px", split_axis=2, concat_axis=1, tiled=True)
        finished = x_transform(x_block, line_field)
        return lax.all_to_all(finished, "px", split_axis=1, concat_axis=2, tiled=True)

    forward_field = jnp.zeros(local_field.shape, jnp.bfloat16)
    outgoing = pick_batch(forward_field, sec_count, 0)
    for step in range(2 * sec_count - 1):
        incoming = shifted(outgoing, "sec", 1)
        batch_index = step - sec_index
        active = (batch_index >= 0) & (batch_index < sec_count)
        clamped = jnp.clip(batch_index, 0, sec_count - 1)
        rhs_batch = pick_batch(rhs_field, sec_count, clamped)
        reduced = (rhs_batch - scale_rows(incoming, local_weights, full_cols)).astype(jnp.bfloat16)
        candidate = apply_front(reduced)
        previous = pick_batch(forward_field, sec_count, clamped)
        kept = jnp.where(active, candidate, previous)
        forward_field = place_batch(forward_field, kept, sec_count, clamped)
        outgoing = candidate
    sweep_field = forward_field
    for step in range(2 * sec_count - 2):
        send_index = jnp.clip(step - (sec_count - 1 - sec_index), 0, sec_count - 1)
        own_batch = pick_batch(sweep_field, sec_count, send_index)
        sent_field = scale_rows(own_batch, local_weights, full_cols).astype(jnp.bfloat16)
        incoming = shifted(sent_field, "sec", -1)
        batch_index = step - (sec_count - 2 - sec_index)
        active = (batch_index >= 0) & (batch_index < sec_count) & (sec_index <= sec_count - 2)
        clamped = jnp.clip(batch_index, 0, sec_count - 1)
        solved = apply_front(incoming)
        forward_batch = pick_batch(forward_field, sec_count, clamped)
        candidate = (forward_batch.astype(jnp.float32) - solved.astype(jnp.float32)).astype(
            jnp.bfloat16
        )
        previous = pick_batch(sweep_field, sec_count, clamped)
        kept = jnp.where(active, candidate, previous)
        sweep_field = place_batch(sweep_field, kept, sec_count, clamped)
    return sweep_field[:, None]


def start_all(copies):
    for copy in copies:
        copy.start()


def wait_all(copies):
    for copy in copies:
        copy.wait()


def row_chunks(order, step):
    step = min(step, order)
    return [slice(first, first + step) for first in range(0, order, step)]


class Either:
    def __init__(self, flag, own, received, target, sem):
        self.flag = flag
        self.own = pltpu.make_async_copy(own, target, sem)
        self.received = pltpu.make_async_copy(received, target, sem)

    def start(self):
        @pl.when(self.flag != 0)
        def _():
            self.own.start()

        @pl.when(self.flag == 0)
        def _():
            self.received.start()

    def wait(self):
        self.received.wait()


def pack_kernel(place, field, c0, c1, c2, c3, *rest):
    pieces, sems = rest[:-1], rest[-1]
    copies = []
    for index, piece in enumerate(pieces):
        width = piece.shape[2]
        offset = pl.multiple_of(place[index] * width, width)
        copies.append(
            pltpu.make_async_copy(field.at[:, :, pl.ds(offset, width)], piece, sems.at[index])
        )
    start_all(copies)
    wait_all(copies)


def early_unpack_kernel(place, p1, p2, p3, field, sems):
    copies = []
    for index, piece in enumerate((p1, p2, p3)):
        width = piece.shape[2]
        offset = pl.multiple_of(place[index + 1] * width, width)
        copies.append(
            pltpu.make_async_copy(piece, field.at[:, :, pl.ds(offset, width)], sems.at[index])
        )
    start_all(copies)
    wait_all(copies)


def late_unpack_kernel(place, own, piece, started, field, sem):
    width = piece.shape[2]
    offset = pl.multiple_of(place[0] * width, width)
    copy = Either(place[4], own, piece, field.at[:, :, pl.ds(offset, width)], sem)
    copy.start()
    copy.wait()


def column_kernel(blocks, weights, p0, p1, p2, p3, x_column, y_turned):
    count, planes, height, order = blocks.shape
    for index in range(count):
        rows = slice(index * height, (index + 1) * height)
        for plane in range(2):
            x_column[rows, plane * order : (plane + 1) * order] = blocks[index, plane]
    for plane in range(2):
        column = blocks[:, 2 + plane].reshape(count * height, order)
        y_turned[plane * order : (plane + 1) * order] = column.astype(f32).T.astype(bf16)


def field_kernel(info, own, p0, p1, p2, p3, rhs, sems):
    height = rhs.shape[2] // 2
    copies = []
    for index, piece in enumerate((p0, p1, p2, p3)):
        slot, half = info[info_piece + 2 * index], info[info_piece + 2 * index + 1]
        rows = pl.ds(pl.multiple_of(half * height, height), height)
        ends = (rhs.at[slot, :, rows, :], sems.at[index])
        copies.append(
            pltpu.make_async_copy(piece, *ends) if index else Either(info[info_self], own, piece, *ends)
        )
    start_all(copies)
    wait_all(copies)


def weight_kernel(info, own, c0, c1, c2, c3, weights, sems):
    height = own.shape[0]
    copies = []
    for index, block in enumerate((c0, c1, c2, c3)):
        slot, half = info[info_piece + 2 * index], info[info_piece + 2 * index + 1]
        rows = pl.ds(pl.multiple_of(half * height, height), height)
        ends = (weights.at[slot, rows, :], sems.at[index])
        copies.append(
            pltpu.make_async_copy(block, *ends) if index else Either(info[info_self], own, block, *ends)
        )
    start_all(copies)
    wait_all(copies)


def both_kernel(info, x_column, x_aside, y_column, y0, y1, rhs, x_both, y_both, sems):
    copies = [
        pltpu.make_async_copy(x_column, x_both.at[0], sems.at[0]),
        pltpu.make_async_copy(x_aside, x_both.at[1], sems.at[1]),
        Either(info[info_self], y_column, y0, y_both.at[0], sems.at[2]),
        pltpu.make_async_copy(y1, y_both.at[1], sems.at[3]),
    ]
    start_all(copies)
    wait_all(copies)


class Layers:
    def __init__(self, info, x_parts, y_parts, held, beside, below, sems):
        self.info, self.order = info, held.shape[1]
        self.x_parts, self.y_parts, self.held = x_parts, y_parts, held
        self.beside, self.below, self.sems = beside, below, sems

    def x_copies(self, slot, part):
        height = self.order // 2
        copies = []
        for far in range(2):
            rows = pl.ds(pl.multiple_of(self.info[info_half + far] * height, height), height)
            copies.append(
                pltpu.make_async_copy(
                    part.at[far], self.held.at[slot, rows], self.sems.at[slot, far]
                )
            )
        return copies

    def start(self, slot):
        own, first, second = self.x_parts
        turn, same = self.info[info_slot + slot], self.info[info_self]
        for hit, part in (
            ((turn == 0) & (same != 0), own),
            ((turn == 0) & (same == 0), first),
            (turn == 1, second),
        ):

            @pl.when(hit)
            def _():
                start_all(self.x_copies(slot, part))

    def apply(self, slot, source, store, fresh):
        order, beside, below = self.order, self.beside, self.below
        turn = self.info[info_slot + slot]
        for rows in row_chunks(order, 256):
            further = slice(rows.start + order, rows.stop + order)
            real, imag = source(0, rows), source(1, rows)
            beside[rows, :order] = real
            beside[rows, order:] = -imag
            beside[further, :order] = imag
            beside[further, order:] = real
        height = order // 2
        for far, part in enumerate(self.y_parts):
            product = jnp.dot(beside[...], part[turn], preferred_element_type=f32).astype(bf16)
            start = self.info[info_half + far] * height
            columns = pl.ds(pl.multiple_of(start, height), height)
            beyond = pl.ds(pl.multiple_of(order + start, height), height)
            below[:order, columns] = product[:order]
            below[:order, beyond] = product[order:]
            below[order:, columns] = -product[order:]
            below[order:, beyond] = product[:order]
        if fresh:
            wait_all(self.x_copies(slot, self.x_parts[0]))
        for plane in range(2):
            for columns in row_chunks(order, 256):
                along = slice(columns.start + plane * order, columns.stop + plane * order)
                store(
                    plane,
                    columns,
                    jnp.dot(self.held[slot], below[:, along], preferred_element_type=f32),
                )


def reduced(rhs, info, slot, weights, incoming):
    def source(plane, rows):
        values = rhs[slot, plane, rows]
        if plane == 0:
            row = lax.broadcasted_iota(jnp.int32, values.shape, 0) + rows.start
            column = lax.broadcasted_iota(jnp.int32, values.shape, 1)
            hit = (row == info[1]) & (column == info[2]) & (info[0] == slot)
            values = values + jnp.where(hit, f32(source_amplitude), f32(0.0)).astype(bf16)
        return values - weights[slot, rows] * incoming(plane, rows)

    return source


def sent(weights, slot, field):
    return lambda plane, rows: weights[slot, rows] * field[plane, rows]


def subtract_into(target, forward):
    def store(plane, columns, values):
        target[plane, :, columns] = forward[plane, :, columns] - values.astype(bf16)

    return store


def round_into(target):
    def store(plane, columns, values):
        target[plane, :, columns] = values.astype(bf16)

    return store


def first_kernel(info, xb, x0, x1, yb, yf, weights, rhs, w_low, w_high, held, beside, below, sems):
    @pl.when(info[info_member] == 0)
    def _():
        layers = Layers(info, (xb, x0, x1), (yb, yf), held, beside, below, sems)
        layers.start(0)
        layers.start(1)
        zero = reduced(rhs, info, 0, weights, lambda plane, rows: bf16(0.0))
        layers.apply(0, zero, round_into(w_low), True)
        one = reduced(rhs, info, 1, weights, lambda plane, rows: w_low[plane, rows])
        layers.apply(1, one, round_into(w_high), True)


def last_kernel(info, xb, x0, x1, yb, yf, weights, rhs, arrived, field, back, forward, held, beside,
                below, sems):
    @pl.when(info[info_member] == 1)
    def _():
        layers = Layers(info, (xb, x0, x1), (yb, yf), held, beside, below, sems)
        layers.start(0)
        layers.start(1)
        low, high = field.at[0], field.at[1]
        two = reduced(rhs, info, 0, weights, lambda plane, rows: arrived[plane, rows])
        layers.apply(0, two, round_into(forward), True)
        three = reduced(rhs, info, 1, weights, lambda plane, rows: forward[plane, rows])
        layers.apply(1, three, round_into(high), True)
        layers.apply(0, sent(weights, 1, high), subtract_into(low, forward), False)
        last = sent(weights, 0, low)
        for plane in range(2):
            for rows in row_chunks(weights.shape[1], 256):
                back[plane, rows] = last(plane, rows)


def back_kernel(info, xb, x0, x1, yb, yf, weights, w_low, w_high, arrived, field, p0, p1, p2, p3,
                kept, held, beside, below, sems, osems):
    def start_pieces(source, slot):
        for index, piece in enumerate((p0, p1, p2, p3)):
            height = piece.shape[1]
            half = info[info_piece + 2 * index + 1]
            rows = pl.ds(pl.multiple_of(half * height, height), height)

            @pl.when(info[info_piece + 2 * index] == slot)
            def _():
                pltpu.make_async_copy(source.at[slot, :, rows, :], piece, osems.at[index]).start()

    @pl.when(info[info_member] == 0)
    def _():
        layers = Layers(info, (xb, x0, x1), (yb, yf), held, beside, below, sems)
        layers.start(1)
        layers.start(0)
        low, high = kept.at[0], kept.at[1]
        layers.apply(
            1, lambda plane, rows: arrived[plane, rows], subtract_into(high, w_high), True
        )
        start_pieces(kept, 1)
        layers.apply(0, sent(weights, 1, high), subtract_into(low, w_low), True)
        start_pieces(kept, 0)

    @pl.when(info[info_member] != 0)
    def _():
        start_pieces(field, 1)
        start_pieces(field, 0)

    for index, piece in enumerate((p0, p1, p2, p3)):
        part = kept.at[0, :, pl.ds(0, piece.shape[1]), :]
        pltpu.make_async_copy(part, piece, osems.at[index]).wait()


def on_device(background, src_pos, coupling, x_factor, y_factor):
    px_count = lax.axis_size("px")
    sec_index, own_x, own_y = (lax.axis_index(axis) for axis in ("sec", "px", "py"))
    group, member = sec_index // 2, sec_index % 2
    groups = lax.axis_size("sec") // 2
    order = y_factor.shape[3]
    field = background[:, 0]
    rows_here = field.shape[1]
    height = x_factor.shape[2]
    params = pltpu.CompilerParams(vmem_limit_bytes=vmem_bytes)
    rounds = [(a, b) for a in range(groups) for b in range(px_count)]

    def pairs(a, b):
        return [
            ((2 * x + c) * px_count + y, (2 * ((c + a) % 2) + x) * px_count + (y + b) % px_count)
            for x in range(groups)
            for c in range(2)
            for y in range(px_count)
            if (a, b, x) != (0, 0, c)
        ]

    def back_pairs(a, b):
        return [(target, source) for source, target in pairs(a, b)]

    own_source = src_pos[own_y * groups * px_count + group * px_count + own_x]
    plane_cells = x_factor.shape[3] * order
    layer = own_source // plane_cells
    remainder = own_source % plane_cells
    py_count = lax.axis_size("py")
    entries = [
        jnp.where(layer // 2 == member, layer % 2, -1),
        remainder // order,
        remainder % order,
        member,
    ]
    for a, b in rounds:
        entries += [(group + a) % 2, (own_x - b) % px_count]
    entries += [group, (group + 1) % 2, own_x, (own_x + 1) % 2]
    entries += [group == member]
    info = jnp.stack([jnp.asarray(entry, jnp.int32) for entry in entries])

    sends_to = jnp.stack(
        [((member + a) % 2) * px_count + (own_x + b) % px_count for a, b in rounds]
        + [group == member]
    ).astype(jnp.int32)
    piece_shape = jax.ShapeDtypeStruct((2, rows_here, order), bf16)
    layer_rows = [lax.ppermute(coupling[0], ("sec", "px"), pairs(a, b)) for a, b in rounds]
    shard = jnp.concatenate([x_factor[0], y_factor[0]], axis=0)
    blocks = jnp.broadcast_to(shard[None], (py_count,) + shard.shape)
    packed = pl.pallas_call(
        pack_kernel,
        out_shape=[piece_shape] * len(rounds),
        in_specs=[in_smem] + [anywhere] * 5,
        out_specs=[in_vmem] * len(rounds),
        scratch_shapes=[pltpu.SemaphoreType.DMA((len(rounds),))],
        compiler_params=params,
    )(sends_to, field, *layer_rows)
    pieces = [
        lax.ppermute(piece, ("sec", "px"), pairs(a, b)) for piece, (a, b) in zip(packed, rounds)
    ]
    blocks = lax.all_to_all(blocks, "py", split_axis=0, concat_axis=0, tiled=True)

    full_shape = jax.ShapeDtypeStruct((2, order, order), bf16)
    double_shape = jax.ShapeDtypeStruct((2, 2, order, order), bf16)
    weights = pl.pallas_call(
        weight_kernel,
        out_shape=full_shape,
        in_specs=[in_smem] + [anywhere] * 5,
        out_specs=in_vmem,
        scratch_shapes=[pltpu.SemaphoreType.DMA((len(rounds),))],
        compiler_params=params,
    )(info, coupling[0], *layer_rows)
    column_shape = jax.ShapeDtypeStruct((rows_here, 2 * order), bf16)
    turned_shape = jax.ShapeDtypeStruct((2 * order, rows_here), bf16)
    x_column, y_turned = pl.pallas_call(
        column_kernel,
        out_shape=[column_shape, turned_shape],
        in_specs=[in_vmem] + [anywhere] * 5,
        out_specs=[in_vmem] * 2,
        compiler_params=params,
    )(blocks, weights, *pieces)

    def across(block, a):
        return lax.ppermute(block, ("sec", "px"), pairs(a, 0))

    def aside(block):
        return lax.ppermute(block, "px", [(y, (y + 1) % 2) for y in range(2)])

    y_near = [across(y_turned, a) for a in range(2)]
    x_aside = aside(x_column)
    rhs = pl.pallas_call(
        field_kernel,
        out_shape=double_shape,
        in_specs=[in_smem] + [anywhere] * 5,
        out_specs=in_vmem,
        scratch_shapes=[pltpu.SemaphoreType.DMA((len(rounds),))],
        compiler_params=params,
    )(info, packed[0], *pieces)
    x_both, y_both = pl.pallas_call(
        both_kernel,
        out_shape=[
            jax.ShapeDtypeStruct((2,) + one.shape, bf16) for one in (column_shape, turned_shape)
        ],
        in_specs=[in_smem] + [anywhere] * 6,
        out_specs=[in_vmem] * 2,
        scratch_shapes=[pltpu.SemaphoreType.DMA((4,))],
        compiler_params=params,
    )(info, x_column, x_aside, y_turned, *y_near, rhs)
    y_far = aside(y_both)
    x_across = [across(x_both, a) for a in range(2)]
    layers = (info, x_both, *x_across, y_both, y_far, weights)
    layer_specs = [in_smem] + [anywhere] * 3 + [in_vmem] * 3
    solver_scratch = [
        pltpu.VMEM((2, order, 2 * order), bf16),
        pltpu.VMEM((2 * order, 2 * order), bf16),
        pltpu.VMEM((2 * order, 2 * order), bf16),
        pltpu.SemaphoreType.DMA((2, 2)),
    ]

    def cost(solves):
        return pl.CostEstimate(
            flops=solves * 16 * order**3, bytes_accessed=16 * order**2 * 2, transcendentals=0
        )

    w_low, w_high = pl.pallas_call(
        first_kernel,
        out_shape=[full_shape] * 2,
        in_specs=layer_specs + [in_vmem],
        out_specs=[in_vmem] * 2,
        scratch_shapes=solver_scratch,
        compiler_params=params,
        cost_estimate=cost(2),
    )(*layers, rhs)

    up = [(2 * x, 2 * x + 1) for x in range(groups)]
    incoming = lax.ppermute(w_high, "sec", up)
    solved, back = pl.pallas_call(
        last_kernel,
        out_shape=[double_shape, full_shape],
        in_specs=layer_specs + [in_vmem] * 2,
        out_specs=[in_vmem] * 2,
        scratch_shapes=[pltpu.VMEM((2, order, order), bf16)] + solver_scratch,
        compiler_params=params,
        cost_estimate=cost(3),
    )(*layers, rhs, incoming)

    down = [(target, source) for source, target in up]
    incoming = lax.ppermute(back, "sec", down)
    results = pl.pallas_call(
        back_kernel,
        out_shape=[piece_shape] * len(rounds),
        in_specs=layer_specs + [in_vmem] * 3 + [anywhere],
        out_specs=[anywhere] * len(rounds),
        scratch_shapes=[pltpu.VMEM((2, 2, order, order), bf16)]
        + solver_scratch
        + [pltpu.SemaphoreType.DMA((len(rounds),))],
        compiler_params=params,
        cost_estimate=cost(2),
    )(*layers, w_low, w_high, incoming, solved)
    received = [
        lax.ppermute(piece, ("sec", "px"), back_pairs(a, b)) for piece, (a, b) in zip(results, rounds)
    ]
    whole_shape = jax.ShapeDtypeStruct(field.shape, bf16)
    started = pl.pallas_call(
        early_unpack_kernel,
        out_shape=whole_shape,
        in_specs=[in_smem] + [in_vmem] * 3,
        out_specs=in_hbm,
        scratch_shapes=[pltpu.SemaphoreType.DMA((3,))],
        compiler_params=params,
    )(sends_to, *received[1:])
    output = pl.pallas_call(
        late_unpack_kernel,
        out_shape=whole_shape,
        in_specs=[in_smem, in_vmem, in_vmem, in_hbm],
        out_specs=in_hbm,
        scratch_shapes=[pltpu.SemaphoreType.DMA(())],
        input_output_aliases={3: 0},
        compiler_params=params,
    )(sends_to, results[0], received[0], started)
    return output[:, None]


def chip_plan_fits(mesh):
    return mesh.shape["sec"] == 4 and mesh.shape["px"] == 2 and mesh.shape["py"] == 4


def solution(mesh):
    placed = (
        P(None, "sec", "px", "py"),
        P(),
        P("sec", "px", None),
        P("sec", None, ("px", "py"), None),
        P("sec", None, ("px", "py"), None),
    )
    return jax.shard_map(
        on_device if chip_plan_fits(mesh) else on_device_by_layer,
        mesh=mesh,
        in_specs=placed,
        out_specs=P(None, "sec", "px", "py"),
        check_vma=False,
    )
```

```python
import functools

import jax
import jax.numpy as jnp
from jax import lax
from jax.experimental import pallas as pl
from jax.experimental.pallas import tpu as pltpu
from jax.sharding import PartitionSpec as P

source_amplitude = 8.0
vmem_bytes = 32 * 1024 * 1024
bf16 = jnp.bfloat16
f32 = jnp.float32
anywhere = pl.BlockSpec(memory_space=pl.ANY)
in_smem = pl.BlockSpec(memory_space=pltpu.SMEM)
in_vmem = pl.BlockSpec(memory_space=pltpu.VMEM)

info_member, info_piece, info_slot, info_half, info_self = 3, 4, 12, 14, 16


def shifted(x, axis, by):
    peers = lax.axis_size(axis)
    pairs = [(i, i + by) for i in range(peers) if 0 <= i + by < peers]
    return lax.ppermute(x, axis, pairs)


def complex_block(factor):
    upper = jnp.concatenate([factor[0], -factor[1]], axis=1)
    lower = jnp.concatenate([factor[1], factor[0]], axis=1)
    return jnp.concatenate([upper, lower], axis=0)


def y_transform(real_turned, imag_turned, field_in):
    real_part = jnp.dot(field_in[0], real_turned, preferred_element_type=jnp.float32) - jnp.dot(
        field_in[1], imag_turned, preferred_element_type=jnp.float32
    )
    imag_part = jnp.dot(field_in[0], imag_turned, preferred_element_type=jnp.float32) + jnp.dot(
        field_in[1], real_turned, preferred_element_type=jnp.float32
    )
    return jnp.stack([real_part, imag_part]).astype(jnp.bfloat16)


def x_transform(x_block, field_in):
    planes, rows_all, width = field_in.shape
    output = jnp.dot(
        x_block, field_in.reshape(planes * rows_all, width), preferred_element_type=jnp.float32
    )
    return output.astype(jnp.bfloat16).reshape(planes, rows_all, width)


def scale_rows(field_in, weights, width):
    planes, rows_here, merged = field_in.shape
    spread = field_in.astype(jnp.float32).reshape(planes, rows_here, merged // width, width)
    return (spread * weights.astype(jnp.float32)[None, :, None, :]).reshape(
        planes, rows_here, merged
    )


def pick_batch(field, batch_count, batch_index):
    planes, rows_here, merged = field.shape
    split_field = field.reshape(planes, rows_here, batch_count, merged // batch_count)
    return lax.dynamic_index_in_dim(split_field, batch_index, 2, keepdims=False)


def place_batch(field, piece, batch_count, batch_index):
    planes, rows_here, merged = field.shape
    split_field = field.reshape(planes, rows_here, batch_count, merged // batch_count)
    shaped = piece.reshape(planes, rows_here, 1, merged // batch_count)
    updated = lax.dynamic_update_slice_in_dim(split_field, shaped, batch_index, 2)
    return updated.reshape(planes, rows_here, merged)


def on_device_by_layer(background, src_pos, coupling, x_factor, y_factor):
    source_count = src_pos.shape[0]
    sec_count = lax.axis_size("sec")
    sec_index = lax.axis_index("sec")
    grid_y = lax.axis_size("py")
    own_x = lax.axis_index("px")
    own_y = lax.axis_index("py")
    local_sources = source_count // grid_y
    x_pieces, y_pieces = (
        lax.all_gather(x_factor[0], ("px", "py"), axis=1, tiled=True),
        lax.all_gather(y_factor[0], ("px", "py"), axis=1, tiled=True),
    )
    x_block = complex_block(x_pieces)
    real_turned = y_pieces[0].T
    imag_turned = y_pieces[1].T
    local_field = background[:, 0]
    local_weights = coupling[0]
    rows_here = local_field.shape[1]
    full_cols = y_factor.shape[3]
    plane_cells = x_factor.shape[3] * full_cols
    own_sources = lax.dynamic_slice_in_dim(src_pos, own_y * local_sources, local_sources)
    layer_of = own_sources // plane_cells
    remainder = own_sources % plane_cells
    row_of = remainder // full_cols
    column_of = remainder % full_cols
    row_start = own_x * rows_here
    row_hit = row_of[None, :] == row_start + jnp.arange(rows_here, dtype=jnp.int32)[:, None]
    col_hit = column_of[:, None] == jnp.arange(full_cols, dtype=jnp.int32)[None, :]
    layer_hit = layer_of == sec_index
    delta = (row_hit[:, :, None] & col_hit[None, :, :] & layer_hit[None, :, None]).astype(
        jnp.float32
    )
    delta = (delta * source_amplitude).reshape(rows_here, local_sources * full_cols)
    real_rhs = local_field[0].astype(jnp.float32) + delta
    rhs_field = jnp.stack([real_rhs, local_field[1].astype(jnp.float32)])

    def apply_front(field_in):
        turned = y_transform(real_turned, imag_turned, field_in)
        line_field = lax.all_to_all(turned, "px", split_axis=2, concat_axis=1, tiled=True)
        finished = x_transform(x_block, line_field)
        return lax.all_to_all(finished, "px", split_axis=1, concat_axis=2, tiled=True)

    forward_field = jnp.zeros(local_field.shape, jnp.bfloat16)
    outgoing = pick_batch(forward_field, sec_count, 0)
    for step in range(2 * sec_count - 1):
        incoming = shifted(outgoing, "sec", 1)
        batch_index = step - sec_index
        active = (batch_index >= 0) & (batch_index < sec_count)
        clamped = jnp.clip(batch_index, 0, sec_count - 1)
        rhs_batch = pick_batch(rhs_field, sec_count, clamped)
        reduced = (rhs_batch - scale_rows(incoming, local_weights, full_cols)).astype(jnp.bfloat16)
        candidate = apply_front(reduced)
        previous = pick_batch(forward_field, sec_count, clamped)
        kept = jnp.where(active, candidate, previous)
        forward_field = place_batch(forward_field, kept, sec_count, clamped)
        outgoing = candidate
    sweep_field = forward_field
    for step in range(2 * sec_count - 2):
        send_index = jnp.clip(step - (sec_count - 1 - sec_index), 0, sec_count - 1)
        own_batch = pick_batch(sweep_field, sec_count, send_index)
        sent_field = scale_rows(own_batch, local_weights, full_cols).astype(jnp.bfloat16)
        incoming = shifted(sent_field, "sec", -1)
        batch_index = step - (sec_count - 2 - sec_index)
        active = (batch_index >= 0) & (batch_index < sec_count) & (sec_index <= sec_count - 2)
        clamped = jnp.clip(batch_index, 0, sec_count - 1)
        solved = apply_front(incoming)
        forward_batch = pick_batch(forward_field, sec_count, clamped)
        candidate = (forward_batch.astype(jnp.float32) - solved.astype(jnp.float32)).astype(
            jnp.bfloat16
        )
        previous = pick_batch(sweep_field, sec_count, clamped)
        kept = jnp.where(active, candidate, previous)
        sweep_field = place_batch(sweep_field, kept, sec_count, clamped)
    return sweep_field[:, None]


def start_all(copies):
    for copy in copies:
        copy.start()


def wait_all(copies):
    for copy in copies:
        copy.wait()


def row_chunks(order, step):
    step = min(step, order)
    return [slice(first, first + step) for first in range(0, order, step)]


class Either:
    def __init__(self, flag, own, received, target, sem):
        self.flag = flag
        self.own = pltpu.make_async_copy(own, target, sem)
        self.received = pltpu.make_async_copy(received, target, sem)

    def start(self):
        @pl.when(self.flag != 0)
        def _():
            self.own.start()

        @pl.when(self.flag == 0)
        def _():
            self.received.start()

    def wait(self):
        self.received.wait()


def block_kernel(x_factor, y_factor, rows, blocks, sems):
    copies = []
    for target in range(blocks.shape[0]):
        for which, factor in enumerate((x_factor, y_factor)):
            part = blocks.at[target, pl.ds(2 * which, 2)]
            copies.append(pltpu.make_async_copy(factor, part, sems.at[target, which]))
    start_all(copies)
    wait_all(copies)


def pack_kernel(place, field, c1, c2, c3, *rest):
    pieces, sems = rest[:-1], rest[-1]
    copies = []
    for index, piece in enumerate(pieces):
        width = piece.shape[2]
        offset = pl.multiple_of(place[index] * width, width)
        copies.append(
            pltpu.make_async_copy(field.at[:, :, pl.ds(offset, width)], piece, sems.at[index])
        )
    start_all(copies)
    wait_all(copies)


def unpack_kernel(place, own, *rest):
    pieces, field, sems = rest[:-2], rest[-2], rest[-1]
    copies = []
    for index, piece in enumerate(pieces):
        width = piece.shape[2]
        offset = pl.multiple_of(place[index] * width, width)
        target = field.at[:, :, pl.ds(offset, width)]
        if index:
            copies.append(pltpu.make_async_copy(piece, target, sems.at[index]))
        else:
            copies.append(Either(place[len(pieces)], own, piece, target, sems.at[index]))
    start_all(copies)
    wait_all(copies)


def column_kernel(blocks, weights, p0, p1, p2, p3, x_column, y_turned):
    count, planes, height, order = blocks.shape
    for index in range(count):
        rows = slice(index * height, (index + 1) * height)
        for plane in range(2):
            x_column[rows, plane * order : (plane + 1) * order] = blocks[index, plane]
    for plane in range(2):
        column = blocks[:, 2 + plane].reshape(count * height, order)
        y_turned[plane * order : (plane + 1) * order] = column.astype(f32).T.astype(bf16)


def field_kernel(info, own, p0, p1, p2, p3, rhs, sems):
    height = rhs.shape[2] // 2
    copies = []
    for index, piece in enumerate((p0, p1, p2, p3)):
        slot, half = info[info_piece + 2 * index], info[info_piece + 2 * index + 1]
        rows = pl.ds(pl.multiple_of(half * height, height), height)
        ends = (rhs.at[slot, :, rows, :], sems.at[index])
        copies.append(
            pltpu.make_async_copy(piece, *ends) if index else Either(info[info_self], own, piece, *ends)
        )
    start_all(copies)
    wait_all(copies)


def weight_kernel(info, own, c0, c1, c2, c3, weights, sems):
    height = own.shape[0]
    copies = []
    for index, block in enumerate((c0, c1, c2, c3)):
        slot, half = info[info_piece + 2 * index], info[info_piece + 2 * index + 1]
        rows = pl.ds(pl.multiple_of(half * height, height), height)
        ends = (weights.at[slot, rows, :], sems.at[index])
        copies.append(
            pltpu.make_async_copy(block, *ends) if index else Either(info[info_self], own, block, *ends)
        )
    start_all(copies)
    wait_all(copies)


def both_kernel(info, x_column, x_aside, y_column, y0, y1, rhs, x_both, y_both, sems):
    copies = [
        pltpu.make_async_copy(x_column, x_both.at[0], sems.at[0]),
        pltpu.make_async_copy(x_aside, x_both.at[1], sems.at[1]),
        Either(info[info_self], y_column, y0, y_both.at[0], sems.at[2]),
        pltpu.make_async_copy(y1, y_both.at[1], sems.at[3]),
    ]
    start_all(copies)
    wait_all(copies)


class Layers:
    def __init__(self, info, x_parts, y_parts, held, beside, below, sems):
        self.info, self.order = info, held.shape[1]
        self.x_parts, self.y_parts, self.held = x_parts, y_parts, held
        self.beside, self.below, self.sems = beside, below, sems

    def x_copies(self, slot, part):
        height = self.order // 2
        copies = []
        for far in range(2):
            rows = pl.ds(pl.multiple_of(self.info[info_half + far] * height, height), height)
            copies.append(
                pltpu.make_async_copy(
                    part.at[far], self.held.at[slot, rows], self.sems.at[slot, far]
                )
            )
        return copies

    def start(self, slot):
        own, first, second = self.x_parts
        turn, same = self.info[info_slot + slot], self.info[info_self]
        for hit, part in (
            ((turn == 0) & (same != 0), own),
            ((turn == 0) & (same == 0), first),
            (turn == 1, second),
        ):

            @pl.when(hit)
            def _():
                start_all(self.x_copies(slot, part))

    def apply(self, slot, source, store, fresh):
        order, beside, below = self.order, self.beside, self.below
        turn = self.info[info_slot + slot]
        for rows in row_chunks(order, 256):
            further = slice(rows.start + order, rows.stop + order)
            real, imag = source(0, rows), source(1, rows)
            beside[rows, :order] = real
            beside[rows, order:] = -imag
            beside[further, :order] = imag
            beside[further, order:] = real
        height = order // 2
        for far, part in enumerate(self.y_parts):
            product = jnp.dot(beside[...], part[turn], preferred_element_type=f32).astype(bf16)
            start = self.info[info_half + far] * height
            columns = pl.ds(pl.multiple_of(start, height), height)
            beyond = pl.ds(pl.multiple_of(order + start, height), height)
            below[:order, columns] = product[:order]
            below[:order, beyond] = product[order:]
            below[order:, columns] = -product[order:]
            below[order:, beyond] = product[:order]
        if fresh:
            wait_all(self.x_copies(slot, self.x_parts[0]))
        for plane in range(2):
            for columns in row_chunks(order, 256):
                along = slice(columns.start + plane * order, columns.stop + plane * order)
                store(
                    plane,
                    columns,
                    jnp.dot(self.held[slot], below[:, along], preferred_element_type=f32),
                )


def reduced(rhs, info, slot, weights, incoming):
    def source(plane, rows):
        values = rhs[slot, plane, rows]
        if plane == 0:
            row = lax.broadcasted_iota(jnp.int32, values.shape, 0) + rows.start
            column = lax.broadcasted_iota(jnp.int32, values.shape, 1)
            hit = (row == info[1]) & (column == info[2]) & (info[0] == slot)
            values = values + jnp.where(hit, f32(source_amplitude), f32(0.0)).astype(bf16)
        return values - weights[slot, rows] * incoming(plane, rows)

    return source


def sent(weights, slot, field):
    return lambda plane, rows: weights[slot, rows] * field[plane, rows]


def subtract_into(target, forward):
    def store(plane, columns, values):
        target[plane, :, columns] = forward[plane, :, columns] - values.astype(bf16)

    return store


def round_into(target):
    def store(plane, columns, values):
        target[plane, :, columns] = values.astype(bf16)

    return store


def first_kernel(info, xb, x0, x1, yb, yf, weights, rhs, w_low, w_high, held, beside, below, sems):
    @pl.when(info[info_member] == 0)
    def _():
        layers = Layers(info, (xb, x0, x1), (yb, yf), held, beside, below, sems)
        layers.start(0)
        layers.start(1)
        zero = reduced(rhs, info, 0, weights, lambda plane, rows: bf16(0.0))
        layers.apply(0, zero, round_into(w_low), True)
        one = reduced(rhs, info, 1, weights, lambda plane, rows: w_low[plane, rows])
        layers.apply(1, one, round_into(w_high), True)


def last_kernel(info, xb, x0, x1, yb, yf, weights, rhs, arrived, field, back, forward, held, beside,
                below, sems):
    @pl.when(info[info_member] == 1)
    def _():
        layers = Layers(info, (xb, x0, x1), (yb, yf), held, beside, below, sems)
        layers.start(0)
        layers.start(1)
        low, high = field.at[0], field.at[1]
        two = reduced(rhs, info, 0, weights, lambda plane, rows: arrived[plane, rows])
        layers.apply(0, two, round_into(forward), True)
        three = reduced(rhs, info, 1, weights, lambda plane, rows: forward[plane, rows])
        layers.apply(1, three, round_into(high), True)
        layers.apply(0, sent(weights, 1, high), subtract_into(low, forward), False)
        last = sent(weights, 0, low)
        for plane in range(2):
            for rows in row_chunks(weights.shape[1], 256):
                back[plane, rows] = last(plane, rows)


def back_kernel(info, xb, x0, x1, yb, yf, weights, w_low, w_high, arrived, field, p0, p1, p2, p3,
                kept, held, beside, below, sems, osems):
    def start_pieces(source, slot):
        for index, piece in enumerate((p0, p1, p2, p3)):
            height = piece.shape[1]
            half = info[info_piece + 2 * index + 1]
            rows = pl.ds(pl.multiple_of(half * height, height), height)

            @pl.when(info[info_piece + 2 * index] == slot)
            def _():
                pltpu.make_async_copy(source.at[slot, :, rows, :], piece, osems.at[index]).start()

    @pl.when(info[info_member] == 0)
    def _():
        layers = Layers(info, (xb, x0, x1), (yb, yf), held, beside, below, sems)
        layers.start(1)
        layers.start(0)
        low, high = kept.at[0], kept.at[1]
        layers.apply(
            1, lambda plane, rows: arrived[plane, rows], subtract_into(high, w_high), True
        )
        start_pieces(kept, 1)
        layers.apply(0, sent(weights, 1, high), subtract_into(low, w_low), True)
        start_pieces(kept, 0)

    @pl.when(info[info_member] != 0)
    def _():
        start_pieces(field, 1)
        start_pieces(field, 0)

    for index, piece in enumerate((p0, p1, p2, p3)):
        part = kept.at[0, :, pl.ds(0, piece.shape[1]), :]
        pltpu.make_async_copy(part, piece, osems.at[index]).wait()


def on_device(background, src_pos, coupling, x_factor, y_factor):
    px_count = lax.axis_size("px")
    sec_index, own_x, own_y = (lax.axis_index(axis) for axis in ("sec", "px", "py"))
    group, member = sec_index // 2, sec_index % 2
    groups = lax.axis_size("sec") // 2
    order = y_factor.shape[3]
    field = background[:, 0]
    rows_here = field.shape[1]
    height = x_factor.shape[2]
    params = pltpu.CompilerParams(vmem_limit_bytes=vmem_bytes)
    rounds = [(a, b) for a in range(groups) for b in range(px_count)]

    def pairs(a, b):
        return [
            ((2 * x + c) * px_count + y, (2 * ((c + a) % 2) + x) * px_count + (y + b) % px_count)
            for x in range(groups)
            for c in range(2)
            for y in range(px_count)
            if (a, b, x) != (0, 0, c)
        ]

    def back_pairs(a, b):
        return [(target, source) for source, target in pairs(a, b)]

    own_source = src_pos[own_y * groups * px_count + group * px_count + own_x]
    plane_cells = x_factor.shape[3] * order
    layer = own_source // plane_cells
    remainder = own_source % plane_cells
    py_count = lax.axis_size("py")
    entries = [
        jnp.where(layer // 2 == member, layer % 2, -1),
        remainder // order,
        remainder % order,
        member,
    ]
    for a, b in rounds:
        entries += [(group + a) % 2, (own_x - b) % px_count]
    entries += [group, (group + 1) % 2, own_x, (own_x + 1) % 2]
    entries += [group == member]
    info = jnp.stack([jnp.asarray(entry, jnp.int32) for entry in entries])

    sends_to = jnp.stack(
        [((member + a) % 2) * px_count + (own_x + b) % px_count for a, b in rounds]
        + [group == member]
    ).astype(jnp.int32)
    piece_shape = jax.ShapeDtypeStruct((2, rows_here, order), bf16)
    layer_rows = [lax.ppermute(coupling[0], ("sec", "px"), pairs(a, b)) for a, b in rounds]
    blocks = pl.pallas_call(
        block_kernel,
        out_shape=jax.ShapeDtypeStruct((py_count, 4, height, order), bf16),
        in_specs=[anywhere] * 3,
        out_specs=in_vmem,
        scratch_shapes=[pltpu.SemaphoreType.DMA((py_count, 2))],
        compiler_params=params,
    )(x_factor[0], y_factor[0], layer_rows[0])
    packed = pl.pallas_call(
        pack_kernel,
        out_shape=[piece_shape] * len(rounds),
        in_specs=[in_smem] + [anywhere] * 4,
        out_specs=[in_vmem] * len(rounds),
        scratch_shapes=[pltpu.SemaphoreType.DMA((len(rounds),))],
        compiler_params=params,
    )(sends_to, field, *layer_rows[1:])
    pieces = [
        lax.ppermute(piece, ("sec", "px"), pairs(a, b)) for piece, (a, b) in zip(packed, rounds)
    ]
    blocks = lax.all_to_all(blocks, "py", split_axis=0, concat_axis=0, tiled=True)

    full_shape = jax.ShapeDtypeStruct((2, order, order), bf16)
    double_shape = jax.ShapeDtypeStruct((2, 2, order, order), bf16)
    weights = pl.pallas_call(
        weight_kernel,
        out_shape=full_shape,
        in_specs=[in_smem] + [anywhere] * 5,
        out_specs=in_vmem,
        scratch_shapes=[pltpu.SemaphoreType.DMA((len(rounds),))],
        compiler_params=params,
    )(info, coupling[0], *layer_rows)
    column_shape = jax.ShapeDtypeStruct((rows_here, 2 * order), bf16)
    turned_shape = jax.ShapeDtypeStruct((2 * order, rows_here), bf16)
    x_column, y_turned = pl.pallas_call(
        column_kernel,
        out_shape=[column_shape, turned_shape],
        in_specs=[in_vmem] + [anywhere] * 5,
        out_specs=[in_vmem] * 2,
        compiler_params=params,
    )(blocks, weights, *pieces)

    def across(block, a):
        return lax.ppermute(block, ("sec", "px"), pairs(a, 0))

    def aside(block):
        return lax.ppermute(block, "px", [(y, (y + 1) % 2) for y in range(2)])

    y_near = [across(y_turned, a) for a in range(2)]
    x_aside = aside(x_column)
    rhs = pl.pallas_call(
        field_kernel,
        out_shape=double_shape,
        in_specs=[in_smem] + [anywhere] * 5,
        out_specs=in_vmem,
        scratch_shapes=[pltpu.SemaphoreType.DMA((len(rounds),))],
        compiler_params=params,
    )(info, packed[0], *pieces)
    x_both, y_both = pl.pallas_call(
        both_kernel,
        out_shape=[
            jax.ShapeDtypeStruct((2,) + one.shape, bf16) for one in (column_shape, turned_shape)
        ],
        in_specs=[in_smem] + [anywhere] * 6,
        out_specs=[in_vmem] * 2,
        scratch_shapes=[pltpu.SemaphoreType.DMA((4,))],
        compiler_params=params,
    )(info, x_column, x_aside, y_turned, *y_near, rhs)
    y_far = aside(y_both)
    x_across = [across(x_both, a) for a in range(2)]
    layers = (info, x_both, *x_across, y_both, y_far, weights)
    layer_specs = [in_smem] + [anywhere] * 3 + [in_vmem] * 3
    solver_scratch = [
        pltpu.VMEM((2, order, 2 * order), bf16),
        pltpu.VMEM((2 * order, 2 * order), bf16),
        pltpu.VMEM((2 * order, 2 * order), bf16),
        pltpu.SemaphoreType.DMA((2, 2)),
    ]

    def cost(solves):
        return pl.CostEstimate(
            flops=solves * 16 * order**3, bytes_accessed=16 * order**2 * 2, transcendentals=0
        )

    w_low, w_high = pl.pallas_call(
        first_kernel,
        out_shape=[full_shape] * 2,
        in_specs=layer_specs + [in_vmem],
        out_specs=[in_vmem] * 2,
        scratch_shapes=solver_scratch,
        compiler_params=params,
        cost_estimate=cost(2),
    )(*layers, rhs)

    up = [(2 * x, 2 * x + 1) for x in range(groups)]
    incoming = lax.ppermute(w_high, "sec", up)
    solved, back = pl.pallas_call(
        last_kernel,
        out_shape=[double_shape, full_shape],
        in_specs=layer_specs + [in_vmem] * 2,
        out_specs=[in_vmem] * 2,
        scratch_shapes=[pltpu.VMEM((2, order, order), bf16)] + solver_scratch,
        compiler_params=params,
        cost_estimate=cost(3),
    )(*layers, rhs, incoming)

    down = [(target, source) for source, target in up]
    incoming = lax.ppermute(back, "sec", down)
    results = pl.pallas_call(
        back_kernel,
        out_shape=[piece_shape] * len(rounds),
        in_specs=layer_specs + [in_vmem] * 3 + [anywhere],
        out_specs=[anywhere] * len(rounds),
        scratch_shapes=[pltpu.VMEM((2, 2, order, order), bf16)]
        + solver_scratch
        + [pltpu.SemaphoreType.DMA((len(rounds),))],
        compiler_params=params,
        cost_estimate=cost(2),
    )(*layers, w_low, w_high, incoming, solved)
    received = [
        lax.ppermute(piece, ("sec", "px"), back_pairs(a, b)) for piece, (a, b) in zip(results, rounds)
    ]
    output = pl.pallas_call(
        unpack_kernel,
        out_shape=jax.ShapeDtypeStruct(field.shape, bf16),
        in_specs=[in_smem] + [anywhere] * (len(rounds) + 1),
        out_specs=in_vmem,
        scratch_shapes=[pltpu.SemaphoreType.DMA((len(rounds),))],
        compiler_params=params,
    )(sends_to, results[0], *received)
    return output[:, None]


def chip_plan_fits(mesh):
    return mesh.shape["sec"] == 4 and mesh.shape["px"] == 2 and mesh.shape["py"] == 4


def solution(mesh):
    placed = (
        P(None, "sec", "px", "py"),
        P(),
        P("sec", "px", None),
        P("sec", None, ("px", "py"), None),
        P("sec", None, ("px", "py"), None),
    )
    return jax.shard_map(
        on_device if chip_plan_fits(mesh) else on_device_by_layer,
        mesh=mesh,
        in_specs=placed,
        out_specs=P(None, "sec", "px", "py"),
        check_vma=False,
    )
```

```python
import functools

import jax
import jax.numpy as jnp
from jax import lax
from jax.experimental import pallas as pl
from jax.experimental.pallas import tpu as pltpu
from jax.sharding import PartitionSpec as P

source_amplitude = 8.0
vmem_bytes = 32 * 1024 * 1024
bf16 = jnp.bfloat16
f32 = jnp.float32
anywhere = pl.BlockSpec(memory_space=pl.ANY)
in_hbm = pl.BlockSpec(memory_space=pltpu.HBM)
in_smem = pl.BlockSpec(memory_space=pltpu.SMEM)
in_vmem = pl.BlockSpec(memory_space=pltpu.VMEM)

info_member, info_piece, info_slot, info_half, info_block, info_self = 3, 4, 12, 14, 16, 20


def shifted(x, axis, by):
    peers = lax.axis_size(axis)
    pairs = [(i, i + by) for i in range(peers) if 0 <= i + by < peers]
    return lax.ppermute(x, axis, pairs)


def complex_block(factor):
    upper = jnp.concatenate([factor[0], -factor[1]], axis=1)
    lower = jnp.concatenate([factor[1], factor[0]], axis=1)
    return jnp.concatenate([upper, lower], axis=0)


def y_transform(real_turned, imag_turned, field_in):
    real_part = jnp.dot(field_in[0], real_turned, preferred_element_type=jnp.float32) - jnp.dot(
        field_in[1], imag_turned, preferred_element_type=jnp.float32
    )
    imag_part = jnp.dot(field_in[0], imag_turned, preferred_element_type=jnp.float32) + jnp.dot(
        field_in[1], real_turned, preferred_element_type=jnp.float32
    )
    return jnp.stack([real_part, imag_part]).astype(jnp.bfloat16)


def x_transform(x_block, field_in):
    planes, rows_all, width = field_in.shape
    output = jnp.dot(
        x_block, field_in.reshape(planes * rows_all, width), preferred_element_type=jnp.float32
    )
    return output.astype(jnp.bfloat16).reshape(planes, rows_all, width)


def scale_rows(field_in, weights, width):
    planes, rows_here, merged = field_in.shape
    spread = field_in.astype(jnp.float32).reshape(planes, rows_here, merged // width, width)
    return (spread * weights.astype(jnp.float32)[None, :, None, :]).reshape(
        planes, rows_here, merged
    )


def pick_batch(field, batch_count, batch_index):
    planes, rows_here, merged = field.shape
    split_field = field.reshape(planes, rows_here, batch_count, merged // batch_count)
    return lax.dynamic_index_in_dim(split_field, batch_index, 2, keepdims=False)


def place_batch(field, piece, batch_count, batch_index):
    planes, rows_here, merged = field.shape
    split_field = field.reshape(planes, rows_here, batch_count, merged // batch_count)
    shaped = piece.reshape(planes, rows_here, 1, merged // batch_count)
    updated = lax.dynamic_update_slice_in_dim(split_field, shaped, batch_index, 2)
    return updated.reshape(planes, rows_here, merged)


def on_device_by_layer(background, src_pos, coupling, x_factor, y_factor):
    source_count = src_pos.shape[0]
    sec_count = lax.axis_size("sec")
    sec_index = lax.axis_index("sec")
    grid_y = lax.axis_size("py")
    own_x = lax.axis_index("px")
    own_y = lax.axis_index("py")
    local_sources = source_count // grid_y
    x_pieces, y_pieces = (
        lax.all_gather(x_factor[0], ("px", "py"), axis=1, tiled=True),
        lax.all_gather(y_factor[0], ("px", "py"), axis=1, tiled=True),
    )
    x_block = complex_block(x_pieces)
    real_turned = y_pieces[0].T
    imag_turned = y_pieces[1].T
    local_field = background[:, 0]
    local_weights = coupling[0]
    rows_here = local_field.shape[1]
    full_cols = y_factor.shape[3]
    plane_cells = x_factor.shape[3] * full_cols
    own_sources = lax.dynamic_slice_in_dim(src_pos, own_y * local_sources, local_sources)
    layer_of = own_sources // plane_cells
    remainder = own_sources % plane_cells
    row_of = remainder // full_cols
    column_of = remainder % full_cols
    row_start = own_x * rows_here
    row_hit = row_of[None, :] == row_start + jnp.arange(rows_here, dtype=jnp.int32)[:, None]
    col_hit = column_of[:, None] == jnp.arange(full_cols, dtype=jnp.int32)[None, :]
    layer_hit = layer_of == sec_index
    delta = (row_hit[:, :, None] & col_hit[None, :, :] & layer_hit[None, :, None]).astype(
        jnp.float32
    )
    delta = (delta * source_amplitude).reshape(rows_here, local_sources * full_cols)
    real_rhs = local_field[0].astype(jnp.float32) + delta
    rhs_field = jnp.stack([real_rhs, local_field[1].astype(jnp.float32)])

    def apply_front(field_in):
        turned = y_transform(real_turned, imag_turned, field_in)
        line_field = lax.all_to_all(turned, "px", split_axis=2, concat_axis=1, tiled=True)
        finished = x_transform(x_block, line_field)
        return lax.all_to_all(finished, "px", split_axis=1, concat_axis=2, tiled=True)

    forward_field = jnp.zeros(local_field.shape, jnp.bfloat16)
    outgoing = pick_batch(forward_field, sec_count, 0)
    for step in range(2 * sec_count - 1):
        incoming = shifted(outgoing, "sec", 1)
        batch_index = step - sec_index
        active = (batch_index >= 0) & (batch_index < sec_count)
        clamped = jnp.clip(batch_index, 0, sec_count - 1)
        rhs_batch = pick_batch(rhs_field, sec_count, clamped)
        reduced = (rhs_batch - scale_rows(incoming, local_weights, full_cols)).astype(jnp.bfloat16)
        candidate = apply_front(reduced)
        previous = pick_batch(forward_field, sec_count, clamped)
        kept = jnp.where(active, candidate, previous)
        forward_field = place_batch(forward_field, kept, sec_count, clamped)
        outgoing = candidate
    sweep_field = forward_field
    for step in range(2 * sec_count - 2):
        send_index = jnp.clip(step - (sec_count - 1 - sec_index), 0, sec_count - 1)
        own_batch = pick_batch(sweep_field, sec_count, send_index)
        sent_field = scale_rows(own_batch, local_weights, full_cols).astype(jnp.bfloat16)
        incoming = shifted(sent_field, "sec", -1)
        batch_index = step - (sec_count - 2 - sec_index)
        active = (batch_index >= 0) & (batch_index < sec_count) & (sec_index <= sec_count - 2)
        clamped = jnp.clip(batch_index, 0, sec_count - 1)
        solved = apply_front(incoming)
        forward_batch = pick_batch(forward_field, sec_count, clamped)
        candidate = (forward_batch.astype(jnp.float32) - solved.astype(jnp.float32)).astype(
            jnp.bfloat16
        )
        previous = pick_batch(sweep_field, sec_count, clamped)
        kept = jnp.where(active, candidate, previous)
        sweep_field = place_batch(sweep_field, kept, sec_count, clamped)
    return sweep_field[:, None]


def start_all(copies):
    for copy in copies:
        copy.start()


def wait_all(copies):
    for copy in copies:
        copy.wait()


def row_chunks(order, step):
    step = min(step, order)
    return [slice(first, first + step) for first in range(0, order, step)]


class Either:
    def __init__(self, flag, own, received, target, sem):
        self.flag = flag
        self.own = pltpu.make_async_copy(own, target, sem)
        self.received = pltpu.make_async_copy(received, target, sem)

    def start(self):
        @pl.when(self.flag != 0)
        def _():
            self.own.start()

        @pl.when(self.flag == 0)
        def _():
            self.received.start()

    def wait(self):
        self.received.wait()


def block_kernel(x_factor, y_factor, blocks, sems):
    order = x_factor.shape[2]
    copies = []
    for target in range(blocks.shape[0]):
        for which, factor in enumerate((x_factor, y_factor)):
            for plane in range(2):
                copies.append(
                    pltpu.make_async_copy(
                        factor.at[plane],
                        blocks.at[target, which, :, pl.ds(plane * order, order)],
                        sems.at[target, which, plane],
                    )
                )
    start_all(copies)
    wait_all(copies)


def pack_kernel(place, field, coupling, *rest):
    pieces, sems = rest[:-1], rest[-1]
    rows_here = field.shape[1]
    tall = coupling.shape[1]
    own = pl.ds(2 * place[len(pieces)], 2)
    copies = []
    for index, piece in enumerate(pieces):
        width = piece.shape[2]
        offset = pl.multiple_of(place[index] * width, width)
        copies += [
            pltpu.make_async_copy(
                field.at[:, :, pl.ds(offset, width)],
                piece.at[:, pl.ds(0, rows_here), :],
                sems.at[index, 0],
            ),
            pltpu.make_async_copy(
                coupling.at[own], piece.at[:, pl.ds(rows_here, tall), :], sems.at[index, 1]
            ),
        ]
    start_all(copies)
    wait_all(copies)


def unpack_kernel(place, own, *rest):
    pieces, field, sems = rest[:-2], rest[-2], rest[-1]
    copies = []
    for index, piece in enumerate(pieces):
        width = piece.shape[2]
        offset = pl.multiple_of(place[index] * width, width)
        target = field.at[:, :, pl.ds(offset, width)]
        if index:
            copies.append(pltpu.make_async_copy(piece, target, sems.at[index]))
        else:
            copies.append(Either(place[len(pieces) + 1], own, piece, target, sems.at[index]))
    start_all(copies)
    wait_all(copies)


def rows_kernel(info, own, p0, p1, p2, p3, rows_held, sems):
    last = pl.ds(own.shape[1] - rows_held.shape[2], rows_held.shape[2])
    parts = [piece.at[:, last, :] for piece in (p0, p1, p2, p3)]
    copies = [Either(info[info_self], own.at[:, last, :], parts[0], rows_held.at[0], sems.at[0])]
    for index in range(1, len(parts)):
        copies.append(pltpu.make_async_copy(parts[index], rows_held.at[index], sems.at[index]))
    start_all(copies)
    wait_all(copies)


def column_kernel(blocks, rows_held, x_column, y_turned):
    count, factors, height, width = blocks.shape
    for index in range(count):
        x_column[index * height : (index + 1) * height] = blocks[index, 0]
    column = blocks[:, 1].reshape(count * height, width)
    y_turned[...] = column.astype(f32).T.astype(bf16)


def field_kernel(info, own, p0, p1, p2, p3, rows_next, rows_far, rhs, sems):
    height = rhs.shape[2] // 2
    copies = []
    for index, piece in enumerate((p0, p1, p2, p3)):
        slot, half = info[info_piece + 2 * index], info[info_piece + 2 * index + 1]
        rows = pl.ds(pl.multiple_of(half * height, height), height)
        part = (slice(None), pl.ds(0, height), slice(None))
        ends = (rhs.at[slot, :, rows, :], sems.at[index])
        if index:
            copies.append(pltpu.make_async_copy(piece.at[part], *ends))
        else:
            copies.append(Either(info[info_self], own.at[part], piece.at[part], *ends))
    start_all(copies)
    wait_all(copies)


def weight_kernel(info, c0, c1, c2, c3, weights, sems):
    height = c0.shape[1]
    half_height = weights.shape[1] // 2
    copies = []
    for index, block in enumerate((c0, c1, c2, c3)):
        for turn in range(block.shape[0]):
            slot, half = info[info_piece + 2 * turn], info[info_piece + 2 * turn + 1]
            start = half * half_height + info[info_block + index] * height
            rows = pl.ds(pl.multiple_of(start, height), height)
            copies.append(
                pltpu.make_async_copy(
                    block.at[turn], weights.at[slot, rows, :], sems.at[index, turn]
                )
            )
    start_all(copies)
    wait_all(copies)


def both_kernel(info, x_column, x_aside, y_column, y0, y1, rhs, x_both, y_both, sems):
    copies = [
        pltpu.make_async_copy(x_column, x_both.at[0], sems.at[0]),
        pltpu.make_async_copy(x_aside, x_both.at[1], sems.at[1]),
        Either(info[info_self], y_column, y0, y_both.at[0], sems.at[2]),
        pltpu.make_async_copy(y1, y_both.at[1], sems.at[3]),
    ]
    start_all(copies)
    wait_all(copies)


class Layers:
    def __init__(self, info, x_parts, y_parts, held, beside, below, sems):
        self.info, self.order = info, held.shape[1]
        self.x_parts, self.y_parts, self.held = x_parts, y_parts, held
        self.beside, self.below, self.sems = beside, below, sems

    def x_copies(self, slot, part):
        height = self.order // 2
        copies = []
        for far in range(2):
            rows = pl.ds(pl.multiple_of(self.info[info_half + far] * height, height), height)
            copies.append(
                pltpu.make_async_copy(
                    part.at[far], self.held.at[slot, rows], self.sems.at[slot, far]
                )
            )
        return copies

    def start(self, slot):
        own, first, second = self.x_parts
        turn, same = self.info[info_slot + slot], self.info[info_self]
        for hit, part in (
            ((turn == 0) & (same != 0), own),
            ((turn == 0) & (same == 0), first),
            (turn == 1, second),
        ):

            @pl.when(hit)
            def _():
                start_all(self.x_copies(slot, part))

    def apply(self, slot, source, store, fresh):
        order, beside, below = self.order, self.beside, self.below
        turn = self.info[info_slot + slot]
        for rows in row_chunks(order, 256):
            further = slice(rows.start + order, rows.stop + order)
            real, imag = source(0, rows), source(1, rows)
            beside[rows, :order] = real
            beside[rows, order:] = -imag
            beside[further, :order] = imag
            beside[further, order:] = real
        height = order // 2
        for far, part in enumerate(self.y_parts):
            product = jnp.dot(beside[...], part[turn], preferred_element_type=f32).astype(bf16)
            start = self.info[info_half + far] * height
            columns = pl.ds(pl.multiple_of(start, height), height)
            beyond = pl.ds(pl.multiple_of(order + start, height), height)
            below[:order, columns] = product[:order]
            below[:order, beyond] = product[order:]
            below[order:, columns] = -product[order:]
            below[order:, beyond] = product[:order]
        if fresh:
            wait_all(self.x_copies(slot, self.x_parts[0]))
        for plane in range(2):
            for columns in row_chunks(order, 256):
                along = slice(columns.start + plane * order, columns.stop + plane * order)
                store(
                    plane,
                    columns,
                    jnp.dot(self.held[slot], below[:, along], preferred_element_type=f32),
                )


def reduced(rhs, info, slot, weights, incoming):
    def source(plane, rows):
        values = rhs[slot, plane, rows]
        if plane == 0:
            row = lax.broadcasted_iota(jnp.int32, values.shape, 0) + rows.start
            column = lax.broadcasted_iota(jnp.int32, values.shape, 1)
            hit = (row == info[1]) & (column == info[2]) & (info[0] == slot)
            values = values + jnp.where(hit, f32(source_amplitude), f32(0.0)).astype(bf16)
        return values - weights[slot, rows] * incoming(plane, rows)

    return source


def sent(weights, slot, field):
    return lambda plane, rows: weights[slot, rows] * field[plane, rows]


def subtract_into(target, forward):
    def store(plane, columns, values):
        target[plane, :, columns] = forward[plane, :, columns] - values.astype(bf16)

    return store


def round_into(target):
    def store(plane, columns, values):
        target[plane, :, columns] = values.astype(bf16)

    return store


def first_kernel(info, xb, x0, x1, yb, yf, weights, rhs, w_low, w_high, held, beside, below, sems):
    @pl.when(info[info_member] == 0)
    def _():
        layers = Layers(info, (xb, x0, x1), (yb, yf), held, beside, below, sems)
        layers.start(0)
        layers.start(1)
        zero = reduced(rhs, info, 0, weights, lambda plane, rows: bf16(0.0))
        layers.apply(0, zero, round_into(w_low), True)
        one = reduced(rhs, info, 1, weights, lambda plane, rows: w_low[plane, rows])
        layers.apply(1, one, round_into(w_high), True)


def last_kernel(info, xb, x0, x1, yb, yf, weights, rhs, arrived, field, back, forward, held, beside,
                below, sems):
    @pl.when(info[info_member] == 1)
    def _():
        layers = Layers(info, (xb, x0, x1), (yb, yf), held, beside, below, sems)
        layers.start(0)
        layers.start(1)
        low, high = field.at[0], field.at[1]
        two = reduced(rhs, info, 0, weights, lambda plane, rows: arrived[plane, rows])
        layers.apply(0, two, round_into(forward), True)
        three = reduced(rhs, info, 1, weights, lambda plane, rows: forward[plane, rows])
        layers.apply(1, three, round_into(high), True)
        layers.apply(0, sent(weights, 1, high), subtract_into(low, forward), False)
        last = sent(weights, 0, low)
        for plane in range(2):
            for rows in row_chunks(weights.shape[1], 256):
                back[plane, rows] = last(plane, rows)


def back_kernel(info, xb, x0, x1, yb, yf, weights, w_low, w_high, arrived, field, p0, p1, p2, p3,
                kept, held, beside, below, sems, osems):
    def start_pieces(source, slot):
        for index, piece in enumerate((p0, p1, p2, p3)):
            height = piece.shape[1]
            half = info[info_piece + 2 * index + 1]
            rows = pl.ds(pl.multiple_of(half * height, height), height)

            @pl.when(info[info_piece + 2 * index] == slot)
            def _():
                pltpu.make_async_copy(source.at[slot, :, rows, :], piece, osems.at[index]).start()

    @pl.when(info[info_member] == 0)
    def _():
        layers = Layers(info, (xb, x0, x1), (yb, yf), held, beside, below, sems)
        layers.start(1)
        layers.start(0)
        low, high = kept.at[0], kept.at[1]
        layers.apply(
            1, lambda plane, rows: arrived[plane, rows], subtract_into(high, w_high), True
        )
        start_pieces(kept, 1)
        layers.apply(0, sent(weights, 1, high), subtract_into(low, w_low), True)
        start_pieces(kept, 0)

    @pl.when(info[info_member] != 0)
    def _():
        start_pieces(field, 1)
        start_pieces(field, 0)

    for index, piece in enumerate((p0, p1, p2, p3)):
        part = kept.at[0, :, pl.ds(0, piece.shape[1]), :]
        pltpu.make_async_copy(part, piece, osems.at[index]).wait()


def on_device(background, src_pos, coupling, x_factor, y_factor):
    px_count = lax.axis_size("px")
    sec_index, own_x, own_y = (lax.axis_index(axis) for axis in ("sec", "px", "py"))
    group, member = sec_index // 2, sec_index % 2
    groups = lax.axis_size("sec") // 2
    order = y_factor.shape[3]
    field = background[:, 0]
    rows_here = field.shape[1]
    height = x_factor.shape[2]
    params = pltpu.CompilerParams(vmem_limit_bytes=vmem_bytes)
    rounds = [(a, b) for a in range(groups) for b in range(px_count)]

    def pairs(a, b):
        return [
            ((2 * x + c) * px_count + y, (2 * ((c + a) % 2) + x) * px_count + (y + b) % px_count)
            for x in range(groups)
            for c in range(2)
            for y in range(px_count)
            if (a, b, x) != (0, 0, c)
        ]

    def back_pairs(a, b):
        return [(target, source) for source, target in pairs(a, b)]

    own_source = src_pos[own_y * groups * px_count + group * px_count + own_x]
    plane_cells = x_factor.shape[3] * order
    layer = own_source // plane_cells
    remainder = own_source % plane_cells
    py_count = lax.axis_size("py")
    entries = [
        jnp.where(layer // 2 == member, layer % 2, -1),
        remainder // order,
        remainder % order,
        member,
    ]
    for a, b in rounds:
        entries += [(group + a) % 2, (own_x - b) % px_count]
    entries += [group, (group + 1) % 2, own_x, (own_x + 1) % 2]
    pair = own_y // 2 * 2
    entries += [own_y, pair + (own_y + 1) % 2, (own_y + 2) % 4, (pair + 2) % 4 + (own_y + 1) % 2]
    entries += [group == member]
    info = jnp.stack([jnp.asarray(entry, jnp.int32) for entry in entries])

    sends_to = jnp.stack(
        [((member + a) % 2) * px_count + (own_x + b) % px_count for a, b in rounds]
        + [own_y, group == member]
    ).astype(jnp.int32)
    piece_shape = jax.ShapeDtypeStruct((2, rows_here, order), bf16)
    blocks = pl.pallas_call(
        block_kernel,
        out_shape=jax.ShapeDtypeStruct((py_count, 2, height, 2 * order), bf16),
        in_specs=[in_hbm] * 2,
        out_specs=in_vmem,
        scratch_shapes=[pltpu.SemaphoreType.DMA((py_count, 2, 2))],
        compiler_params=params,
    )(x_factor[0], y_factor[0])
    tall = height // 2
    packed = pl.pallas_call(
        pack_kernel,
        out_shape=[jax.ShapeDtypeStruct((2, rows_here + tall, order), bf16)] * len(rounds),
        in_specs=[in_smem] + [in_hbm] * 2,
        out_specs=[in_vmem] * len(rounds),
        scratch_shapes=[pltpu.SemaphoreType.DMA((len(rounds), 2))],
        compiler_params=params,
    )(sends_to, field, coupling[0].reshape(rows_here // tall, tall, order))
    pieces = [
        lax.ppermute(piece, ("sec", "px"), pairs(a, b)) for piece, (a, b) in zip(packed, rounds)
    ]
    blocks = lax.all_to_all(blocks, "py", split_axis=0, concat_axis=0, tiled=True)

    column_shape = jax.ShapeDtypeStruct((rows_here, 2 * order), bf16)
    turned_shape = jax.ShapeDtypeStruct((2 * order, rows_here), bf16)
    first = pl.CostEstimate(flops=3 * 10**10, bytes_accessed=2**20, transcendentals=0)
    rows_held = pl.pallas_call(
        rows_kernel,
        out_shape=jax.ShapeDtypeStruct((len(rounds), 2, tall, order), bf16),
        in_specs=[in_smem] + [anywhere] * 5,
        out_specs=in_vmem,
        scratch_shapes=[pltpu.SemaphoreType.DMA((len(rounds),))],
        compiler_params=params,
        cost_estimate=first,
    )(info, packed[0], *pieces)
    x_column, y_turned = pl.pallas_call(
        column_kernel,
        out_shape=[column_shape, turned_shape],
        in_specs=[in_vmem, anywhere],
        out_specs=[in_vmem] * 2,
        compiler_params=params,
    )(blocks, rows_held)
    rows_held = rows_held.reshape(len(rounds), height, order)

    def across(block, a):
        return lax.ppermute(block, ("sec", "px"), pairs(a, 0))

    def aside(block):
        return lax.ppermute(block, "px", [(y, (y + 1) % 2) for y in range(2)])

    def over_z(block, bit):
        return lax.ppermute(block, "py", [(z, z ^ bit) for z in range(py_count)])

    y_near = [across(y_turned, a) for a in range(2)]
    x_aside = aside(x_column)
    rows_next = over_z(rows_held, 1)
    rows_far = over_z(rows_held, 2)
    full_shape = jax.ShapeDtypeStruct((2, order, order), bf16)
    double_shape = jax.ShapeDtypeStruct((2, 2, order, order), bf16)
    rhs = pl.pallas_call(
        field_kernel,
        out_shape=double_shape,
        in_specs=[in_smem] + [anywhere] * 7,
        out_specs=in_vmem,
        scratch_shapes=[pltpu.SemaphoreType.DMA((len(rounds),))],
        compiler_params=params,
        cost_estimate=first,
    )(info, packed[0], *pieces, rows_next, rows_far)
    x_both, y_both = pl.pallas_call(
        both_kernel,
        out_shape=[
            jax.ShapeDtypeStruct((2,) + one.shape, bf16) for one in (column_shape, turned_shape)
        ],
        in_specs=[in_smem] + [anywhere] * 6,
        out_specs=[in_vmem] * 2,
        scratch_shapes=[pltpu.SemaphoreType.DMA((4,))],
        compiler_params=params,
    )(info, x_column, x_aside, y_turned, *y_near, rhs)
    y_far = aside(y_both)
    x_across = [across(x_both, a) for a in range(2)]
    weights = pl.pallas_call(
        weight_kernel,
        out_shape=full_shape,
        in_specs=[in_smem] + [anywhere] * 4,
        out_specs=in_vmem,
        scratch_shapes=[pltpu.SemaphoreType.DMA((4, len(rounds)))],
        compiler_params=params,
    )(info, rows_held, rows_next, rows_far, over_z(rows_next, 2))
    layers = (info, x_both, *x_across, y_both, y_far, weights)
    layer_specs = [in_smem] + [anywhere] * 3 + [in_vmem] * 3
    solver_scratch = [
        pltpu.VMEM((2, order, 2 * order), bf16),
        pltpu.VMEM((2 * order, 2 * order), bf16),
        pltpu.VMEM((2 * order, 2 * order), bf16),
        pltpu.SemaphoreType.DMA((2, 2)),
    ]

    def cost(solves):
        return pl.CostEstimate(
            flops=solves * 16 * order**3, bytes_accessed=16 * order**2 * 2, transcendentals=0
        )

    w_low, w_high = pl.pallas_call(
        first_kernel,
        out_shape=[full_shape] * 2,
        in_specs=layer_specs + [in_vmem],
        out_specs=[in_vmem] * 2,
        scratch_shapes=solver_scratch,
        compiler_params=params,
        cost_estimate=cost(2),
    )(*layers, rhs)

    up = [(2 * x, 2 * x + 1) for x in range(groups)]
    incoming = lax.ppermute(w_high, "sec", up)
    solved, back = pl.pallas_call(
        last_kernel,
        out_shape=[double_shape, full_shape],
        in_specs=layer_specs + [in_vmem] * 2,
        out_specs=[in_vmem] * 2,
        scratch_shapes=[pltpu.VMEM((2, order, order), bf16)] + solver_scratch,
        compiler_params=params,
        cost_estimate=cost(3),
    )(*layers, rhs, incoming)

    down = [(target, source) for source, target in up]
    incoming = lax.ppermute(back, "sec", down)
    results = pl.pallas_call(
        back_kernel,
        out_shape=[piece_shape] * len(rounds),
        in_specs=layer_specs + [in_vmem] * 3 + [anywhere],
        out_specs=[anywhere] * len(rounds),
        scratch_shapes=[pltpu.VMEM((2, 2, order, order), bf16)]
        + solver_scratch
        + [pltpu.SemaphoreType.DMA((len(rounds),))],
        compiler_params=params,
        cost_estimate=cost(2),
    )(*layers, w_low, w_high, incoming, solved)
    received = [
        lax.ppermute(piece, ("sec", "px"), back_pairs(a, b)) for piece, (a, b) in zip(results, rounds)
    ]
    output = pl.pallas_call(
        unpack_kernel,
        out_shape=jax.ShapeDtypeStruct(field.shape, bf16),
        in_specs=[in_smem] + [anywhere] * (len(rounds) + 1),
        out_specs=in_vmem,
        scratch_shapes=[pltpu.SemaphoreType.DMA((len(rounds),))],
        compiler_params=params,
    )(sends_to, results[0], *received)
    return output[:, None]


def chip_plan_fits(mesh):
    return mesh.shape["sec"] == 4 and mesh.shape["px"] == 2 and mesh.shape["py"] == 4


def solution(mesh):
    placed = (
        P(None, "sec", "px", "py"),
        P(),
        P("sec", "px", None),
        P("sec", None, ("px", "py"), None),
        P("sec", None, ("px", "py"), None),
    )
    return jax.shard_map(
        on_device if chip_plan_fits(mesh) else on_device_by_layer,
        mesh=mesh,
        in_specs=placed,
        out_specs=P(None, "sec", "px", "py"),
        check_vma=False,
    )
```

```python
import functools

import jax
import jax.numpy as jnp
from jax import lax
from jax.experimental import pallas as pl
from jax.experimental.pallas import tpu as pltpu
from jax.sharding import PartitionSpec as P

source_amplitude = 8.0
vmem_bytes = 32 * 1024 * 1024
bf16 = jnp.bfloat16
f32 = jnp.float32
anywhere = pl.BlockSpec(memory_space=pl.ANY)
in_hbm = pl.BlockSpec(memory_space=pltpu.HBM)
in_smem = pl.BlockSpec(memory_space=pltpu.SMEM)
in_vmem = pl.BlockSpec(memory_space=pltpu.VMEM)

info_member, info_piece, info_slot, info_half, info_block, info_self = 3, 4, 12, 14, 16, 20


def shifted(x, axis, by):
    peers = lax.axis_size(axis)
    pairs = [(i, i + by) for i in range(peers) if 0 <= i + by < peers]
    return lax.ppermute(x, axis, pairs)


def complex_block(factor):
    upper = jnp.concatenate([factor[0], -factor[1]], axis=1)
    lower = jnp.concatenate([factor[1], factor[0]], axis=1)
    return jnp.concatenate([upper, lower], axis=0)


def y_transform(real_turned, imag_turned, field_in):
    real_part = jnp.dot(field_in[0], real_turned, preferred_element_type=jnp.float32) - jnp.dot(
        field_in[1], imag_turned, preferred_element_type=jnp.float32
    )
    imag_part = jnp.dot(field_in[0], imag_turned, preferred_element_type=jnp.float32) + jnp.dot(
        field_in[1], real_turned, preferred_element_type=jnp.float32
    )
    return jnp.stack([real_part, imag_part]).astype(jnp.bfloat16)


def x_transform(x_block, field_in):
    planes, rows_all, width = field_in.shape
    output = jnp.dot(
        x_block, field_in.reshape(planes * rows_all, width), preferred_element_type=jnp.float32
    )
    return output.astype(jnp.bfloat16).reshape(planes, rows_all, width)


def scale_rows(field_in, weights, width):
    planes, rows_here, merged = field_in.shape
    spread = field_in.astype(jnp.float32).reshape(planes, rows_here, merged // width, width)
    return (spread * weights.astype(jnp.float32)[None, :, None, :]).reshape(
        planes, rows_here, merged
    )


def pick_batch(field, batch_count, batch_index):
    planes, rows_here, merged = field.shape
    split_field = field.reshape(planes, rows_here, batch_count, merged // batch_count)
    return lax.dynamic_index_in_dim(split_field, batch_index, 2, keepdims=False)


def place_batch(field, piece, batch_count, batch_index):
    planes, rows_here, merged = field.shape
    split_field = field.reshape(planes, rows_here, batch_count, merged // batch_count)
    shaped = piece.reshape(planes, rows_here, 1, merged // batch_count)
    updated = lax.dynamic_update_slice_in_dim(split_field, shaped, batch_index, 2)
    return updated.reshape(planes, rows_here, merged)


def on_device_by_layer(background, src_pos, coupling, x_factor, y_factor):
    source_count = src_pos.shape[0]
    sec_count = lax.axis_size("sec")
    sec_index = lax.axis_index("sec")
    grid_y = lax.axis_size("py")
    own_x = lax.axis_index("px")
    own_y = lax.axis_index("py")
    local_sources = source_count // grid_y
    x_pieces, y_pieces = (
        lax.all_gather(x_factor[0], ("px", "py"), axis=1, tiled=True),
        lax.all_gather(y_factor[0], ("px", "py"), axis=1, tiled=True),
    )
    x_block = complex_block(x_pieces)
    real_turned = y_pieces[0].T
    imag_turned = y_pieces[1].T
    local_field = background[:, 0]
    local_weights = coupling[0]
    rows_here = local_field.shape[1]
    full_cols = y_factor.shape[3]
    plane_cells = x_factor.shape[3] * full_cols
    own_sources = lax.dynamic_slice_in_dim(src_pos, own_y * local_sources, local_sources)
    layer_of = own_sources // plane_cells
    remainder = own_sources % plane_cells
    row_of = remainder // full_cols
    column_of = remainder % full_cols
    row_start = own_x * rows_here
    row_hit = row_of[None, :] == row_start + jnp.arange(rows_here, dtype=jnp.int32)[:, None]
    col_hit = column_of[:, None] == jnp.arange(full_cols, dtype=jnp.int32)[None, :]
    layer_hit = layer_of == sec_index
    delta = (row_hit[:, :, None] & col_hit[None, :, :] & layer_hit[None, :, None]).astype(
        jnp.float32
    )
    delta = (delta * source_amplitude).reshape(rows_here, local_sources * full_cols)
    real_rhs = local_field[0].astype(jnp.float32) + delta
    rhs_field = jnp.stack([real_rhs, local_field[1].astype(jnp.float32)])

    def apply_front(field_in):
        turned = y_transform(real_turned, imag_turned, field_in)
        line_field = lax.all_to_all(turned, "px", split_axis=2, concat_axis=1, tiled=True)
        finished = x_transform(x_block, line_field)
        return lax.all_to_all(finished, "px", split_axis=1, concat_axis=2, tiled=True)

    forward_field = jnp.zeros(local_field.shape, jnp.bfloat16)
    outgoing = pick_batch(forward_field, sec_count, 0)
    for step in range(2 * sec_count - 1):
        incoming = shifted(outgoing, "sec", 1)
        batch_index = step - sec_index
        active = (batch_index >= 0) & (batch_index < sec_count)
        clamped = jnp.clip(batch_index, 0, sec_count - 1)
        rhs_batch = pick_batch(rhs_field, sec_count, clamped)
        reduced = (rhs_batch - scale_rows(incoming, local_weights, full_cols)).astype(jnp.bfloat16)
        candidate = apply_front(reduced)
        previous = pick_batch(forward_field, sec_count, clamped)
        kept = jnp.where(active, candidate, previous)
        forward_field = place_batch(forward_field, kept, sec_count, clamped)
        outgoing = candidate
    sweep_field = forward_field
    for step in range(2 * sec_count - 2):
        send_index = jnp.clip(step - (sec_count - 1 - sec_index), 0, sec_count - 1)
        own_batch = pick_batch(sweep_field, sec_count, send_index)
        sent_field = scale_rows(own_batch, local_weights, full_cols).astype(jnp.bfloat16)
        incoming = shifted(sent_field, "sec", -1)
        batch_index = step - (sec_count - 2 - sec_index)
        active = (batch_index >= 0) & (batch_index < sec_count) & (sec_index <= sec_count - 2)
        clamped = jnp.clip(batch_index, 0, sec_count - 1)
        solved = apply_front(incoming)
        forward_batch = pick_batch(forward_field, sec_count, clamped)
        candidate = (forward_batch.astype(jnp.float32) - solved.astype(jnp.float32)).astype(
            jnp.bfloat16
        )
        previous = pick_batch(sweep_field, sec_count, clamped)
        kept = jnp.where(active, candidate, previous)
        sweep_field = place_batch(sweep_field, kept, sec_count, clamped)
    return sweep_field[:, None]


def start_all(copies):
    for copy in copies:
        copy.start()


def wait_all(copies):
    for copy in copies:
        copy.wait()


def row_chunks(order, step):
    step = min(step, order)
    return [slice(first, first + step) for first in range(0, order, step)]


class Either:
    def __init__(self, flag, own, received, target, sem):
        self.flag = flag
        self.own = pltpu.make_async_copy(own, target, sem)
        self.received = pltpu.make_async_copy(received, target, sem)

    def start(self):
        @pl.when(self.flag != 0)
        def _():
            self.own.start()

        @pl.when(self.flag == 0)
        def _():
            self.received.start()

    def wait(self):
        self.received.wait()


def block_kernel(x_factor, y_factor, blocks, sems):
    order = x_factor.shape[2]
    copies = []
    for target in range(blocks.shape[0]):
        for which, factor in enumerate((x_factor, y_factor)):
            for plane in range(2):
                copies.append(
                    pltpu.make_async_copy(
                        factor.at[plane],
                        blocks.at[target, which, :, pl.ds(plane * order, order)],
                        sems.at[target, which, plane],
                    )
                )
    start_all(copies)
    wait_all(copies)


def pack_kernel(place, field, coupling, *rest):
    pieces, sems = rest[:-1], rest[-1]
    rows_here = field.shape[1]
    tall = coupling.shape[1]
    own = pl.ds(2 * place[len(pieces)], 2)
    copies = []
    for index, piece in enumerate(pieces):
        width = piece.shape[2]
        offset = pl.multiple_of(place[index] * width, width)
        copies += [
            pltpu.make_async_copy(
                field.at[:, :, pl.ds(offset, width)],
                piece.at[:, pl.ds(0, rows_here), :],
                sems.at[index, 0],
            ),
            pltpu.make_async_copy(
                coupling.at[own], piece.at[:, pl.ds(rows_here, tall), :], sems.at[index, 1]
            ),
        ]
    start_all(copies)
    wait_all(copies)


def unpack_kernel(place, own, *rest):
    pieces, field, sems = rest[:-2], rest[-2], rest[-1]
    copies = []
    for index, piece in enumerate(pieces):
        width = piece.shape[2]
        offset = pl.multiple_of(place[index] * width, width)
        target = field.at[:, :, pl.ds(offset, width)]
        if index:
            copies.append(pltpu.make_async_copy(piece, target, sems.at[index]))
        else:
            copies.append(Either(place[len(pieces) + 1], own, piece, target, sems.at[index]))
    start_all(copies)
    wait_all(copies)


def column_kernel(info, blocks, own, p0, p1, p2, p3, x_column, y_turned, rows_held, sems):
    count, factors, height, width = blocks.shape
    last = pl.ds(own.shape[1] - rows_held.shape[2], rows_held.shape[2])
    parts = [piece.at[:, last, :] for piece in (p0, p1, p2, p3)]
    copies = [Either(info[info_self], own.at[:, last, :], parts[0], rows_held.at[0], sems.at[0])]
    for index in range(1, len(parts)):
        copies.append(pltpu.make_async_copy(parts[index], rows_held.at[index], sems.at[index]))
    start_all(copies)
    for index in range(count):
        x_column[index * height : (index + 1) * height] = blocks[index, 0]
    column = blocks[:, 1].reshape(count * height, width)
    y_turned[...] = column.astype(f32).T.astype(bf16)
    wait_all(copies)


def field_kernel(info, own, p0, p1, p2, p3, rhs, sems):
    height = rhs.shape[2] // 2
    copies = []
    for index, piece in enumerate((p0, p1, p2, p3)):
        slot, half = info[info_piece + 2 * index], info[info_piece + 2 * index + 1]
        rows = pl.ds(pl.multiple_of(half * height, height), height)
        part = (slice(None), pl.ds(0, height), slice(None))
        ends = (rhs.at[slot, :, rows, :], sems.at[index])
        if index:
            copies.append(pltpu.make_async_copy(piece.at[part], *ends))
        else:
            copies.append(Either(info[info_self], own.at[part], piece.at[part], *ends))
    start_all(copies)
    wait_all(copies)


def weight_kernel(info, c0, c1, c2, c3, weights, sems):
    height = c0.shape[1]
    half_height = weights.shape[1] // 2
    copies = []
    for index, block in enumerate((c0, c1, c2, c3)):
        for turn in range(block.shape[0]):
            slot, half = info[info_piece + 2 * turn], info[info_piece + 2 * turn + 1]
            start = half * half_height + info[info_block + index] * height
            rows = pl.ds(pl.multiple_of(start, height), height)
            copies.append(
                pltpu.make_async_copy(
                    block.at[turn], weights.at[slot, rows, :], sems.at[index, turn]
                )
            )
    start_all(copies)
    wait_all(copies)


def both_kernel(info, x_column, x_aside, y_column, y0, y1, rhs, x_both, y_both, sems):
    copies = [
        pltpu.make_async_copy(x_column, x_both.at[0], sems.at[0]),
        pltpu.make_async_copy(x_aside, x_both.at[1], sems.at[1]),
        Either(info[info_self], y_column, y0, y_both.at[0], sems.at[2]),
        pltpu.make_async_copy(y1, y_both.at[1], sems.at[3]),
    ]
    start_all(copies)
    wait_all(copies)


class Layers:
    def __init__(self, info, x_parts, y_parts, held, beside, below, sems):
        self.info, self.order = info, held.shape[1]
        self.x_parts, self.y_parts, self.held = x_parts, y_parts, held
        self.beside, self.below, self.sems = beside, below, sems

    def x_copies(self, slot, part):
        height = self.order // 2
        copies = []
        for far in range(2):
            rows = pl.ds(pl.multiple_of(self.info[info_half + far] * height, height), height)
            copies.append(
                pltpu.make_async_copy(
                    part.at[far], self.held.at[slot, rows], self.sems.at[slot, far]
                )
            )
        return copies

    def start(self, slot):
        own, first, second = self.x_parts
        turn, same = self.info[info_slot + slot], self.info[info_self]
        for hit, part in (
            ((turn == 0) & (same != 0), own),
            ((turn == 0) & (same == 0), first),
            (turn == 1, second),
        ):

            @pl.when(hit)
            def _():
                start_all(self.x_copies(slot, part))

    def apply(self, slot, source, store, fresh):
        order, beside, below = self.order, self.beside, self.below
        turn = self.info[info_slot + slot]
        for rows in row_chunks(order, 256):
            further = slice(rows.start + order, rows.stop + order)
            real, imag = source(0, rows), source(1, rows)
            beside[rows, :order] = real
            beside[rows, order:] = -imag
            beside[further, :order] = imag
            beside[further, order:] = real
        height = order // 2
        for far, part in enumerate(self.y_parts):
            product = jnp.dot(beside[...], part[turn], preferred_element_type=f32).astype(bf16)
            start = self.info[info_half + far] * height
            columns = pl.ds(pl.multiple_of(start, height), height)
            beyond = pl.ds(pl.multiple_of(order + start, height), height)
            below[:order, columns] = product[:order]
            below[:order, beyond] = product[order:]
            below[order:, columns] = -product[order:]
            below[order:, beyond] = product[:order]
        if fresh:
            wait_all(self.x_copies(slot, self.x_parts[0]))
        for plane in range(2):
            for columns in row_chunks(order, 256):
                along = slice(columns.start + plane * order, columns.stop + plane * order)
                store(
                    plane,
                    columns,
                    jnp.dot(self.held[slot], below[:, along], preferred_element_type=f32),
                )


def reduced(rhs, info, slot, weights, incoming):
    def source(plane, rows):
        values = rhs[slot, plane, rows]
        if plane == 0:
            row = lax.broadcasted_iota(jnp.int32, values.shape, 0) + rows.start
            column = lax.broadcasted_iota(jnp.int32, values.shape, 1)
            hit = (row == info[1]) & (column == info[2]) & (info[0] == slot)
            values = values + jnp.where(hit, f32(source_amplitude), f32(0.0)).astype(bf16)
        return values - weights[slot, rows] * incoming(plane, rows)

    return source


def sent(weights, slot, field):
    return lambda plane, rows: weights[slot, rows] * field[plane, rows]


def subtract_into(target, forward):
    def store(plane, columns, values):
        target[plane, :, columns] = forward[plane, :, columns] - values.astype(bf16)

    return store


def round_into(target):
    def store(plane, columns, values):
        target[plane, :, columns] = values.astype(bf16)

    return store


def first_kernel(info, xb, x0, x1, yb, yf, weights, rhs, w_low, w_high, held, beside, below, sems):
    @pl.when(info[info_member] == 0)
    def _():
        layers = Layers(info, (xb, x0, x1), (yb, yf), held, beside, below, sems)
        layers.start(0)
        layers.start(1)
        zero = reduced(rhs, info, 0, weights, lambda plane, rows: bf16(0.0))
        layers.apply(0, zero, round_into(w_low), True)
        one = reduced(rhs, info, 1, weights, lambda plane, rows: w_low[plane, rows])
        layers.apply(1, one, round_into(w_high), True)


def last_kernel(info, xb, x0, x1, yb, yf, weights, rhs, arrived, field, back, forward, held, beside,
                below, sems):
    @pl.when(info[info_member] == 1)
    def _():
        layers = Layers(info, (xb, x0, x1), (yb, yf), held, beside, below, sems)
        layers.start(0)
        layers.start(1)
        low, high = field.at[0], field.at[1]
        two = reduced(rhs, info, 0, weights, lambda plane, rows: arrived[plane, rows])
        layers.apply(0, two, round_into(forward), True)
        three = reduced(rhs, info, 1, weights, lambda plane, rows: forward[plane, rows])
        layers.apply(1, three, round_into(high), True)
        layers.apply(0, sent(weights, 1, high), subtract_into(low, forward), False)
        last = sent(weights, 0, low)
        for plane in range(2):
            for rows in row_chunks(weights.shape[1], 256):
                back[plane, rows] = last(plane, rows)


def back_kernel(info, xb, x0, x1, yb, yf, weights, w_low, w_high, arrived, field, p0, p1, p2, p3,
                kept, held, beside, below, sems, osems):
    def start_pieces(source, slot):
        for index, piece in enumerate((p0, p1, p2, p3)):
            height = piece.shape[1]
            half = info[info_piece + 2 * index + 1]
            rows = pl.ds(pl.multiple_of(half * height, height), height)

            @pl.when(info[info_piece + 2 * index] == slot)
            def _():
                pltpu.make_async_copy(source.at[slot, :, rows, :], piece, osems.at[index]).start()

    @pl.when(info[info_member] == 0)
    def _():
        layers = Layers(info, (xb, x0, x1), (yb, yf), held, beside, below, sems)
        layers.start(1)
        layers.start(0)
        low, high = kept.at[0], kept.at[1]
        layers.apply(
            1, lambda plane, rows: arrived[plane, rows], subtract_into(high, w_high), True
        )
        start_pieces(kept, 1)
        layers.apply(0, sent(weights, 1, high), subtract_into(low, w_low), True)
        start_pieces(kept, 0)

    @pl.when(info[info_member] != 0)
    def _():
        start_pieces(field, 1)
        start_pieces(field, 0)

    for index, piece in enumerate((p0, p1, p2, p3)):
        part = kept.at[0, :, pl.ds(0, piece.shape[1]), :]
        pltpu.make_async_copy(part, piece, osems.at[index]).wait()


def on_device(background, src_pos, coupling, x_factor, y_factor):
    px_count = lax.axis_size("px")
    sec_index, own_x, own_y = (lax.axis_index(axis) for axis in ("sec", "px", "py"))
    group, member = sec_index // 2, sec_index % 2
    groups = lax.axis_size("sec") // 2
    order = y_factor.shape[3]
    field = background[:, 0]
    rows_here = field.shape[1]
    height = x_factor.shape[2]
    params = pltpu.CompilerParams(vmem_limit_bytes=vmem_bytes)
    rounds = [(a, b) for a in range(groups) for b in range(px_count)]

    def pairs(a, b):
        return [
            ((2 * x + c) * px_count + y, (2 * ((c + a) % 2) + x) * px_count + (y + b) % px_count)
            for x in range(groups)
            for c in range(2)
            for y in range(px_count)
            if (a, b, x) != (0, 0, c)
        ]

    def back_pairs(a, b):
        return [(target, source) for source, target in pairs(a, b)]

    own_source = src_pos[own_y * groups * px_count + group * px_count + own_x]
    plane_cells = x_factor.shape[3] * order
    layer = own_source // plane_cells
    remainder = own_source % plane_cells
    py_count = lax.axis_size("py")
    entries = [
        jnp.where(layer // 2 == member, layer % 2, -1),
        remainder // order,
        remainder % order,
        member,
    ]
    for a, b in rounds:
        entries += [(group + a) % 2, (own_x - b) % px_count]
    entries += [group, (group + 1) % 2, own_x, (own_x + 1) % 2]
    pair = own_y // 2 * 2
    entries += [own_y, pair + (own_y + 1) % 2, (own_y + 2) % 4, (pair + 2) % 4 + (own_y + 1) % 2]
    entries += [group == member]
    info = jnp.stack([jnp.asarray(entry, jnp.int32) for entry in entries])

    sends_to = jnp.stack(
        [((member + a) % 2) * px_count + (own_x + b) % px_count for a, b in rounds]
        + [own_y, group == member]
    ).astype(jnp.int32)
    piece_shape = jax.ShapeDtypeStruct((2, rows_here, order), bf16)
    blocks = pl.pallas_call(
        block_kernel,
        out_shape=jax.ShapeDtypeStruct((py_count, 2, height, 2 * order), bf16),
        in_specs=[in_hbm] * 2,
        out_specs=in_vmem,
        scratch_shapes=[pltpu.SemaphoreType.DMA((py_count, 2, 2))],
        compiler_params=params,
    )(x_factor[0], y_factor[0])
    tall = height // 2
    packed = pl.pallas_call(
        pack_kernel,
        out_shape=[jax.ShapeDtypeStruct((2, rows_here + tall, order), bf16)] * len(rounds),
        in_specs=[in_smem] + [in_hbm] * 2,
        out_specs=[in_vmem] * len(rounds),
        scratch_shapes=[pltpu.SemaphoreType.DMA((len(rounds), 2))],
        compiler_params=params,
    )(sends_to, field, coupling[0].reshape(rows_here // tall, tall, order))
    pieces = [
        lax.ppermute(piece, ("sec", "px"), pairs(a, b)) for piece, (a, b) in zip(packed, rounds)
    ]
    blocks = lax.all_to_all(blocks, "py", split_axis=0, concat_axis=0, tiled=True)

    column_shape = jax.ShapeDtypeStruct((rows_here, 2 * order), bf16)
    turned_shape = jax.ShapeDtypeStruct((2 * order, rows_here), bf16)
    x_column, y_turned, rows_held = pl.pallas_call(
        column_kernel,
        out_shape=[
            column_shape,
            turned_shape,
            jax.ShapeDtypeStruct((len(rounds), 2, tall, order), bf16),
        ],
        in_specs=[in_smem, in_vmem] + [anywhere] * 5,
        out_specs=[in_vmem] * 3,
        scratch_shapes=[pltpu.SemaphoreType.DMA((len(rounds),))],
        compiler_params=params,
    )(info, blocks, packed[0], *pieces)
    rows_held = rows_held.reshape(len(rounds), height, order)

    def across(block, a):
        return lax.ppermute(block, ("sec", "px"), pairs(a, 0))

    def aside(block):
        return lax.ppermute(block, "px", [(y, (y + 1) % 2) for y in range(2)])

    def over_z(block, bit):
        return lax.ppermute(block, "py", [(z, z ^ bit) for z in range(py_count)])

    y_near = [across(y_turned, a) for a in range(2)]
    x_aside = aside(x_column)
    rows_next = over_z(rows_held, 1)
    rows_far = over_z(rows_held, 2)
    full_shape = jax.ShapeDtypeStruct((2, order, order), bf16)
    double_shape = jax.ShapeDtypeStruct((2, 2, order, order), bf16)
    rhs = pl.pallas_call(
        field_kernel,
        out_shape=double_shape,
        in_specs=[in_smem] + [anywhere] * 5,
        out_specs=in_vmem,
        scratch_shapes=[pltpu.SemaphoreType.DMA((len(rounds),))],
        compiler_params=params,
    )(info, packed[0], *pieces)
    x_both, y_both = pl.pallas_call(
        both_kernel,
        out_shape=[
            jax.ShapeDtypeStruct((2,) + one.shape, bf16) for one in (column_shape, turned_shape)
        ],
        in_specs=[in_smem] + [anywhere] * 6,
        out_specs=[in_vmem] * 2,
        scratch_shapes=[pltpu.SemaphoreType.DMA((4,))],
        compiler_params=params,
    )(info, x_column, x_aside, y_turned, *y_near, rhs)
    y_far = aside(y_both)
    x_across = [across(x_both, a) for a in range(2)]
    weights = pl.pallas_call(
        weight_kernel,
        out_shape=full_shape,
        in_specs=[in_smem] + [anywhere] * 4,
        out_specs=in_vmem,
        scratch_shapes=[pltpu.SemaphoreType.DMA((4, len(rounds)))],
        compiler_params=params,
        cost_estimate=pl.CostEstimate(
            flops=3 * 10**10, bytes_accessed=2**21, transcendentals=0
        ),
    )(info, rows_held, rows_next, rows_far, over_z(rows_next, 2))
    layers = (info, x_both, *x_across, y_both, y_far, weights)
    layer_specs = [in_smem] + [anywhere] * 3 + [in_vmem] * 3
    solver_scratch = [
        pltpu.VMEM((2, order, 2 * order), bf16),
        pltpu.VMEM((2 * order, 2 * order), bf16),
        pltpu.VMEM((2 * order, 2 * order), bf16),
        pltpu.SemaphoreType.DMA((2, 2)),
    ]

    def cost(solves):
        return pl.CostEstimate(
            flops=solves * 16 * order**3, bytes_accessed=16 * order**2 * 2, transcendentals=0
        )

    w_low, w_high = pl.pallas_call(
        first_kernel,
        out_shape=[full_shape] * 2,
        in_specs=layer_specs + [in_vmem],
        out_specs=[in_vmem] * 2,
        scratch_shapes=solver_scratch,
        compiler_params=params,
        cost_estimate=cost(2),
    )(*layers, rhs)

    up = [(2 * x, 2 * x + 1) for x in range(groups)]
    incoming = lax.ppermute(w_high, "sec", up)
    solved, back = pl.pallas_call(
        last_kernel,
        out_shape=[double_shape, full_shape],
        in_specs=layer_specs + [in_vmem] * 2,
        out_specs=[in_vmem] * 2,
        scratch_shapes=[pltpu.VMEM((2, order, order), bf16)] + solver_scratch,
        compiler_params=params,
        cost_estimate=cost(3),
    )(*layers, rhs, incoming)

    down = [(target, source) for source, target in up]
    incoming = lax.ppermute(back, "sec", down)
    results = pl.pallas_call(
        back_kernel,
        out_shape=[piece_shape] * len(rounds),
        in_specs=layer_specs + [in_vmem] * 3 + [anywhere],
        out_specs=[anywhere] * len(rounds),
        scratch_shapes=[pltpu.VMEM((2, 2, order, order), bf16)]
        + solver_scratch
        + [pltpu.SemaphoreType.DMA((len(rounds),))],
        compiler_params=params,
        cost_estimate=cost(2),
    )(*layers, w_low, w_high, incoming, solved)
    received = [
        lax.ppermute(piece, ("sec", "px"), back_pairs(a, b)) for piece, (a, b) in zip(results, rounds)
    ]
    output = pl.pallas_call(
        unpack_kernel,
        out_shape=jax.ShapeDtypeStruct(field.shape, bf16),
        in_specs=[in_smem] + [anywhere] * (len(rounds) + 1),
        out_specs=in_vmem,
        scratch_shapes=[pltpu.SemaphoreType.DMA((len(rounds),))],
        compiler_params=params,
    )(sends_to, results[0], *received)
    return output[:, None]


def chip_plan_fits(mesh):
    return mesh.shape["sec"] == 4 and mesh.shape["px"] == 2 and mesh.shape["py"] == 4


def solution(mesh):
    placed = (
        P(None, "sec", "px", "py"),
        P(),
        P("sec", "px", None),
        P("sec", None, ("px", "py"), None),
        P("sec", None, ("px", "py"), None),
    )
    return jax.shard_map(
        on_device if chip_plan_fits(mesh) else on_device_by_layer,
        mesh=mesh,
        in_specs=placed,
        out_specs=P(None, "sec", "px", "py"),
        check_vma=False,
    )
```

```python
import functools

import jax
import jax.numpy as jnp
from jax import lax
from jax.experimental import pallas as pl
from jax.experimental.pallas import tpu as pltpu
from jax.sharding import PartitionSpec as P

source_amplitude = 8.0
vmem_bytes = 32 * 1024 * 1024
bf16 = jnp.bfloat16
f32 = jnp.float32
anywhere = pl.BlockSpec(memory_space=pl.ANY)
in_hbm = pl.BlockSpec(memory_space=pltpu.HBM)
in_smem = pl.BlockSpec(memory_space=pltpu.SMEM)
in_vmem = pl.BlockSpec(memory_space=pltpu.VMEM)

info_member, info_piece, info_slot, info_half, info_block, info_self = 3, 4, 12, 14, 16, 18


def shifted(x, axis, by):
    peers = lax.axis_size(axis)
    pairs = [(i, i + by) for i in range(peers) if 0 <= i + by < peers]
    return lax.ppermute(x, axis, pairs)


def complex_block(factor):
    upper = jnp.concatenate([factor[0], -factor[1]], axis=1)
    lower = jnp.concatenate([factor[1], factor[0]], axis=1)
    return jnp.concatenate([upper, lower], axis=0)


def y_transform(real_turned, imag_turned, field_in):
    real_part = jnp.dot(field_in[0], real_turned, preferred_element_type=jnp.float32) - jnp.dot(
        field_in[1], imag_turned, preferred_element_type=jnp.float32
    )
    imag_part = jnp.dot(field_in[0], imag_turned, preferred_element_type=jnp.float32) + jnp.dot(
        field_in[1], real_turned, preferred_element_type=jnp.float32
    )
    return jnp.stack([real_part, imag_part]).astype(jnp.bfloat16)


def x_transform(x_block, field_in):
    planes, rows_all, width = field_in.shape
    output = jnp.dot(
        x_block, field_in.reshape(planes * rows_all, width), preferred_element_type=jnp.float32
    )
    return output.astype(jnp.bfloat16).reshape(planes, rows_all, width)


def scale_rows(field_in, weights, width):
    planes, rows_here, merged = field_in.shape
    spread = field_in.astype(jnp.float32).reshape(planes, rows_here, merged // width, width)
    return (spread * weights.astype(jnp.float32)[None, :, None, :]).reshape(
        planes, rows_here, merged
    )


def pick_batch(field, batch_count, batch_index):
    planes, rows_here, merged = field.shape
    split_field = field.reshape(planes, rows_here, batch_count, merged // batch_count)
    return lax.dynamic_index_in_dim(split_field, batch_index, 2, keepdims=False)


def place_batch(field, piece, batch_count, batch_index):
    planes, rows_here, merged = field.shape
    split_field = field.reshape(planes, rows_here, batch_count, merged // batch_count)
    shaped = piece.reshape(planes, rows_here, 1, merged // batch_count)
    updated = lax.dynamic_update_slice_in_dim(split_field, shaped, batch_index, 2)
    return updated.reshape(planes, rows_here, merged)


def on_device_by_layer(background, src_pos, coupling, x_factor, y_factor):
    source_count = src_pos.shape[0]
    sec_count = lax.axis_size("sec")
    sec_index = lax.axis_index("sec")
    grid_y = lax.axis_size("py")
    own_x = lax.axis_index("px")
    own_y = lax.axis_index("py")
    local_sources = source_count // grid_y
    x_pieces, y_pieces = (
        lax.all_gather(x_factor[0], ("px", "py"), axis=1, tiled=True),
        lax.all_gather(y_factor[0], ("px", "py"), axis=1, tiled=True),
    )
    x_block = complex_block(x_pieces)
    real_turned = y_pieces[0].T
    imag_turned = y_pieces[1].T
    local_field = background[:, 0]
    local_weights = coupling[0]
    rows_here = local_field.shape[1]
    full_cols = y_factor.shape[3]
    plane_cells = x_factor.shape[3] * full_cols
    own_sources = lax.dynamic_slice_in_dim(src_pos, own_y * local_sources, local_sources)
    layer_of = own_sources // plane_cells
    remainder = own_sources % plane_cells
    row_of = remainder // full_cols
    column_of = remainder % full_cols
    row_start = own_x * rows_here
    row_hit = row_of[None, :] == row_start + jnp.arange(rows_here, dtype=jnp.int32)[:, None]
    col_hit = column_of[:, None] == jnp.arange(full_cols, dtype=jnp.int32)[None, :]
    layer_hit = layer_of == sec_index
    delta = (row_hit[:, :, None] & col_hit[None, :, :] & layer_hit[None, :, None]).astype(
        jnp.float32
    )
    delta = (delta * source_amplitude).reshape(rows_here, local_sources * full_cols)
    real_rhs = local_field[0].astype(jnp.float32) + delta
    rhs_field = jnp.stack([real_rhs, local_field[1].astype(jnp.float32)])

    def apply_front(field_in):
        turned = y_transform(real_turned, imag_turned, field_in)
        line_field = lax.all_to_all(turned, "px", split_axis=2, concat_axis=1, tiled=True)
        finished = x_transform(x_block, line_field)
        return lax.all_to_all(finished, "px", split_axis=1, concat_axis=2, tiled=True)

    forward_field = jnp.zeros(local_field.shape, jnp.bfloat16)
    outgoing = pick_batch(forward_field, sec_count, 0)
    for step in range(2 * sec_count - 1):
        incoming = shifted(outgoing, "sec", 1)
        batch_index = step - sec_index
        active = (batch_index >= 0) & (batch_index < sec_count)
        clamped = jnp.clip(batch_index, 0, sec_count - 1)
        rhs_batch = pick_batch(rhs_field, sec_count, clamped)
        reduced = (rhs_batch - scale_rows(incoming, local_weights, full_cols)).astype(jnp.bfloat16)
        candidate = apply_front(reduced)
        previous = pick_batch(forward_field, sec_count, clamped)
        kept = jnp.where(active, candidate, previous)
        forward_field = place_batch(forward_field, kept, sec_count, clamped)
        outgoing = candidate
    sweep_field = forward_field
    for step in range(2 * sec_count - 2):
        send_index = jnp.clip(step - (sec_count - 1 - sec_index), 0, sec_count - 1)
        own_batch = pick_batch(sweep_field, sec_count, send_index)
        sent_field = scale_rows(own_batch, local_weights, full_cols).astype(jnp.bfloat16)
        incoming = shifted(sent_field, "sec", -1)
        batch_index = step - (sec_count - 2 - sec_index)
        active = (batch_index >= 0) & (batch_index < sec_count) & (sec_index <= sec_count - 2)
        clamped = jnp.clip(batch_index, 0, sec_count - 1)
        solved = apply_front(incoming)
        forward_batch = pick_batch(forward_field, sec_count, clamped)
        candidate = (forward_batch.astype(jnp.float32) - solved.astype(jnp.float32)).astype(
            jnp.bfloat16
        )
        previous = pick_batch(sweep_field, sec_count, clamped)
        kept = jnp.where(active, candidate, previous)
        sweep_field = place_batch(sweep_field, kept, sec_count, clamped)
    return sweep_field[:, None]


def start_all(copies):
    for copy in copies:
        copy.start()


def wait_all(copies):
    for copy in copies:
        copy.wait()


def row_chunks(order, step):
    step = min(step, order)
    return [slice(first, first + step) for first in range(0, order, step)]


class Either:
    def __init__(self, flag, own, received, target, sem):
        self.flag = flag
        self.own = pltpu.make_async_copy(own, target, sem)
        self.received = pltpu.make_async_copy(received, target, sem)

    def start(self):
        @pl.when(self.flag != 0)
        def _():
            self.own.start()

        @pl.when(self.flag == 0)
        def _():
            self.received.start()

    def wait(self):
        self.received.wait()


def block_kernel(x_factor, y_factor, blocks, sems):
    order = x_factor.shape[2]
    copies = []
    for target in range(blocks.shape[0]):
        for which, factor in enumerate((x_factor, y_factor)):
            for plane in range(2):
                copies.append(
                    pltpu.make_async_copy(
                        factor.at[plane],
                        blocks.at[target, which, :, pl.ds(plane * order, order)],
                        sems.at[target, which, plane],
                    )
                )
    start_all(copies)
    wait_all(copies)


def pack_kernel(place, field, coupling, *rest):
    pieces, sems = rest[:-1], rest[-1]
    rows_here = field.shape[1]
    tall = coupling.shape[1]
    own = pl.ds(2 * place[len(pieces)], 2)
    copies = []
    for index, piece in enumerate(pieces):
        width = piece.shape[2]
        offset = pl.multiple_of(place[index] * width, width)
        copies += [
            pltpu.make_async_copy(
                field.at[:, :, pl.ds(offset, width)],
                piece.at[:, pl.ds(0, rows_here), :],
                sems.at[index, 0],
            ),
            pltpu.make_async_copy(
                coupling.at[own], piece.at[:, pl.ds(rows_here, tall), :], sems.at[index, 1]
            ),
        ]
    start_all(copies)
    wait_all(copies)


def unpack_kernel(place, own, *rest):
    pieces, field, sems = rest[:-2], rest[-2], rest[-1]
    copies = []
    for index, piece in enumerate(pieces):
        width = piece.shape[2]
        offset = pl.multiple_of(place[index] * width, width)
        target = field.at[:, :, pl.ds(offset, width)]
        if index:
            copies.append(pltpu.make_async_copy(piece, target, sems.at[index]))
        else:
            copies.append(Either(place[len(pieces) + 1], own, piece, target, sems.at[index]))
    start_all(copies)
    wait_all(copies)


def column_kernel(info, blocks, own, p0, p1, p2, p3, x_column, y_turned, rows_held, sems):
    count, factors, height, width = blocks.shape
    last = pl.ds(own.shape[1] - rows_held.shape[2], rows_held.shape[2])
    parts = [piece.at[:, last, :] for piece in (p0, p1, p2, p3)]
    copies = [Either(info[info_self], own.at[:, last, :], parts[0], rows_held.at[0], sems.at[0])]
    for index in range(1, len(parts)):
        copies.append(pltpu.make_async_copy(parts[index], rows_held.at[index], sems.at[index]))
    start_all(copies)
    for index in range(count):
        x_column[index * height : (index + 1) * height] = blocks[index, 0]
    column = blocks[:, 1].reshape(count * height, width)
    y_turned[...] = column.astype(f32).T.astype(bf16)
    wait_all(copies)


def field_kernel(info, own, p0, p1, p2, p3, rhs, sems):
    height = rhs.shape[2] // 2
    copies = []
    for index, piece in enumerate((p0, p1, p2, p3)):
        slot, half = info[info_piece + 2 * index], info[info_piece + 2 * index + 1]
        rows = pl.ds(pl.multiple_of(half * height, height), height)
        part = (slice(None), pl.ds(0, height), slice(None))
        ends = (rhs.at[slot, :, rows, :], sems.at[index])
        if index:
            copies.append(pltpu.make_async_copy(piece.at[part], *ends))
        else:
            copies.append(Either(info[info_self], own.at[part], piece.at[part], *ends))
    start_all(copies)
    wait_all(copies)


def weight_kernel(info, c0, c1, weights, sems):
    height = c0.shape[1]
    half_height = weights.shape[1] // 2
    copies = []
    for index, block in enumerate((c0, c1)):
        for turn in range(block.shape[0]):
            slot, half = info[info_piece + 2 * turn], info[info_piece + 2 * turn + 1]
            start = half * half_height + info[info_block + index] * height
            rows = pl.ds(pl.multiple_of(start, height), height)
            copies.append(
                pltpu.make_async_copy(
                    block.at[turn], weights.at[slot, rows, :], sems.at[index, turn]
                )
            )
    start_all(copies)
    wait_all(copies)


def both_kernel(info, x_column, x_aside, y_column, y0, y1, rhs, x_both, y_both, sems):
    copies = [
        pltpu.make_async_copy(x_column, x_both.at[0], sems.at[0]),
        pltpu.make_async_copy(x_aside, x_both.at[1], sems.at[1]),
        Either(info[info_self], y_column, y0, y_both.at[0], sems.at[2]),
        pltpu.make_async_copy(y1, y_both.at[1], sems.at[3]),
    ]
    start_all(copies)
    wait_all(copies)


class Layers:
    def __init__(self, info, x_parts, y_parts, held, beside, below, sems):
        self.info, self.order = info, held.shape[1]
        self.x_parts, self.y_parts, self.held = x_parts, y_parts, held
        self.beside, self.below, self.sems = beside, below, sems

    def x_copies(self, slot, part):
        height = self.order // 2
        copies = []
        for far in range(2):
            rows = pl.ds(pl.multiple_of(self.info[info_half + far] * height, height), height)
            copies.append(
                pltpu.make_async_copy(
                    part.at[far], self.held.at[slot, rows], self.sems.at[slot, far]
                )
            )
        return copies

    def start(self, slot):
        own, first, second = self.x_parts
        turn, same = self.info[info_slot + slot], self.info[info_self]
        for hit, part in (
            ((turn == 0) & (same != 0), own),
            ((turn == 0) & (same == 0), first),
            (turn == 1, second),
        ):

            @pl.when(hit)
            def _():
                start_all(self.x_copies(slot, part))

    def apply(self, slot, source, store, fresh):
        order, beside, below = self.order, self.beside, self.below
        turn = self.info[info_slot + slot]
        for rows in row_chunks(order, 256):
            further = slice(rows.start + order, rows.stop + order)
            real, imag = source(0, rows), source(1, rows)
            beside[rows, :order] = real
            beside[rows, order:] = -imag
            beside[further, :order] = imag
            beside[further, order:] = real
        height = order // 2
        for far, part in enumerate(self.y_parts):
            product = jnp.dot(beside[...], part[turn], preferred_element_type=f32).astype(bf16)
            start = self.info[info_half + far] * height
            columns = pl.ds(pl.multiple_of(start, height), height)
            beyond = pl.ds(pl.multiple_of(order + start, height), height)
            below[:order, columns] = product[:order]
            below[:order, beyond] = product[order:]
            below[order:, columns] = -product[order:]
            below[order:, beyond] = product[:order]
        if fresh:
            wait_all(self.x_copies(slot, self.x_parts[0]))
        for plane in range(2):
            for columns in row_chunks(order, 256):
                along = slice(columns.start + plane * order, columns.stop + plane * order)
                store(
                    plane,
                    columns,
                    jnp.dot(self.held[slot], below[:, along], preferred_element_type=f32),
                )


def reduced(rhs, info, slot, weights, incoming):
    def source(plane, rows):
        values = rhs[slot, plane, rows]
        if plane == 0:
            row = lax.broadcasted_iota(jnp.int32, values.shape, 0) + rows.start
            column = lax.broadcasted_iota(jnp.int32, values.shape, 1)
            hit = (row == info[1]) & (column == info[2]) & (info[0] == slot)
            values = values + jnp.where(hit, f32(source_amplitude), f32(0.0)).astype(bf16)
        return values - weights[slot, rows] * incoming(plane, rows)

    return source


def sent(weights, slot, field):
    return lambda plane, rows: weights[slot, rows] * field[plane, rows]


def subtract_into(target, forward):
    def store(plane, columns, values):
        target[plane, :, columns] = forward[plane, :, columns] - values.astype(bf16)

    return store


def round_into(target):
    def store(plane, columns, values):
        target[plane, :, columns] = values.astype(bf16)

    return store


def first_kernel(info, xb, x0, x1, yb, yf, weights, rhs, w_low, w_high, held, beside, below, sems):
    @pl.when(info[info_member] == 0)
    def _():
        layers = Layers(info, (xb, x0, x1), (yb, yf), held, beside, below, sems)
        layers.start(0)
        layers.start(1)
        zero = reduced(rhs, info, 0, weights, lambda plane, rows: bf16(0.0))
        layers.apply(0, zero, round_into(w_low), True)
        one = reduced(rhs, info, 1, weights, lambda plane, rows: w_low[plane, rows])
        layers.apply(1, one, round_into(w_high), True)


def last_kernel(info, xb, x0, x1, yb, yf, weights, rhs, arrived, field, back, forward, held, beside,
                below, sems):
    @pl.when(info[info_member] == 1)
    def _():
        layers = Layers(info, (xb, x0, x1), (yb, yf), held, beside, below, sems)
        layers.start(0)
        layers.start(1)
        low, high = field.at[0], field.at[1]
        two = reduced(rhs, info, 0, weights, lambda plane, rows: arrived[plane, rows])
        layers.apply(0, two, round_into(forward), True)
        three = reduced(rhs, info, 1, weights, lambda plane, rows: forward[plane, rows])
        layers.apply(1, three, round_into(high), True)
        layers.apply(0, sent(weights, 1, high), subtract_into(low, forward), False)
        last = sent(weights, 0, low)
        for plane in range(2):
            for rows in row_chunks(weights.shape[1], 256):
                back[plane, rows] = last(plane, rows)


def back_kernel(info, xb, x0, x1, yb, yf, weights, w_low, w_high, arrived, field, p0, p1, p2, p3,
                kept, held, beside, below, sems, osems):
    def start_pieces(source, slot):
        for index, piece in enumerate((p0, p1, p2, p3)):
            height = piece.shape[1]
            half = info[info_piece + 2 * index + 1]
            rows = pl.ds(pl.multiple_of(half * height, height), height)

            @pl.when(info[info_piece + 2 * index] == slot)
            def _():
                pltpu.make_async_copy(source.at[slot, :, rows, :], piece, osems.at[index]).start()

    @pl.when(info[info_member] == 0)
    def _():
        layers = Layers(info, (xb, x0, x1), (yb, yf), held, beside, below, sems)
        layers.start(1)
        layers.start(0)
        low, high = kept.at[0], kept.at[1]
        layers.apply(
            1, lambda plane, rows: arrived[plane, rows], subtract_into(high, w_high), True
        )
        start_pieces(kept, 1)
        layers.apply(0, sent(weights, 1, high), subtract_into(low, w_low), True)
        start_pieces(kept, 0)

    @pl.when(info[info_member] != 0)
    def _():
        start_pieces(field, 1)
        start_pieces(field, 0)

    for index, piece in enumerate((p0, p1, p2, p3)):
        part = kept.at[0, :, pl.ds(0, piece.shape[1]), :]
        pltpu.make_async_copy(part, piece, osems.at[index]).wait()


def on_device(background, src_pos, coupling, x_factor, y_factor):
    px_count = lax.axis_size("px")
    sec_index, own_x, own_y = (lax.axis_index(axis) for axis in ("sec", "px", "py"))
    group, member = sec_index // 2, sec_index % 2
    groups = lax.axis_size("sec") // 2
    order = y_factor.shape[3]
    field = background[:, 0]
    rows_here = field.shape[1]
    height = x_factor.shape[2]
    params = pltpu.CompilerParams(vmem_limit_bytes=vmem_bytes)
    rounds = [(a, b) for a in range(groups) for b in range(px_count)]

    def pairs(a, b):
        return [
            ((2 * x + c) * px_count + y, (2 * ((c + a) % 2) + x) * px_count + (y + b) % px_count)
            for x in range(groups)
            for c in range(2)
            for y in range(px_count)
            if (a, b, x) != (0, 0, c)
        ]

    def back_pairs(a, b):
        return [(target, source) for source, target in pairs(a, b)]

    own_source = src_pos[own_y * groups * px_count + group * px_count + own_x]
    plane_cells = x_factor.shape[3] * order
    layer = own_source // plane_cells
    remainder = own_source % plane_cells
    py_count = lax.axis_size("py")
    entries = [
        jnp.where(layer // 2 == member, layer % 2, -1),
        remainder // order,
        remainder % order,
        member,
    ]
    for a, b in rounds:
        entries += [(group + a) % 2, (own_x - b) % px_count]
    entries += [group, (group + 1) % 2, own_x, (own_x + 1) % 2]
    entries += [own_y % 2, (own_y + 1) % 2, group == member]
    info = jnp.stack([jnp.asarray(entry, jnp.int32) for entry in entries])

    sends_to = jnp.stack(
        [((member + a) % 2) * px_count + (own_x + b) % px_count for a, b in rounds]
        + [own_y % 2, group == member]
    ).astype(jnp.int32)
    piece_shape = jax.ShapeDtypeStruct((2, rows_here, order), bf16)
    blocks = pl.pallas_call(
        block_kernel,
        out_shape=jax.ShapeDtypeStruct((py_count, 2, height, 2 * order), bf16),
        in_specs=[in_hbm] * 2,
        out_specs=in_vmem,
        scratch_shapes=[pltpu.SemaphoreType.DMA((py_count, 2, 2))],
        compiler_params=params,
    )(x_factor[0], y_factor[0])
    tall = rows_here // 4
    packed = pl.pallas_call(
        pack_kernel,
        out_shape=[jax.ShapeDtypeStruct((2, rows_here + tall, order), bf16)] * len(rounds),
        in_specs=[in_smem] + [in_hbm] * 2,
        out_specs=[in_vmem] * len(rounds),
        scratch_shapes=[pltpu.SemaphoreType.DMA((len(rounds), 2))],
        compiler_params=params,
    )(sends_to, field, coupling[0].reshape(rows_here // tall, tall, order))
    pieces = [
        lax.ppermute(piece, ("sec", "px"), pairs(a, b)) for piece, (a, b) in zip(packed, rounds)
    ]
    blocks = lax.all_to_all(blocks, "py", split_axis=0, concat_axis=0, tiled=True)

    column_shape = jax.ShapeDtypeStruct((rows_here, 2 * order), bf16)
    turned_shape = jax.ShapeDtypeStruct((2 * order, rows_here), bf16)
    x_column, y_turned, rows_held = pl.pallas_call(
        column_kernel,
        out_shape=[
            column_shape,
            turned_shape,
            jax.ShapeDtypeStruct((len(rounds), 2, tall, order), bf16),
        ],
        in_specs=[in_smem, in_vmem] + [anywhere] * 5,
        out_specs=[in_vmem] * 3,
        scratch_shapes=[pltpu.SemaphoreType.DMA((len(rounds),))],
        compiler_params=params,
    )(info, blocks, packed[0], *pieces)
    rows_held = rows_held.reshape(len(rounds), 2 * tall, order)

    def across(block, a):
        return lax.ppermute(block, ("sec", "px"), pairs(a, 0))

    def aside(block):
        return lax.ppermute(block, "px", [(y, (y + 1) % 2) for y in range(2)])

    def over_z(block, bit):
        return lax.ppermute(block, "py", [(z, z ^ bit) for z in range(py_count)])

    y_near = [across(y_turned, a) for a in range(2)]
    x_aside = aside(x_column)
    rows_next = over_z(rows_held, 1)
    full_shape = jax.ShapeDtypeStruct((2, order, order), bf16)
    double_shape = jax.ShapeDtypeStruct((2, 2, order, order), bf16)
    rhs = pl.pallas_call(
        field_kernel,
        out_shape=double_shape,
        in_specs=[in_smem] + [anywhere] * 5,
        out_specs=in_vmem,
        scratch_shapes=[pltpu.SemaphoreType.DMA((len(rounds),))],
        compiler_params=params,
    )(info, packed[0], *pieces)
    x_both, y_both = pl.pallas_call(
        both_kernel,
        out_shape=[
            jax.ShapeDtypeStruct((2,) + one.shape, bf16) for one in (column_shape, turned_shape)
        ],
        in_specs=[in_smem] + [anywhere] * 6,
        out_specs=[in_vmem] * 2,
        scratch_shapes=[pltpu.SemaphoreType.DMA((4,))],
        compiler_params=params,
    )(info, x_column, x_aside, y_turned, *y_near, rhs)
    y_far = aside(y_both)
    x_across = [across(x_both, a) for a in range(2)]
    weights = pl.pallas_call(
        weight_kernel,
        out_shape=full_shape,
        in_specs=[in_smem] + [anywhere] * 2,
        out_specs=in_vmem,
        scratch_shapes=[pltpu.SemaphoreType.DMA((2, len(rounds)))],
        compiler_params=params,
    )(info, rows_held, rows_next)
    layers = (info, x_both, *x_across, y_both, y_far, weights)
    layer_specs = [in_smem] + [anywhere] * 3 + [in_vmem] * 3
    solver_scratch = [
        pltpu.VMEM((2, order, 2 * order), bf16),
        pltpu.VMEM((2 * order, 2 * order), bf16),
        pltpu.VMEM((2 * order, 2 * order), bf16),
        pltpu.SemaphoreType.DMA((2, 2)),
    ]

    def cost(solves):
        return pl.CostEstimate(
            flops=solves * 16 * order**3, bytes_accessed=16 * order**2 * 2, transcendentals=0
        )

    w_low, w_high = pl.pallas_call(
        first_kernel,
        out_shape=[full_shape] * 2,
        in_specs=layer_specs + [in_vmem],
        out_specs=[in_vmem] * 2,
        scratch_shapes=solver_scratch,
        compiler_params=params,
        cost_estimate=cost(2),
    )(*layers, rhs)

    up = [(2 * x, 2 * x + 1) for x in range(groups)]
    incoming = lax.ppermute(w_high, "sec", up)
    solved, back = pl.pallas_call(
        last_kernel,
        out_shape=[double_shape, full_shape],
        in_specs=layer_specs + [in_vmem] * 2,
        out_specs=[in_vmem] * 2,
        scratch_shapes=[pltpu.VMEM((2, order, order), bf16)] + solver_scratch,
        compiler_params=params,
        cost_estimate=cost(3),
    )(*layers, rhs, incoming)

    down = [(target, source) for source, target in up]
    incoming = lax.ppermute(back, "sec", down)
    results = pl.pallas_call(
        back_kernel,
        out_shape=[piece_shape] * len(rounds),
        in_specs=layer_specs + [in_vmem] * 3 + [anywhere],
        out_specs=[anywhere] * len(rounds),
        scratch_shapes=[pltpu.VMEM((2, 2, order, order), bf16)]
        + solver_scratch
        + [pltpu.SemaphoreType.DMA((len(rounds),))],
        compiler_params=params,
        cost_estimate=cost(2),
    )(*layers, w_low, w_high, incoming, solved)
    received = [
        lax.ppermute(piece, ("sec", "px"), back_pairs(a, b)) for piece, (a, b) in zip(results, rounds)
    ]
    output = pl.pallas_call(
        unpack_kernel,
        out_shape=jax.ShapeDtypeStruct(field.shape, bf16),
        in_specs=[in_smem] + [anywhere] * (len(rounds) + 1),
        out_specs=in_vmem,
        scratch_shapes=[pltpu.SemaphoreType.DMA((len(rounds),))],
        compiler_params=params,
    )(sends_to, results[0], *received)
    return output[:, None]


def chip_plan_fits(mesh):
    return mesh.shape["sec"] == 4 and mesh.shape["px"] == 2 and mesh.shape["py"] == 4


def solution(mesh):
    placed = (
        P(None, "sec", "px", "py"),
        P(),
        P("sec", "px", None),
        P("sec", None, ("px", "py"), None),
        P("sec", None, ("px", "py"), None),
    )
    return jax.shard_map(
        on_device if chip_plan_fits(mesh) else on_device_by_layer,
        mesh=mesh,
        in_specs=placed,
        out_specs=P(None, "sec", "px", "py"),
        check_vma=False,
    )
```

```python
import functools

import jax
import jax.numpy as jnp
from jax import lax
from jax.experimental import pallas as pl
from jax.experimental.pallas import tpu as pltpu
from jax.sharding import PartitionSpec as P

source_amplitude = 8.0
vmem_bytes = 32 * 1024 * 1024
bf16 = jnp.bfloat16
f32 = jnp.float32
anywhere = pl.BlockSpec(memory_space=pl.ANY)
in_hbm = pl.BlockSpec(memory_space=pltpu.HBM)
in_smem = pl.BlockSpec(memory_space=pltpu.SMEM)
in_vmem = pl.BlockSpec(memory_space=pltpu.VMEM)

info_member, info_piece, info_slot, info_half, info_block, info_self = 3, 4, 12, 14, 16, 20


def shifted(x, axis, by):
    peers = lax.axis_size(axis)
    pairs = [(i, i + by) for i in range(peers) if 0 <= i + by < peers]
    return lax.ppermute(x, axis, pairs)


def complex_block(factor):
    upper = jnp.concatenate([factor[0], -factor[1]], axis=1)
    lower = jnp.concatenate([factor[1], factor[0]], axis=1)
    return jnp.concatenate([upper, lower], axis=0)


def y_transform(real_turned, imag_turned, field_in):
    real_part = jnp.dot(field_in[0], real_turned, preferred_element_type=jnp.float32) - jnp.dot(
        field_in[1], imag_turned, preferred_element_type=jnp.float32
    )
    imag_part = jnp.dot(field_in[0], imag_turned, preferred_element_type=jnp.float32) + jnp.dot(
        field_in[1], real_turned, preferred_element_type=jnp.float32
    )
    return jnp.stack([real_part, imag_part]).astype(jnp.bfloat16)


def x_transform(x_block, field_in):
    planes, rows_all, width = field_in.shape
    output = jnp.dot(
        x_block, field_in.reshape(planes * rows_all, width), preferred_element_type=jnp.float32
    )
    return output.astype(jnp.bfloat16).reshape(planes, rows_all, width)


def scale_rows(field_in, weights, width):
    planes, rows_here, merged = field_in.shape
    spread = field_in.astype(jnp.float32).reshape(planes, rows_here, merged // width, width)
    return (spread * weights.astype(jnp.float32)[None, :, None, :]).reshape(
        planes, rows_here, merged
    )


def pick_batch(field, batch_count, batch_index):
    planes, rows_here, merged = field.shape
    split_field = field.reshape(planes, rows_here, batch_count, merged // batch_count)
    return lax.dynamic_index_in_dim(split_field, batch_index, 2, keepdims=False)


def place_batch(field, piece, batch_count, batch_index):
    planes, rows_here, merged = field.shape
    split_field = field.reshape(planes, rows_here, batch_count, merged // batch_count)
    shaped = piece.reshape(planes, rows_here, 1, merged // batch_count)
    updated = lax.dynamic_update_slice_in_dim(split_field, shaped, batch_index, 2)
    return updated.reshape(planes, rows_here, merged)


def on_device_by_layer(background, src_pos, coupling, x_factor, y_factor):
    source_count = src_pos.shape[0]
    sec_count = lax.axis_size("sec")
    sec_index = lax.axis_index("sec")
    grid_y = lax.axis_size("py")
    own_x = lax.axis_index("px")
    own_y = lax.axis_index("py")
    local_sources = source_count // grid_y
    x_pieces, y_pieces = (
        lax.all_gather(x_factor[0], ("px", "py"), axis=1, tiled=True),
        lax.all_gather(y_factor[0], ("px", "py"), axis=1, tiled=True),
    )
    x_block = complex_block(x_pieces)
    real_turned = y_pieces[0].T
    imag_turned = y_pieces[1].T
    local_field = background[:, 0]
    local_weights = coupling[0]
    rows_here = local_field.shape[1]
    full_cols = y_factor.shape[3]
    plane_cells = x_factor.shape[3] * full_cols
    own_sources = lax.dynamic_slice_in_dim(src_pos, own_y * local_sources, local_sources)
    layer_of = own_sources // plane_cells
    remainder = own_sources % plane_cells
    row_of = remainder // full_cols
    column_of = remainder % full_cols
    row_start = own_x * rows_here
    row_hit = row_of[None, :] == row_start + jnp.arange(rows_here, dtype=jnp.int32)[:, None]
    col_hit = column_of[:, None] == jnp.arange(full_cols, dtype=jnp.int32)[None, :]
    layer_hit = layer_of == sec_index
    delta = (row_hit[:, :, None] & col_hit[None, :, :] & layer_hit[None, :, None]).astype(
        jnp.float32
    )
    delta = (delta * source_amplitude).reshape(rows_here, local_sources * full_cols)
    real_rhs = local_field[0].astype(jnp.float32) + delta
    rhs_field = jnp.stack([real_rhs, local_field[1].astype(jnp.float32)])

    def apply_front(field_in):
        turned = y_transform(real_turned, imag_turned, field_in)
        line_field = lax.all_to_all(turned, "px", split_axis=2, concat_axis=1, tiled=True)
        finished = x_transform(x_block, line_field)
        return lax.all_to_all(finished, "px", split_axis=1, concat_axis=2, tiled=True)

    forward_field = jnp.zeros(local_field.shape, jnp.bfloat16)
    outgoing = pick_batch(forward_field, sec_count, 0)
    for step in range(2 * sec_count - 1):
        incoming = shifted(outgoing, "sec", 1)
        batch_index = step - sec_index
        active = (batch_index >= 0) & (batch_index < sec_count)
        clamped = jnp.clip(batch_index, 0, sec_count - 1)
        rhs_batch = pick_batch(rhs_field, sec_count, clamped)
        reduced = (rhs_batch - scale_rows(incoming, local_weights, full_cols)).astype(jnp.bfloat16)
        candidate = apply_front(reduced)
        previous = pick_batch(forward_field, sec_count, clamped)
        kept = jnp.where(active, candidate, previous)
        forward_field = place_batch(forward_field, kept, sec_count, clamped)
        outgoing = candidate
    sweep_field = forward_field
    for step in range(2 * sec_count - 2):
        send_index = jnp.clip(step - (sec_count - 1 - sec_index), 0, sec_count - 1)
        own_batch = pick_batch(sweep_field, sec_count, send_index)
        sent_field = scale_rows(own_batch, local_weights, full_cols).astype(jnp.bfloat16)
        incoming = shifted(sent_field, "sec", -1)
        batch_index = step - (sec_count - 2 - sec_index)
        active = (batch_index >= 0) & (batch_index < sec_count) & (sec_index <= sec_count - 2)
        clamped = jnp.clip(batch_index, 0, sec_count - 1)
        solved = apply_front(incoming)
        forward_batch = pick_batch(forward_field, sec_count, clamped)
        candidate = (forward_batch.astype(jnp.float32) - solved.astype(jnp.float32)).astype(
            jnp.bfloat16
        )
        previous = pick_batch(sweep_field, sec_count, clamped)
        kept = jnp.where(active, candidate, previous)
        sweep_field = place_batch(sweep_field, kept, sec_count, clamped)
    return sweep_field[:, None]


def start_all(copies):
    for copy in copies:
        copy.start()


def wait_all(copies):
    for copy in copies:
        copy.wait()


def row_chunks(order, step):
    step = min(step, order)
    return [slice(first, first + step) for first in range(0, order, step)]


class Either:
    def __init__(self, flag, own, received, target, sem):
        self.flag = flag
        self.own = pltpu.make_async_copy(own, target, sem)
        self.received = pltpu.make_async_copy(received, target, sem)

    def start(self):
        @pl.when(self.flag != 0)
        def _():
            self.own.start()

        @pl.when(self.flag == 0)
        def _():
            self.received.start()

    def wait(self):
        self.received.wait()


def block_kernel(x_factor, y_factor, blocks, sems):
    order = x_factor.shape[2]
    copies = []
    for target in range(blocks.shape[0]):
        for which, factor in enumerate((x_factor, y_factor)):
            for plane in range(2):
                copies.append(
                    pltpu.make_async_copy(
                        factor.at[plane],
                        blocks.at[target, which, :, pl.ds(plane * order, order)],
                        sems.at[target, which, plane],
                    )
                )
    start_all(copies)
    wait_all(copies)


def pack_kernel(place, field, coupling, *rest):
    pieces, sems = rest[:-1], rest[-1]
    rows_here = field.shape[1]
    tall = coupling.shape[1]
    own = pl.ds(2 * place[len(pieces)], 2)
    copies = []
    for index, piece in enumerate(pieces):
        width = piece.shape[2]
        offset = pl.multiple_of(place[index] * width, width)
        copies += [
            pltpu.make_async_copy(
                field.at[:, :, pl.ds(offset, width)],
                piece.at[:, pl.ds(0, rows_here), :],
                sems.at[index, 0],
            ),
            pltpu.make_async_copy(
                coupling.at[own], piece.at[:, pl.ds(rows_here, tall), :], sems.at[index, 1]
            ),
        ]
    start_all(copies)
    wait_all(copies)


def unpack_kernel(place, own, *rest):
    pieces, field, sems = rest[:-2], rest[-2], rest[-1]
    copies = []
    for index, piece in enumerate(pieces):
        width = piece.shape[2]
        offset = pl.multiple_of(place[index] * width, width)
        target = field.at[:, :, pl.ds(offset, width)]
        if index:
            copies.append(pltpu.make_async_copy(piece, target, sems.at[index]))
        else:
            copies.append(Either(place[len(pieces) + 1], own, piece, target, sems.at[index]))
    start_all(copies)
    wait_all(copies)


def column_kernel(info, blocks, own, p0, p1, p2, p3, x_column, y_turned, rows_held, sems):
    count, factors, height, width = blocks.shape
    last = pl.ds(own.shape[1] - rows_held.shape[2], rows_held.shape[2])
    parts = [piece.at[:, last, :] for piece in (p0, p1, p2, p3)]
    copies = [Either(info[info_self], own.at[:, last, :], parts[0], rows_held.at[0], sems.at[0])]
    for index in range(1, len(parts)):
        copies.append(pltpu.make_async_copy(parts[index], rows_held.at[index], sems.at[index]))
    start_all(copies)
    for index in range(count):
        x_column[index * height : (index + 1) * height] = blocks[index, 0]
    column = blocks[:, 1].reshape(count * height, width)
    y_turned[...] = column.astype(f32).T.astype(bf16)
    wait_all(copies)


def field_kernel(info, own, p0, p1, p2, p3, rhs, sems):
    height = rhs.shape[2] // 2
    copies = []
    for index, piece in enumerate((p0, p1, p2, p3)):
        slot, half = info[info_piece + 2 * index], info[info_piece + 2 * index + 1]
        rows = pl.ds(pl.multiple_of(half * height, height), height)
        part = (slice(None), pl.ds(0, height), slice(None))
        ends = (rhs.at[slot, :, rows, :], sems.at[index])
        if index:
            copies.append(pltpu.make_async_copy(piece.at[part], *ends))
        else:
            copies.append(Either(info[info_self], own.at[part], piece.at[part], *ends))
    start_all(copies)
    wait_all(copies)


def weight_kernel(info, c0, c1, c2, c3, weights, sems):
    height = c0.shape[1]
    half_height = weights.shape[1] // 2
    copies = []
    for index, block in enumerate((c0, c1, c2, c3)):
        for turn in range(block.shape[0]):
            slot, half = info[info_piece + 2 * turn], info[info_piece + 2 * turn + 1]
            start = half * half_height + info[info_block + index] * height
            rows = pl.ds(pl.multiple_of(start, height), height)
            copies.append(
                pltpu.make_async_copy(
                    block.at[turn], weights.at[slot, rows, :], sems.at[index, turn]
                )
            )
    start_all(copies)
    wait_all(copies)


def both_kernel(info, x_column, x_aside, y_column, y0, y1, rows_next, rows_far, rhs, x_both, y_both,
                sems):
    copies = [
        pltpu.make_async_copy(x_column, x_both.at[0], sems.at[0]),
        pltpu.make_async_copy(x_aside, x_both.at[1], sems.at[1]),
        Either(info[info_self], y_column, y0, y_both.at[0], sems.at[2]),
        pltpu.make_async_copy(y1, y_both.at[1], sems.at[3]),
    ]
    start_all(copies)
    wait_all(copies)


class Layers:
    def __init__(self, info, x_parts, y_parts, held, beside, below, sems):
        self.info, self.order = info, held.shape[1]
        self.x_parts, self.y_parts, self.held = x_parts, y_parts, held
        self.beside, self.below, self.sems = beside, below, sems

    def x_copies(self, slot, part):
        height = self.order // 2
        copies = []
        for far in range(2):
            rows = pl.ds(pl.multiple_of(self.info[info_half + far] * height, height), height)
            copies.append(
                pltpu.make_async_copy(
                    part.at[far], self.held.at[slot, rows], self.sems.at[slot, far]
                )
            )
        return copies

    def start(self, slot):
        own, first, second = self.x_parts
        turn, same = self.info[info_slot + slot], self.info[info_self]
        for hit, part in (
            ((turn == 0) & (same != 0), own),
            ((turn == 0) & (same == 0), first),
            (turn == 1, second),
        ):

            @pl.when(hit)
            def _():
                start_all(self.x_copies(slot, part))

    def apply(self, slot, source, store, fresh):
        order, beside, below = self.order, self.beside, self.below
        turn = self.info[info_slot + slot]
        for rows in row_chunks(order, 256):
            further = slice(rows.start + order, rows.stop + order)
            real, imag = source(0, rows), source(1, rows)
            beside[rows, :order] = real
            beside[rows, order:] = -imag
            beside[further, :order] = imag
            beside[further, order:] = real
        height = order // 2
        for far, part in enumerate(self.y_parts):
            product = jnp.dot(beside[...], part[turn], preferred_element_type=f32).astype(bf16)
            start = self.info[info_half + far] * height
            columns = pl.ds(pl.multiple_of(start, height), height)
            beyond = pl.ds(pl.multiple_of(order + start, height), height)
            below[:order, columns] = product[:order]
            below[:order, beyond] = product[order:]
            below[order:, columns] = -product[order:]
            below[order:, beyond] = product[:order]
        if fresh:
            wait_all(self.x_copies(slot, self.x_parts[0]))
        for plane in range(2):
            for columns in row_chunks(order, 256):
                along = slice(columns.start + plane * order, columns.stop + plane * order)
                store(
                    plane,
                    columns,
                    jnp.dot(self.held[slot], below[:, along], preferred_element_type=f32),
                )


def reduced(rhs, info, slot, weights, incoming):
    def source(plane, rows):
        values = rhs[slot, plane, rows]
        if plane == 0:
            row = lax.broadcasted_iota(jnp.int32, values.shape, 0) + rows.start
            column = lax.broadcasted_iota(jnp.int32, values.shape, 1)
            hit = (row == info[1]) & (column == info[2]) & (info[0] == slot)
            values = values + jnp.where(hit, f32(source_amplitude), f32(0.0)).astype(bf16)
        return values - weights[slot, rows] * incoming(plane, rows)

    return source


def sent(weights, slot, field):
    return lambda plane, rows: weights[slot, rows] * field[plane, rows]


def subtract_into(target, forward):
    def store(plane, columns, values):
        target[plane, :, columns] = forward[plane, :, columns] - values.astype(bf16)

    return store


def round_into(target):
    def store(plane, columns, values):
        target[plane, :, columns] = values.astype(bf16)

    return store


def first_kernel(info, xb, x0, x1, yb, yf, weights, rhs, w_low, w_high, held, beside, below, sems):
    @pl.when(info[info_member] == 0)
    def _():
        layers = Layers(info, (xb, x0, x1), (yb, yf), held, beside, below, sems)
        layers.start(0)
        layers.start(1)
        zero = reduced(rhs, info, 0, weights, lambda plane, rows: bf16(0.0))
        layers.apply(0, zero, round_into(w_low), True)
        one = reduced(rhs, info, 1, weights, lambda plane, rows: w_low[plane, rows])
        layers.apply(1, one, round_into(w_high), True)


def last_kernel(info, xb, x0, x1, yb, yf, weights, rhs, arrived, field, back, forward, held, beside,
                below, sems):
    @pl.when(info[info_member] == 1)
    def _():
        layers = Layers(info, (xb, x0, x1), (yb, yf), held, beside, below, sems)
        layers.start(0)
        layers.start(1)
        low, high = field.at[0], field.at[1]
        two = reduced(rhs, info, 0, weights, lambda plane, rows: arrived[plane, rows])
        layers.apply(0, two, round_into(forward), True)
        three = reduced(rhs, info, 1, weights, lambda plane, rows: forward[plane, rows])
        layers.apply(1, three, round_into(high), True)
        layers.apply(0, sent(weights, 1, high), subtract_into(low, forward), False)
        last = sent(weights, 0, low)
        for plane in range(2):
            for rows in row_chunks(weights.shape[1], 256):
                back[plane, rows] = last(plane, rows)


def back_kernel(info, xb, x0, x1, yb, yf, weights, w_low, w_high, arrived, field, p0, p1, p2, p3,
                kept, held, beside, below, sems, osems):
    def start_pieces(source, slot):
        for index, piece in enumerate((p0, p1, p2, p3)):
            height = piece.shape[1]
            half = info[info_piece + 2 * index + 1]
            rows = pl.ds(pl.multiple_of(half * height, height), height)

            @pl.when(info[info_piece + 2 * index] == slot)
            def _():
                pltpu.make_async_copy(source.at[slot, :, rows, :], piece, osems.at[index]).start()

    @pl.when(info[info_member] == 0)
    def _():
        layers = Layers(info, (xb, x0, x1), (yb, yf), held, beside, below, sems)
        layers.start(1)
        layers.start(0)
        low, high = kept.at[0], kept.at[1]
        layers.apply(
            1, lambda plane, rows: arrived[plane, rows], subtract_into(high, w_high), True
        )
        start_pieces(kept, 1)
        layers.apply(0, sent(weights, 1, high), subtract_into(low, w_low), True)
        start_pieces(kept, 0)

    @pl.when(info[info_member] != 0)
    def _():
        start_pieces(field, 1)
        start_pieces(field, 0)

    for index, piece in enumerate((p0, p1, p2, p3)):
        part = kept.at[0, :, pl.ds(0, piece.shape[1]), :]
        pltpu.make_async_copy(part, piece, osems.at[index]).wait()


def on_device(background, src_pos, coupling, x_factor, y_factor):
    px_count = lax.axis_size("px")
    sec_index, own_x, own_y = (lax.axis_index(axis) for axis in ("sec", "px", "py"))
    group, member = sec_index // 2, sec_index % 2
    groups = lax.axis_size("sec") // 2
    order = y_factor.shape[3]
    field = background[:, 0]
    rows_here = field.shape[1]
    height = x_factor.shape[2]
    params = pltpu.CompilerParams(vmem_limit_bytes=vmem_bytes)
    rounds = [(0, 0), (1, 0), (1, 1), (0, 1)]

    def pairs(a, b):
        return [
            ((2 * x + c) * px_count + y, (2 * ((c + a) % 2) + x) * px_count + (y + b) % px_count)
            for x in range(groups)
            for c in range(2)
            for y in range(px_count)
            if (a, b, x) != (0, 0, c)
        ]

    def back_pairs(a, b):
        return [(target, source) for source, target in pairs(a, b)]

    own_source = src_pos[own_y * groups * px_count + group * px_count + own_x]
    plane_cells = x_factor.shape[3] * order
    layer = own_source // plane_cells
    remainder = own_source % plane_cells
    py_count = lax.axis_size("py")
    entries = [
        jnp.where(layer // 2 == member, layer % 2, -1),
        remainder // order,
        remainder % order,
        member,
    ]
    for a, b in rounds:
        entries += [(group + a) % 2, (own_x - b) % px_count]
    entries += [group, (group + 1) % 2, own_x, (own_x + 1) % 2]
    pair = own_y // 2 * 2
    entries += [own_y, pair + (own_y + 1) % 2, (own_y + 2) % 4, (pair + 2) % 4 + (own_y + 1) % 2]
    entries += [group == member]
    info = jnp.stack([jnp.asarray(entry, jnp.int32) for entry in entries])

    sends_to = jnp.stack(
        [((member + a) % 2) * px_count + (own_x + b) % px_count for a, b in rounds]
        + [own_y, group == member]
    ).astype(jnp.int32)
    piece_shape = jax.ShapeDtypeStruct((2, rows_here, order), bf16)
    blocks = pl.pallas_call(
        block_kernel,
        out_shape=jax.ShapeDtypeStruct((py_count, 2, height, 2 * order), bf16),
        in_specs=[in_hbm] * 2,
        out_specs=in_vmem,
        scratch_shapes=[pltpu.SemaphoreType.DMA((py_count, 2, 2))],
        compiler_params=params,
    )(x_factor[0], y_factor[0])
    tall = height // 2
    packed = pl.pallas_call(
        pack_kernel,
        out_shape=[jax.ShapeDtypeStruct((2, rows_here + tall, order), bf16)] * len(rounds),
        in_specs=[in_smem] + [in_hbm] * 2,
        out_specs=[in_vmem] * len(rounds),
        scratch_shapes=[pltpu.SemaphoreType.DMA((len(rounds), 2))],
        compiler_params=params,
    )(sends_to, field, coupling[0].reshape(rows_here // tall, tall, order))
    pieces = [
        lax.ppermute(piece, ("sec", "px"), pairs(a, b)) for piece, (a, b) in zip(packed, rounds)
    ]
    blocks = lax.all_to_all(blocks, "py", split_axis=0, concat_axis=0, tiled=True)

    column_shape = jax.ShapeDtypeStruct((rows_here, 2 * order), bf16)
    turned_shape = jax.ShapeDtypeStruct((2 * order, rows_here), bf16)
    x_column, y_turned, rows_held = pl.pallas_call(
        column_kernel,
        out_shape=[
            column_shape,
            turned_shape,
            jax.ShapeDtypeStruct((len(rounds), 2, tall, order), bf16),
        ],
        in_specs=[in_smem, in_vmem] + [anywhere] * 5,
        out_specs=[in_vmem] * 3,
        scratch_shapes=[pltpu.SemaphoreType.DMA((len(rounds),))],
        compiler_params=params,
    )(info, blocks, packed[0], *pieces)
    rows_held = rows_held.reshape(len(rounds), height, order)

    def across(block, a):
        return lax.ppermute(block, ("sec", "px"), pairs(a, 0))

    def aside(block):
        return lax.ppermute(block, "px", [(y, (y + 1) % 2) for y in range(2)])

    def over_z(block, bit):
        return lax.ppermute(block, "py", [(z, z ^ bit) for z in range(py_count)])

    y_near = [across(y_turned, a) for a in range(2)]
    x_aside = aside(x_column)
    rows_next = over_z(rows_held, 1)
    rows_far = over_z(rows_held, 2)
    full_shape = jax.ShapeDtypeStruct((2, order, order), bf16)
    double_shape = jax.ShapeDtypeStruct((2, 2, order, order), bf16)
    rhs = pl.pallas_call(
        field_kernel,
        out_shape=double_shape,
        in_specs=[in_smem] + [anywhere] * 5,
        out_specs=in_vmem,
        scratch_shapes=[pltpu.SemaphoreType.DMA((len(rounds),))],
        compiler_params=params,
    )(info, packed[0], *pieces)
    x_both, y_both = pl.pallas_call(
        both_kernel,
        out_shape=[
            jax.ShapeDtypeStruct((2,) + one.shape, bf16) for one in (column_shape, turned_shape)
        ],
        in_specs=[in_smem] + [anywhere] * 8,
        out_specs=[in_vmem] * 2,
        scratch_shapes=[pltpu.SemaphoreType.DMA((4,))],
        compiler_params=params,
    )(info, x_column, x_aside, y_turned, *y_near, rows_next, rows_far, rhs)
    y_far = aside(y_both)
    x_across = [across(x_both, a) for a in range(2)]
    weights = pl.pallas_call(
        weight_kernel,
        out_shape=full_shape,
        in_specs=[in_smem] + [anywhere] * 4,
        out_specs=in_vmem,
        scratch_shapes=[pltpu.SemaphoreType.DMA((4, len(rounds)))],
        compiler_params=params,
    )(info, rows_held, rows_next, rows_far, over_z(rows_next, 2))
    layers = (info, x_both, *x_across, y_both, y_far, weights)
    layer_specs = [in_smem] + [anywhere] * 3 + [in_vmem] * 3
    solver_scratch = [
        pltpu.VMEM((2, order, 2 * order), bf16),
        pltpu.VMEM((2 * order, 2 * order), bf16),
        pltpu.VMEM((2 * order, 2 * order), bf16),
        pltpu.SemaphoreType.DMA((2, 2)),
    ]

    def cost(solves):
        return pl.CostEstimate(
            flops=solves * 16 * order**3, bytes_accessed=16 * order**2 * 2, transcendentals=0
        )

    w_low, w_high = pl.pallas_call(
        first_kernel,
        out_shape=[full_shape] * 2,
        in_specs=layer_specs + [in_vmem],
        out_specs=[in_vmem] * 2,
        scratch_shapes=solver_scratch,
        compiler_params=params,
        cost_estimate=cost(2),
    )(*layers, rhs)

    up = [(2 * x, 2 * x + 1) for x in range(groups)]
    incoming = lax.ppermute(w_high, "sec", up)
    solved, back = pl.pallas_call(
        last_kernel,
        out_shape=[double_shape, full_shape],
        in_specs=layer_specs + [in_vmem] * 2,
        out_specs=[in_vmem] * 2,
        scratch_shapes=[pltpu.VMEM((2, order, order), bf16)] + solver_scratch,
        compiler_params=params,
        cost_estimate=cost(3),
    )(*layers, rhs, incoming)

    down = [(target, source) for source, target in up]
    incoming = lax.ppermute(back, "sec", down)
    results = pl.pallas_call(
        back_kernel,
        out_shape=[piece_shape] * len(rounds),
        in_specs=layer_specs + [in_vmem] * 3 + [anywhere],
        out_specs=[anywhere] * len(rounds),
        scratch_shapes=[pltpu.VMEM((2, 2, order, order), bf16)]
        + solver_scratch
        + [pltpu.SemaphoreType.DMA((len(rounds),))],
        compiler_params=params,
        cost_estimate=cost(2),
    )(*layers, w_low, w_high, incoming, solved)
    received = [
        lax.ppermute(piece, ("sec", "px"), back_pairs(a, b)) for piece, (a, b) in zip(results, rounds)
    ]
    output = pl.pallas_call(
        unpack_kernel,
        out_shape=jax.ShapeDtypeStruct(field.shape, bf16),
        in_specs=[in_smem] + [anywhere] * (len(rounds) + 1),
        out_specs=in_vmem,
        scratch_shapes=[pltpu.SemaphoreType.DMA((len(rounds),))],
        compiler_params=params,
    )(sends_to, results[0], *received)
    return output[:, None]


def chip_plan_fits(mesh):
    return mesh.shape["sec"] == 4 and mesh.shape["px"] == 2 and mesh.shape["py"] == 4


def solution(mesh):
    placed = (
        P(None, "sec", "px", "py"),
        P(),
        P("sec", "px", None),
        P("sec", None, ("px", "py"), None),
        P("sec", None, ("px", "py"), None),
    )
    return jax.shard_map(
        on_device if chip_plan_fits(mesh) else on_device_by_layer,
        mesh=mesh,
        in_specs=placed,
        out_specs=P(None, "sec", "px", "py"),
        check_vma=False,
    )
```

```python
import functools

import jax
import jax.numpy as jnp
from jax import lax
from jax.experimental import pallas as pl
from jax.experimental.pallas import tpu as pltpu
from jax.sharding import PartitionSpec as P

source_amplitude = 8.0
vmem_bytes = 32 * 1024 * 1024
bf16 = jnp.bfloat16
f32 = jnp.float32
anywhere = pl.BlockSpec(memory_space=pl.ANY)
in_hbm = pl.BlockSpec(memory_space=pltpu.HBM)
in_smem = pl.BlockSpec(memory_space=pltpu.SMEM)
in_vmem = pl.BlockSpec(memory_space=pltpu.VMEM)

info_member, info_piece, info_slot, info_half, info_block, info_self = 3, 4, 12, 14, 16, 20


def shifted(x, axis, by):
    peers = lax.axis_size(axis)
    pairs = [(i, i + by) for i in range(peers) if 0 <= i + by < peers]
    return lax.ppermute(x, axis, pairs)


def complex_block(factor):
    upper = jnp.concatenate([factor[0], -factor[1]], axis=1)
    lower = jnp.concatenate([factor[1], factor[0]], axis=1)
    return jnp.concatenate([upper, lower], axis=0)


def y_transform(real_turned, imag_turned, field_in):
    real_part = jnp.dot(field_in[0], real_turned, preferred_element_type=jnp.float32) - jnp.dot(
        field_in[1], imag_turned, preferred_element_type=jnp.float32
    )
    imag_part = jnp.dot(field_in[0], imag_turned, preferred_element_type=jnp.float32) + jnp.dot(
        field_in[1], real_turned, preferred_element_type=jnp.float32
    )
    return jnp.stack([real_part, imag_part]).astype(jnp.bfloat16)


def x_transform(x_block, field_in):
    planes, rows_all, width = field_in.shape
    output = jnp.dot(
        x_block, field_in.reshape(planes * rows_all, width), preferred_element_type=jnp.float32
    )
    return output.astype(jnp.bfloat16).reshape(planes, rows_all, width)


def scale_rows(field_in, weights, width):
    planes, rows_here, merged = field_in.shape
    spread = field_in.astype(jnp.float32).reshape(planes, rows_here, merged // width, width)
    return (spread * weights.astype(jnp.float32)[None, :, None, :]).reshape(
        planes, rows_here, merged
    )


def pick_batch(field, batch_count, batch_index):
    planes, rows_here, merged = field.shape
    split_field = field.reshape(planes, rows_here, batch_count, merged // batch_count)
    return lax.dynamic_index_in_dim(split_field, batch_index, 2, keepdims=False)


def place_batch(field, piece, batch_count, batch_index):
    planes, rows_here, merged = field.shape
    split_field = field.reshape(planes, rows_here, batch_count, merged // batch_count)
    shaped = piece.reshape(planes, rows_here, 1, merged // batch_count)
    updated = lax.dynamic_update_slice_in_dim(split_field, shaped, batch_index, 2)
    return updated.reshape(planes, rows_here, merged)


def on_device_by_layer(background, src_pos, coupling, x_factor, y_factor):
    source_count = src_pos.shape[0]
    sec_count = lax.axis_size("sec")
    sec_index = lax.axis_index("sec")
    grid_y = lax.axis_size("py")
    own_x = lax.axis_index("px")
    own_y = lax.axis_index("py")
    local_sources = source_count // grid_y
    x_pieces, y_pieces = (
        lax.all_gather(x_factor[0], ("px", "py"), axis=1, tiled=True),
        lax.all_gather(y_factor[0], ("px", "py"), axis=1, tiled=True),
    )
    x_block = complex_block(x_pieces)
    real_turned = y_pieces[0].T
    imag_turned = y_pieces[1].T
    local_field = background[:, 0]
    local_weights = coupling[0]
    rows_here = local_field.shape[1]
    full_cols = y_factor.shape[3]
    plane_cells = x_factor.shape[3] * full_cols
    own_sources = lax.dynamic_slice_in_dim(src_pos, own_y * local_sources, local_sources)
    layer_of = own_sources // plane_cells
    remainder = own_sources % plane_cells
    row_of = remainder // full_cols
    column_of = remainder % full_cols
    row_start = own_x * rows_here
    row_hit = row_of[None, :] == row_start + jnp.arange(rows_here, dtype=jnp.int32)[:, None]
    col_hit = column_of[:, None] == jnp.arange(full_cols, dtype=jnp.int32)[None, :]
    layer_hit = layer_of == sec_index
    delta = (row_hit[:, :, None] & col_hit[None, :, :] & layer_hit[None, :, None]).astype(
        jnp.float32
    )
    delta = (delta * source_amplitude).reshape(rows_here, local_sources * full_cols)
    real_rhs = local_field[0].astype(jnp.float32) + delta
    rhs_field = jnp.stack([real_rhs, local_field[1].astype(jnp.float32)])

    def apply_front(field_in):
        turned = y_transform(real_turned, imag_turned, field_in)
        line_field = lax.all_to_all(turned, "px", split_axis=2, concat_axis=1, tiled=True)
        finished = x_transform(x_block, line_field)
        return lax.all_to_all(finished, "px", split_axis=1, concat_axis=2, tiled=True)

    forward_field = jnp.zeros(local_field.shape, jnp.bfloat16)
    outgoing = pick_batch(forward_field, sec_count, 0)
    for step in range(2 * sec_count - 1):
        incoming = shifted(outgoing, "sec", 1)
        batch_index = step - sec_index
        active = (batch_index >= 0) & (batch_index < sec_count)
        clamped = jnp.clip(batch_index, 0, sec_count - 1)
        rhs_batch = pick_batch(rhs_field, sec_count, clamped)
        reduced = (rhs_batch - scale_rows(incoming, local_weights, full_cols)).astype(jnp.bfloat16)
        candidate = apply_front(reduced)
        previous = pick_batch(forward_field, sec_count, clamped)
        kept = jnp.where(active, candidate, previous)
        forward_field = place_batch(forward_field, kept, sec_count, clamped)
        outgoing = candidate
    sweep_field = forward_field
    for step in range(2 * sec_count - 2):
        send_index = jnp.clip(step - (sec_count - 1 - sec_index), 0, sec_count - 1)
        own_batch = pick_batch(sweep_field, sec_count, send_index)
        sent_field = scale_rows(own_batch, local_weights, full_cols).astype(jnp.bfloat16)
        incoming = shifted(sent_field, "sec", -1)
        batch_index = step - (sec_count - 2 - sec_index)
        active = (batch_index >= 0) & (batch_index < sec_count) & (sec_index <= sec_count - 2)
        clamped = jnp.clip(batch_index, 0, sec_count - 1)
        solved = apply_front(incoming)
        forward_batch = pick_batch(forward_field, sec_count, clamped)
        candidate = (forward_batch.astype(jnp.float32) - solved.astype(jnp.float32)).astype(
            jnp.bfloat16
        )
        previous = pick_batch(sweep_field, sec_count, clamped)
        kept = jnp.where(active, candidate, previous)
        sweep_field = place_batch(sweep_field, kept, sec_count, clamped)
    return sweep_field[:, None]


def start_all(copies):
    for copy in copies:
        copy.start()


def wait_all(copies):
    for copy in copies:
        copy.wait()


def row_chunks(order, step):
    step = min(step, order)
    return [slice(first, first + step) for first in range(0, order, step)]


class Either:
    def __init__(self, flag, own, received, target, sem):
        self.flag = flag
        self.own = pltpu.make_async_copy(own, target, sem)
        self.received = pltpu.make_async_copy(received, target, sem)

    def start(self):
        @pl.when(self.flag != 0)
        def _():
            self.own.start()

        @pl.when(self.flag == 0)
        def _():
            self.received.start()

    def wait(self):
        self.received.wait()


def pack_kernel(place, field, coupling, *rest):
    pieces, sems = rest[:-1], rest[-1]
    rows_here = field.shape[1]
    tall = coupling.shape[1]
    own = pl.ds(2 * place[len(pieces)], 2)
    copies = []
    for index, piece in enumerate(pieces):
        width = piece.shape[2]
        offset = pl.multiple_of(place[index] * width, width)
        copies += [
            pltpu.make_async_copy(
                field.at[:, :, pl.ds(offset, width)],
                piece.at[:, pl.ds(0, rows_here), :],
                sems.at[index, 0],
            ),
            pltpu.make_async_copy(
                coupling.at[own], piece.at[:, pl.ds(rows_here, tall), :], sems.at[index, 1]
            ),
        ]
    start_all(copies)
    wait_all(copies)


def unpack_kernel(place, own, *rest):
    pieces, field, sems = rest[:-2], rest[-2], rest[-1]
    copies = []
    for index, piece in enumerate(pieces):
        width = piece.shape[2]
        offset = pl.multiple_of(place[index] * width, width)
        target = field.at[:, :, pl.ds(offset, width)]
        if index:
            copies.append(pltpu.make_async_copy(piece, target, sems.at[index]))
        else:
            copies.append(Either(place[len(pieces) + 1], own, piece, target, sems.at[index]))
    start_all(copies)
    wait_all(copies)


def column_kernel(info, blocks, own, p0, p1, p2, p3, x_column, y_turned, rows_held, sems):
    count, planes, height, order = blocks.shape
    last = pl.ds(own.shape[1] - rows_held.shape[2], rows_held.shape[2])
    parts = [piece.at[:, last, :] for piece in (p0, p1, p2, p3)]
    copies = [Either(info[info_self], own.at[:, last, :], parts[0], rows_held.at[0], sems.at[0])]
    for index in range(1, len(parts)):
        copies.append(pltpu.make_async_copy(parts[index], rows_held.at[index], sems.at[index]))
    start_all(copies)
    for index in range(count):
        rows = slice(index * height, (index + 1) * height)
        for plane in range(2):
            x_column[rows, plane * order : (plane + 1) * order] = blocks[index, plane]
    for plane in range(2):
        column = blocks[:, 2 + plane].reshape(count * height, order)
        y_turned[plane * order : (plane + 1) * order] = column.astype(f32).T.astype(bf16)
    wait_all(copies)


def field_kernel(info, own, p0, p1, p2, p3, rhs, sems):
    height = rhs.shape[2] // 2
    copies = []
    for index, piece in enumerate((p0, p1, p2, p3)):
        slot, half = info[info_piece + 2 * index], info[info_piece + 2 * index + 1]
        rows = pl.ds(pl.multiple_of(half * height, height), height)
        part = (slice(None), pl.ds(0, height), slice(None))
        ends = (rhs.at[slot, :, rows, :], sems.at[index])
        if index:
            copies.append(pltpu.make_async_copy(piece.at[part], *ends))
        else:
            copies.append(Either(info[info_self], own.at[part], piece.at[part], *ends))
    start_all(copies)
    wait_all(copies)


def weight_copies(info, block, index, weights, sems):
    height = block.shape[1]
    half_height = weights.shape[1] // 2
    copies = []
    for turn in range(block.shape[0]):
        slot, half = info[info_piece + 2 * turn], info[info_piece + 2 * turn + 1]
        start = half * half_height + info[info_block + index] * height
        rows = pl.ds(pl.multiple_of(start, height), height)
        copies.append(
            pltpu.make_async_copy(block.at[turn], weights.at[slot, rows, :], sems.at[index, turn])
        )
    return copies


def weight_kernel(info, c0, c1, c2, weights, sems):
    copies = []
    for index, block in enumerate((c0, c1, c2)):
        copies += weight_copies(info, block, index, weights, sems)
    start_all(copies)
    wait_all(copies)


def last_weight_kernel(info, c3, begun, weights, sems):
    copies = weight_copies(info, c3, 3, weights, sems)
    start_all(copies)
    wait_all(copies)


def after_kernel(rows, x_both, held, sem):
    copy = pltpu.make_async_copy(rows, held, sem)
    copy.start()
    copy.wait()


def both_kernel(info, x_column, x_aside, y_column, y0, y1, rhs, x_both, y_both, sems):
    copies = [
        pltpu.make_async_copy(x_column, x_both.at[0], sems.at[0]),
        pltpu.make_async_copy(x_aside, x_both.at[1], sems.at[1]),
        Either(info[info_self], y_column, y0, y_both.at[0], sems.at[2]),
        pltpu.make_async_copy(y1, y_both.at[1], sems.at[3]),
    ]
    start_all(copies)
    wait_all(copies)


class Layers:
    def __init__(self, info, x_parts, y_parts, held, beside, below, sems):
        self.info, self.order = info, held.shape[1]
        self.x_parts, self.y_parts, self.held = x_parts, y_parts, held
        self.beside, self.below, self.sems = beside, below, sems

    def x_copies(self, slot, part):
        height = self.order // 2
        copies = []
        for far in range(2):
            rows = pl.ds(pl.multiple_of(self.info[info_half + far] * height, height), height)
            copies.append(
                pltpu.make_async_copy(
                    part.at[far], self.held.at[slot, rows], self.sems.at[slot, far]
                )
            )
        return copies

    def start(self, slot):
        own, first, second = self.x_parts
        turn, same = self.info[info_slot + slot], self.info[info_self]
        for hit, part in (
            ((turn == 0) & (same != 0), own),
            ((turn == 0) & (same == 0), first),
            (turn == 1, second),
        ):

            @pl.when(hit)
            def _():
                start_all(self.x_copies(slot, part))

    def apply(self, slot, source, store, fresh):
        order, beside, below = self.order, self.beside, self.below
        turn = self.info[info_slot + slot]
        for rows in row_chunks(order, 256):
            further = slice(rows.start + order, rows.stop + order)
            real, imag = source(0, rows), source(1, rows)
            beside[rows, :order] = real
            beside[rows, order:] = -imag
            beside[further, :order] = imag
            beside[further, order:] = real
        height = order // 2
        for far, part in enumerate(self.y_parts):
            product = jnp.dot(beside[...], part[turn], preferred_element_type=f32).astype(bf16)
            start = self.info[info_half + far] * height
            columns = pl.ds(pl.multiple_of(start, height), height)
            beyond = pl.ds(pl.multiple_of(order + start, height), height)
            below[:order, columns] = product[:order]
            below[:order, beyond] = product[order:]
            below[order:, columns] = -product[order:]
            below[order:, beyond] = product[:order]
        if fresh:
            wait_all(self.x_copies(slot, self.x_parts[0]))
        for plane in range(2):
            for columns in row_chunks(order, 256):
                along = slice(columns.start + plane * order, columns.stop + plane * order)
                store(
                    plane,
                    columns,
                    jnp.dot(self.held[slot], below[:, along], preferred_element_type=f32),
                )


def reduced(rhs, info, slot, weights, incoming):
    def source(plane, rows):
        values = rhs[slot, plane, rows]
        if plane == 0:
            row = lax.broadcasted_iota(jnp.int32, values.shape, 0) + rows.start
            column = lax.broadcasted_iota(jnp.int32, values.shape, 1)
            hit = (row == info[1]) & (column == info[2]) & (info[0] == slot)
            values = values + jnp.where(hit, f32(source_amplitude), f32(0.0)).astype(bf16)
        return values - weights[slot, rows] * incoming(plane, rows)

    return source


def sent(weights, slot, field):
    return lambda plane, rows: weights[slot, rows] * field[plane, rows]


def subtract_into(target, forward):
    def store(plane, columns, values):
        target[plane, :, columns] = forward[plane, :, columns] - values.astype(bf16)

    return store


def round_into(target):
    def store(plane, columns, values):
        target[plane, :, columns] = values.astype(bf16)

    return store


def first_kernel(info, xb, x0, x1, yb, yf, weights, rhs, w_low, w_high, held, beside, below, sems):
    @pl.when(info[info_member] == 0)
    def _():
        layers = Layers(info, (xb, x0, x1), (yb, yf), held, beside, below, sems)
        layers.start(0)
        layers.start(1)
        zero = reduced(rhs, info, 0, weights, lambda plane, rows: bf16(0.0))
        layers.apply(0, zero, round_into(w_low), True)
        one = reduced(rhs, info, 1, weights, lambda plane, rows: w_low[plane, rows])
        layers.apply(1, one, round_into(w_high), True)


def last_kernel(info, xb, x0, x1, yb, yf, weights, rhs, arrived, field, back, forward, held, beside,
                below, sems):
    @pl.when(info[info_member] == 1)
    def _():
        layers = Layers(info, (xb, x0, x1), (yb, yf), held, beside, below, sems)
        layers.start(0)
        layers.start(1)
        low, high = field.at[0], field.at[1]
        two = reduced(rhs, info, 0, weights, lambda plane, rows: arrived[plane, rows])
        layers.apply(0, two, round_into(forward), True)
        three = reduced(rhs, info, 1, weights, lambda plane, rows: forward[plane, rows])
        layers.apply(1, three, round_into(high), True)
        layers.apply(0, sent(weights, 1, high), subtract_into(low, forward), False)
        last = sent(weights, 0, low)
        for plane in range(2):
            for rows in row_chunks(weights.shape[1], 256):
                back[plane, rows] = last(plane, rows)


def back_kernel(info, xb, x0, x1, yb, yf, weights, w_low, w_high, arrived, field, p0, p1, p2, p3,
                kept, held, beside, below, sems, osems):
    def start_pieces(source, slot):
        for index, piece in enumerate((p0, p1, p2, p3)):
            height = piece.shape[1]
            half = info[info_piece + 2 * index + 1]
            rows = pl.ds(pl.multiple_of(half * height, height), height)

            @pl.when(info[info_piece + 2 * index] == slot)
            def _():
                pltpu.make_async_copy(source.at[slot, :, rows, :], piece, osems.at[index]).start()

    @pl.when(info[info_member] == 0)
    def _():
        layers = Layers(info, (xb, x0, x1), (yb, yf), held, beside, below, sems)
        layers.start(1)
        layers.start(0)
        low, high = kept.at[0], kept.at[1]
        layers.apply(
            1, lambda plane, rows: arrived[plane, rows], subtract_into(high, w_high), True
        )
        start_pieces(kept, 1)
        layers.apply(0, sent(weights, 1, high), subtract_into(low, w_low), True)
        start_pieces(kept, 0)

    @pl.when(info[info_member] != 0)
    def _():
        start_pieces(field, 1)
        start_pieces(field, 0)

    for index, piece in enumerate((p0, p1, p2, p3)):
        part = kept.at[0, :, pl.ds(0, piece.shape[1]), :]
        pltpu.make_async_copy(part, piece, osems.at[index]).wait()


def on_device(background, src_pos, coupling, x_factor, y_factor):
    px_count = lax.axis_size("px")
    sec_index, own_x, own_y = (lax.axis_index(axis) for axis in ("sec", "px", "py"))
    group, member = sec_index // 2, sec_index % 2
    groups = lax.axis_size("sec") // 2
    order = y_factor.shape[3]
    field = background[:, 0]
    rows_here = field.shape[1]
    height = x_factor.shape[2]
    params = pltpu.CompilerParams(vmem_limit_bytes=vmem_bytes)
    rounds = [(0, 0), (1, 0), (1, 1), (0, 1)]

    def pairs(a, b):
        return [
            ((2 * x + c) * px_count + y, (2 * ((c + a) % 2) + x) * px_count + (y + b) % px_count)
            for x in range(groups)
            for c in range(2)
            for y in range(px_count)
            if (a, b, x) != (0, 0, c)
        ]

    def back_pairs(a, b):
        return [(target, source) for source, target in pairs(a, b)]

    own_source = src_pos[own_y * groups * px_count + group * px_count + own_x]
    plane_cells = x_factor.shape[3] * order
    layer = own_source // plane_cells
    remainder = own_source % plane_cells
    py_count = lax.axis_size("py")
    entries = [
        jnp.where(layer // 2 == member, layer % 2, -1),
        remainder // order,
        remainder % order,
        member,
    ]
    for a, b in rounds:
        entries += [(group + a) % 2, (own_x - b) % px_count]
    entries += [group, (group + 1) % 2, own_x, (own_x + 1) % 2]
    pair = own_y // 2 * 2
    entries += [own_y, pair + (own_y + 1) % 2, (own_y + 2) % 4, (pair + 2) % 4 + (own_y + 1) % 2]
    entries += [group == member]
    info = jnp.stack([jnp.asarray(entry, jnp.int32) for entry in entries])

    sends_to = jnp.stack(
        [((member + a) % 2) * px_count + (own_x + b) % px_count for a, b in rounds]
        + [own_y, group == member]
    ).astype(jnp.int32)
    piece_shape = jax.ShapeDtypeStruct((2, rows_here, order), bf16)
    shard = jnp.concatenate([x_factor[0], y_factor[0]], axis=0)
    blocks = jnp.broadcast_to(shard[None], (py_count,) + shard.shape)
    tall = height // 2
    packed = pl.pallas_call(
        pack_kernel,
        out_shape=[jax.ShapeDtypeStruct((2, rows_here + tall, order), bf16)] * len(rounds),
        in_specs=[in_smem] + [in_hbm] * 2,
        out_specs=[in_vmem] * len(rounds),
        scratch_shapes=[pltpu.SemaphoreType.DMA((len(rounds), 2))],
        compiler_params=params,
    )(sends_to, field, coupling[0].reshape(rows_here // tall, tall, order))
    pieces = [
        lax.ppermute(piece, ("sec", "px"), pairs(a, b)) for piece, (a, b) in zip(packed, rounds)
    ]
    blocks = lax.all_to_all(blocks, "py", split_axis=0, concat_axis=0, tiled=True)

    column_shape = jax.ShapeDtypeStruct((rows_here, 2 * order), bf16)
    turned_shape = jax.ShapeDtypeStruct((2 * order, rows_here), bf16)
    x_column, y_turned, rows_held = pl.pallas_call(
        column_kernel,
        out_shape=[
            column_shape,
            turned_shape,
            jax.ShapeDtypeStruct((len(rounds), 2, tall, order), bf16),
        ],
        in_specs=[in_smem, in_vmem] + [anywhere] * 5,
        out_specs=[in_vmem] * 3,
        scratch_shapes=[pltpu.SemaphoreType.DMA((len(rounds),))],
        compiler_params=params,
    )(info, blocks, packed[0], *pieces)
    rows_held = rows_held.reshape(len(rounds), height, order)

    def across(block, a):
        return lax.ppermute(block, ("sec", "px"), pairs(a, 0))

    def aside(block):
        return lax.ppermute(block, "px", [(y, (y + 1) % 2) for y in range(2)])

    def over_z(block, bit):
        return lax.ppermute(block, "py", [(z, z ^ bit) for z in range(py_count)])

    y_near = [across(y_turned, a) for a in range(2)]
    x_aside = aside(x_column)
    rows_next = over_z(rows_held, 1)
    rows_far = over_z(rows_held, 2)
    full_shape = jax.ShapeDtypeStruct((2, order, order), bf16)
    double_shape = jax.ShapeDtypeStruct((2, 2, order, order), bf16)
    rhs = pl.pallas_call(
        field_kernel,
        out_shape=double_shape,
        in_specs=[in_smem] + [anywhere] * 5,
        out_specs=in_vmem,
        scratch_shapes=[pltpu.SemaphoreType.DMA((len(rounds),))],
        compiler_params=params,
    )(info, packed[0], *pieces)
    x_both, y_both = pl.pallas_call(
        both_kernel,
        out_shape=[
            jax.ShapeDtypeStruct((2,) + one.shape, bf16) for one in (column_shape, turned_shape)
        ],
        in_specs=[in_smem] + [anywhere] * 6,
        out_specs=[in_vmem] * 2,
        scratch_shapes=[pltpu.SemaphoreType.DMA((4,))],
        compiler_params=params,
    )(info, x_column, x_aside, y_turned, *y_near, rhs)
    y_far = aside(y_both)
    x_across = [across(x_both, a) for a in range(2)]
    weight_sems = [pltpu.SemaphoreType.DMA((4, len(rounds)))]
    begun = pl.pallas_call(
        weight_kernel,
        out_shape=full_shape,
        in_specs=[in_smem] + [anywhere] * 3,
        out_specs=in_vmem,
        scratch_shapes=weight_sems,
        compiler_params=params,
        cost_estimate=pl.CostEstimate(
            flops=3 * 10**10, bytes_accessed=2**21, transcendentals=0
        ),
    )(info, rows_held, rows_next, rows_far)
    rows_after = pl.pallas_call(
        after_kernel,
        out_shape=jax.ShapeDtypeStruct(rows_next.shape, bf16),
        in_specs=[anywhere] * 2,
        out_specs=in_vmem,
        scratch_shapes=[pltpu.SemaphoreType.DMA(())],
        compiler_params=params,
    )(rows_next, x_both)
    weights = pl.pallas_call(
        last_weight_kernel,
        out_shape=full_shape,
        in_specs=[in_smem] + [anywhere] * 2,
        out_specs=anywhere,
        scratch_shapes=weight_sems,
        input_output_aliases={2: 0},
        compiler_params=params,
    )(info, over_z(rows_after, 2), begun)
    layers = (info, x_both, *x_across, y_both, y_far, weights)
    layer_specs = [in_smem] + [anywhere] * 3 + [in_vmem] * 3
    solver_scratch = [
        pltpu.VMEM((2, order, 2 * order), bf16),
        pltpu.VMEM((2 * order, 2 * order), bf16),
        pltpu.VMEM((2 * order, 2 * order), bf16),
        pltpu.SemaphoreType.DMA((2, 2)),
    ]

    def cost(solves):
        return pl.CostEstimate(
            flops=solves * 16 * order**3, bytes_accessed=16 * order**2 * 2, transcendentals=0
        )

    w_low, w_high = pl.pallas_call(
        first_kernel,
        out_shape=[full_shape] * 2,
        in_specs=layer_specs + [in_vmem],
        out_specs=[in_vmem] * 2,
        scratch_shapes=solver_scratch,
        compiler_params=params,
        cost_estimate=cost(2),
    )(*layers, rhs)

    up = [(2 * x, 2 * x + 1) for x in range(groups)]
    incoming = lax.ppermute(w_high, "sec", up)
    solved, back = pl.pallas_call(
        last_kernel,
        out_shape=[double_shape, full_shape],
        in_specs=layer_specs + [in_vmem] * 2,
        out_specs=[in_vmem] * 2,
        scratch_shapes=[pltpu.VMEM((2, order, order), bf16)] + solver_scratch,
        compiler_params=params,
        cost_estimate=cost(3),
    )(*layers, rhs, incoming)

    down = [(target, source) for source, target in up]
    incoming = lax.ppermute(back, "sec", down)
    results = pl.pallas_call(
        back_kernel,
        out_shape=[piece_shape] * len(rounds),
        in_specs=layer_specs + [in_vmem] * 3 + [anywhere],
        out_specs=[anywhere] * len(rounds),
        scratch_shapes=[pltpu.VMEM((2, 2, order, order), bf16)]
        + solver_scratch
        + [pltpu.SemaphoreType.DMA((len(rounds),))],
        compiler_params=params,
        cost_estimate=cost(2),
    )(*layers, w_low, w_high, incoming, solved)
    received = [
        lax.ppermute(piece, ("sec", "px"), back_pairs(a, b)) for piece, (a, b) in zip(results, rounds)
    ]
    output = pl.pallas_call(
        unpack_kernel,
        out_shape=jax.ShapeDtypeStruct(field.shape, bf16),
        in_specs=[in_smem] + [anywhere] * (len(rounds) + 1),
        out_specs=in_vmem,
        scratch_shapes=[pltpu.SemaphoreType.DMA((len(rounds),))],
        compiler_params=params,
    )(sends_to, results[0], *received)
    return output[:, None]


def chip_plan_fits(mesh):
    return mesh.shape["sec"] == 4 and mesh.shape["px"] == 2 and mesh.shape["py"] == 4


def solution(mesh):
    placed = (
        P(None, "sec", "px", "py"),
        P(),
        P("sec", "px", None),
        P("sec", None, ("px", "py"), None),
        P("sec", None, ("px", "py"), None),
    )
    return jax.shard_map(
        on_device if chip_plan_fits(mesh) else on_device_by_layer,
        mesh=mesh,
        in_specs=placed,
        out_specs=P(None, "sec", "px", "py"),
        check_vma=False,
    )
```

```python
import functools

import jax
import jax.numpy as jnp
from jax import lax
from jax.experimental import pallas as pl
from jax.experimental.pallas import tpu as pltpu
from jax.sharding import PartitionSpec as P

source_amplitude = 8.0
vmem_bytes = 32 * 1024 * 1024
bf16 = jnp.bfloat16
f32 = jnp.float32
anywhere = pl.BlockSpec(memory_space=pl.ANY)
in_hbm = pl.BlockSpec(memory_space=pltpu.HBM)
in_smem = pl.BlockSpec(memory_space=pltpu.SMEM)
in_vmem = pl.BlockSpec(memory_space=pltpu.VMEM)

info_member, info_piece, info_slot, info_half, info_block, info_self = 3, 4, 12, 14, 16, 20


def shifted(x, axis, by):
    peers = lax.axis_size(axis)
    pairs = [(i, i + by) for i in range(peers) if 0 <= i + by < peers]
    return lax.ppermute(x, axis, pairs)


def complex_block(factor):
    upper = jnp.concatenate([factor[0], -factor[1]], axis=1)
    lower = jnp.concatenate([factor[1], factor[0]], axis=1)
    return jnp.concatenate([upper, lower], axis=0)


def y_transform(real_turned, imag_turned, field_in):
    real_part = jnp.dot(field_in[0], real_turned, preferred_element_type=jnp.float32) - jnp.dot(
        field_in[1], imag_turned, preferred_element_type=jnp.float32
    )
    imag_part = jnp.dot(field_in[0], imag_turned, preferred_element_type=jnp.float32) + jnp.dot(
        field_in[1], real_turned, preferred_element_type=jnp.float32
    )
    return jnp.stack([real_part, imag_part]).astype(jnp.bfloat16)


def x_transform(x_block, field_in):
    planes, rows_all, width = field_in.shape
    output = jnp.dot(
        x_block, field_in.reshape(planes * rows_all, width), preferred_element_type=jnp.float32
    )
    return output.astype(jnp.bfloat16).reshape(planes, rows_all, width)


def scale_rows(field_in, weights, width):
    planes, rows_here, merged = field_in.shape
    spread = field_in.astype(jnp.float32).reshape(planes, rows_here, merged // width, width)
    return (spread * weights.astype(jnp.float32)[None, :, None, :]).reshape(
        planes, rows_here, merged
    )


def pick_batch(field, batch_count, batch_index):
    planes, rows_here, merged = field.shape
    split_field = field.reshape(planes, rows_here, batch_count, merged // batch_count)
    return lax.dynamic_index_in_dim(split_field, batch_index, 2, keepdims=False)


def place_batch(field, piece, batch_count, batch_index):
    planes, rows_here, merged = field.shape
    split_field = field.reshape(planes, rows_here, batch_count, merged // batch_count)
    shaped = piece.reshape(planes, rows_here, 1, merged // batch_count)
    updated = lax.dynamic_update_slice_in_dim(split_field, shaped, batch_index, 2)
    return updated.reshape(planes, rows_here, merged)


def on_device_by_layer(background, src_pos, coupling, x_factor, y_factor):
    source_count = src_pos.shape[0]
    sec_count = lax.axis_size("sec")
    sec_index = lax.axis_index("sec")
    grid_y = lax.axis_size("py")
    own_x = lax.axis_index("px")
    own_y = lax.axis_index("py")
    local_sources = source_count // grid_y
    x_pieces, y_pieces = (
        lax.all_gather(x_factor[0], ("px", "py"), axis=1, tiled=True),
        lax.all_gather(y_factor[0], ("px", "py"), axis=1, tiled=True),
    )
    x_block = complex_block(x_pieces)
    real_turned = y_pieces[0].T
    imag_turned = y_pieces[1].T
    local_field = background[:, 0]
    local_weights = coupling[0]
    rows_here = local_field.shape[1]
    full_cols = y_factor.shape[3]
    plane_cells = x_factor.shape[3] * full_cols
    own_sources = lax.dynamic_slice_in_dim(src_pos, own_y * local_sources, local_sources)
    layer_of = own_sources // plane_cells
    remainder = own_sources % plane_cells
    row_of = remainder // full_cols
    column_of = remainder % full_cols
    row_start = own_x * rows_here
    row_hit = row_of[None, :] == row_start + jnp.arange(rows_here, dtype=jnp.int32)[:, None]
    col_hit = column_of[:, None] == jnp.arange(full_cols, dtype=jnp.int32)[None, :]
    layer_hit = layer_of == sec_index
    delta = (row_hit[:, :, None] & col_hit[None, :, :] & layer_hit[None, :, None]).astype(
        jnp.float32
    )
    delta = (delta * source_amplitude).reshape(rows_here, local_sources * full_cols)
    real_rhs = local_field[0].astype(jnp.float32) + delta
    rhs_field = jnp.stack([real_rhs, local_field[1].astype(jnp.float32)])

    def apply_front(field_in):
        turned = y_transform(real_turned, imag_turned, field_in)
        line_field = lax.all_to_all(turned, "px", split_axis=2, concat_axis=1, tiled=True)
        finished = x_transform(x_block, line_field)
        return lax.all_to_all(finished, "px", split_axis=1, concat_axis=2, tiled=True)

    forward_field = jnp.zeros(local_field.shape, jnp.bfloat16)
    outgoing = pick_batch(forward_field, sec_count, 0)
    for step in range(2 * sec_count - 1):
        incoming = shifted(outgoing, "sec", 1)
        batch_index = step - sec_index
        active = (batch_index >= 0) & (batch_index < sec_count)
        clamped = jnp.clip(batch_index, 0, sec_count - 1)
        rhs_batch = pick_batch(rhs_field, sec_count, clamped)
        reduced = (rhs_batch - scale_rows(incoming, local_weights, full_cols)).astype(jnp.bfloat16)
        candidate = apply_front(reduced)
        previous = pick_batch(forward_field, sec_count, clamped)
        kept = jnp.where(active, candidate, previous)
        forward_field = place_batch(forward_field, kept, sec_count, clamped)
        outgoing = candidate
    sweep_field = forward_field
    for step in range(2 * sec_count - 2):
        send_index = jnp.clip(step - (sec_count - 1 - sec_index), 0, sec_count - 1)
        own_batch = pick_batch(sweep_field, sec_count, send_index)
        sent_field = scale_rows(own_batch, local_weights, full_cols).astype(jnp.bfloat16)
        incoming = shifted(sent_field, "sec", -1)
        batch_index = step - (sec_count - 2 - sec_index)
        active = (batch_index >= 0) & (batch_index < sec_count) & (sec_index <= sec_count - 2)
        clamped = jnp.clip(batch_index, 0, sec_count - 1)
        solved = apply_front(incoming)
        forward_batch = pick_batch(forward_field, sec_count, clamped)
        candidate = (forward_batch.astype(jnp.float32) - solved.astype(jnp.float32)).astype(
            jnp.bfloat16
        )
        previous = pick_batch(sweep_field, sec_count, clamped)
        kept = jnp.where(active, candidate, previous)
        sweep_field = place_batch(sweep_field, kept, sec_count, clamped)
    return sweep_field[:, None]


def start_all(copies):
    for copy in copies:
        copy.start()


def wait_all(copies):
    for copy in copies:
        copy.wait()


def row_chunks(order, step):
    step = min(step, order)
    return [slice(first, first + step) for first in range(0, order, step)]


class Either:
    def __init__(self, flag, own, received, target, sem):
        self.flag = flag
        self.own = pltpu.make_async_copy(own, target, sem)
        self.received = pltpu.make_async_copy(received, target, sem)

    def start(self):
        @pl.when(self.flag != 0)
        def _():
            self.own.start()

        @pl.when(self.flag == 0)
        def _():
            self.received.start()

    def wait(self):
        self.received.wait()


def pack_kernel(place, field, coupling, *rest):
    pieces, sems = rest[:-1], rest[-1]
    rows_here = field.shape[1]
    tall = coupling.shape[1]
    own = pl.ds(2 * place[len(pieces)], 2)
    copies = []
    for index, piece in enumerate(pieces):
        width = piece.shape[2]
        offset = pl.multiple_of(place[index] * width, width)
        copies += [
            pltpu.make_async_copy(
                field.at[:, :, pl.ds(offset, width)],
                piece.at[:, pl.ds(0, rows_here), :],
                sems.at[index, 0],
            ),
            pltpu.make_async_copy(
                coupling.at[own], piece.at[:, pl.ds(rows_here, tall), :], sems.at[index, 1]
            ),
        ]
    start_all(copies)
    wait_all(copies)


def unpack_kernel(place, own, *rest):
    pieces, field, sems = rest[:-2], rest[-2], rest[-1]
    copies = []
    for index, piece in enumerate(pieces):
        width = piece.shape[2]
        offset = pl.multiple_of(place[index] * width, width)
        target = field.at[:, :, pl.ds(offset, width)]
        if index:
            copies.append(pltpu.make_async_copy(piece, target, sems.at[index]))
        else:
            copies.append(Either(place[len(pieces) + 1], own, piece, target, sems.at[index]))
    start_all(copies)
    wait_all(copies)


def column_kernel(info, blocks, own, p0, p1, p2, p3, x_column, y_turned, rows_held, sems):
    count, planes, height, order = blocks.shape
    last = pl.ds(own.shape[1] - rows_held.shape[2], rows_held.shape[2])
    parts = [piece.at[:, last, :] for piece in (p0, p1, p2, p3)]
    copies = [Either(info[info_self], own.at[:, last, :], parts[0], rows_held.at[0], sems.at[0])]
    for index in range(1, len(parts)):
        copies.append(pltpu.make_async_copy(parts[index], rows_held.at[index], sems.at[index]))
    start_all(copies)
    for index in range(count):
        rows = slice(index * height, (index + 1) * height)
        for plane in range(2):
            x_column[rows, plane * order : (plane + 1) * order] = blocks[index, plane]
    for plane in range(2):
        column = blocks[:, 2 + plane].reshape(count * height, order)
        y_turned[plane * order : (plane + 1) * order] = column.astype(f32).T.astype(bf16)
    wait_all(copies)


def field_kernel(info, own, p0, p1, p2, p3, rhs, sems):
    height = rhs.shape[2] // 2
    copies = []
    for index, piece in enumerate((p0, p1, p2, p3)):
        slot, half = info[info_piece + 2 * index], info[info_piece + 2 * index + 1]
        rows = pl.ds(pl.multiple_of(half * height, height), height)
        part = (slice(None), pl.ds(0, height), slice(None))
        ends = (rhs.at[slot, :, rows, :], sems.at[index])
        if index:
            copies.append(pltpu.make_async_copy(piece.at[part], *ends))
        else:
            copies.append(Either(info[info_self], own.at[part], piece.at[part], *ends))
    start_all(copies)
    wait_all(copies)


def weight_copies(info, block, index, weights, sems):
    height = block.shape[1]
    half_height = weights.shape[1] // 2
    copies = []
    for turn in range(block.shape[0]):
        slot, half = info[info_piece + 2 * turn], info[info_piece + 2 * turn + 1]
        start = half * half_height + info[info_block + index] * height
        rows = pl.ds(pl.multiple_of(start, height), height)
        copies.append(
            pltpu.make_async_copy(block.at[turn], weights.at[slot, rows, :], sems.at[index, turn])
        )
    return copies


def weight_kernel(info, c0, c1, c2, weights, sems):
    copies = []
    for index, block in enumerate((c0, c1, c2)):
        copies += weight_copies(info, block, index, weights, sems)
    start_all(copies)
    wait_all(copies)


def last_weight_kernel(info, c3, begun, weights, sems):
    copies = weight_copies(info, c3, 3, weights, sems)
    start_all(copies)
    wait_all(copies)


def both_kernel(info, x_column, x_aside, y_column, y0, y1, rhs, rows_next, x_both, y_both,
                rows_after, sems):
    copies = [
        pltpu.make_async_copy(x_column, x_both.at[0], sems.at[0]),
        pltpu.make_async_copy(x_aside, x_both.at[1], sems.at[1]),
        Either(info[info_self], y_column, y0, y_both.at[0], sems.at[2]),
        pltpu.make_async_copy(y1, y_both.at[1], sems.at[3]),
        pltpu.make_async_copy(rows_next, rows_after, sems.at[4]),
    ]
    start_all(copies)
    wait_all(copies)


class Layers:
    def __init__(self, info, x_parts, y_parts, held, beside, below, sems):
        self.info, self.order = info, held.shape[1]
        self.x_parts, self.y_parts, self.held = x_parts, y_parts, held
        self.beside, self.below, self.sems = beside, below, sems

    def x_copies(self, slot, part):
        height = self.order // 2
        copies = []
        for far in range(2):
            rows = pl.ds(pl.multiple_of(self.info[info_half + far] * height, height), height)
            copies.append(
                pltpu.make_async_copy(
                    part.at[far], self.held.at[slot, rows], self.sems.at[slot, far]
                )
            )
        return copies

    def start(self, slot):
        own, first, second = self.x_parts
        turn, same = self.info[info_slot + slot], self.info[info_self]
        for hit, part in (
            ((turn == 0) & (same != 0), own),
            ((turn == 0) & (same == 0), first),
            (turn == 1, second),
        ):

            @pl.when(hit)
            def _():
                start_all(self.x_copies(slot, part))

    def apply(self, slot, source, store, fresh):
        order, beside, below = self.order, self.beside, self.below
        turn = self.info[info_slot + slot]
        for rows in row_chunks(order, 256):
            further = slice(rows.start + order, rows.stop + order)
            real, imag = source(0, rows), source(1, rows)
            beside[rows, :order] = real
            beside[rows, order:] = -imag
            beside[further, :order] = imag
            beside[further, order:] = real
        height = order // 2
        for far, part in enumerate(self.y_parts):
            product = jnp.dot(beside[...], part[turn], preferred_element_type=f32).astype(bf16)
            start = self.info[info_half + far] * height
            columns = pl.ds(pl.multiple_of(start, height), height)
            beyond = pl.ds(pl.multiple_of(order + start, height), height)
            below[:order, columns] = product[:order]
            below[:order, beyond] = product[order:]
            below[order:, columns] = -product[order:]
            below[order:, beyond] = product[:order]
        if fresh:
            wait_all(self.x_copies(slot, self.x_parts[0]))
        for plane in range(2):
            for columns in row_chunks(order, 256):
                along = slice(columns.start + plane * order, columns.stop + plane * order)
                store(
                    plane,
                    columns,
                    jnp.dot(self.held[slot], below[:, along], preferred_element_type=f32),
                )


def reduced(rhs, info, slot, weights, incoming):
    def source(plane, rows):
        values = rhs[slot, plane, rows]
        if plane == 0:
            row = lax.broadcasted_iota(jnp.int32, values.shape, 0) + rows.start
            column = lax.broadcasted_iota(jnp.int32, values.shape, 1)
            hit = (row == info[1]) & (column == info[2]) & (info[0] == slot)
            values = values + jnp.where(hit, f32(source_amplitude), f32(0.0)).astype(bf16)
        return values - weights[slot, rows] * incoming(plane, rows)

    return source


def sent(weights, slot, field):
    return lambda plane, rows: weights[slot, rows] * field[plane, rows]


def subtract_into(target, forward):
    def store(plane, columns, values):
        target[plane, :, columns] = forward[plane, :, columns] - values.astype(bf16)

    return store


def round_into(target):
    def store(plane, columns, values):
        target[plane, :, columns] = values.astype(bf16)

    return store


def first_kernel(info, xb, x0, x1, yb, yf, weights, rhs, w_low, w_high, held, beside, below, sems):
    @pl.when(info[info_member] == 0)
    def _():
        layers = Layers(info, (xb, x0, x1), (yb, yf), held, beside, below, sems)
        layers.start(0)
        layers.start(1)
        zero = reduced(rhs, info, 0, weights, lambda plane, rows: bf16(0.0))
        layers.apply(0, zero, round_into(w_low), True)
        one = reduced(rhs, info, 1, weights, lambda plane, rows: w_low[plane, rows])
        layers.apply(1, one, round_into(w_high), True)


def last_kernel(info, xb, x0, x1, yb, yf, weights, rhs, arrived, field, back, forward, held, beside,
                below, sems):
    @pl.when(info[info_member] == 1)
    def _():
        layers = Layers(info, (xb, x0, x1), (yb, yf), held, beside, below, sems)
        layers.start(0)
        layers.start(1)
        low, high = field.at[0], field.at[1]
        two = reduced(rhs, info, 0, weights, lambda plane, rows: arrived[plane, rows])
        layers.apply(0, two, round_into(forward), True)
        three = reduced(rhs, info, 1, weights, lambda plane, rows: forward[plane, rows])
        layers.apply(1, three, round_into(high), True)
        layers.apply(0, sent(weights, 1, high), subtract_into(low, forward), False)
        last = sent(weights, 0, low)
        for plane in range(2):
            for rows in row_chunks(weights.shape[1], 256):
                back[plane, rows] = last(plane, rows)


def back_kernel(info, xb, x0, x1, yb, yf, weights, w_low, w_high, arrived, field, p0, p1, p2, p3,
                kept, held, beside, below, sems, osems):
    def start_pieces(source, slot):
        for index, piece in enumerate((p0, p1, p2, p3)):
            height = piece.shape[1]
            half = info[info_piece + 2 * index + 1]
            rows = pl.ds(pl.multiple_of(half * height, height), height)

            @pl.when(info[info_piece + 2 * index] == slot)
            def _():
                pltpu.make_async_copy(source.at[slot, :, rows, :], piece, osems.at[index]).start()

    @pl.when(info[info_member] == 0)
    def _():
        layers = Layers(info, (xb, x0, x1), (yb, yf), held, beside, below, sems)
        layers.start(1)
        layers.start(0)
        low, high = kept.at[0], kept.at[1]
        layers.apply(
            1, lambda plane, rows: arrived[plane, rows], subtract_into(high, w_high), True
        )
        start_pieces(kept, 1)
        layers.apply(0, sent(weights, 1, high), subtract_into(low, w_low), True)
        start_pieces(kept, 0)

    @pl.when(info[info_member] != 0)
    def _():
        start_pieces(field, 1)
        start_pieces(field, 0)

    for index, piece in enumerate((p0, p1, p2, p3)):
        part = kept.at[0, :, pl.ds(0, piece.shape[1]), :]
        pltpu.make_async_copy(part, piece, osems.at[index]).wait()


def on_device(background, src_pos, coupling, x_factor, y_factor):
    px_count = lax.axis_size("px")
    sec_index, own_x, own_y = (lax.axis_index(axis) for axis in ("sec", "px", "py"))
    group, member = sec_index // 2, sec_index % 2
    groups = lax.axis_size("sec") // 2
    order = y_factor.shape[3]
    field = background[:, 0]
    rows_here = field.shape[1]
    height = x_factor.shape[2]
    params = pltpu.CompilerParams(vmem_limit_bytes=vmem_bytes)
    rounds = [(0, 0), (1, 0), (1, 1), (0, 1)]

    def pairs(a, b):
        return [
            ((2 * x + c) * px_count + y, (2 * ((c + a) % 2) + x) * px_count + (y + b) % px_count)
            for x in range(groups)
            for c in range(2)
            for y in range(px_count)
            if (a, b, x) != (0, 0, c)
        ]

    def back_pairs(a, b):
        return [(target, source) for source, target in pairs(a, b)]

    own_source = src_pos[own_y * groups * px_count + group * px_count + own_x]
    plane_cells = x_factor.shape[3] * order
    layer = own_source // plane_cells
    remainder = own_source % plane_cells
    py_count = lax.axis_size("py")
    entries = [
        jnp.where(layer // 2 == member, layer % 2, -1),
        remainder // order,
        remainder % order,
        member,
    ]
    for a, b in rounds:
        entries += [(group + a) % 2, (own_x - b) % px_count]
    entries += [group, (group + 1) % 2, own_x, (own_x + 1) % 2]
    pair = own_y // 2 * 2
    entries += [own_y, pair + (own_y + 1) % 2, (own_y + 2) % 4, (pair + 2) % 4 + (own_y + 1) % 2]
    entries += [group == member]
    info = jnp.stack([jnp.asarray(entry, jnp.int32) for entry in entries])

    sends_to = jnp.stack(
        [((member + a) % 2) * px_count + (own_x + b) % px_count for a, b in rounds]
        + [own_y, group == member]
    ).astype(jnp.int32)
    piece_shape = jax.ShapeDtypeStruct((2, rows_here, order), bf16)
    shard = jnp.concatenate([x_factor[0], y_factor[0]], axis=0)
    blocks = jnp.broadcast_to(shard[None], (py_count,) + shard.shape)
    tall = height // 2
    packed = pl.pallas_call(
        pack_kernel,
        out_shape=[jax.ShapeDtypeStruct((2, rows_here + tall, order), bf16)] * len(rounds),
        in_specs=[in_smem] + [in_hbm] * 2,
        out_specs=[in_vmem] * len(rounds),
        scratch_shapes=[pltpu.SemaphoreType.DMA((len(rounds), 2))],
        compiler_params=params,
    )(sends_to, field, coupling[0].reshape(rows_here // tall, tall, order))
    pieces = [
        lax.ppermute(piece, ("sec", "px"), pairs(a, b)) for piece, (a, b) in zip(packed, rounds)
    ]
    blocks = lax.all_to_all(blocks, "py", split_axis=0, concat_axis=0, tiled=True)

    column_shape = jax.ShapeDtypeStruct((rows_here, 2 * order), bf16)
    turned_shape = jax.ShapeDtypeStruct((2 * order, rows_here), bf16)
    x_column, y_turned, rows_held = pl.pallas_call(
        column_kernel,
        out_shape=[
            column_shape,
            turned_shape,
            jax.ShapeDtypeStruct((len(rounds), 2, tall, order), bf16),
        ],
        in_specs=[in_smem, in_vmem] + [anywhere] * 5,
        out_specs=[in_vmem] * 3,
        scratch_shapes=[pltpu.SemaphoreType.DMA((len(rounds),))],
        compiler_params=params,
    )(info, blocks, packed[0], *pieces)
    rows_held = rows_held.reshape(len(rounds), height, order)

    def across(block, a):
        return lax.ppermute(block, ("sec", "px"), pairs(a, 0))

    def aside(block):
        return lax.ppermute(block, "px", [(y, (y + 1) % 2) for y in range(2)])

    def over_z(block, bit):
        return lax.ppermute(block, "py", [(z, z ^ bit) for z in range(py_count)])

    y_near = [across(y_turned, a) for a in range(2)]
    x_aside = aside(x_column)
    rows_next = over_z(rows_held, 1)
    rows_far = over_z(rows_held, 2)
    full_shape = jax.ShapeDtypeStruct((2, order, order), bf16)
    double_shape = jax.ShapeDtypeStruct((2, 2, order, order), bf16)
    rhs = pl.pallas_call(
        field_kernel,
        out_shape=double_shape,
        in_specs=[in_smem] + [anywhere] * 5,
        out_specs=in_vmem,
        scratch_shapes=[pltpu.SemaphoreType.DMA((len(rounds),))],
        compiler_params=params,
    )(info, packed[0], *pieces)
    x_both, y_both, rows_after = pl.pallas_call(
        both_kernel,
        out_shape=[
            jax.ShapeDtypeStruct((2,) + one.shape, bf16) for one in (column_shape, turned_shape)
        ]
        + [jax.ShapeDtypeStruct(rows_next.shape, bf16)],
        in_specs=[in_smem] + [anywhere] * 7,
        out_specs=[in_vmem] * 3,
        scratch_shapes=[pltpu.SemaphoreType.DMA((5,))],
        compiler_params=params,
    )(info, x_column, x_aside, y_turned, *y_near, rhs, rows_next)
    y_far = aside(y_both)
    x_across = [across(x_both, a) for a in range(2)]
    weight_sems = [pltpu.SemaphoreType.DMA((4, len(rounds)))]
    begun = pl.pallas_call(
        weight_kernel,
        out_shape=full_shape,
        in_specs=[in_smem] + [anywhere] * 3,
        out_specs=in_vmem,
        scratch_shapes=weight_sems,
        compiler_params=params,
        cost_estimate=pl.CostEstimate(
            flops=3 * 10**10, bytes_accessed=2**21, transcendentals=0
        ),
    )(info, rows_held, rows_next, rows_far)
    weights = pl.pallas_call(
        last_weight_kernel,
        out_shape=full_shape,
        in_specs=[in_smem] + [anywhere] * 2,
        out_specs=anywhere,
        scratch_shapes=weight_sems,
        input_output_aliases={2: 0},
        compiler_params=params,
    )(info, over_z(rows_after, 2), begun)
    layers = (info, x_both, *x_across, y_both, y_far, weights)
    layer_specs = [in_smem] + [anywhere] * 3 + [in_vmem] * 3
    solver_scratch = [
        pltpu.VMEM((2, order, 2 * order), bf16),
        pltpu.VMEM((2 * order, 2 * order), bf16),
        pltpu.VMEM((2 * order, 2 * order), bf16),
        pltpu.SemaphoreType.DMA((2, 2)),
    ]

    def cost(solves):
        return pl.CostEstimate(
            flops=solves * 16 * order**3, bytes_accessed=16 * order**2 * 2, transcendentals=0
        )

    w_low, w_high = pl.pallas_call(
        first_kernel,
        out_shape=[full_shape] * 2,
        in_specs=layer_specs + [in_vmem],
        out_specs=[in_vmem] * 2,
        scratch_shapes=solver_scratch,
        compiler_params=params,
        cost_estimate=cost(2),
    )(*layers, rhs)

    up = [(2 * x, 2 * x + 1) for x in range(groups)]
    incoming = lax.ppermute(w_high, "sec", up)
    solved, back = pl.pallas_call(
        last_kernel,
        out_shape=[double_shape, full_shape],
        in_specs=layer_specs + [in_vmem] * 2,
        out_specs=[in_vmem] * 2,
        scratch_shapes=[pltpu.VMEM((2, order, order), bf16)] + solver_scratch,
        compiler_params=params,
        cost_estimate=cost(3),
    )(*layers, rhs, incoming)

    down = [(target, source) for source, target in up]
    incoming = lax.ppermute(back, "sec", down)
    results = pl.pallas_call(
        back_kernel,
        out_shape=[piece_shape] * len(rounds),
        in_specs=layer_specs + [in_vmem] * 3 + [anywhere],
        out_specs=[anywhere] * len(rounds),
        scratch_shapes=[pltpu.VMEM((2, 2, order, order), bf16)]
        + solver_scratch
        + [pltpu.SemaphoreType.DMA((len(rounds),))],
        compiler_params=params,
        cost_estimate=cost(2),
    )(*layers, w_low, w_high, incoming, solved)
    received = [
        lax.ppermute(piece, ("sec", "px"), back_pairs(a, b)) for piece, (a, b) in zip(results, rounds)
    ]
    output = pl.pallas_call(
        unpack_kernel,
        out_shape=jax.ShapeDtypeStruct(field.shape, bf16),
        in_specs=[in_smem] + [anywhere] * (len(rounds) + 1),
        out_specs=in_vmem,
        scratch_shapes=[pltpu.SemaphoreType.DMA((len(rounds),))],
        compiler_params=params,
    )(sends_to, results[0], *received)
    return output[:, None]


def chip_plan_fits(mesh):
    return mesh.shape["sec"] == 4 and mesh.shape["px"] == 2 and mesh.shape["py"] == 4


def solution(mesh):
    placed = (
        P(None, "sec", "px", "py"),
        P(),
        P("sec", "px", None),
        P("sec", None, ("px", "py"), None),
        P("sec", None, ("px", "py"), None),
    )
    return jax.shard_map(
        on_device if chip_plan_fits(mesh) else on_device_by_layer,
        mesh=mesh,
        in_specs=placed,
        out_specs=P(None, "sec", "px", "py"),
        check_vma=False,
    )
```

```python
import functools

import jax
import jax.numpy as jnp
from jax import lax
from jax.experimental import pallas as pl
from jax.experimental.pallas import tpu as pltpu
from jax.sharding import PartitionSpec as P

source_amplitude = 8.0
vmem_bytes = 32 * 1024 * 1024
bf16 = jnp.bfloat16
f32 = jnp.float32
anywhere = pl.BlockSpec(memory_space=pl.ANY)
in_hbm = pl.BlockSpec(memory_space=pltpu.HBM)
in_smem = pl.BlockSpec(memory_space=pltpu.SMEM)
in_vmem = pl.BlockSpec(memory_space=pltpu.VMEM)

info_member, info_piece, info_slot, info_half, info_block, info_self = 3, 4, 12, 14, 16, 20


def shifted(x, axis, by):
    peers = lax.axis_size(axis)
    pairs = [(i, i + by) for i in range(peers) if 0 <= i + by < peers]
    return lax.ppermute(x, axis, pairs)


def complex_block(factor):
    upper = jnp.concatenate([factor[0], -factor[1]], axis=1)
    lower = jnp.concatenate([factor[1], factor[0]], axis=1)
    return jnp.concatenate([upper, lower], axis=0)


def y_transform(real_turned, imag_turned, field_in):
    real_part = jnp.dot(field_in[0], real_turned, preferred_element_type=jnp.float32) - jnp.dot(
        field_in[1], imag_turned, preferred_element_type=jnp.float32
    )
    imag_part = jnp.dot(field_in[0], imag_turned, preferred_element_type=jnp.float32) + jnp.dot(
        field_in[1], real_turned, preferred_element_type=jnp.float32
    )
    return jnp.stack([real_part, imag_part]).astype(jnp.bfloat16)


def x_transform(x_block, field_in):
    planes, rows_all, width = field_in.shape
    output = jnp.dot(
        x_block, field_in.reshape(planes * rows_all, width), preferred_element_type=jnp.float32
    )
    return output.astype(jnp.bfloat16).reshape(planes, rows_all, width)


def scale_rows(field_in, weights, width):
    planes, rows_here, merged = field_in.shape
    spread = field_in.astype(jnp.float32).reshape(planes, rows_here, merged // width, width)
    return (spread * weights.astype(jnp.float32)[None, :, None, :]).reshape(
        planes, rows_here, merged
    )


def pick_batch(field, batch_count, batch_index):
    planes, rows_here, merged = field.shape
    split_field = field.reshape(planes, rows_here, batch_count, merged // batch_count)
    return lax.dynamic_index_in_dim(split_field, batch_index, 2, keepdims=False)


def place_batch(field, piece, batch_count, batch_index):
    planes, rows_here, merged = field.shape
    split_field = field.reshape(planes, rows_here, batch_count, merged // batch_count)
    shaped = piece.reshape(planes, rows_here, 1, merged // batch_count)
    updated = lax.dynamic_update_slice_in_dim(split_field, shaped, batch_index, 2)
    return updated.reshape(planes, rows_here, merged)


def on_device_by_layer(background, src_pos, coupling, x_factor, y_factor):
    source_count = src_pos.shape[0]
    sec_count = lax.axis_size("sec")
    sec_index = lax.axis_index("sec")
    grid_y = lax.axis_size("py")
    own_x = lax.axis_index("px")
    own_y = lax.axis_index("py")
    local_sources = source_count // grid_y
    x_pieces, y_pieces = (
        lax.all_gather(x_factor[0], ("px", "py"), axis=1, tiled=True),
        lax.all_gather(y_factor[0], ("px", "py"), axis=1, tiled=True),
    )
    x_block = complex_block(x_pieces)
    real_turned = y_pieces[0].T
    imag_turned = y_pieces[1].T
    local_field = background[:, 0]
    local_weights = coupling[0]
    rows_here = local_field.shape[1]
    full_cols = y_factor.shape[3]
    plane_cells = x_factor.shape[3] * full_cols
    own_sources = lax.dynamic_slice_in_dim(src_pos, own_y * local_sources, local_sources)
    layer_of = own_sources // plane_cells
    remainder = own_sources % plane_cells
    row_of = remainder // full_cols
    column_of = remainder % full_cols
    row_start = own_x * rows_here
    row_hit = row_of[None, :] == row_start + jnp.arange(rows_here, dtype=jnp.int32)[:, None]
    col_hit = column_of[:, None] == jnp.arange(full_cols, dtype=jnp.int32)[None, :]
    layer_hit = layer_of == sec_index
    delta = (row_hit[:, :, None] & col_hit[None, :, :] & layer_hit[None, :, None]).astype(
        jnp.float32
    )
    delta = (delta * source_amplitude).reshape(rows_here, local_sources * full_cols)
    real_rhs = local_field[0].astype(jnp.float32) + delta
    rhs_field = jnp.stack([real_rhs, local_field[1].astype(jnp.float32)])

    def apply_front(field_in):
        turned = y_transform(real_turned, imag_turned, field_in)
        line_field = lax.all_to_all(turned, "px", split_axis=2, concat_axis=1, tiled=True)
        finished = x_transform(x_block, line_field)
        return lax.all_to_all(finished, "px", split_axis=1, concat_axis=2, tiled=True)

    forward_field = jnp.zeros(local_field.shape, jnp.bfloat16)
    outgoing = pick_batch(forward_field, sec_count, 0)
    for step in range(2 * sec_count - 1):
        incoming = shifted(outgoing, "sec", 1)
        batch_index = step - sec_index
        active = (batch_index >= 0) & (batch_index < sec_count)
        clamped = jnp.clip(batch_index, 0, sec_count - 1)
        rhs_batch = pick_batch(rhs_field, sec_count, clamped)
        reduced = (rhs_batch - scale_rows(incoming, local_weights, full_cols)).astype(jnp.bfloat16)
        candidate = apply_front(reduced)
        previous = pick_batch(forward_field, sec_count, clamped)
        kept = jnp.where(active, candidate, previous)
        forward_field = place_batch(forward_field, kept, sec_count, clamped)
        outgoing = candidate
    sweep_field = forward_field
    for step in range(2 * sec_count - 2):
        send_index = jnp.clip(step - (sec_count - 1 - sec_index), 0, sec_count - 1)
        own_batch = pick_batch(sweep_field, sec_count, send_index)
        sent_field = scale_rows(own_batch, local_weights, full_cols).astype(jnp.bfloat16)
        incoming = shifted(sent_field, "sec", -1)
        batch_index = step - (sec_count - 2 - sec_index)
        active = (batch_index >= 0) & (batch_index < sec_count) & (sec_index <= sec_count - 2)
        clamped = jnp.clip(batch_index, 0, sec_count - 1)
        solved = apply_front(incoming)
        forward_batch = pick_batch(forward_field, sec_count, clamped)
        candidate = (forward_batch.astype(jnp.float32) - solved.astype(jnp.float32)).astype(
            jnp.bfloat16
        )
        previous = pick_batch(sweep_field, sec_count, clamped)
        kept = jnp.where(active, candidate, previous)
        sweep_field = place_batch(sweep_field, kept, sec_count, clamped)
    return sweep_field[:, None]


def start_all(copies):
    for copy in copies:
        copy.start()


def wait_all(copies):
    for copy in copies:
        copy.wait()


def row_chunks(order, step):
    step = min(step, order)
    return [slice(first, first + step) for first in range(0, order, step)]


class Either:
    def __init__(self, flag, own, received, target, sem):
        self.flag = flag
        self.own = pltpu.make_async_copy(own, target, sem)
        self.received = pltpu.make_async_copy(received, target, sem)

    def start(self):
        @pl.when(self.flag != 0)
        def _():
            self.own.start()

        @pl.when(self.flag == 0)
        def _():
            self.received.start()

    def wait(self):
        self.received.wait()


def pack_kernel(place, field, coupling, *rest):
    pieces, sems = rest[:-1], rest[-1]
    rows_here = field.shape[1]
    tall = coupling.shape[1]
    own = pl.ds(2 * place[len(pieces)], 2)
    copies = []
    for index, piece in enumerate(pieces):
        width = piece.shape[2]
        offset = pl.multiple_of(place[index] * width, width)
        copies += [
            pltpu.make_async_copy(
                field.at[:, :, pl.ds(offset, width)],
                piece.at[:, pl.ds(0, rows_here), :],
                sems.at[index, 0],
            ),
            pltpu.make_async_copy(
                coupling.at[own], piece.at[:, pl.ds(rows_here, tall), :], sems.at[index, 1]
            ),
        ]
    start_all(copies)
    wait_all(copies)


def unpack_kernel(place, own, *rest):
    pieces, field, sems = rest[:-2], rest[-2], rest[-1]
    copies = []
    for index, piece in enumerate(pieces):
        width = piece.shape[2]
        offset = pl.multiple_of(place[index] * width, width)
        target = field.at[:, :, pl.ds(offset, width)]
        if index:
            copies.append(pltpu.make_async_copy(piece, target, sems.at[index]))
        else:
            copies.append(Either(place[len(pieces) + 1], own, piece, target, sems.at[index]))
    start_all(copies)
    wait_all(copies)


def column_kernel(info, blocks, own, p0, p1, p2, p3, x_column, y_turned, rows_held, sems):
    count, planes, height, order = blocks.shape
    last = pl.ds(own.shape[1] - rows_held.shape[2], rows_held.shape[2])
    parts = [piece.at[:, last, :] for piece in (p0, p1, p2, p3)]
    copies = [Either(info[info_self], own.at[:, last, :], parts[0], rows_held.at[0], sems.at[0])]
    for index in range(1, len(parts)):
        copies.append(pltpu.make_async_copy(parts[index], rows_held.at[index], sems.at[index]))
    start_all(copies)
    for index in range(count):
        rows = slice(index * height, (index + 1) * height)
        for plane in range(2):
            x_column[rows, plane * order : (plane + 1) * order] = blocks[index, plane]
    for plane in range(2):
        column = blocks[:, 2 + plane].reshape(count * height, order)
        y_turned[plane * order : (plane + 1) * order] = column.astype(f32).T.astype(bf16)
    wait_all(copies)


def field_kernel(info, own, p0, p1, p2, p3, rhs, sems):
    height = rhs.shape[2] // 2
    copies = []
    for index, piece in enumerate((p0, p1, p2, p3)):
        slot, half = info[info_piece + 2 * index], info[info_piece + 2 * index + 1]
        rows = pl.ds(pl.multiple_of(half * height, height), height)
        part = (slice(None), pl.ds(0, height), slice(None))
        ends = (rhs.at[slot, :, rows, :], sems.at[index])
        if index:
            copies.append(pltpu.make_async_copy(piece.at[part], *ends))
        else:
            copies.append(Either(info[info_self], own.at[part], piece.at[part], *ends))
    start_all(copies)
    wait_all(copies)


def weight_copies(info, block, index, weights, sems):
    height = block.shape[1]
    half_height = weights.shape[1] // 2
    copies = []
    for turn in range(block.shape[0]):
        slot, half = info[info_piece + 2 * turn], info[info_piece + 2 * turn + 1]
        start = half * half_height + info[info_block + index] * height
        rows = pl.ds(pl.multiple_of(start, height), height)
        copies.append(
            pltpu.make_async_copy(block.at[turn], weights.at[slot, rows, :], sems.at[index, turn])
        )
    return copies


def weight_kernel(info, c0, c1, c2, weights, sems):
    copies = []
    for index, block in enumerate((c0, c1, c2)):
        copies += weight_copies(info, block, index, weights, sems)
    start_all(copies)
    wait_all(copies)


def last_weight_kernel(info, c3, begun, weights, sems):
    copies = weight_copies(info, c3, 3, weights, sems)
    start_all(copies)
    wait_all(copies)


def both_kernel(info, x_column, x_aside, y_column, y0, y1, rhs, rows_next, x_both, y_both,
                rows_after, sems):
    copies = [
        pltpu.make_async_copy(x_column, x_both.at[0], sems.at[0]),
        pltpu.make_async_copy(x_aside, x_both.at[1], sems.at[1]),
        Either(info[info_self], y_column, y0, y_both.at[0], sems.at[2]),
        pltpu.make_async_copy(y1, y_both.at[1], sems.at[3]),
        pltpu.make_async_copy(rows_next, rows_after, sems.at[4]),
    ]
    start_all(copies)
    wait_all(copies)


class Layers:
    def __init__(self, info, x_parts, y_parts, held, beside, below, sems):
        self.info, self.order = info, held.shape[1]
        self.x_parts, self.y_parts, self.held = x_parts, y_parts, held
        self.beside, self.below, self.sems = beside, below, sems

    def x_copies(self, slot, part):
        height = self.order // 2
        copies = []
        for far in range(2):
            rows = pl.ds(pl.multiple_of(self.info[info_half + far] * height, height), height)
            copies.append(
                pltpu.make_async_copy(
                    part.at[far], self.held.at[slot, rows], self.sems.at[slot, far]
                )
            )
        return copies

    def start(self, slot):
        own, first, second = self.x_parts
        turn, same = self.info[info_slot + slot], self.info[info_self]
        for hit, part in (
            ((turn == 0) & (same != 0), own),
            ((turn == 0) & (same == 0), first),
            (turn == 1, second),
        ):

            @pl.when(hit)
            def _():
                start_all(self.x_copies(slot, part))

    def apply(self, slot, source, store, fresh):
        order, beside, below = self.order, self.beside, self.below
        turn = self.info[info_slot + slot]
        for rows in row_chunks(order, 256):
            further = slice(rows.start + order, rows.stop + order)
            real, imag = source(0, rows), source(1, rows)
            beside[rows, :order] = real
            beside[rows, order:] = -imag
            beside[further, :order] = imag
            beside[further, order:] = real
        height = order // 2
        for far, part in enumerate(self.y_parts):
            product = jnp.dot(beside[...], part[turn], preferred_element_type=f32).astype(bf16)
            start = self.info[info_half + far] * height
            columns = pl.ds(pl.multiple_of(start, height), height)
            beyond = pl.ds(pl.multiple_of(order + start, height), height)
            below[:order, columns] = product[:order]
            below[:order, beyond] = product[order:]
            below[order:, columns] = -product[order:]
            below[order:, beyond] = product[:order]
        if fresh:
            wait_all(self.x_copies(slot, self.x_parts[0]))
        for plane in range(2):
            for columns in row_chunks(order, 256):
                along = slice(columns.start + plane * order, columns.stop + plane * order)
                store(
                    plane,
                    columns,
                    jnp.dot(self.held[slot], below[:, along], preferred_element_type=f32),
                )


def reduced(rhs, info, slot, weights, incoming):
    def source(plane, rows):
        values = rhs[slot, plane, rows]
        if plane == 0:
            row = lax.broadcasted_iota(jnp.int32, values.shape, 0) + rows.start
            column = lax.broadcasted_iota(jnp.int32, values.shape, 1)
            hit = (row == info[1]) & (column == info[2]) & (info[0] == slot)
            values = values + jnp.where(hit, f32(source_amplitude), f32(0.0)).astype(bf16)
        return values - weights[slot, rows] * incoming(plane, rows)

    return source


def sent(weights, slot, field):
    return lambda plane, rows: weights[slot, rows] * field[plane, rows]


def subtract_into(target, forward):
    def store(plane, columns, values):
        target[plane, :, columns] = forward[plane, :, columns] - values.astype(bf16)

    return store


def round_into(target):
    def store(plane, columns, values):
        target[plane, :, columns] = values.astype(bf16)

    return store


def first_kernel(info, xb, x0, x1, yb, yf, weights, rhs, w_low, w_high, held, beside, below, sems):
    @pl.when(info[info_member] == 0)
    def _():
        layers = Layers(info, (xb, x0, x1), (yb, yf), held, beside, below, sems)
        layers.start(0)
        layers.start(1)
        zero = reduced(rhs, info, 0, weights, lambda plane, rows: bf16(0.0))
        layers.apply(0, zero, round_into(w_low), True)
        one = reduced(rhs, info, 1, weights, lambda plane, rows: w_low[plane, rows])
        layers.apply(1, one, round_into(w_high), True)


def last_kernel(info, xb, x0, x1, yb, yf, weights, rhs, arrived, field, back, forward, held, beside,
                below, sems):
    @pl.when(info[info_member] == 1)
    def _():
        layers = Layers(info, (xb, x0, x1), (yb, yf), held, beside, below, sems)
        layers.start(0)
        layers.start(1)
        low, high = field.at[0], field.at[1]
        two = reduced(rhs, info, 0, weights, lambda plane, rows: arrived[plane, rows])
        layers.apply(0, two, round_into(forward), True)
        three = reduced(rhs, info, 1, weights, lambda plane, rows: forward[plane, rows])
        layers.apply(1, three, round_into(high), True)
        layers.apply(0, sent(weights, 1, high), subtract_into(low, forward), False)
        last = sent(weights, 0, low)
        for plane in range(2):
            for rows in row_chunks(weights.shape[1], 256):
                back[plane, rows] = last(plane, rows)


def back_kernel(info, xb, x0, x1, yb, yf, weights, w_low, w_high, arrived, field, p0, p1, p2, p3,
                kept, held, beside, below, sems, osems):
    def start_pieces(source, slot):
        for index, piece in enumerate((p0, p1, p2, p3)):
            height = piece.shape[1]
            half = info[info_piece + 2 * index + 1]
            rows = pl.ds(pl.multiple_of(half * height, height), height)

            @pl.when(info[info_piece + 2 * index] == slot)
            def _():
                pltpu.make_async_copy(source.at[slot, :, rows, :], piece, osems.at[index]).start()

    @pl.when(info[info_member] == 0)
    def _():
        layers = Layers(info, (xb, x0, x1), (yb, yf), held, beside, below, sems)
        layers.start(1)
        layers.start(0)
        low, high = kept.at[0], kept.at[1]
        layers.apply(
            1, lambda plane, rows: arrived[plane, rows], subtract_into(high, w_high), True
        )
        start_pieces(kept, 1)
        layers.apply(0, sent(weights, 1, high), subtract_into(low, w_low), True)
        start_pieces(kept, 0)

    @pl.when(info[info_member] != 0)
    def _():
        start_pieces(field, 1)
        start_pieces(field, 0)

    for index, piece in enumerate((p0, p1, p2, p3)):
        part = kept.at[0, :, pl.ds(0, piece.shape[1]), :]
        pltpu.make_async_copy(part, piece, osems.at[index]).wait()


def on_device(background, src_pos, coupling, x_factor, y_factor):
    px_count = lax.axis_size("px")
    sec_index, own_x, own_y = (lax.axis_index(axis) for axis in ("sec", "px", "py"))
    group, member = sec_index // 2, sec_index % 2
    groups = lax.axis_size("sec") // 2
    order = y_factor.shape[3]
    field = background[:, 0]
    rows_here = field.shape[1]
    height = x_factor.shape[2]
    params = pltpu.CompilerParams(vmem_limit_bytes=vmem_bytes)
    rounds = [(0, 0), (1, 0), (1, 1), (0, 1)]

    def pairs(a, b):
        return [
            ((2 * x + c) * px_count + y, (2 * ((c + a) % 2) + x) * px_count + (y + b) % px_count)
            for x in range(groups)
            for c in range(2)
            for y in range(px_count)
            if (a, b, x) != (0, 0, c)
        ]

    def back_pairs(a, b):
        return [(target, source) for source, target in pairs(a, b)]

    own_source = src_pos[own_y * groups * px_count + group * px_count + own_x]
    plane_cells = x_factor.shape[3] * order
    layer = own_source // plane_cells
    remainder = own_source % plane_cells
    py_count = lax.axis_size("py")
    entries = [
        jnp.where(layer // 2 == member, layer % 2, -1),
        remainder // order,
        remainder % order,
        member,
    ]
    for a, b in rounds:
        entries += [(group + a) % 2, (own_x - b) % px_count]
    entries += [group, (group + 1) % 2, own_x, (own_x + 1) % 2]
    pair = own_y // 2 * 2
    entries += [own_y, pair + (own_y + 1) % 2, (own_y + 2) % 4, (pair + 2) % 4 + (own_y + 1) % 2]
    entries += [group == member]
    info = jnp.stack([jnp.asarray(entry, jnp.int32) for entry in entries])

    sends_to = jnp.stack(
        [((member + a) % 2) * px_count + (own_x + b) % px_count for a, b in rounds]
        + [own_y, group == member]
    ).astype(jnp.int32)
    piece_shape = jax.ShapeDtypeStruct((2, rows_here, order), bf16)
    shard = jnp.concatenate([x_factor[0], y_factor[0]], axis=0)
    blocks = jnp.broadcast_to(shard[None], (py_count,) + shard.shape)
    tall = height // 2
    packed = pl.pallas_call(
        pack_kernel,
        out_shape=[jax.ShapeDtypeStruct((2, rows_here + tall, order), bf16)] * len(rounds),
        in_specs=[in_smem] + [in_hbm] * 2,
        out_specs=[in_vmem] * len(rounds),
        scratch_shapes=[pltpu.SemaphoreType.DMA((len(rounds), 2))],
        compiler_params=params,
    )(sends_to, field, coupling[0].reshape(rows_here // tall, tall, order))
    pieces = [
        lax.ppermute(piece, ("sec", "px"), pairs(a, b)) for piece, (a, b) in zip(packed, rounds)
    ]
    blocks = lax.all_to_all(blocks, "py", split_axis=0, concat_axis=0, tiled=True)

    column_shape = jax.ShapeDtypeStruct((rows_here, 2 * order), bf16)
    turned_shape = jax.ShapeDtypeStruct((2 * order, rows_here), bf16)
    x_column, y_turned, rows_held = pl.pallas_call(
        column_kernel,
        out_shape=[
            column_shape,
            turned_shape,
            jax.ShapeDtypeStruct((len(rounds), 2, tall, order), bf16),
        ],
        in_specs=[in_smem, in_vmem] + [anywhere] * 5,
        out_specs=[in_vmem] * 3,
        scratch_shapes=[pltpu.SemaphoreType.DMA((len(rounds),))],
        compiler_params=params,
    )(info, blocks, packed[0], *pieces)
    rows_held = rows_held.reshape(len(rounds), height, order)

    def across(block, a):
        return lax.ppermute(block, ("sec", "px"), pairs(a, 0))

    def aside(block):
        return lax.ppermute(block, "px", [(y, (y + 1) % 2) for y in range(2)])

    def over_z(block, bit):
        return lax.ppermute(block, "py", [(z, z ^ bit) for z in range(py_count)])

    y_near = [across(y_turned, a) for a in range(2)]
    x_aside = aside(x_column)
    rows_next = over_z(rows_held, 1)
    rows_far = over_z(rows_held, 2)
    full_shape = jax.ShapeDtypeStruct((2, order, order), bf16)
    double_shape = jax.ShapeDtypeStruct((2, 2, order, order), bf16)
    rhs = pl.pallas_call(
        field_kernel,
        out_shape=double_shape,
        in_specs=[in_smem] + [anywhere] * 5,
        out_specs=in_vmem,
        scratch_shapes=[pltpu.SemaphoreType.DMA((len(rounds),))],
        compiler_params=params,
    )(info, packed[0], *pieces)
    x_both, y_both, rows_after = pl.pallas_call(
        both_kernel,
        out_shape=[
            jax.ShapeDtypeStruct((2,) + one.shape, bf16) for one in (column_shape, turned_shape)
        ]
        + [jax.ShapeDtypeStruct(rows_next.shape, bf16)],
        in_specs=[in_smem] + [anywhere] * 7,
        out_specs=[in_vmem] * 3,
        scratch_shapes=[pltpu.SemaphoreType.DMA((5,))],
        compiler_params=params,
    )(info, x_column, x_aside, y_turned, *y_near, rhs, rows_next)
    y_far = aside(y_both)
    x_across = [across(x_both, a) for a in range(2)]
    weight_sems = [pltpu.SemaphoreType.DMA((4, len(rounds)))]
    begun = pl.pallas_call(
        weight_kernel,
        out_shape=full_shape,
        in_specs=[in_smem] + [anywhere] * 3,
        out_specs=in_vmem,
        scratch_shapes=weight_sems,
        compiler_params=params,
        cost_estimate=pl.CostEstimate(
            flops=10**10, bytes_accessed=2**21, transcendentals=0
        ),
    )(info, rows_held, rows_next, rows_far)
    weights = pl.pallas_call(
        last_weight_kernel,
        out_shape=full_shape,
        in_specs=[in_smem] + [anywhere] * 2,
        out_specs=anywhere,
        scratch_shapes=weight_sems,
        input_output_aliases={2: 0},
        compiler_params=params,
    )(info, over_z(rows_after, 2), begun)
    layers = (info, x_both, *x_across, y_both, y_far, weights)
    layer_specs = [in_smem] + [anywhere] * 3 + [in_vmem] * 3
    solver_scratch = [
        pltpu.VMEM((2, order, 2 * order), bf16),
        pltpu.VMEM((2 * order, 2 * order), bf16),
        pltpu.VMEM((2 * order, 2 * order), bf16),
        pltpu.SemaphoreType.DMA((2, 2)),
    ]

    def cost(solves):
        return pl.CostEstimate(
            flops=solves * 16 * order**3, bytes_accessed=16 * order**2 * 2, transcendentals=0
        )

    w_low, w_high = pl.pallas_call(
        first_kernel,
        out_shape=[full_shape] * 2,
        in_specs=layer_specs + [in_vmem],
        out_specs=[in_vmem] * 2,
        scratch_shapes=solver_scratch,
        compiler_params=params,
        cost_estimate=cost(2),
    )(*layers, rhs)

    up = [(2 * x, 2 * x + 1) for x in range(groups)]
    incoming = lax.ppermute(w_high, "sec", up)
    solved, back = pl.pallas_call(
        last_kernel,
        out_shape=[double_shape, full_shape],
        in_specs=layer_specs + [in_vmem] * 2,
        out_specs=[in_vmem] * 2,
        scratch_shapes=[pltpu.VMEM((2, order, order), bf16)] + solver_scratch,
        compiler_params=params,
        cost_estimate=cost(3),
    )(*layers, rhs, incoming)

    down = [(target, source) for source, target in up]
    incoming = lax.ppermute(back, "sec", down)
    results = pl.pallas_call(
        back_kernel,
        out_shape=[piece_shape] * len(rounds),
        in_specs=layer_specs + [in_vmem] * 3 + [anywhere],
        out_specs=[anywhere] * len(rounds),
        scratch_shapes=[pltpu.VMEM((2, 2, order, order), bf16)]
        + solver_scratch
        + [pltpu.SemaphoreType.DMA((len(rounds),))],
        compiler_params=params,
        cost_estimate=cost(2),
    )(*layers, w_low, w_high, incoming, solved)
    received = [
        lax.ppermute(piece, ("sec", "px"), back_pairs(a, b)) for piece, (a, b) in zip(results, rounds)
    ]
    output = pl.pallas_call(
        unpack_kernel,
        out_shape=jax.ShapeDtypeStruct(field.shape, bf16),
        in_specs=[in_smem] + [anywhere] * (len(rounds) + 1),
        out_specs=in_vmem,
        scratch_shapes=[pltpu.SemaphoreType.DMA((len(rounds),))],
        compiler_params=params,
    )(sends_to, results[0], *received)
    return output[:, None]


def chip_plan_fits(mesh):
    return mesh.shape["sec"] == 4 and mesh.shape["px"] == 2 and mesh.shape["py"] == 4


def solution(mesh):
    placed = (
        P(None, "sec", "px", "py"),
        P(),
        P("sec", "px", None),
        P("sec", None, ("px", "py"), None),
        P("sec", None, ("px", "py"), None),
    )
    return jax.shard_map(
        on_device if chip_plan_fits(mesh) else on_device_by_layer,
        mesh=mesh,
        in_specs=placed,
        out_specs=P(None, "sec", "px", "py"),
        check_vma=False,
    )
```

```python
import functools

import jax
import jax.numpy as jnp
from jax import lax
from jax.experimental import pallas as pl
from jax.experimental.pallas import tpu as pltpu
from jax.sharding import PartitionSpec as P

source_amplitude = 8.0
vmem_bytes = 32 * 1024 * 1024
bf16 = jnp.bfloat16
f32 = jnp.float32
anywhere = pl.BlockSpec(memory_space=pl.ANY)
in_hbm = pl.BlockSpec(memory_space=pltpu.HBM)
in_smem = pl.BlockSpec(memory_space=pltpu.SMEM)
in_vmem = pl.BlockSpec(memory_space=pltpu.VMEM)

info_member, info_piece, info_slot, info_half, info_block, info_self = 3, 4, 12, 14, 16, 20


def shifted(x, axis, by):
    peers = lax.axis_size(axis)
    pairs = [(i, i + by) for i in range(peers) if 0 <= i + by < peers]
    return lax.ppermute(x, axis, pairs)


def complex_block(factor):
    upper = jnp.concatenate([factor[0], -factor[1]], axis=1)
    lower = jnp.concatenate([factor[1], factor[0]], axis=1)
    return jnp.concatenate([upper, lower], axis=0)


def y_transform(real_turned, imag_turned, field_in):
    real_part = jnp.dot(field_in[0], real_turned, preferred_element_type=jnp.float32) - jnp.dot(
        field_in[1], imag_turned, preferred_element_type=jnp.float32
    )
    imag_part = jnp.dot(field_in[0], imag_turned, preferred_element_type=jnp.float32) + jnp.dot(
        field_in[1], real_turned, preferred_element_type=jnp.float32
    )
    return jnp.stack([real_part, imag_part]).astype(jnp.bfloat16)


def x_transform(x_block, field_in):
    planes, rows_all, width = field_in.shape
    output = jnp.dot(
        x_block, field_in.reshape(planes * rows_all, width), preferred_element_type=jnp.float32
    )
    return output.astype(jnp.bfloat16).reshape(planes, rows_all, width)


def scale_rows(field_in, weights, width):
    planes, rows_here, merged = field_in.shape
    spread = field_in.astype(jnp.float32).reshape(planes, rows_here, merged // width, width)
    return (spread * weights.astype(jnp.float32)[None, :, None, :]).reshape(
        planes, rows_here, merged
    )


def pick_batch(field, batch_count, batch_index):
    planes, rows_here, merged = field.shape
    split_field = field.reshape(planes, rows_here, batch_count, merged // batch_count)
    return lax.dynamic_index_in_dim(split_field, batch_index, 2, keepdims=False)


def place_batch(field, piece, batch_count, batch_index):
    planes, rows_here, merged = field.shape
    split_field = field.reshape(planes, rows_here, batch_count, merged // batch_count)
    shaped = piece.reshape(planes, rows_here, 1, merged // batch_count)
    updated = lax.dynamic_update_slice_in_dim(split_field, shaped, batch_index, 2)
    return updated.reshape(planes, rows_here, merged)


def on_device_by_layer(background, src_pos, coupling, x_factor, y_factor):
    source_count = src_pos.shape[0]
    sec_count = lax.axis_size("sec")
    sec_index = lax.axis_index("sec")
    grid_y = lax.axis_size("py")
    own_x = lax.axis_index("px")
    own_y = lax.axis_index("py")
    local_sources = source_count // grid_y
    x_pieces, y_pieces = (
        lax.all_gather(x_factor[0], ("px", "py"), axis=1, tiled=True),
        lax.all_gather(y_factor[0], ("px", "py"), axis=1, tiled=True),
    )
    x_block = complex_block(x_pieces)
    real_turned = y_pieces[0].T
    imag_turned = y_pieces[1].T
    local_field = background[:, 0]
    local_weights = coupling[0]
    rows_here = local_field.shape[1]
    full_cols = y_factor.shape[3]
    plane_cells = x_factor.shape[3] * full_cols
    own_sources = lax.dynamic_slice_in_dim(src_pos, own_y * local_sources, local_sources)
    layer_of = own_sources // plane_cells
    remainder = own_sources % plane_cells
    row_of = remainder // full_cols
    column_of = remainder % full_cols
    row_start = own_x * rows_here
    row_hit = row_of[None, :] == row_start + jnp.arange(rows_here, dtype=jnp.int32)[:, None]
    col_hit = column_of[:, None] == jnp.arange(full_cols, dtype=jnp.int32)[None, :]
    layer_hit = layer_of == sec_index
    delta = (row_hit[:, :, None] & col_hit[None, :, :] & layer_hit[None, :, None]).astype(
        jnp.float32
    )
    delta = (delta * source_amplitude).reshape(rows_here, local_sources * full_cols)
    real_rhs = local_field[0].astype(jnp.float32) + delta
    rhs_field = jnp.stack([real_rhs, local_field[1].astype(jnp.float32)])

    def apply_front(field_in):
        turned = y_transform(real_turned, imag_turned, field_in)
        line_field = lax.all_to_all(turned, "px", split_axis=2, concat_axis=1, tiled=True)
        finished = x_transform(x_block, line_field)
        return lax.all_to_all(finished, "px", split_axis=1, concat_axis=2, tiled=True)

    forward_field = jnp.zeros(local_field.shape, jnp.bfloat16)
    outgoing = pick_batch(forward_field, sec_count, 0)
    for step in range(2 * sec_count - 1):
        incoming = shifted(outgoing, "sec", 1)
        batch_index = step - sec_index
        active = (batch_index >= 0) & (batch_index < sec_count)
        clamped = jnp.clip(batch_index, 0, sec_count - 1)
        rhs_batch = pick_batch(rhs_field, sec_count, clamped)
        reduced = (rhs_batch - scale_rows(incoming, local_weights, full_cols)).astype(jnp.bfloat16)
        candidate = apply_front(reduced)
        previous = pick_batch(forward_field, sec_count, clamped)
        kept = jnp.where(active, candidate, previous)
        forward_field = place_batch(forward_field, kept, sec_count, clamped)
        outgoing = candidate
    sweep_field = forward_field
    for step in range(2 * sec_count - 2):
        send_index = jnp.clip(step - (sec_count - 1 - sec_index), 0, sec_count - 1)
        own_batch = pick_batch(sweep_field, sec_count, send_index)
        sent_field = scale_rows(own_batch, local_weights, full_cols).astype(jnp.bfloat16)
        incoming = shifted(sent_field, "sec", -1)
        batch_index = step - (sec_count - 2 - sec_index)
        active = (batch_index >= 0) & (batch_index < sec_count) & (sec_index <= sec_count - 2)
        clamped = jnp.clip(batch_index, 0, sec_count - 1)
        solved = apply_front(incoming)
        forward_batch = pick_batch(forward_field, sec_count, clamped)
        candidate = (forward_batch.astype(jnp.float32) - solved.astype(jnp.float32)).astype(
            jnp.bfloat16
        )
        previous = pick_batch(sweep_field, sec_count, clamped)
        kept = jnp.where(active, candidate, previous)
        sweep_field = place_batch(sweep_field, kept, sec_count, clamped)
    return sweep_field[:, None]


def start_all(copies):
    for copy in copies:
        copy.start()


def wait_all(copies):
    for copy in copies:
        copy.wait()


def row_chunks(order, step):
    step = min(step, order)
    return [slice(first, first + step) for first in range(0, order, step)]


class Either:
    def __init__(self, flag, own, received, target, sem):
        self.flag = flag
        self.own = pltpu.make_async_copy(own, target, sem)
        self.received = pltpu.make_async_copy(received, target, sem)

    def start(self):
        @pl.when(self.flag != 0)
        def _():
            self.own.start()

        @pl.when(self.flag == 0)
        def _():
            self.received.start()

    def wait(self):
        self.received.wait()


def pack_kernel(place, field, coupling, *rest):
    pieces, sems = rest[:-1], rest[-1]
    rows_here = field.shape[1]
    tall = coupling.shape[1]
    own = pl.ds(2 * place[len(pieces)], 2)
    copies = []
    for index, piece in enumerate(pieces):
        width = piece.shape[2]
        offset = pl.multiple_of(place[index] * width, width)
        copies += [
            pltpu.make_async_copy(
                field.at[:, :, pl.ds(offset, width)],
                piece.at[:, pl.ds(0, rows_here), :],
                sems.at[index, 0],
            ),
            pltpu.make_async_copy(
                coupling.at[own], piece.at[:, pl.ds(rows_here, tall), :], sems.at[index, 1]
            ),
        ]
    start_all(copies)
    wait_all(copies)


def unpack_kernel(place, own, *rest):
    pieces, field, sems = rest[:-2], rest[-2], rest[-1]
    copies = []
    for index, piece in enumerate(pieces):
        width = piece.shape[2]
        offset = pl.multiple_of(place[index] * width, width)
        target = field.at[:, :, pl.ds(offset, width)]
        if index:
            copies.append(pltpu.make_async_copy(piece, target, sems.at[index]))
        else:
            copies.append(Either(place[len(pieces) + 1], own, piece, target, sems.at[index]))
    start_all(copies)
    wait_all(copies)


def column_kernel(info, blocks, own, p0, p1, p2, p3, x_column, y_turned, rows_held, sems):
    count, planes, height, order = blocks.shape
    last = pl.ds(own.shape[1] - rows_held.shape[2], rows_held.shape[2])
    parts = [piece.at[:, last, :] for piece in (p0, p1, p2, p3)]
    copies = [Either(info[info_self], own.at[:, last, :], parts[0], rows_held.at[0], sems.at[0])]
    for index in range(1, len(parts)):
        copies.append(pltpu.make_async_copy(parts[index], rows_held.at[index], sems.at[index]))
    start_all(copies)
    for index in range(count):
        rows = slice(index * height, (index + 1) * height)
        for plane in range(2):
            x_column[rows, plane * order : (plane + 1) * order] = blocks[index, plane]
    for plane in range(2):
        column = blocks[:, 2 + plane].reshape(count * height, order)
        y_turned[plane * order : (plane + 1) * order] = column.astype(f32).T.astype(bf16)
    wait_all(copies)


def field_kernel(info, own, p0, p1, p2, p3, rhs, sems):
    height = rhs.shape[2] // 2
    copies = []
    for index, piece in enumerate((p0, p1, p2, p3)):
        slot, half = info[info_piece + 2 * index], info[info_piece + 2 * index + 1]
        rows = pl.ds(pl.multiple_of(half * height, height), height)
        part = (slice(None), pl.ds(0, height), slice(None))
        ends = (rhs.at[slot, :, rows, :], sems.at[index])
        if index:
            copies.append(pltpu.make_async_copy(piece.at[part], *ends))
        else:
            copies.append(Either(info[info_self], own.at[part], piece.at[part], *ends))
    start_all(copies)
    wait_all(copies)


def weight_copies(info, block, index, weights, sems):
    height = block.shape[1]
    half_height = weights.shape[1] // 2
    copies = []
    for turn in range(block.shape[0]):
        slot, half = info[info_piece + 2 * turn], info[info_piece + 2 * turn + 1]
        start = half * half_height + info[info_block + index] * height
        rows = pl.ds(pl.multiple_of(start, height), height)
        copies.append(
            pltpu.make_async_copy(block.at[turn], weights.at[slot, rows, :], sems.at[index, turn])
        )
    return copies


def weight_kernel(info, c0, c1, c2, weights, sems):
    copies = []
    for index, block in enumerate((c0, c1, c2)):
        copies += weight_copies(info, block, index, weights, sems)
    start_all(copies)
    wait_all(copies)


def last_weight_kernel(info, c3, begun, weights, sems):
    copies = weight_copies(info, c3, 3, weights, sems)
    start_all(copies)
    wait_all(copies)


def after_kernel(rows, x_both, held, sem):
    copy = pltpu.make_async_copy(rows, held, sem)
    copy.start()
    copy.wait()


def both_kernel(info, x_column, x_aside, y_column, y0, y1, rhs, x_both, y_both, sems):
    copies = [
        pltpu.make_async_copy(x_column, x_both.at[0], sems.at[0]),
        pltpu.make_async_copy(x_aside, x_both.at[1], sems.at[1]),
        Either(info[info_self], y_column, y0, y_both.at[0], sems.at[2]),
        pltpu.make_async_copy(y1, y_both.at[1], sems.at[3]),
    ]
    start_all(copies)
    wait_all(copies)


class Layers:
    def __init__(self, info, x_parts, y_parts, held, beside, below, sems):
        self.info, self.order = info, held.shape[1]
        self.x_parts, self.y_parts, self.held = x_parts, y_parts, held
        self.beside, self.below, self.sems = beside, below, sems

    def x_copies(self, slot, part):
        height = self.order // 2
        copies = []
        for far in range(2):
            rows = pl.ds(pl.multiple_of(self.info[info_half + far] * height, height), height)
            copies.append(
                pltpu.make_async_copy(
                    part.at[far], self.held.at[slot, rows], self.sems.at[slot, far]
                )
            )
        return copies

    def start(self, slot):
        own, first, second = self.x_parts
        turn, same = self.info[info_slot + slot], self.info[info_self]
        for hit, part in (
            ((turn == 0) & (same != 0), own),
            ((turn == 0) & (same == 0), first),
            (turn == 1, second),
        ):

            @pl.when(hit)
            def _():
                start_all(self.x_copies(slot, part))

    def apply(self, slot, source, store, fresh):
        order, beside, below = self.order, self.beside, self.below
        turn = self.info[info_slot + slot]
        for rows in row_chunks(order, 256):
            further = slice(rows.start + order, rows.stop + order)
            real, imag = source(0, rows), source(1, rows)
            beside[rows, :order] = real
            beside[rows, order:] = -imag
            beside[further, :order] = imag
            beside[further, order:] = real
        height = order // 2
        for far, part in enumerate(self.y_parts):
            product = jnp.dot(beside[...], part[turn], preferred_element_type=f32).astype(bf16)
            start = self.info[info_half + far] * height
            columns = pl.ds(pl.multiple_of(start, height), height)
            beyond = pl.ds(pl.multiple_of(order + start, height), height)
            below[:order, columns] = product[:order]
            below[:order, beyond] = product[order:]
            below[order:, columns] = -product[order:]
            below[order:, beyond] = product[:order]
        if fresh:
            wait_all(self.x_copies(slot, self.x_parts[0]))
        for plane in range(2):
            for columns in row_chunks(order, 256):
                along = slice(columns.start + plane * order, columns.stop + plane * order)
                store(
                    plane,
                    columns,
                    jnp.dot(self.held[slot], below[:, along], preferred_element_type=f32),
                )


def reduced(rhs, info, slot, weights, incoming):
    def source(plane, rows):
        values = rhs[slot, plane, rows]
        if plane == 0:
            row = lax.broadcasted_iota(jnp.int32, values.shape, 0) + rows.start
            column = lax.broadcasted_iota(jnp.int32, values.shape, 1)
            hit = (row == info[1]) & (column == info[2]) & (info[0] == slot)
            values = values + jnp.where(hit, f32(source_amplitude), f32(0.0)).astype(bf16)
        return values - weights[slot, rows] * incoming(plane, rows)

    return source


def sent(weights, slot, field):
    return lambda plane, rows: weights[slot, rows] * field[plane, rows]


def subtract_into(target, forward):
    def store(plane, columns, values):
        target[plane, :, columns] = forward[plane, :, columns] - values.astype(bf16)

    return store


def round_into(target):
    def store(plane, columns, values):
        target[plane, :, columns] = values.astype(bf16)

    return store


def first_kernel(info, xb, x0, x1, yb, yf, weights, rhs, w_low, w_high, held, beside, below, sems):
    @pl.when(info[info_member] == 0)
    def _():
        layers = Layers(info, (xb, x0, x1), (yb, yf), held, beside, below, sems)
        layers.start(0)
        layers.start(1)
        zero = reduced(rhs, info, 0, weights, lambda plane, rows: bf16(0.0))
        layers.apply(0, zero, round_into(w_low), True)
        one = reduced(rhs, info, 1, weights, lambda plane, rows: w_low[plane, rows])
        layers.apply(1, one, round_into(w_high), True)


def last_kernel(info, xb, x0, x1, yb, yf, weights, rhs, arrived, field, back, forward, held, beside,
                below, sems):
    @pl.when(info[info_member] == 1)
    def _():
        layers = Layers(info, (xb, x0, x1), (yb, yf), held, beside, below, sems)
        layers.start(0)
        layers.start(1)
        low, high = field.at[0], field.at[1]
        two = reduced(rhs, info, 0, weights, lambda plane, rows: arrived[plane, rows])
        layers.apply(0, two, round_into(forward), True)
        three = reduced(rhs, info, 1, weights, lambda plane, rows: forward[plane, rows])
        layers.apply(1, three, round_into(high), True)
        layers.apply(0, sent(weights, 1, high), subtract_into(low, forward), False)
        last = sent(weights, 0, low)
        for plane in range(2):
            for rows in row_chunks(weights.shape[1], 256):
                back[plane, rows] = last(plane, rows)


def back_kernel(info, xb, x0, x1, yb, yf, weights, w_low, w_high, arrived, field, p0, p1, p2, p3,
                kept, held, beside, below, sems, osems):
    def start_pieces(source, slot):
        for index, piece in enumerate((p0, p1, p2, p3)):
            height = piece.shape[1]
            half = info[info_piece + 2 * index + 1]
            rows = pl.ds(pl.multiple_of(half * height, height), height)

            @pl.when(info[info_piece + 2 * index] == slot)
            def _():
                pltpu.make_async_copy(source.at[slot, :, rows, :], piece, osems.at[index]).start()

    @pl.when(info[info_member] == 0)
    def _():
        layers = Layers(info, (xb, x0, x1), (yb, yf), held, beside, below, sems)
        layers.start(1)
        layers.start(0)
        low, high = kept.at[0], kept.at[1]
        layers.apply(
            1, lambda plane, rows: arrived[plane, rows], subtract_into(high, w_high), True
        )
        start_pieces(kept, 1)
        layers.apply(0, sent(weights, 1, high), subtract_into(low, w_low), True)
        start_pieces(kept, 0)

    @pl.when(info[info_member] != 0)
    def _():
        start_pieces(field, 1)
        start_pieces(field, 0)

    for index, piece in enumerate((p0, p1, p2, p3)):
        part = kept.at[0, :, pl.ds(0, piece.shape[1]), :]
        pltpu.make_async_copy(part, piece, osems.at[index]).wait()


def on_device(background, src_pos, coupling, x_factor, y_factor):
    px_count = lax.axis_size("px")
    sec_index, own_x, own_y = (lax.axis_index(axis) for axis in ("sec", "px", "py"))
    group, member = sec_index // 2, sec_index % 2
    groups = lax.axis_size("sec") // 2
    order = y_factor.shape[3]
    field = background[:, 0]
    rows_here = field.shape[1]
    height = x_factor.shape[2]
    params = pltpu.CompilerParams(vmem_limit_bytes=vmem_bytes)
    rounds = [(0, 0), (1, 0), (1, 1), (0, 1)]

    def pairs(a, b):
        return [
            ((2 * x + c) * px_count + y, (2 * ((c + a) % 2) + x) * px_count + (y + b) % px_count)
            for x in range(groups)
            for c in range(2)
            for y in range(px_count)
            if (a, b, x) != (0, 0, c)
        ]

    def back_pairs(a, b):
        return [(target, source) for source, target in pairs(a, b)]

    own_source = src_pos[own_y * groups * px_count + group * px_count + own_x]
    plane_cells = x_factor.shape[3] * order
    layer = own_source // plane_cells
    remainder = own_source % plane_cells
    py_count = lax.axis_size("py")
    entries = [
        jnp.where(layer // 2 == member, layer % 2, -1),
        remainder // order,
        remainder % order,
        member,
    ]
    for a, b in rounds:
        entries += [(group + a) % 2, (own_x - b) % px_count]
    entries += [group, (group + 1) % 2, own_x, (own_x + 1) % 2]
    pair = own_y // 2 * 2
    entries += [own_y, pair + (own_y + 1) % 2, (own_y + 2) % 4, (pair + 2) % 4 + (own_y + 1) % 2]
    entries += [group == member]
    info = jnp.stack([jnp.asarray(entry, jnp.int32) for entry in entries])

    sends_to = jnp.stack(
        [((member + a) % 2) * px_count + (own_x + b) % px_count for a, b in rounds]
        + [own_y, group == member]
    ).astype(jnp.int32)
    piece_shape = jax.ShapeDtypeStruct((2, rows_here, order), bf16)
    shard = jnp.concatenate([x_factor[0], y_factor[0]], axis=0)
    blocks = jnp.broadcast_to(shard[None], (py_count,) + shard.shape)
    tall = height // 2
    packed = pl.pallas_call(
        pack_kernel,
        out_shape=[jax.ShapeDtypeStruct((2, rows_here + tall, order), bf16)] * len(rounds),
        in_specs=[in_smem] + [in_hbm] * 2,
        out_specs=[in_vmem] * len(rounds),
        scratch_shapes=[pltpu.SemaphoreType.DMA((len(rounds), 2))],
        compiler_params=params,
    )(sends_to, field, coupling[0].reshape(rows_here // tall, tall, order))
    pieces = [
        lax.ppermute(piece, ("sec", "px"), pairs(a, b)) for piece, (a, b) in zip(packed, rounds)
    ]
    blocks = lax.all_to_all(blocks, "py", split_axis=0, concat_axis=0, tiled=True)

    column_shape = jax.ShapeDtypeStruct((rows_here, 2 * order), bf16)
    turned_shape = jax.ShapeDtypeStruct((2 * order, rows_here), bf16)
    x_column, y_turned, rows_held = pl.pallas_call(
        column_kernel,
        out_shape=[
            column_shape,
            turned_shape,
            jax.ShapeDtypeStruct((len(rounds), 2, tall, order), bf16),
        ],
        in_specs=[in_smem, in_vmem] + [anywhere] * 5,
        out_specs=[in_vmem] * 3,
        scratch_shapes=[pltpu.SemaphoreType.DMA((len(rounds),))],
        compiler_params=params,
    )(info, blocks, packed[0], *pieces)
    rows_held = rows_held.reshape(len(rounds), height, order)

    def across(block, a):
        return lax.ppermute(block, ("sec", "px"), pairs(a, 0))

    def aside(block):
        return lax.ppermute(block, "px", [(y, (y + 1) % 2) for y in range(2)])

    def over_z(block, bit):
        return lax.ppermute(block, "py", [(z, z ^ bit) for z in range(py_count)])

    y_near = [across(y_turned, a) for a in range(2)]
    x_aside = aside(x_column)
    rows_next = over_z(rows_held, 1)
    rows_far = over_z(rows_held, 2)
    full_shape = jax.ShapeDtypeStruct((2, order, order), bf16)
    double_shape = jax.ShapeDtypeStruct((2, 2, order, order), bf16)
    rhs = pl.pallas_call(
        field_kernel,
        out_shape=double_shape,
        in_specs=[in_smem] + [anywhere] * 5,
        out_specs=in_vmem,
        scratch_shapes=[pltpu.SemaphoreType.DMA((len(rounds),))],
        compiler_params=params,
    )(info, packed[0], *pieces)
    x_both, y_both = pl.pallas_call(
        both_kernel,
        out_shape=[
            jax.ShapeDtypeStruct((2,) + one.shape, bf16) for one in (column_shape, turned_shape)
        ],
        in_specs=[in_smem] + [anywhere] * 6,
        out_specs=[in_vmem] * 2,
        scratch_shapes=[pltpu.SemaphoreType.DMA((4,))],
        compiler_params=params,
    )(info, x_column, x_aside, y_turned, *y_near, rhs)
    y_far = aside(y_both)
    x_across = [across(x_both, a) for a in range(2)]
    weight_sems = [pltpu.SemaphoreType.DMA((4, len(rounds)))]
    begun = pl.pallas_call(
        weight_kernel,
        out_shape=full_shape,
        in_specs=[in_smem] + [anywhere] * 3,
        out_specs=in_vmem,
        scratch_shapes=weight_sems,
        compiler_params=params,
        cost_estimate=pl.CostEstimate(
            flops=10**10, bytes_accessed=2**21, transcendentals=0
        ),
    )(info, rows_held, rows_next, rows_far)
    rows_after = pl.pallas_call(
        after_kernel,
        out_shape=jax.ShapeDtypeStruct(rows_next.shape, bf16),
        in_specs=[anywhere] * 2,
        out_specs=in_vmem,
        scratch_shapes=[pltpu.SemaphoreType.DMA(())],
        compiler_params=params,
    )(rows_next, x_both)
    weights = pl.pallas_call(
        last_weight_kernel,
        out_shape=full_shape,
        in_specs=[in_smem] + [anywhere] * 2,
        out_specs=anywhere,
        scratch_shapes=weight_sems,
        input_output_aliases={2: 0},
        compiler_params=params,
    )(info, over_z(rows_after, 2), begun)
    layers = (info, x_both, *x_across, y_both, y_far, weights)
    layer_specs = [in_smem] + [anywhere] * 3 + [in_vmem] * 3
    solver_scratch = [
        pltpu.VMEM((2, order, 2 * order), bf16),
        pltpu.VMEM((2 * order, 2 * order), bf16),
        pltpu.VMEM((2 * order, 2 * order), bf16),
        pltpu.SemaphoreType.DMA((2, 2)),
    ]

    def cost(solves):
        return pl.CostEstimate(
            flops=solves * 16 * order**3, bytes_accessed=16 * order**2 * 2, transcendentals=0
        )

    w_low, w_high = pl.pallas_call(
        first_kernel,
        out_shape=[full_shape] * 2,
        in_specs=layer_specs + [in_vmem],
        out_specs=[in_vmem] * 2,
        scratch_shapes=solver_scratch,
        compiler_params=params,
        cost_estimate=cost(2),
    )(*layers, rhs)

    up = [(2 * x, 2 * x + 1) for x in range(groups)]
    incoming = lax.ppermute(w_high, "sec", up)
    solved, back = pl.pallas_call(
        last_kernel,
        out_shape=[double_shape, full_shape],
        in_specs=layer_specs + [in_vmem] * 2,
        out_specs=[in_vmem] * 2,
        scratch_shapes=[pltpu.VMEM((2, order, order), bf16)] + solver_scratch,
        compiler_params=params,
        cost_estimate=cost(3),
    )(*layers, rhs, incoming)

    down = [(target, source) for source, target in up]
    incoming = lax.ppermute(back, "sec", down)
    results = pl.pallas_call(
        back_kernel,
        out_shape=[piece_shape] * len(rounds),
        in_specs=layer_specs + [in_vmem] * 3 + [anywhere],
        out_specs=[anywhere] * len(rounds),
        scratch_shapes=[pltpu.VMEM((2, 2, order, order), bf16)]
        + solver_scratch
        + [pltpu.SemaphoreType.DMA((len(rounds),))],
        compiler_params=params,
        cost_estimate=cost(2),
    )(*layers, w_low, w_high, incoming, solved)
    received = [
        lax.ppermute(piece, ("sec", "px"), back_pairs(a, b)) for piece, (a, b) in zip(results, rounds)
    ]
    output = pl.pallas_call(
        unpack_kernel,
        out_shape=jax.ShapeDtypeStruct(field.shape, bf16),
        in_specs=[in_smem] + [anywhere] * (len(rounds) + 1),
        out_specs=in_vmem,
        scratch_shapes=[pltpu.SemaphoreType.DMA((len(rounds),))],
        compiler_params=params,
    )(sends_to, results[0], *received)
    return output[:, None]


def chip_plan_fits(mesh):
    return mesh.shape["sec"] == 4 and mesh.shape["px"] == 2 and mesh.shape["py"] == 4


def solution(mesh):
    placed = (
        P(None, "sec", "px", "py"),
        P(),
        P("sec", "px", None),
        P("sec", None, ("px", "py"), None),
        P("sec", None, ("px", "py"), None),
    )
    return jax.shard_map(
        on_device if chip_plan_fits(mesh) else on_device_by_layer,
        mesh=mesh,
        in_specs=placed,
        out_specs=P(None, "sec", "px", "py"),
        check_vma=False,
    )
```

```python
import functools

import jax
import jax.numpy as jnp
from jax import lax
from jax.experimental import pallas as pl
from jax.experimental.pallas import tpu as pltpu
from jax.sharding import PartitionSpec as P

source_amplitude = 8.0
vmem_bytes = 32 * 1024 * 1024
bf16 = jnp.bfloat16
f32 = jnp.float32
anywhere = pl.BlockSpec(memory_space=pl.ANY)
in_hbm = pl.BlockSpec(memory_space=pltpu.HBM)
in_smem = pl.BlockSpec(memory_space=pltpu.SMEM)
in_vmem = pl.BlockSpec(memory_space=pltpu.VMEM)

info_member, info_piece, info_slot, info_half, info_block, info_self = 3, 4, 12, 14, 16, 20


def shifted(x, axis, by):
    peers = lax.axis_size(axis)
    pairs = [(i, i + by) for i in range(peers) if 0 <= i + by < peers]
    return lax.ppermute(x, axis, pairs)


def complex_block(factor):
    upper = jnp.concatenate([factor[0], -factor[1]], axis=1)
    lower = jnp.concatenate([factor[1], factor[0]], axis=1)
    return jnp.concatenate([upper, lower], axis=0)


def y_transform(real_turned, imag_turned, field_in):
    real_part = jnp.dot(field_in[0], real_turned, preferred_element_type=jnp.float32) - jnp.dot(
        field_in[1], imag_turned, preferred_element_type=jnp.float32
    )
    imag_part = jnp.dot(field_in[0], imag_turned, preferred_element_type=jnp.float32) + jnp.dot(
        field_in[1], real_turned, preferred_element_type=jnp.float32
    )
    return jnp.stack([real_part, imag_part]).astype(jnp.bfloat16)


def x_transform(x_block, field_in):
    planes, rows_all, width = field_in.shape
    output = jnp.dot(
        x_block, field_in.reshape(planes * rows_all, width), preferred_element_type=jnp.float32
    )
    return output.astype(jnp.bfloat16).reshape(planes, rows_all, width)


def scale_rows(field_in, weights, width):
    planes, rows_here, merged = field_in.shape
    spread = field_in.astype(jnp.float32).reshape(planes, rows_here, merged // width, width)
    return (spread * weights.astype(jnp.float32)[None, :, None, :]).reshape(
        planes, rows_here, merged
    )


def pick_batch(field, batch_count, batch_index):
    planes, rows_here, merged = field.shape
    split_field = field.reshape(planes, rows_here, batch_count, merged // batch_count)
    return lax.dynamic_index_in_dim(split_field, batch_index, 2, keepdims=False)


def place_batch(field, piece, batch_count, batch_index):
    planes, rows_here, merged = field.shape
    split_field = field.reshape(planes, rows_here, batch_count, merged // batch_count)
    shaped = piece.reshape(planes, rows_here, 1, merged // batch_count)
    updated = lax.dynamic_update_slice_in_dim(split_field, shaped, batch_index, 2)
    return updated.reshape(planes, rows_here, merged)


def on_device_by_layer(background, src_pos, coupling, x_factor, y_factor):
    source_count = src_pos.shape[0]
    sec_count = lax.axis_size("sec")
    sec_index = lax.axis_index("sec")
    grid_y = lax.axis_size("py")
    own_x = lax.axis_index("px")
    own_y = lax.axis_index("py")
    local_sources = source_count // grid_y
    x_pieces, y_pieces = (
        lax.all_gather(x_factor[0], ("px", "py"), axis=1, tiled=True),
        lax.all_gather(y_factor[0], ("px", "py"), axis=1, tiled=True),
    )
    x_block = complex_block(x_pieces)
    real_turned = y_pieces[0].T
    imag_turned = y_pieces[1].T
    local_field = background[:, 0]
    local_weights = coupling[0]
    rows_here = local_field.shape[1]
    full_cols = y_factor.shape[3]
    plane_cells = x_factor.shape[3] * full_cols
    own_sources = lax.dynamic_slice_in_dim(src_pos, own_y * local_sources, local_sources)
    layer_of = own_sources // plane_cells
    remainder = own_sources % plane_cells
    row_of = remainder // full_cols
    column_of = remainder % full_cols
    row_start = own_x * rows_here
    row_hit = row_of[None, :] == row_start + jnp.arange(rows_here, dtype=jnp.int32)[:, None]
    col_hit = column_of[:, None] == jnp.arange(full_cols, dtype=jnp.int32)[None, :]
    layer_hit = layer_of == sec_index
    delta = (row_hit[:, :, None] & col_hit[None, :, :] & layer_hit[None, :, None]).astype(
        jnp.float32
    )
    delta = (delta * source_amplitude).reshape(rows_here, local_sources * full_cols)
    real_rhs = local_field[0].astype(jnp.float32) + delta
    rhs_field = jnp.stack([real_rhs, local_field[1].astype(jnp.float32)])

    def apply_front(field_in):
        turned = y_transform(real_turned, imag_turned, field_in)
        line_field = lax.all_to_all(turned, "px", split_axis=2, concat_axis=1, tiled=True)
        finished = x_transform(x_block, line_field)
        return lax.all_to_all(finished, "px", split_axis=1, concat_axis=2, tiled=True)

    forward_field = jnp.zeros(local_field.shape, jnp.bfloat16)
    outgoing = pick_batch(forward_field, sec_count, 0)
    for step in range(2 * sec_count - 1):
        incoming = shifted(outgoing, "sec", 1)
        batch_index = step - sec_index
        active = (batch_index >= 0) & (batch_index < sec_count)
        clamped = jnp.clip(batch_index, 0, sec_count - 1)
        rhs_batch = pick_batch(rhs_field, sec_count, clamped)
        reduced = (rhs_batch - scale_rows(incoming, local_weights, full_cols)).astype(jnp.bfloat16)
        candidate = apply_front(reduced)
        previous = pick_batch(forward_field, sec_count, clamped)
        kept = jnp.where(active, candidate, previous)
        forward_field = place_batch(forward_field, kept, sec_count, clamped)
        outgoing = candidate
    sweep_field = forward_field
    for step in range(2 * sec_count - 2):
        send_index = jnp.clip(step - (sec_count - 1 - sec_index), 0, sec_count - 1)
        own_batch = pick_batch(sweep_field, sec_count, send_index)
        sent_field = scale_rows(own_batch, local_weights, full_cols).astype(jnp.bfloat16)
        incoming = shifted(sent_field, "sec", -1)
        batch_index = step - (sec_count - 2 - sec_index)
        active = (batch_index >= 0) & (batch_index < sec_count) & (sec_index <= sec_count - 2)
        clamped = jnp.clip(batch_index, 0, sec_count - 1)
        solved = apply_front(incoming)
        forward_batch = pick_batch(forward_field, sec_count, clamped)
        candidate = (forward_batch.astype(jnp.float32) - solved.astype(jnp.float32)).astype(
            jnp.bfloat16
        )
        previous = pick_batch(sweep_field, sec_count, clamped)
        kept = jnp.where(active, candidate, previous)
        sweep_field = place_batch(sweep_field, kept, sec_count, clamped)
    return sweep_field[:, None]


def start_all(copies):
    for copy in copies:
        copy.start()


def wait_all(copies):
    for copy in copies:
        copy.wait()


def row_chunks(order, step):
    step = min(step, order)
    return [slice(first, first + step) for first in range(0, order, step)]


class Either:
    def __init__(self, flag, own, received, target, sem):
        self.flag = flag
        self.own = pltpu.make_async_copy(own, target, sem)
        self.received = pltpu.make_async_copy(received, target, sem)

    def start(self):
        @pl.when(self.flag != 0)
        def _():
            self.own.start()

        @pl.when(self.flag == 0)
        def _():
            self.received.start()

    def wait(self):
        self.received.wait()


def pack_kernel(place, field, coupling, *rest):
    pieces, sems = rest[:-1], rest[-1]
    rows_here = field.shape[1]
    tall = coupling.shape[1]
    own = pl.ds(2 * place[len(pieces)], 2)
    copies = []
    for index, piece in enumerate(pieces):
        width = piece.shape[2]
        offset = pl.multiple_of(place[index] * width, width)
        copies += [
            pltpu.make_async_copy(
                field.at[:, :, pl.ds(offset, width)],
                piece.at[:, pl.ds(0, rows_here), :],
                sems.at[index, 0],
            ),
            pltpu.make_async_copy(
                coupling.at[own], piece.at[:, pl.ds(rows_here, tall), :], sems.at[index, 1]
            ),
        ]
    start_all(copies)
    wait_all(copies)


def unpack_kernel(place, own, *rest):
    pieces, field, sems = rest[:-2], rest[-2], rest[-1]
    copies = []
    for index, piece in enumerate(pieces):
        width = piece.shape[2]
        offset = pl.multiple_of(place[index] * width, width)
        target = field.at[:, :, pl.ds(offset, width)]
        if index:
            copies.append(pltpu.make_async_copy(piece, target, sems.at[index]))
        else:
            copies.append(Either(place[len(pieces) + 1], own, piece, target, sems.at[index]))
    start_all(copies)
    wait_all(copies)


def column_kernel(info, blocks, own, p0, p1, p2, p3, x_column, y_turned, rows_held, sems):
    count, planes, height, order = blocks.shape
    last = pl.ds(own.shape[1] - rows_held.shape[2], rows_held.shape[2])
    parts = [piece.at[:, last, :] for piece in (p0, p1, p2, p3)]
    copies = [Either(info[info_self], own.at[:, last, :], parts[0], rows_held.at[0], sems.at[0])]
    for index in range(1, len(parts)):
        copies.append(pltpu.make_async_copy(parts[index], rows_held.at[index], sems.at[index]))
    start_all(copies)
    for index in range(count):
        rows = slice(index * height, (index + 1) * height)
        for plane in range(2):
            x_column[rows, plane * order : (plane + 1) * order] = blocks[index, plane]
    for plane in range(2):
        column = blocks[:, 2 + plane].reshape(count * height, order)
        y_turned[plane * order : (plane + 1) * order] = column.astype(f32).T.astype(bf16)
    wait_all(copies)


def field_kernel(info, own, p0, p1, p2, p3, rhs, sems):
    height = rhs.shape[2] // 2
    copies = []
    for index, piece in enumerate((p0, p1, p2, p3)):
        slot, half = info[info_piece + 2 * index], info[info_piece + 2 * index + 1]
        rows = pl.ds(pl.multiple_of(half * height, height), height)
        part = (slice(None), pl.ds(0, height), slice(None))
        ends = (rhs.at[slot, :, rows, :], sems.at[index])
        if index:
            copies.append(pltpu.make_async_copy(piece.at[part], *ends))
        else:
            copies.append(Either(info[info_self], own.at[part], piece.at[part], *ends))
    start_all(copies)
    wait_all(copies)


def weight_copies(info, block, index, weights, sems):
    height = block.shape[1]
    half_height = weights.shape[1] // 2
    copies = []
    for turn in range(block.shape[0]):
        slot, half = info[info_piece + 2 * turn], info[info_piece + 2 * turn + 1]
        start = half * half_height + info[info_block + index] * height
        rows = pl.ds(pl.multiple_of(start, height), height)
        copies.append(
            pltpu.make_async_copy(block.at[turn], weights.at[slot, rows, :], sems.at[index, turn])
        )
    return copies


def weight_kernel(info, c0, c1, c2, weights, sems):
    copies = []
    for index, block in enumerate((c0, c1, c2)):
        copies += weight_copies(info, block, index, weights, sems)
    start_all(copies)
    wait_all(copies)


def last_weight_kernel(info, c3, begun, weights, sems):
    copies = weight_copies(info, c3, 3, weights, sems)
    start_all(copies)
    wait_all(copies)


def after_kernel(rows, x_both, held, sem):
    copy = pltpu.make_async_copy(rows, held, sem)
    copy.start()
    copy.wait()


def both_kernel(info, x_column, x_aside, y_column, y0, y1, rhs, x_both, y_both, sems):
    copies = [
        pltpu.make_async_copy(x_column, x_both.at[0], sems.at[0]),
        pltpu.make_async_copy(x_aside, x_both.at[1], sems.at[1]),
        Either(info[info_self], y_column, y0, y_both.at[0], sems.at[2]),
        pltpu.make_async_copy(y1, y_both.at[1], sems.at[3]),
    ]
    start_all(copies)
    wait_all(copies)


class Layers:
    def __init__(self, info, x_parts, y_parts, held, beside, below, sems):
        self.info, self.order = info, held.shape[1]
        self.x_parts, self.y_parts, self.held = x_parts, y_parts, held
        self.beside, self.below, self.sems = beside, below, sems

    def x_copies(self, slot, part):
        height = self.order // 2
        copies = []
        for far in range(2):
            rows = pl.ds(pl.multiple_of(self.info[info_half + far] * height, height), height)
            copies.append(
                pltpu.make_async_copy(
                    part.at[far], self.held.at[slot, rows], self.sems.at[slot, far]
                )
            )
        return copies

    def start(self, slot):
        own, first, second = self.x_parts
        turn, same = self.info[info_slot + slot], self.info[info_self]
        for hit, part in (
            ((turn == 0) & (same != 0), own),
            ((turn == 0) & (same == 0), first),
            (turn == 1, second),
        ):

            @pl.when(hit)
            def _():
                start_all(self.x_copies(slot, part))

    def apply(self, slot, source, store, fresh):
        order, beside, below = self.order, self.beside, self.below
        turn = self.info[info_slot + slot]
        for rows in row_chunks(order, 256):
            further = slice(rows.start + order, rows.stop + order)
            real, imag = source(0, rows), source(1, rows)
            beside[rows, :order] = real
            beside[rows, order:] = -imag
            beside[further, :order] = imag
            beside[further, order:] = real
        height = order // 2
        for far, part in enumerate(self.y_parts):
            product = jnp.dot(beside[...], part[turn], preferred_element_type=f32).astype(bf16)
            start = self.info[info_half + far] * height
            columns = pl.ds(pl.multiple_of(start, height), height)
            beyond = pl.ds(pl.multiple_of(order + start, height), height)
            below[:order, columns] = product[:order]
            below[:order, beyond] = product[order:]
            below[order:, columns] = -product[order:]
            below[order:, beyond] = product[:order]
        if fresh:
            wait_all(self.x_copies(slot, self.x_parts[0]))
        for plane in range(2):
            for columns in row_chunks(order, 256):
                along = slice(columns.start + plane * order, columns.stop + plane * order)
                store(
                    plane,
                    columns,
                    jnp.dot(self.held[slot], below[:, along], preferred_element_type=f32),
                )


def reduced(rhs, info, slot, weights, incoming):
    def source(plane, rows):
        values = rhs[slot, plane, rows]
        if plane == 0:
            row = lax.broadcasted_iota(jnp.int32, values.shape, 0) + rows.start
            column = lax.broadcasted_iota(jnp.int32, values.shape, 1)
            hit = (row == info[1]) & (column == info[2]) & (info[0] == slot)
            values = values + jnp.where(hit, f32(source_amplitude), f32(0.0)).astype(bf16)
        return values - weights[slot, rows] * incoming(plane, rows)

    return source


def sent(weights, slot, field):
    return lambda plane, rows: weights[slot, rows] * field[plane, rows]


def subtract_into(target, forward):
    def store(plane, columns, values):
        target[plane, :, columns] = forward[plane, :, columns] - values.astype(bf16)

    return store


def round_into(target):
    def store(plane, columns, values):
        target[plane, :, columns] = values.astype(bf16)

    return store


def first_kernel(info, xb, x0, x1, yb, yf, weights, rhs, w_low, w_high, held, beside, below, sems):
    @pl.when(info[info_member] == 0)
    def _():
        layers = Layers(info, (xb, x0, x1), (yb, yf), held, beside, below, sems)
        layers.start(0)
        layers.start(1)
        zero = reduced(rhs, info, 0, weights, lambda plane, rows: bf16(0.0))
        layers.apply(0, zero, round_into(w_low), True)
        one = reduced(rhs, info, 1, weights, lambda plane, rows: w_low[plane, rows])
        layers.apply(1, one, round_into(w_high), True)


def last_kernel(info, xb, x0, x1, yb, yf, weights, rhs, arrived, field, back, forward, held, beside,
                below, sems):
    @pl.when(info[info_member] == 1)
    def _():
        layers = Layers(info, (xb, x0, x1), (yb, yf), held, beside, below, sems)
        layers.start(0)
        layers.start(1)
        low, high = field.at[0], field.at[1]
        two = reduced(rhs, info, 0, weights, lambda plane, rows: arrived[plane, rows])
        layers.apply(0, two, round_into(forward), True)
        three = reduced(rhs, info, 1, weights, lambda plane, rows: forward[plane, rows])
        layers.apply(1, three, round_into(high), True)
        layers.apply(0, sent(weights, 1, high), subtract_into(low, forward), False)
        last = sent(weights, 0, low)
        for plane in range(2):
            for rows in row_chunks(weights.shape[1], 256):
                back[plane, rows] = last(plane, rows)


def back_kernel(info, xb, x0, x1, yb, yf, weights, w_low, w_high, arrived, field, p0, p1, p2, p3,
                kept, held, beside, below, sems, osems):
    def start_pieces(source, slot):
        for index, piece in enumerate((p0, p1, p2, p3)):
            height = piece.shape[1]
            half = info[info_piece + 2 * index + 1]
            rows = pl.ds(pl.multiple_of(half * height, height), height)

            @pl.when(info[info_piece + 2 * index] == slot)
            def _():
                pltpu.make_async_copy(source.at[slot, :, rows, :], piece, osems.at[index]).start()

    @pl.when(info[info_member] == 0)
    def _():
        layers = Layers(info, (xb, x0, x1), (yb, yf), held, beside, below, sems)
        layers.start(1)
        layers.start(0)
        low, high = kept.at[0], kept.at[1]
        layers.apply(
            1, lambda plane, rows: arrived[plane, rows], subtract_into(high, w_high), True
        )
        start_pieces(kept, 1)
        layers.apply(0, sent(weights, 1, high), subtract_into(low, w_low), True)
        start_pieces(kept, 0)

    @pl.when(info[info_member] != 0)
    def _():
        start_pieces(field, 1)
        start_pieces(field, 0)

    for index, piece in enumerate((p0, p1, p2, p3)):
        part = kept.at[0, :, pl.ds(0, piece.shape[1]), :]
        pltpu.make_async_copy(part, piece, osems.at[index]).wait()


def on_device(background, src_pos, coupling, x_factor, y_factor):
    px_count = lax.axis_size("px")
    sec_index, own_x, own_y = (lax.axis_index(axis) for axis in ("sec", "px", "py"))
    group, member = sec_index // 2, sec_index % 2
    groups = lax.axis_size("sec") // 2
    order = y_factor.shape[3]
    field = background[:, 0]
    rows_here = field.shape[1]
    height = x_factor.shape[2]
    params = pltpu.CompilerParams(vmem_limit_bytes=vmem_bytes)
    rounds = [(0, 0), (1, 0), (1, 1), (0, 1)]

    def pairs(a, b):
        return [
            ((2 * x + c) * px_count + y, (2 * ((c + a) % 2) + x) * px_count + (y + b) % px_count)
            for x in range(groups)
            for c in range(2)
            for y in range(px_count)
            if (a, b, x) != (0, 0, c)
        ]

    def back_pairs(a, b):
        return [(target, source) for source, target in pairs(a, b)]

    own_source = src_pos[own_y * groups * px_count + group * px_count + own_x]
    plane_cells = x_factor.shape[3] * order
    layer = own_source // plane_cells
    remainder = own_source % plane_cells
    py_count = lax.axis_size("py")
    entries = [
        jnp.where(layer // 2 == member, layer % 2, -1),
        remainder // order,
        remainder % order,
        member,
    ]
    for a, b in rounds:
        entries += [(group + a) % 2, (own_x - b) % px_count]
    entries += [group, (group + 1) % 2, own_x, (own_x + 1) % 2]
    pair = own_y // 2 * 2
    entries += [own_y, pair + (own_y + 1) % 2, (own_y + 2) % 4, (pair + 2) % 4 + (own_y + 1) % 2]
    entries += [group == member]
    info = jnp.stack([jnp.asarray(entry, jnp.int32) for entry in entries])

    sends_to = jnp.stack(
        [((member + a) % 2) * px_count + (own_x + b) % px_count for a, b in rounds]
        + [own_y, group == member]
    ).astype(jnp.int32)
    piece_shape = jax.ShapeDtypeStruct((2, rows_here, order), bf16)
    shard = jnp.concatenate([x_factor[0], y_factor[0]], axis=0)
    blocks = jnp.broadcast_to(shard[None], (py_count,) + shard.shape)
    tall = height // 2
    packed = pl.pallas_call(
        pack_kernel,
        out_shape=[jax.ShapeDtypeStruct((2, rows_here + tall, order), bf16)] * len(rounds),
        in_specs=[in_smem] + [in_hbm] * 2,
        out_specs=[in_vmem] * len(rounds),
        scratch_shapes=[pltpu.SemaphoreType.DMA((len(rounds), 2))],
        compiler_params=params,
    )(sends_to, field, coupling[0].reshape(rows_here // tall, tall, order))
    pieces = [
        lax.ppermute(piece, ("sec", "px"), pairs(a, b)) for piece, (a, b) in zip(packed, rounds)
    ]
    blocks = lax.all_to_all(blocks, "py", split_axis=0, concat_axis=0, tiled=True)

    column_shape = jax.ShapeDtypeStruct((rows_here, 2 * order), bf16)
    turned_shape = jax.ShapeDtypeStruct((2 * order, rows_here), bf16)
    x_column, y_turned, rows_held = pl.pallas_call(
        column_kernel,
        out_shape=[
            column_shape,
            turned_shape,
            jax.ShapeDtypeStruct((len(rounds), 2, tall, order), bf16),
        ],
        in_specs=[in_smem, in_vmem] + [anywhere] * 5,
        out_specs=[in_vmem] * 3,
        scratch_shapes=[pltpu.SemaphoreType.DMA((len(rounds),))],
        compiler_params=params,
    )(info, blocks, packed[0], *pieces)
    rows_held = rows_held.reshape(len(rounds), height, order)

    def across(block, a):
        return lax.ppermute(block, ("sec", "px"), pairs(a, 0))

    def aside(block):
        return lax.ppermute(block, "px", [(y, (y + 1) % 2) for y in range(2)])

    def over_z(block, bit):
        return lax.ppermute(block, "py", [(z, z ^ bit) for z in range(py_count)])

    y_near = [across(y_turned, a) for a in range(2)]
    x_aside = aside(x_column)
    rows_next = over_z(rows_held, 1)
    rows_far = over_z(rows_held, 2)
    full_shape = jax.ShapeDtypeStruct((2, order, order), bf16)
    double_shape = jax.ShapeDtypeStruct((2, 2, order, order), bf16)
    rhs = pl.pallas_call(
        field_kernel,
        out_shape=double_shape,
        in_specs=[in_smem] + [anywhere] * 5,
        out_specs=in_vmem,
        scratch_shapes=[pltpu.SemaphoreType.DMA((len(rounds),))],
        compiler_params=params,
    )(info, packed[0], *pieces)
    x_both, y_both = pl.pallas_call(
        both_kernel,
        out_shape=[
            jax.ShapeDtypeStruct((2,) + one.shape, bf16) for one in (column_shape, turned_shape)
        ],
        in_specs=[in_smem] + [anywhere] * 6,
        out_specs=[in_vmem] * 2,
        scratch_shapes=[pltpu.SemaphoreType.DMA((4,))],
        compiler_params=params,
    )(info, x_column, x_aside, y_turned, *y_near, rhs)
    y_far = aside(y_both)
    x_across = [across(x_both, a) for a in range(2)]
    weight_sems = [pltpu.SemaphoreType.DMA((4, len(rounds)))]
    begun = pl.pallas_call(
        weight_kernel,
        out_shape=full_shape,
        in_specs=[in_smem] + [anywhere] * 3,
        out_specs=in_vmem,
        scratch_shapes=weight_sems,
        compiler_params=params,
        cost_estimate=pl.CostEstimate(
            flops=10**10, bytes_accessed=2**21, transcendentals=0
        ),
    )(info, rows_held, rows_next, rows_far)
    rows_after = pl.pallas_call(
        after_kernel,
        out_shape=jax.ShapeDtypeStruct(rows_next.shape, bf16),
        in_specs=[anywhere] * 2,
        out_specs=in_vmem,
        scratch_shapes=[pltpu.SemaphoreType.DMA(())],
        compiler_params=params,
    )(rows_next, x_both)
    weights = pl.pallas_call(
        last_weight_kernel,
        out_shape=full_shape,
        in_specs=[in_smem] + [anywhere] * 2,
        out_specs=anywhere,
        scratch_shapes=weight_sems,
        input_output_aliases={2: 0},
        compiler_params=params,
    )(info, over_z(rows_after, 2), begun)
    layers = (info, x_both, *x_across, y_both, y_far, weights)
    layer_specs = [in_smem] + [anywhere] * 3 + [in_vmem] * 3
    solver_scratch = [
        pltpu.VMEM((2, order, 2 * order), bf16),
        pltpu.VMEM((2 * order, 2 * order), bf16),
        pltpu.VMEM((2 * order, 2 * order), bf16),
        pltpu.SemaphoreType.DMA((2, 2)),
    ]

    def cost(solves):
        return pl.CostEstimate(
            flops=solves * 16 * order**3, bytes_accessed=16 * order**2 * 2, transcendentals=0
        )

    w_low, w_high = pl.pallas_call(
        first_kernel,
        out_shape=[full_shape] * 2,
        in_specs=layer_specs + [in_vmem],
        out_specs=[in_vmem] * 2,
        scratch_shapes=solver_scratch,
        compiler_params=params,
        cost_estimate=cost(2),
    )(*layers, rhs)

    up = [(2 * x, 2 * x + 1) for x in range(groups)]
    incoming = lax.ppermute(w_high, "sec", up)
    solved, back = pl.pallas_call(
        last_kernel,
        out_shape=[double_shape, full_shape],
        in_specs=layer_specs + [in_vmem] * 2,
        out_specs=[in_vmem] * 2,
        scratch_shapes=[pltpu.VMEM((2, order, order), bf16)] + solver_scratch,
        compiler_params=params,
        cost_estimate=cost(3),
    )(*layers, rhs, incoming)

    down = [(target, source) for source, target in up]
    incoming = lax.ppermute(back, "sec", down)
    results = pl.pallas_call(
        back_kernel,
        out_shape=[piece_shape] * len(rounds),
        in_specs=layer_specs + [in_vmem] * 3 + [anywhere],
        out_specs=[anywhere] * len(rounds),
        scratch_shapes=[pltpu.VMEM((2, 2, order, order), bf16)]
        + solver_scratch
        + [pltpu.SemaphoreType.DMA((len(rounds),))],
        compiler_params=params,
        cost_estimate=cost(2),
    )(*layers, w_low, w_high, incoming, solved)
    received = [
        lax.ppermute(piece, ("sec", "px"), back_pairs(a, b)) for piece, (a, b) in zip(results, rounds)
    ]
    output = pl.pallas_call(
        unpack_kernel,
        out_shape=jax.ShapeDtypeStruct(field.shape, bf16),
        in_specs=[in_smem] + [anywhere] * (len(rounds) + 1),
        out_specs=anywhere,
        scratch_shapes=[pltpu.SemaphoreType.DMA((len(rounds),))],
        compiler_params=params,
    )(sends_to, results[0], *received)
    return output[:, None]


def chip_plan_fits(mesh):
    return mesh.shape["sec"] == 4 and mesh.shape["px"] == 2 and mesh.shape["py"] == 4


def solution(mesh):
    placed = (
        P(None, "sec", "px", "py"),
        P(),
        P("sec", "px", None),
        P("sec", None, ("px", "py"), None),
        P("sec", None, ("px", "py"), None),
    )
    return jax.shard_map(
        on_device if chip_plan_fits(mesh) else on_device_by_layer,
        mesh=mesh,
        in_specs=placed,
        out_specs=P(None, "sec", "px", "py"),
        check_vma=False,
    )
```
